32 devices in a mesh: side: 2 (over core), dp: 4 (over z), tp: 4 (over y, x).
Axes of the slice: x: 2, y: 2, z: 4, core: 2. Of those that a mesh axis runs over, the one named last changes fastest.
Arguments:
- prompt_keys: bfloat16 [8, 2048, 1024], P(('side', 'dp'), None, 'tp'), may hold values from -6 to 6
- prompt_values: bfloat16 [8, 2048, 1024], P(('side', 'dp'), None, 'tp'), may hold values from -6 to 6
- prompt_lengths: int32 [8], replicated, may hold values from 512 to 2048
- assignment: int32 [8, 1], replicated, may hold values from 0 to 3; in each aligned block of 8 rows (0 to 7, 8 to 15, ...) at most 4 rows name the same one
- new_queries: bfloat16 [2, 8, 8192], P(None, None, 'tp'), may hold values from -576 to 576
- incoming_token_keys: bfloat16 [2, 8, 1024], P(None, None, 'tp'), may hold values from -6 to 6
- incoming_token_values: bfloat16 [2, 8, 1024], P(None, None, 'tp'), may hold values from -6 to 6
- stored_keys: bfloat16 [4, 4096, 1024], P('dp', 'side', 'tp'), may hold values from -6 to 6
- stored_values: bfloat16 [4, 4096, 1024], P('dp', 'side', 'tp'), may hold values from -6 to 6
- resident_lengths: int32 [4], P('dp'), may hold values from 1024 to 4096
- resident_queries: bfloat16 [2, 4, 8192], P(None, 'dp', 'tp'), may hold values from -576 to 576
- stored_token_keys: bfloat16 [2, 4, 1024], P(None, 'dp', 'tp'), may hold values from -6 to 6
- stored_token_values: bfloat16 [2, 4, 1024], P(None, 'dp', 'tp'), may hold values from -6 to 6
Outputs:
- resident_out: bfloat16 [2, 4, 8192], P(None, 'dp', 'tp')
- new_out: bfloat16 [2, 8, 8192], P(None, None, 'tp')
- incoming_keys: bfloat16 [16, 2048, 1024], P('dp', 'side', 'tp')
- incoming_values: bfloat16 [16, 2048, 1024], P('dp', 'side', 'tp')
The draws below stay inside these ranges and needn't reach their ends.
Inputs may be any that keep to these rules, and one draw needn't show every extreme that they name: `assignment`: no decode group takes more than 4 new requests, and some group takes exactly 4.
All inputs are finite; a program needn't handle non-finite values.
Results may differ from the reference program's by a relative error of at most 0.0055.
Values may be sent and summed in bfloat16 or wider, within the bound.
No kernel may reach another device: no remote copies, remote signals or barrier semaphores. Data moves between devices by JAX's collectives and lax.ppermute only.
A program may use at most 64 MiB of HBM per device.

```python
import math
import jax
import jax.numpy as jnp
import numpy as np
from jax import lax

QUERY_HEADS = 64
KEY_VALUE_HEADS = 8
HEAD_WIDTH = 128
CONTEXT_LENGTH = 4096
CAP = 4
PROMPT_LENGTH = 2048
DECODE_STEPS = 2
RESIDENT_COUNT = 4
NEW_REQUESTS = 8
SLOT_COUNT = 16
N_DP = 4


def ragged_lengths(key, row_count, longest):
    key_draw, key_top, key_low = jax.random.split(key, 3)
    lengths_raw = jax.random.randint(key_draw, (row_count,), longest // 4, longest + 1, dtype=jnp.int32)
    top_slot = jax.random.randint(key_top, (), 0, row_count, dtype=jnp.int32)
    low_slot = (top_slot + 1 + jax.random.randint(key_low, (), 0, row_count - 1, dtype=jnp.int32)) % row_count
    return lengths_raw.at[top_slot].set(longest).at[low_slot].set(longest // 4)


def query_rows(key, request_count, largest):
    key_base, key_scale = jax.random.split(key)
    base = jnp.clip(jax.random.normal(key_base, (DECODE_STEPS, request_count, QUERY_HEADS, HEAD_WIDTH), jnp.float32), -6.0, 6.0)
    factor = jnp.exp(jax.random.uniform(key_scale, (DECODE_STEPS, request_count, QUERY_HEADS, 1), jnp.float32, 0.0, math.log(largest)))
    return (base * factor).reshape(DECODE_STEPS, request_count, QUERY_HEADS * HEAD_WIDTH)


def draw_prompt_lengths(key, part):
    key = jax.random.fold_in(key, 11)
    return ragged_lengths(key, NEW_REQUESTS, PROMPT_LENGTH)


def draw_resident_lengths(key, part):
    key = jax.random.fold_in(key, 17)
    return ragged_lengths(key, RESIDENT_COUNT, CONTEXT_LENGTH)


def draw_new_queries(key, part):
    key = jax.random.fold_in(key, 23)
    return query_rows(key, NEW_REQUESTS, 1.0).astype(jnp.bfloat16)


def draw_resident_queries(key, part):
    key = jax.random.fold_in(key, 29)
    return query_rows(key, RESIDENT_COUNT, 1.0).astype(jnp.bfloat16)


def levels(rng, extent, pieces, least, top_value):
    gain, own = 1.0, jax.random.fold_in(rng, 6)
    for axis_at, parts in pieces:
        steps = jnp.exp(jax.random.uniform(jax.random.fold_in(own, axis_at), (parts,), jnp.float32, least / len(pieces), top_value / len(pieces)))
        gain = gain * jnp.repeat(steps, extent[axis_at] // parts).reshape([-1 if axis == axis_at else 1 for axis in range(len(extent))])
    return gain


def assign_block(own_key, own, number, rows, amount, top, limit, skew):
    order = jax.random.permutation(own_key, amount)
    heavy_load, common = load_shares(amount, rows * top, limit, skew, True), load_shares(amount, rows * top, limit, skew, False)
    places = jnp.arange(amount)

    def named(sizes, rotation):
        used = int((sizes > 0).sum())
        fixed = max(1, used // 4)
        shifted = fixed + (places - fixed + rotation * (used - fixed)) % max(1, amount - fixed)
        return jnp.zeros((amount,), jnp.int32).at[order[jnp.where(places < fixed, places, shifted)]].set(jnp.asarray(sizes, jnp.int32))

    sizes = jnp.where(number % 4 == 0, named(heavy_load, number // 4), named(common, number - number // 4 - 1))
    mixed = jax.random.permutation(jax.random.fold_in(own, 3), amount)
    source_of, receiver = mixed[0:amount // 2 * 2:2], mixed[1:amount // 2 * 2:2]
    room = jnp.minimum(sizes[source_of] - 1, limit - sizes[receiver]) // 2
    room = jnp.where((source_of == order[0]) | (receiver == order[0]) | (sizes[receiver] == 0), 0, jnp.maximum(room, 0))
    shifted = jax.random.randint(jax.random.fold_in(own, 4), (amount // 2,), 0, 1 << 20) % (room + 1)
    sizes = sizes.at[source_of].add(-shifted).at[receiver].add(shifted)
    items = jnp.searchsorted(jnp.cumsum(sizes), jnp.arange(rows * top), side="right").astype(jnp.int32)
    listing = items.reshape(top, rows).T
    listing = listing[jax.random.permutation(jax.random.fold_in(own, 1), rows)]
    rotation = jax.random.randint(jax.random.fold_in(own, 2), (rows, 1), 0, top)
    return jnp.take_along_axis(listing, (jnp.arange(top)[None, :] + rotation) % top, axis=1)


def load_shares(count, total, reach, slope, full):
    loads = [(1 << 20) // math.isqrt(grade ** slope) + 1 for grade in range(1, count + 1)]
    largest = reach if full else min(reach, max(-(-total // count), total * loads[0] // sum(loads)))
    least = 1 if total - largest >= count - 1 else 0
    given, rest = [largest] + [least] * (count - 1), total - largest - least * (count - 1)
    while rest > 0:
        movable = [i for i in range(1, count) if given[i] < largest] or [i for i in range(1, count) if given[i] < reach]
        whole, budget = sum([loads[i] for i in movable]), rest
        for i in movable:
            more = min(reach - given[i], max(1, budget * loads[i] // whole), rest)
            given[i] = given[i] + more
            rest = rest - more
    return np.array(given)


def noise(own_key, extent, width, limit, cuts=(), kind=jnp.bfloat16):
    factor_of = levels(own_key, extent, cuts, -0.22, 0.18) if cuts else 1.0
    result = jax.random.normal(own_key, extent, jnp.float32) * width * factor_of
    return jnp.minimum(jnp.maximum(result, -limit), limit).astype(kind)


def setup_inputs(seed: int = 0) -> dict:
    arg_keys = jax.random.split(jax.random.key(seed), 14)
    prompt_keys = noise(arg_keys[0], (NEW_REQUESTS, PROMPT_LENGTH, KEY_VALUE_HEADS * HEAD_WIDTH), 1.0, 6.0, ((0, 8), (2, 4)))
    prompt_values = noise(arg_keys[1], (NEW_REQUESTS, PROMPT_LENGTH, KEY_VALUE_HEADS * HEAD_WIDTH), 1.0, 6.0, ((0, 8), (2, 4)))
    prompt_lengths = draw_prompt_lengths(jax.random.fold_in(arg_keys[13], 71), 0)
    assignment_keys = jax.random.split(jax.random.fold_in(arg_keys[3], 1), NEW_REQUESTS // NEW_REQUESTS)
    assignment_turns = jax.random.permutation(jax.random.fold_in(arg_keys[3], 3), NEW_REQUESTS // NEW_REQUESTS)
    assignment = jax.vmap(lambda own, number: assign_block(jax.random.fold_in(arg_keys[3], 2), own, number, NEW_REQUESTS, N_DP, 1, CAP, 2))(assignment_keys, assignment_turns).reshape((NEW_REQUESTS, 1))
    new_queries = draw_new_queries(jax.random.fold_in(arg_keys[13], 71), 0)
    incoming_token_keys = noise(arg_keys[5], (DECODE_STEPS, NEW_REQUESTS, KEY_VALUE_HEADS * HEAD_WIDTH), 1.0, 6.0, ((2, 4),))
    incoming_token_values = noise(arg_keys[6], (DECODE_STEPS, NEW_REQUESTS, KEY_VALUE_HEADS * HEAD_WIDTH), 1.0, 6.0, ((2, 4),))
    stored_keys = noise(arg_keys[7], (RESIDENT_COUNT, CONTEXT_LENGTH, KEY_VALUE_HEADS * HEAD_WIDTH), 1.0, 6.0, ((0, 4), (1, 2), (2, 4)))
    stored_values = noise(arg_keys[8], (RESIDENT_COUNT, CONTEXT_LENGTH, KEY_VALUE_HEADS * HEAD_WIDTH), 1.0, 6.0, ((0, 4), (1, 2), (2, 4)))
    resident_lengths = draw_resident_lengths(jax.random.fold_in(arg_keys[13], 71), 0)
    resident_queries = draw_resident_queries(jax.random.fold_in(arg_keys[13], 71), 0)
    stored_token_keys = noise(arg_keys[11], (DECODE_STEPS, RESIDENT_COUNT, KEY_VALUE_HEADS * HEAD_WIDTH), 1.0, 6.0, ((1, 4), (2, 4)))
    stored_token_values = noise(arg_keys[12], (DECODE_STEPS, RESIDENT_COUNT, KEY_VALUE_HEADS * HEAD_WIDTH), 1.0, 6.0, ((1, 4), (2, 4)))
    return {"prompt_keys": prompt_keys, "prompt_values": prompt_values, "prompt_lengths": prompt_lengths, "assignment": assignment, "new_queries": new_queries, "incoming_token_keys": incoming_token_keys, "incoming_token_values": incoming_token_values, "stored_keys": stored_keys, "stored_values": stored_values, "resident_lengths": resident_lengths, "resident_queries": resident_queries, "stored_token_keys": stored_token_keys, "stored_token_values": stored_token_values}


masked_score = -1.0e30


def attend_one(single_query, key_matrix, value_matrix, usable):
    queries_per_group = QUERY_HEADS // KEY_VALUE_HEADS
    head_queries = single_query.astype(jnp.float32).reshape(KEY_VALUE_HEADS, queries_per_group, HEAD_WIDTH)
    head_keys = key_matrix.astype(jnp.float32).reshape(-1, KEY_VALUE_HEADS, HEAD_WIDTH)
    head_values = value_matrix.astype(jnp.float32).reshape(-1, KEY_VALUE_HEADS, HEAD_WIDTH)
    scores = jnp.einsum("kgd,nkd->kgn", head_queries, head_keys) * (HEAD_WIDTH ** -0.5)
    scores = jnp.where(usable, scores, masked_score)
    row_top = jnp.max(scores, axis=-1, keepdims=True)
    weight = jnp.where(usable, jnp.exp(scores - row_top), 0.0)
    row_sum = jnp.sum(weight, axis=-1, keepdims=True)
    rounded = lax.optimization_barrier(weight.astype(jnp.bfloat16)).astype(jnp.float32)
    mixed = jnp.einsum("kgn,nkd->kgd", rounded, head_values) / row_sum
    return mixed.reshape(QUERY_HEADS * HEAD_WIDTH)


def attend_request(items):
    query_steps, cache_keys, cache_values, length, step_keys, step_values = items
    key_matrix = jnp.concatenate([cache_keys, step_keys], axis=0)
    value_matrix = jnp.concatenate([cache_values, step_values], axis=0)
    cached = cache_keys.shape[0]
    position = jnp.arange(cached + DECODE_STEPS, dtype=jnp.int32)
    results = []
    for step_no in range(DECODE_STEPS):
        usable = jnp.where(position < cached, position < length, position - cached <= step_no)
        results.append(attend_one(query_steps[step_no], key_matrix, value_matrix, usable))
    return jnp.stack(results)


def attend_all(queries, cache_keys, cache_values, lengths, step_keys, step_values):
    order = (1, 0, 2)
    rows = lax.map(attend_request, (jnp.transpose(queries, order), cache_keys, cache_values, lengths, jnp.transpose(step_keys, order), jnp.transpose(step_values, order)))
    return jnp.transpose(rows, order).astype(jnp.bfloat16)


def reference(prompt_keys, prompt_values, prompt_lengths, assignment, new_queries, incoming_token_keys, incoming_token_values, stored_keys, stored_values, resident_lengths, resident_queries, stored_token_keys, stored_token_values):
    resident_out = attend_all(resident_queries, stored_keys, stored_values, resident_lengths, stored_token_keys, stored_token_values)
    new_out = attend_all(new_queries, prompt_keys, prompt_values, prompt_lengths, incoming_token_keys, incoming_token_values)
    routed = assignment[:, 0]
    request_ids = jnp.arange(routed.shape[0], dtype=jnp.int32)
    earlier_rows = (routed[:, None] == routed[None, :]) & (request_ids[None, :] < request_ids[:, None])
    slot_index = (routed * CAP + jnp.sum(earlier_rows, axis=1)).astype(jnp.int32)
    counted = jnp.arange(PROMPT_LENGTH, dtype=jnp.int32)[None, :] < prompt_lengths[:, None]
    retained_keys = jnp.where(counted[:, :, None], prompt_keys, jnp.zeros((), prompt_keys.dtype))
    retained_values = jnp.where(counted[:, :, None], prompt_values, jnp.zeros((), prompt_values.dtype))
    incoming_keys = jnp.zeros((SLOT_COUNT, PROMPT_LENGTH, KEY_VALUE_HEADS * HEAD_WIDTH), jnp.bfloat16).at[slot_index].set(retained_keys)
    incoming_values = jnp.zeros((SLOT_COUNT, PROMPT_LENGTH, KEY_VALUE_HEADS * HEAD_WIDTH), jnp.bfloat16).at[slot_index].set(retained_values)
    return (resident_out, new_out, incoming_keys, incoming_values)
```

```python
import jax
import jax.numpy as jnp
from jax import lax
from jax.experimental import pallas as pl
from jax.experimental.pallas import tpu as pltpu
from jax.sharding import PartitionSpec as P

HEAD_WIDTH = 128
CAP = 4
CHUNK = 256
UNROLL = 4
LAG = 2
LOW = -1e30

ANY = pl.BlockSpec(memory_space=pl.ANY)
VM = pl.BlockSpec(memory_space=pltpu.VMEM)
SM = pl.BlockSpec(memory_space=pltpu.SMEM)


def attend(q_ref, q_rows, k_ref, v_ref, tk_ref, tv_ref, first, length, tokens_on, emit):
    steps = q_ref.shape[0]
    keys, width = k_ref.shape
    heads_kv = width // HEAD_WIDTH
    members = q_ref.shape[1] // width
    rows = members * steps
    for kv in range(heads_kv):
        lanes = slice(kv * HEAD_WIDTH, (kv + 1) * HEAD_WIDTH)
        for g in range(members):
            at = (kv * members + g) * HEAD_WIDTH
            q_rows[g * steps:(g + 1) * steps, :] = q_ref[:, at:at + HEAD_WIDTH].astype(jnp.float32)
        q = q_rows[...].astype(jnp.bfloat16)
        dims = (((1,), (1,)), ((), ()))
        scale = HEAD_WIDTH ** -0.5
        scores = lax.dot_general(q, k_ref[:, lanes], dims, preferred_element_type=jnp.float32) * scale
        position = first + lax.broadcasted_iota(jnp.int32, (rows, keys), 1)
        usable = position < length
        scores = jnp.where(usable, scores, LOW)
        q32 = q.astype(jnp.float32)
        row_step = lax.rem(lax.broadcasted_iota(jnp.int32, (rows, 1), 0), steps)
        top = jnp.max(scores, axis=1, keepdims=True)
        extra = []
        for n in range(steps):
            s = jnp.sum(q32 * tk_ref[n:n + 1, lanes].astype(jnp.float32), axis=1, keepdims=True) * scale
            on = (row_step >= n) & tokens_on
            s = jnp.where(on, s, LOW)
            extra.append((on, s))
            top = jnp.maximum(top, s)
        weight = jnp.where(usable, jnp.exp(scores - top), 0.0)
        total = jnp.sum(weight, axis=1, keepdims=True)
        acc = lax.dot_general(
            weight.astype(jnp.bfloat16), v_ref[:, lanes], (((1,), (0,)), ((), ())),
            preferred_element_type=jnp.float32,
        )
        for n, (on, s) in enumerate(extra):
            w = jnp.where(on, jnp.exp(s - top), 0.0)
            total = total + w
            acc = acc + w.astype(jnp.bfloat16).astype(jnp.float32) * tv_ref[n:n + 1, lanes].astype(jnp.float32)
        emit(kv, top, total, acc)


def attention_kernel(
    info, rq, rk, rv, rtk, rtv, nq, nk, nv, ntk, ntv, part, own_out, q_rows, o_rows
):
    steps, members_width = rq.shape
    width = rk.shape[1]
    members = members_width // width
    rows = members * steps

    def emit_part(kv, top, total, acc):
        at = slice(kv * rows, (kv + 1) * rows)
        part[at, 0:HEAD_WIDTH] = acc
        part[at, HEAD_WIDTH:2 * HEAD_WIDTH] = jnp.broadcast_to(top, (rows, HEAD_WIDTH))
        part[at, 2 * HEAD_WIDTH:] = jnp.broadcast_to(total, (rows, HEAD_WIDTH))

    attend(rq, q_rows, rk, rv, rtk, rtv, info[1], info[0], info[2] == 1, emit_part)

    def emit_out(kv, top, total, acc):
        o_rows[...] = acc / total
        for g in range(members):
            at = (kv * members + g) * HEAD_WIDTH
            own_out[:, at:at + HEAD_WIDTH] = o_rows[g * steps:(g + 1) * steps, :]

    attend(nq, q_rows, nk, nv, ntk, ntv, 0, info[3], info[3] >= 0, emit_out)


def resident_kernel(a, b, out, o_rows):
    steps = out.shape[0]
    heads = out.shape[1] // HEAD_WIDTH
    w = HEAD_WIDTH
    top = jnp.maximum(a[:, w:2 * w], b[:, w:2 * w])
    ga = jnp.exp(a[:, w:2 * w] - top)
    gb = jnp.exp(b[:, w:2 * w] - top)
    o_rows[...] = (a[:, 0:w] * ga + b[:, 0:w] * gb) / (a[:, 2 * w:] * ga + b[:, 2 * w:] * gb)
    for h in range(heads):
        out[:, h * w:(h + 1) * w] = o_rows[h * steps:(h + 1) * steps, :].astype(out.dtype)


def link_plan(src, goal, count, links, ahead):
    link = jnp.arange(links, dtype=jnp.int32)[:, None]
    cross = (src[None, :] <= link) & (goal[None, :] > link)
    counts = jnp.where(cross[None], count[:, None, :], 0)
    base = jnp.sum(jnp.where(ahead[None, None], counts[:, :, :, None], 0), axis=2)
    load = jnp.sum(counts, axis=2)
    start = [jnp.zeros_like(load[:, 0])]
    for d in range(1, links):
        both = (cross[d - 1] & cross[d])[None] & (count > 0)
        gap = jnp.where(both, base[:, d - 1] - base[:, d] + (start[-1] + LAG)[:, None], 0)
        start.append(jnp.maximum(jnp.max(gap, axis=1), 0))
    start = jnp.stack(start, axis=1)
    last = jnp.max(jnp.where(load > 0, load + start, 0))
    return cross, base, counts, start, last


def step_tables(side, me, dp, half, ring_chunks, steps_max, lengths, goal, slot):
    request_count = lengths.shape[0]
    ids = jnp.arange(request_count, dtype=jnp.int32)
    src = ids % dp
    rows = jnp.clip(lengths[None, :] - half * jnp.arange(2, dtype=jnp.int32)[:, None], 0, half)
    count = (rows + CHUNK - 1) // CHUNK
    times = jnp.arange(steps_max, dtype=jnp.int32)[:, None]
    tables, lasts = [], []
    for flip in (False, True):
        s, g, m = (dp - 1 - src, dp - 1 - goal, dp - 1 - me) if flip else (src, goal, me)
        ahead = (g[:, None] > g[None, :]) | (
            (g[:, None] == g[None, :])
            & ((s[:, None] > s[None, :]) | ((s[:, None] == s[None, :]) & (ids[:, None] < ids[None, :])))
        )
        cross, base, counts, start, last = link_plan(s, g, count, dp - 1, ahead)
        lasts.append(last)
        base, counts, start = base[side], counts[side], start[side]

        def at(link):
            on = (link >= 0) & (link < dp - 1)
            link = jnp.clip(link, 0, dp - 2)
            p = times - start[link]
            c = p - base[link][None, :]
            hit = on & (c >= 0) & (c < counts[link][None, :])
            return p, c, hit

        def pick(hit, value):
            return jnp.sum(jnp.where(hit, value + 1, 0), axis=1) - 1

        p, c, hit = at(m)
        own = jnp.where(ids // dp == side, 0, half)[None, :] + c * CHUNK
        ring = 2 * half + (p % ring_chunks) * CHUNK
        send = pick(hit, jnp.where((s == m)[None, :], own, ring))
        next_base = base[jnp.clip(m, 0, dp - 2)][None, :]
        p, c, hit = at(m - 1)
        ring = CAP * half + ((next_base + c) % ring_chunks) * CHUNK
        take = pick(hit, jnp.where((g == m)[None, :], slot[None, :] * half + c * CHUNK, ring))
        tables.append((send, take))
    table = jnp.stack([tables[0][0], tables[1][0], tables[0][1], tables[1][1]])
    return table, jnp.maximum(lasts[0], lasts[1])


def run_all(copies):
    for on, a, b, sem in copies:
        @pl.when(on)
        def _():
            pltpu.make_async_copy(a, b, sem).start()
    for on, a, b, sem in copies:
        @pl.when(on)
        def _():
            pltpu.make_async_copy(a, b, sem).wait()


def prepare(table, t, half, mine, other, ring, sends, sem):
    copies = []
    for j, send in enumerate(sends):
        code = table[j, t]
        row = lambda start: pl.ds(pl.multiple_of(start, CHUNK), CHUNK)
        own_row = jnp.clip(code, 0, half - CHUNK)
        other_row = jnp.clip(code - half, 0, half - CHUNK)
        ring_row = jnp.clip(code - 2 * half, 0, ring.shape[2] - CHUNK)
        copies.append(((code >= 0) & (code < half), mine.at[:, row(own_row)], send, sem.at[j, 0]))
        copies.append(((code >= half) & (code < 2 * half), other.at[:, row(other_row)], send, sem.at[j, 1]))
        copies.append((code >= 2 * half, ring.at[j, :, row(ring_row)], send, sem.at[j, 2]))
    run_all(copies)


def place(table, t, half, takes, ring, out_k, out_v, sem):
    copies = []
    for j, take in enumerate(takes):
        code = table[2 + j, t]
        slot = jnp.clip(code // half, 0, CAP - 1)
        row = pl.ds(pl.multiple_of(jnp.clip(code - slot * half, 0, half - CHUNK), CHUNK), CHUNK)
        ring_row = pl.ds(pl.multiple_of(jnp.clip(code - CAP * half, 0, ring.shape[2] - CHUNK), CHUNK), CHUNK)
        final = (code >= 0) & (code < CAP * half)
        copies.append((final, take.at[0], out_k.at[slot, row], sem.at[j, 0]))
        copies.append((final, take.at[1], out_v.at[slot, row], sem.at[j, 1]))
        copies.append((code >= CAP * half, take, ring.at[j, :, ring_row], sem.at[j, 2]))
    run_all(copies)


def first_kernel(table, home, mine, other, ok, ov, ring, s0, s1, s2, s3, out_k, out_v, sem):
    half = mine.shape[1]
    copies = []
    for j, source in enumerate((mine, other)):
        slot = home[j]
        to = jnp.clip(slot, 0, CAP - 1)
        copies.append((slot >= 0, source.at[0], out_k.at[to], sem.at[2 + j, 0]))
        copies.append((slot >= 0, source.at[1], out_v.at[to], sem.at[2 + j, 1]))
    prepare(table, 0, half, mine, other, ring, (s0, s1), sem)
    prepare(table, 1, half, mine, other, ring, (s2, s3), sem)
    run_all(copies)


def step_kernel(table, now, mine, other, take_r, take_l, ring_in, ok, ov, send_r, send_l, ring, out_k, out_v, sem):
    half = mine.shape[1]
    t = now[0]
    place(table, t, half, (take_r, take_l), ring, out_k, out_v, sem)
    prepare(table, t + LAG, half, mine, other, ring, (send_r, send_l), sem)


def body(
    prompt_keys,
    prompt_values,
    prompt_lengths,
    assignment,
    new_queries,
    incoming_token_keys,
    incoming_token_values,
    stored_keys,
    stored_values,
    resident_lengths,
    resident_queries,
    stored_token_keys,
    stored_token_values,
):
    step_count = resident_queries.shape[0]
    side = lax.axis_index("side")
    me = lax.axis_index("dp")
    dp = lax.axis_size("dp")
    owner = side * dp + me
    request_count = prompt_lengths.shape[0]
    prompt_len, width = prompt_keys.shape[1:]
    query_width = new_queries.shape[2]
    half = prompt_len // 2
    bf16, f32, i32 = jnp.bfloat16, jnp.float32, jnp.int32
    swap = [(0, 1), (1, 0)]

    own_length = lax.dynamic_slice_in_dim(prompt_lengths, owner, 1, 0)[0]

    def masked_half(which):
        first = which * half
        counted = (first + jnp.arange(half, dtype=i32))[:, None] < own_length
        return jnp.stack([
            jnp.where(counted, lax.dynamic_slice_in_dim(a[0], first, half, 0), jnp.zeros((), a.dtype))
            for a in (prompt_keys, prompt_values)
        ])

    other = lax.ppermute(masked_half(1 - side), "side", swap)
    mine = masked_half(side)

    goal = assignment[:, 0]
    ids = jnp.arange(request_count, dtype=i32)
    slot = jnp.sum((goal[:, None] == goal[None, :]) & (ids[None, :] < ids[:, None]), axis=1, dtype=i32)
    most = half // CHUNK
    ring_chunks = 2 * most + 2 * LAG
    steps_max = request_count * most + LAG * dp + 2 * UNROLL + 2 * LAG
    table, last = step_tables(side, me, dp, half, ring_chunks, steps_max, prompt_lengths, goal, slot)
    stays = jnp.where((ids % dp == me) & (goal == me), slot, -1)
    home = jnp.stack([
        lax.dynamic_index_in_dim(stays, side * dp + me, 0, False),
        lax.dynamic_index_in_dim(stays, (1 - side) * dp + me, 0, False),
    ])

    chunk = jax.ShapeDtypeStruct((2, CHUNK, width), bf16)
    slots = jax.ShapeDtypeStruct((CAP, half, width), bf16)
    ring_shape = jax.ShapeDtypeStruct((2, 2, ring_chunks * CHUNK, width), bf16)
    out_k = jnp.zeros(slots.shape, bf16)
    out_v = jnp.zeros(slots.shape, bf16)
    ring = jnp.zeros(ring_shape.shape, bf16)
    s0, s1, s2, s3, out_k, out_v = pl.pallas_call(
        first_kernel,
        out_shape=(chunk, chunk, chunk, chunk, slots, slots),
        in_specs=[SM, SM, ANY, ANY, ANY, ANY, ANY],
        out_specs=[ANY] * 6,
        scratch_shapes=[pltpu.SemaphoreType.DMA((4, 3))],
        input_output_aliases={4: 4, 5: 5},
    )(table, home, mine, other, out_k, out_v, ring)

    to_right = [(i, i + 1) for i in range(dp - 1)]
    to_left = [(i + 1, i) for i in range(dp - 1)]

    def cross(send_r, send_l):
        return lax.ppermute(send_r, "dp", to_right), lax.ppermute(send_l, "dp", to_left)

    def step(t, takes, ring, out_k, out_v):
        return pl.pallas_call(
            step_kernel,
            out_shape=(chunk, chunk, ring_shape, slots, slots),
            in_specs=[SM, SM] + [ANY] * 7,
            out_specs=[ANY] * 5,
            scratch_shapes=[pltpu.SemaphoreType.DMA((2, 3))],
            input_output_aliases={6: 2, 7: 3, 8: 4},
        )(table, jnp.reshape(t, (1,)), mine, other, *takes, ring, out_k, out_v)

    def turn(state):
        t, a, b, ring, out_k, out_v = state
        for i in range(UNROLL):
            got = cross(*a)
            new_r, new_l, ring, out_k, out_v = step(t + i, got, ring, out_k, out_v)
            a, b = b, (new_r, new_l)
        return t + UNROLL, a, b, ring, out_k, out_v

    state = turn((jnp.zeros((), i32), (s0, s1), (s2, s3), ring, out_k, out_v))

    tied = lax.optimization_barrier((s0, new_queries, resident_queries))
    nq, rq = tied[1], tied[2]
    info = jnp.stack([resident_lengths[0], side * stored_keys.shape[1], side, own_length, owner]).astype(i32)
    own_query = lax.dynamic_index_in_dim(nq, owner, 1, False)
    own_tk = lax.dynamic_index_in_dim(incoming_token_keys, owner, 1, False)
    own_tv = lax.dynamic_index_in_dim(incoming_token_values, owner, 1, False)
    rows = step_count * query_width // HEAD_WIDTH
    rows_kv = step_count * query_width // width
    part, own_out = pl.pallas_call(
        attention_kernel,
        out_shape=(
            jax.ShapeDtypeStruct((rows, 3 * HEAD_WIDTH), f32),
            jax.ShapeDtypeStruct((step_count, query_width), f32),
        ),
        in_specs=[SM] + [VM] * 10,
        out_specs=[VM, VM],
        scratch_shapes=[pltpu.VMEM((rows_kv, HEAD_WIDTH), f32), pltpu.VMEM((rows_kv, HEAD_WIDTH), f32)],
        compiler_params=pltpu.CompilerParams(vmem_limit_bytes=32 << 20),
    )(
        info,
        rq[:, 0], stored_keys[0], stored_values[0], stored_token_keys[:, 0], stored_token_values[:, 0],
        own_query, prompt_keys[0], prompt_values[0], own_tk, own_tv,
    )
    part_other = lax.ppermute(part, "side", swap)
    resident_out = pl.pallas_call(
        resident_kernel,
        out_shape=jax.ShapeDtypeStruct((step_count, query_width), bf16),
        in_specs=[VM, VM],
        out_specs=VM,
        scratch_shapes=[pltpu.VMEM((rows, HEAD_WIDTH), f32)],
    )(part, part_other)[:, None, :]

    state = lax.while_loop(lambda state: state[0] < last, turn, state)
    out_k, out_v = state[4], state[5]
    own_out = own_out.astype(bf16)[:, None, :]
    own_out, out_k, out_v = lax.optimization_barrier((own_out, out_k, out_v))
    new_out = lax.all_gather(own_out, ("side", "dp"), axis=1, tiled=True)
    return (resident_out, new_out, out_k, out_v)


def solution(mesh):
    placed = (
        P(("side", "dp"), None, "tp"),
        P(("side", "dp"), None, "tp"),
        P(),
        P(),
        P(None, None, "tp"),
        P(None, None, "tp"),
        P(None, None, "tp"),
        P("dp", "side", "tp"),
        P("dp", "side", "tp"),
        P("dp"),
        P(None, "dp", "tp"),
        P(None, "dp", "tp"),
        P(None, "dp", "tp"),
    )
    return jax.shard_map(
        body,
        mesh=mesh,
        in_specs=placed,
        out_specs=(
            P(None, "dp", "tp"),
            P(None, None, "tp"),
            P("dp", "side", "tp"),
            P("dp", "side", "tp"),
        ),
        check_vma=False,
    )
```

```python
import functools

import jax
import jax.numpy as jnp
from jax import lax
from jax.experimental import pallas as pl
from jax.experimental.pallas import tpu as pltpu
from jax.sharding import PartitionSpec as P

HEAD_WIDTH = 128
CAP = 4
CHUNK = 256
UNROLL = 2
LAG = 2
LOW = -1e30

ANY = pl.BlockSpec(memory_space=pl.ANY)
VM = pl.BlockSpec(memory_space=pltpu.VMEM)
SM = pl.BlockSpec(memory_space=pltpu.SMEM)


def attend(q_ref, q_rows, k_ref, v_ref, tk_ref, tv_ref, first, length, tokens_on, emit):
    steps = q_ref.shape[0]
    keys, width = k_ref.shape
    heads_kv = width // HEAD_WIDTH
    members = q_ref.shape[1] // width
    rows = members * steps
    for kv in range(heads_kv):
        lanes = slice(kv * HEAD_WIDTH, (kv + 1) * HEAD_WIDTH)
        for g in range(members):
            at = (kv * members + g) * HEAD_WIDTH
            q_rows[g * steps:(g + 1) * steps, :] = q_ref[:, at:at + HEAD_WIDTH].astype(jnp.float32)
        q = q_rows[...].astype(jnp.bfloat16)
        dims = (((1,), (1,)), ((), ()))
        scale = HEAD_WIDTH ** -0.5
        scores = lax.dot_general(q, k_ref[:, lanes], dims, preferred_element_type=jnp.float32) * scale
        position = first + lax.broadcasted_iota(jnp.int32, (rows, keys), 1)
        usable = position < length
        scores = jnp.where(usable, scores, LOW)
        q32 = q.astype(jnp.float32)
        row_step = lax.rem(lax.broadcasted_iota(jnp.int32, (rows, 1), 0), steps)
        top = jnp.max(scores, axis=1, keepdims=True)
        extra = []
        for n in range(steps):
            s = jnp.sum(q32 * tk_ref[n:n + 1, lanes].astype(jnp.float32), axis=1, keepdims=True) * scale
            on = (row_step >= n) & tokens_on
            s = jnp.where(on, s, LOW)
            extra.append((on, s))
            top = jnp.maximum(top, s)
        weight = jnp.where(usable, jnp.exp(scores - top), 0.0)
        total = jnp.sum(weight, axis=1, keepdims=True)
        acc = lax.dot_general(
            weight.astype(jnp.bfloat16), v_ref[:, lanes], (((1,), (0,)), ((), ())),
            preferred_element_type=jnp.float32,
        )
        for n, (on, s) in enumerate(extra):
            w = jnp.where(on, jnp.exp(s - top), 0.0)
            total = total + w
            acc = acc + w.astype(jnp.bfloat16).astype(jnp.float32) * tv_ref[n:n + 1, lanes].astype(jnp.float32)
        emit(kv, top, total, acc)


def attention_kernel(
    info, rq, rk, rv, rtk, rtv, nq, nk, nv, ntk, ntv, part, own_out, q_rows, o_rows
):
    steps, members_width = rq.shape
    width = rk.shape[1]
    members = members_width // width
    rows = members * steps

    def emit_part(kv, top, total, acc):
        at = slice(kv * rows, (kv + 1) * rows)
        part[at, 0:HEAD_WIDTH] = acc
        part[at, HEAD_WIDTH:2 * HEAD_WIDTH] = jnp.broadcast_to(top, (rows, HEAD_WIDTH))
        part[at, 2 * HEAD_WIDTH:] = jnp.broadcast_to(total, (rows, HEAD_WIDTH))

    attend(rq, q_rows, rk, rv, rtk, rtv, info[1], info[0], info[2] == 1, emit_part)

    def emit_out(kv, top, total, acc):
        o_rows[...] = acc / total
        for g in range(members):
            at = (kv * members + g) * HEAD_WIDTH
            own_out[:, at:at + HEAD_WIDTH] = o_rows[g * steps:(g + 1) * steps, :]

    attend(nq, q_rows, nk, nv, ntk, ntv, 0, info[3], info[3] >= 0, emit_out)


def resident_kernel(a, b, out, o_rows):
    steps = out.shape[0]
    heads = out.shape[1] // HEAD_WIDTH
    w = HEAD_WIDTH
    top = jnp.maximum(a[:, w:2 * w], b[:, w:2 * w])
    ga = jnp.exp(a[:, w:2 * w] - top)
    gb = jnp.exp(b[:, w:2 * w] - top)
    o_rows[...] = (a[:, 0:w] * ga + b[:, 0:w] * gb) / (a[:, 2 * w:] * ga + b[:, 2 * w:] * gb)
    for h in range(heads):
        out[:, h * w:(h + 1) * w] = o_rows[h * steps:(h + 1) * steps, :].astype(out.dtype)


def split_kernel(info, keys, values, mine, away, stage, sem):
    half = mine.shape[1]
    side, length = info[0], info[1]
    for j, source in enumerate((keys, values)):
        pltpu.make_async_copy(source, stage.at[j], sem.at[j]).start()
    row = lax.broadcasted_iota(jnp.int32, (half, mine.shape[2]), 0)
    for j, source in enumerate((keys, values)):
        pltpu.make_async_copy(source, stage.at[j], sem.at[j]).wait()
        for which, target in ((1 - side, away), (side, mine)):
            first = pl.multiple_of(which * half, half)
            block = stage[j, pl.ds(first, half), :]
            target[j] = jnp.where(row < length - first, block, jnp.zeros_like(block))


def plan_kernel(dp, half, ring_chunks, info, lengths, goal, table, out_k, out_v, blank, sem):
    blank[...] = jnp.zeros_like(blank)
    fills = [
        pltpu.make_async_copy(blank, out.at[slot], sem.at[i, slot])
        for i, out in enumerate((out_k, out_v)) for slot in range(CAP)
    ]
    for fill in fills:
        fill.start()
    f32 = jnp.float32
    side, me = info[0], info[1]
    count = lengths.shape[1]
    wide = table.shape[1]
    id_row = lax.broadcasted_iota(jnp.int32, (count, count), 1).astype(f32)
    id_col = lax.broadcasted_iota(jnp.int32, (count, count), 0).astype(f32)
    eye = id_row == id_col

    def col(row):
        return jnp.sum(jnp.where(eye, jnp.broadcast_to(row, (count, count)), 0.0), axis=1, keepdims=True)

    ids = id_row[0:1]
    late = jnp.where(ids >= dp, 1.0, 0.0)
    src0 = ids - dp * late
    goal0 = goal[...].astype(f32)
    side_f, me_f = side.astype(f32), me.astype(f32)
    rows = jnp.clip(lengths[...].astype(f32) - half * side_f, 0.0, float(half))
    chunks = jnp.floor((rows + (CHUNK - 1)) * (1.0 / CHUNK))
    chunks_col = col(chunks)
    ids_col, late_col = col(ids), col(late)
    goal0_col = col(goal0)
    slot = jnp.sum(jnp.where((goal0_col == goal0) & (id_col < id_row), 1.0, 0.0), axis=0, keepdims=True)
    slot_col = col(slot)
    time = lax.broadcasted_iota(jnp.int32, (1, wide), 1).astype(f32)
    own_first = jnp.where(late_col == side_f, 0.0, float(half))
    steps = jnp.zeros((1, 1), f32)
    for flip in (False, True):
        s, g, m = (dp - 1 - src0, dp - 1 - goal0, dp - 1 - me_f) if flip else (src0, goal0, me_f)
        s_col, g_col = col(s), col(g)
        ahead = (g_col > g) | ((g_col == g) & ((s_col > s) | ((s_col == s) & (id_col < id_row))))
        crosses, bases, loads, starts = [], [], [], []
        for d in range(dp - 1):
            cross = (s <= d) & (g > d) & (chunks > 0)
            cross_col = (s_col <= d) & (g_col > d)
            base = jnp.sum(jnp.where(ahead & cross_col, chunks_col, 0.0), axis=0, keepdims=True)
            load = jnp.sum(jnp.where(cross, chunks, 0.0), axis=1, keepdims=True)
            start = jnp.zeros((1, 1), f32)
            if d > 0:
                gap = jnp.where(cross & crosses[-1], bases[-1] - base + starts[-1] + LAG, 0.0)
                start = jnp.maximum(jnp.max(gap, axis=1, keepdims=True), 0.0)
            steps = jnp.maximum(steps, jnp.where(load > 0, load + start, 0.0))
            crosses.append(cross)
            bases.append(base)
            loads.append(load)
            starts.append(start)

        def at(link):
            base, start, used = jnp.zeros((1, count), f32), jnp.zeros((1, 1), f32), jnp.zeros((1, count), f32)
            for d in range(dp - 1):
                base = jnp.where(link == d, bases[d], base)
                start = jnp.where(link == d, starts[d], start)
                used = jnp.where(link == d, jnp.where(crosses[d], chunks, 0.0), used)
            return col(base), start, col(used)

        def ring_row(p):
            return (p - ring_chunks * jnp.floor((p + 0.5) * (1.0 / ring_chunks))) * CHUNK

        def pick(hit, value):
            return (jnp.sum(jnp.where(hit, value + 1.0, 0.0), axis=0, keepdims=True) - 1.0).astype(jnp.int32)

        base, start, used = at(m)
        p = time - start
        c = p - base
        hit = (c >= 0) & (c < used)
        row = jnp.where(s_col == m, own_first + c * CHUNK, 2 * half + ring_row(p))
        r = 1 if flip else 0
        table[r:r + 1, :] = pick(hit, row)
        here, start, used = at(m - 1)
        c = time - start - here
        hit = (c >= 0) & (c < used)
        row = jnp.where(g_col == m, slot_col * half + c * CHUNK, CAP * half + ring_row(base + c))
        table[2 + r:3 + r, :] = pick(hit, row)
    stay = jnp.where((src0 == me_f) & (goal0 == me_f), slot + 1.0, 0.0)
    home = [
        jnp.sum(jnp.where(late == which, stay, 0.0), axis=1, keepdims=True) - 1.0 for which in (side_f, 1.0 - side_f)
    ]
    last = jnp.where(time == 0, steps, jnp.where(time == 1, home[0], home[1]))
    table[4:5, :] = last.astype(jnp.int32)
    table[5:8, :] = jnp.zeros((3, wide), jnp.int32)
    for fill in fills:
        fill.wait()


def run_all(copies):
    for on, a, b, sem in copies:
        @pl.when(on)
        def _():
            pltpu.make_async_copy(a, b, sem).start()
    for on, a, b, sem in copies:
        @pl.when(on)
        def _():
            pltpu.make_async_copy(a, b, sem).wait()


def rows_at(start, limit):
    return pl.ds(pl.multiple_of(jnp.clip(start, 0, limit - CHUNK), CHUNK), CHUNK)


def first_kernel(table, mine, other, ok, ov, s0, s1, s2, s3, own, ring, out_k, out_v, sem):
    half = mine.shape[1]
    copies = []
    for j, source in enumerate((mine, other)):
        slot = table[4, 1 + j]
        to = jnp.clip(slot, 0, CAP - 1)
        copies.append((slot >= 0, source.at[0], out_k.at[to], sem.at[j, 0]))
        copies.append((slot >= 0, source.at[1], out_v.at[to], sem.at[j, 1]))
        copies.append((slot >= -1, source, own.at[j], sem.at[j, 2]))
    for on, a, b, s in copies:
        @pl.when(on)
        def _():
            pltpu.make_async_copy(a, b, s).start()
    for t, sends in ((0, (s0, s1)), (1, (s2, s3))):
        for j, send in enumerate(sends):
            code = table[j, t]

            @pl.when((code >= 0) & (code < half))
            def _():
                send[...] = mine[:, rows_at(code, half), :]

            @pl.when((code >= half) & (code < 2 * half))
            def _():
                send[...] = other[:, rows_at(code - half, half), :]
    for on, a, b, s in copies:
        @pl.when(on)
        def _():
            pltpu.make_async_copy(a, b, s).wait()


def step_kernel(table, now, own, take_r, take_l, ring_in, ok, ov, send_r, send_l, ring, out_k, out_v, sem):
    half = own.shape[2]
    ring_rows = ring.shape[2]
    t = now[0]
    copies = []
    for j, take in enumerate((take_r, take_l)):
        code = table[2 + j, t]
        slot = jnp.clip(code // half, 0, CAP - 1)
        row = rows_at(code - slot * half, half)
        final = (code >= 0) & (code < CAP * half)
        copies.append((final, take.at[0], out_k.at[slot, row], sem.at[j, 0]))
        copies.append((final, take.at[1], out_v.at[slot, row], sem.at[j, 1]))
        copies.append((code >= CAP * half, take, ring.at[j, :, rows_at(code - CAP * half, ring_rows)], sem.at[j, 2]))
    run_all(copies)
    copies = []
    for j, send in enumerate((send_r, send_l)):
        code = table[j, t + LAG]
        which = jnp.clip(code // half, 0, 1)
        copies.append((
            (code >= 0) & (code < 2 * half), own.at[which, :, rows_at(code - which * half, half)], send, sem.at[j, 0]
        ))
        copies.append((code >= 2 * half, ring.at[j, :, rows_at(code - 2 * half, ring_rows)], send, sem.at[j, 1]))
    run_all(copies)


def body(
    prompt_keys,
    prompt_values,
    prompt_lengths,
    assignment,
    new_queries,
    incoming_token_keys,
    incoming_token_values,
    stored_keys,
    stored_values,
    resident_lengths,
    resident_queries,
    stored_token_keys,
    stored_token_values,
):
    step_count = resident_queries.shape[0]
    side = lax.axis_index("side")
    me = lax.axis_index("dp")
    dp = lax.axis_size("dp")
    owner = side * dp + me
    request_count = prompt_lengths.shape[0]
    prompt_len, width = prompt_keys.shape[1:]
    query_width = new_queries.shape[2]
    half = prompt_len // 2
    bf16, f32, i32 = jnp.bfloat16, jnp.float32, jnp.int32
    swap = [(0, 1), (1, 0)]

    own_length = lax.dynamic_index_in_dim(prompt_lengths, owner, 0, False)
    halves = jax.ShapeDtypeStruct((2, half, width), bf16)
    mine, away = pl.pallas_call(
        split_kernel,
        out_shape=(halves, halves),
        in_specs=[SM, ANY, ANY],
        out_specs=[VM, VM],
        scratch_shapes=[pltpu.VMEM((2, prompt_len, width), bf16), pltpu.SemaphoreType.DMA((2,))],
        compiler_params=pltpu.CompilerParams(vmem_limit_bytes=16 << 20),
    )(jnp.stack([side, own_length]).astype(i32), prompt_keys[0], prompt_values[0])
    other = lax.ppermute(away, "side", swap)

    most = half // CHUNK
    ring_chunks = 2 * most + 2 * LAG
    steps_max = request_count * most + LAG * dp + 2 * UNROLL + 2 * LAG
    wide = -(-steps_max // 128) * 128
    slots = jax.ShapeDtypeStruct((CAP, half, width), bf16)
    table, out_k, out_v = pl.pallas_call(
        functools.partial(plan_kernel, dp, half, ring_chunks),
        out_shape=(jax.ShapeDtypeStruct((8, wide), i32), slots, slots),
        in_specs=[SM, VM, VM],
        out_specs=[VM, ANY, ANY],
        scratch_shapes=[pltpu.VMEM((half, width), bf16), pltpu.SemaphoreType.DMA((2, CAP))],
    )(
        jnp.stack([side, me]).astype(i32),
        jnp.reshape(prompt_lengths, (1, request_count)),
        jnp.reshape(assignment, (1, request_count)),
    )
    last = table[4, 0]

    chunk = jax.ShapeDtypeStruct((2, CHUNK, width), bf16)
    own_shape = jax.ShapeDtypeStruct((2, 2, half, width), bf16)
    ring_shape = jax.ShapeDtypeStruct((2, 2, ring_chunks * CHUNK, width), bf16)
    s0, s1, s2, s3, own, ring, out_k, out_v = pl.pallas_call(
        first_kernel,
        out_shape=(chunk, chunk, chunk, chunk, own_shape, ring_shape, slots, slots),
        in_specs=[SM, VM, VM, ANY, ANY],
        out_specs=[VM] * 4 + [ANY] * 4,
        scratch_shapes=[pltpu.SemaphoreType.DMA((2, 3))],
        input_output_aliases={3: 6, 4: 7},
        compiler_params=pltpu.CompilerParams(vmem_limit_bytes=16 << 20),
    )(table, mine, other, out_k, out_v)

    to_right = [(i, i + 1) for i in range(dp - 1)]
    to_left = [(i + 1, i) for i in range(dp - 1)]

    def cross(send_r, send_l):
        return lax.ppermute(send_r, "dp", to_right), lax.ppermute(send_l, "dp", to_left)

    def step(t, takes, ring, out_k, out_v):
        return pl.pallas_call(
            step_kernel,
            out_shape=(chunk, chunk, ring_shape, slots, slots),
            in_specs=[SM, SM, ANY, VM, VM, ANY, ANY, ANY],
            out_specs=[VM, VM, ANY, ANY, ANY],
            scratch_shapes=[pltpu.SemaphoreType.DMA((2, 3))],
            input_output_aliases={5: 2, 6: 3, 7: 4},
            compiler_params=pltpu.CompilerParams(vmem_limit_bytes=16 << 20),
        )(table, jnp.reshape(t, (1,)), own, *takes, ring, out_k, out_v)

    def turn(state):
        t, a, b, ring, out_k, out_v = state
        for i in range(UNROLL):
            got = cross(*a)
            new_r, new_l, ring, out_k, out_v = step(t + i, got, ring, out_k, out_v)
            a, b = b, (new_r, new_l)
        return t + UNROLL, a, b, ring, out_k, out_v

    state = turn((jnp.zeros((), i32), (s0, s1), (s2, s3), ring, out_k, out_v))

    tied = lax.optimization_barrier((s0, new_queries, resident_queries))
    nq, rq = tied[1], tied[2]
    info = jnp.stack([resident_lengths[0], side * stored_keys.shape[1], side, own_length, owner]).astype(i32)
    own_query = lax.dynamic_index_in_dim(nq, owner, 1, False)
    own_tk = lax.dynamic_index_in_dim(incoming_token_keys, owner, 1, False)
    own_tv = lax.dynamic_index_in_dim(incoming_token_values, owner, 1, False)
    rows = step_count * query_width // HEAD_WIDTH
    rows_kv = step_count * query_width // width
    part, own_out = pl.pallas_call(
        attention_kernel,
        out_shape=(
            jax.ShapeDtypeStruct((rows, 3 * HEAD_WIDTH), f32),
            jax.ShapeDtypeStruct((step_count, query_width), f32),
        ),
        in_specs=[SM] + [VM] * 10,
        out_specs=[VM, VM],
        scratch_shapes=[pltpu.VMEM((rows_kv, HEAD_WIDTH), f32), pltpu.VMEM((rows_kv, HEAD_WIDTH), f32)],
        compiler_params=pltpu.CompilerParams(vmem_limit_bytes=32 << 20),
    )(
        info,
        rq[:, 0], stored_keys[0], stored_values[0], stored_token_keys[:, 0], stored_token_values[:, 0],
        own_query, prompt_keys[0], prompt_values[0], own_tk, own_tv,
    )
    part_other = lax.ppermute(part, "side", swap)
    resident_out = pl.pallas_call(
        resident_kernel,
        out_shape=jax.ShapeDtypeStruct((step_count, query_width), bf16),
        in_specs=[VM, VM],
        out_specs=VM,
        scratch_shapes=[pltpu.VMEM((rows, HEAD_WIDTH), f32)],
    )(part, part_other)[:, None, :]

    state = lax.while_loop(lambda state: state[0] < last, turn, state)
    out_k, out_v = state[4], state[5]
    own_out = own_out.astype(bf16)[:, None, :]
    own_out, out_k, out_v = lax.optimization_barrier((own_out, out_k, out_v))
    new_out = lax.all_gather(own_out, ("side", "dp"), axis=1, tiled=True)
    return (resident_out, new_out, out_k, out_v)


def solution(mesh):
    placed = (
        P(("side", "dp"), None, "tp"),
        P(("side", "dp"), None, "tp"),
        P(),
        P(),
        P(None, None, "tp"),
        P(None, None, "tp"),
        P(None, None, "tp"),
        P("dp", "side", "tp"),
        P("dp", "side", "tp"),
        P("dp"),
        P(None, "dp", "tp"),
        P(None, "dp", "tp"),
        P(None, "dp", "tp"),
    )
    return jax.shard_map(
        body,
        mesh=mesh,
        in_specs=placed,
        out_specs=(
            P(None, "dp", "tp"),
            P(None, None, "tp"),
            P("dp", "side", "tp"),
            P("dp", "side", "tp"),
        ),
        check_vma=False,
    )
```

```python
import functools

import jax
import jax.numpy as jnp
from jax import lax
from jax.experimental import pallas as pl
from jax.experimental.pallas import tpu as pltpu
from jax.sharding import PartitionSpec as P

HEAD_WIDTH = 128
CAP = 4
CHUNK = 512
UNROLL = 2
LAG = 2
LOW = -1e30

HBM = pl.BlockSpec(memory_space=pltpu.HBM)
VM = pl.BlockSpec(memory_space=pltpu.VMEM)
SM = pl.BlockSpec(memory_space=pltpu.SMEM)


def attend(q_ref, q_rows, k_ref, v_ref, tk_ref, tv_ref, first, length, tokens_on, emit):
    steps = q_ref.shape[0]
    keys, width = k_ref.shape
    heads_kv = width // HEAD_WIDTH
    members = q_ref.shape[1] // width
    rows = members * steps
    for kv in range(heads_kv):
        lanes = slice(kv * HEAD_WIDTH, (kv + 1) * HEAD_WIDTH)
        for g in range(members):
            at = (kv * members + g) * HEAD_WIDTH
            q_rows[g * steps:(g + 1) * steps, :] = q_ref[:, at:at + HEAD_WIDTH].astype(jnp.float32)
        q = q_rows[...].astype(jnp.bfloat16)
        dims = (((1,), (1,)), ((), ()))
        scale = HEAD_WIDTH ** -0.5
        scores = lax.dot_general(q, k_ref[:, lanes], dims, preferred_element_type=jnp.float32) * scale
        position = first + lax.broadcasted_iota(jnp.int32, (rows, keys), 1)
        usable = position < length
        scores = jnp.where(usable, scores, LOW)
        q32 = q.astype(jnp.float32)
        row_step = lax.rem(lax.broadcasted_iota(jnp.int32, (rows, 1), 0), steps)
        top = jnp.max(scores, axis=1, keepdims=True)
        extra = []
        for n in range(steps):
            s = jnp.sum(q32 * tk_ref[n:n + 1, lanes].astype(jnp.float32), axis=1, keepdims=True) * scale
            on = (row_step >= n) & tokens_on
            s = jnp.where(on, s, LOW)
            extra.append((on, s))
            top = jnp.maximum(top, s)
        weight = jnp.where(usable, jnp.exp(scores - top), 0.0)
        total = jnp.sum(weight, axis=1, keepdims=True)
        acc = lax.dot_general(
            weight.astype(jnp.bfloat16), v_ref[:, lanes], (((1,), (0,)), ((), ())),
            preferred_element_type=jnp.float32,
        )
        for n, (on, s) in enumerate(extra):
            w = jnp.where(on, jnp.exp(s - top), 0.0)
            total = total + w
            acc = acc + w.astype(jnp.bfloat16).astype(jnp.float32) * tv_ref[n:n + 1, lanes].astype(jnp.float32)
        emit(kv, top, total, acc)


def attention_kernel(
    info, rq, rk, rv, rtk, rtv, nq, nk, nv, ntk, ntv, part, own_out, q_rows
):
    steps, members_width = rq.shape
    width = rk.shape[1]
    members = members_width // width
    rows = members * steps

    def emit_part(kv, top, total, acc):
        at = slice(kv * rows, (kv + 1) * rows)
        part[at, 0:HEAD_WIDTH] = acc
        part[at, HEAD_WIDTH:2 * HEAD_WIDTH] = jnp.broadcast_to(top, (rows, HEAD_WIDTH))
        part[at, 2 * HEAD_WIDTH:] = jnp.broadcast_to(total, (rows, HEAD_WIDTH))

    attend(rq, q_rows, rk, rv, rtk, rtv, info[1], info[0], info[2] == 1, emit_part)

    def emit_out(kv, top, total, acc):
        own_out[kv * rows:(kv + 1) * rows, :] = acc / total

    attend(nq, q_rows, nk, nv, ntk, ntv, 0, info[3], info[3] >= 0, emit_out)


def gather_outputs(own, dp):
    block = jnp.stack([own, lax.ppermute(own, "side", [(0, 1), (1, 0)])])
    if dp & (dp - 1):
        rest = [lax.ppermute(block, "dp", [((i + x) % dp, i) for i in range(dp)]) for x in range(1, dp)]
        return jnp.concatenate([block] + rest)
    reach = 1
    while reach < dp:
        block = jnp.concatenate([block, lax.ppermute(block, "dp", [(i, i ^ reach) for i in range(dp)])])
        reach *= 2
    return block


def finish_kernel(dp, steps, info, a, b, everyone, resident, new, o_rows):
    w = HEAD_WIDTH
    heads = resident.shape[2] // w
    top = jnp.maximum(a[:, w:2 * w], b[:, w:2 * w])
    ga = jnp.exp(a[:, w:2 * w] - top)
    gb = jnp.exp(b[:, w:2 * w] - top)
    o_rows[...] = (a[:, 0:w] * ga + b[:, 0:w] * gb) / (a[:, 2 * w:] * ga + b[:, 2 * w:] * gb)
    for n in range(steps):
        for h in range(heads):
            resident[n, :, h * w:(h + 1) * w] = o_rows[h * steps + n:h * steps + n + 1, :].astype(resident.dtype)
    side, me = info[0], info[1]
    count = everyone.shape[0]
    order = []
    for r in range(count):
        far = lax.bitwise_xor(me, r % dp) if dp & (dp - 1) == 0 else lax.rem(r % dp - me + dp, dp)
        order.append(far * 2 + lax.bitwise_xor(side, r // dp))
    at_row = lax.broadcasted_iota(jnp.int32, (count, w), 0)
    for n in range(steps):
        for h in range(heads):
            k = h * steps + n
            block = jnp.zeros((count, w), jnp.float32)
            for r in range(count):
                block = jnp.where(at_row == r, everyone[order[r], k:k + 1, :], block)
            new[n, :, h * w:(h + 1) * w] = block.astype(new.dtype)


def split_kernel(info, keys, values, mine, away, stage, sem):
    half = mine.shape[1]
    side, length = info[0], info[1]
    for j, source in enumerate((keys, values)):
        pltpu.make_async_copy(source, stage.at[j], sem.at[j]).start()
    row = lax.broadcasted_iota(jnp.int32, (half, mine.shape[2]), 0)
    for j, source in enumerate((keys, values)):
        pltpu.make_async_copy(source, stage.at[j], sem.at[j]).wait()
        for which, target in ((1 - side, away), (side, mine)):
            first = pl.multiple_of(which * half, half)
            block = stage[j, pl.ds(first, half), :]
            target[j] = jnp.where(row < length - first, block, jnp.zeros_like(block))


def plan_kernel(dp, half, ring_chunks, info, lengths, goal, table, out_k, out_v, blank, sem):
    blank[...] = jnp.zeros_like(blank)
    fills = [
        pltpu.make_async_copy(blank, out.at[slot], sem.at[i, slot])
        for i, out in enumerate((out_k, out_v)) for slot in range(CAP)
    ]
    for fill in fills:
        fill.start()
    f32 = jnp.float32
    side, me = info[0], info[1]
    count = lengths.shape[1]
    wide = table.shape[1]
    id_row = lax.broadcasted_iota(jnp.int32, (count, count), 1).astype(f32)
    id_col = lax.broadcasted_iota(jnp.int32, (count, count), 0).astype(f32)
    eye = id_row == id_col

    def col(row):
        return jnp.sum(jnp.where(eye, jnp.broadcast_to(row, (count, count)), 0.0), axis=1, keepdims=True)

    ids = id_row[0:1]
    late = jnp.where(ids >= dp, 1.0, 0.0)
    src0 = ids - dp * late
    goal0 = goal[...].astype(f32)
    side_f, me_f = side.astype(f32), me.astype(f32)
    rows = jnp.clip(lengths[...].astype(f32) - half * side_f, 0.0, float(half))
    chunks = jnp.floor((rows + (CHUNK - 1)) * (1.0 / CHUNK))
    chunks_col = col(chunks)
    ids_col, late_col = col(ids), col(late)
    goal0_col = col(goal0)
    slot = jnp.sum(jnp.where((goal0_col == goal0) & (id_col < id_row), 1.0, 0.0), axis=0, keepdims=True)
    slot_col = col(slot)
    time = lax.broadcasted_iota(jnp.int32, (1, wide), 1).astype(f32)
    own_first = jnp.where(late_col == side_f, 0.0, float(half))
    steps = jnp.zeros((1, 1), f32)
    for flip in (False, True):
        s, g, m = (dp - 1 - src0, dp - 1 - goal0, dp - 1 - me_f) if flip else (src0, goal0, me_f)
        s_col, g_col = col(s), col(g)
        ahead = (g_col > g) | ((g_col == g) & ((s_col > s) | ((s_col == s) & (id_col < id_row))))
        crosses, bases, loads, starts = [], [], [], []
        for d in range(dp - 1):
            cross = (s <= d) & (g > d) & (chunks > 0)
            cross_col = (s_col <= d) & (g_col > d)
            base = jnp.sum(jnp.where(ahead & cross_col, chunks_col, 0.0), axis=0, keepdims=True)
            load = jnp.sum(jnp.where(cross, chunks, 0.0), axis=1, keepdims=True)
            start = jnp.zeros((1, 1), f32)
            if d > 0:
                gap = jnp.where(cross & crosses[-1], bases[-1] - base + starts[-1] + LAG, 0.0)
                start = jnp.maximum(jnp.max(gap, axis=1, keepdims=True), 0.0)
            steps = jnp.maximum(steps, jnp.where(load > 0, load + start, 0.0))
            crosses.append(cross)
            bases.append(base)
            loads.append(load)
            starts.append(start)

        def at(link):
            base, start, used = jnp.zeros((1, count), f32), jnp.zeros((1, 1), f32), jnp.zeros((1, count), f32)
            for d in range(dp - 1):
                base = jnp.where(link == d, bases[d], base)
                start = jnp.where(link == d, starts[d], start)
                used = jnp.where(link == d, jnp.where(crosses[d], chunks, 0.0), used)
            return col(base), start, col(used)

        def ring_row(p):
            return (p - ring_chunks * jnp.floor((p + 0.5) * (1.0 / ring_chunks))) * CHUNK

        def pick(hit, value):
            return (jnp.sum(jnp.where(hit, value + 1.0, 0.0), axis=0, keepdims=True) - 1.0).astype(jnp.int32)

        base, start, used = at(m)
        p = time - start
        c = p - base
        hit = (c >= 0) & (c < used)
        row = jnp.where(s_col == m, own_first + c * CHUNK, 2 * half + ring_row(p))
        r = 1 if flip else 0
        table[r:r + 1, :] = pick(hit, row)
        here, start, used = at(m - 1)
        c = time - start - here
        hit = (c >= 0) & (c < used)
        row = jnp.where(g_col == m, slot_col * half + c * CHUNK, CAP * half + ring_row(base + c))
        table[2 + r:3 + r, :] = pick(hit, row)
    stay = jnp.where((src0 == me_f) & (goal0 == me_f), slot + 1.0, 0.0)
    home = [
        jnp.sum(jnp.where(late == which, stay, 0.0), axis=1, keepdims=True) - 1.0 for which in (side_f, 1.0 - side_f)
    ]
    last = jnp.where(time == 0, steps, jnp.where(time == 1, home[0], home[1]))
    table[4:5, :] = last.astype(jnp.int32)
    table[5:8, :] = jnp.zeros((3, wide), jnp.int32)
    for fill in fills:
        fill.wait()


def run_all(copies):
    for on, a, b, sem in copies:
        @pl.when(on)
        def _():
            pltpu.make_async_copy(a, b, sem).start()
    for on, a, b, sem in copies:
        @pl.when(on)
        def _():
            pltpu.make_async_copy(a, b, sem).wait()


def rows_at(start, limit):
    return pl.ds(pl.multiple_of(jnp.clip(start, 0, limit - CHUNK), CHUNK), CHUNK)


def first_kernel(table, mine, other, ok, ov, s0, s1, s2, s3, own, ring, out_k, out_v, sem):
    half = mine.shape[1]
    copies = []
    for j, source in enumerate((mine, other)):
        slot = table[4, 1 + j]
        to = jnp.clip(slot, 0, CAP - 1)
        copies.append((slot >= 0, source.at[0], out_k.at[to], sem.at[j, 0]))
        copies.append((slot >= 0, source.at[1], out_v.at[to], sem.at[j, 1]))
        copies.append((slot >= -1, source, own.at[j], sem.at[j, 2]))
    for on, a, b, s in copies:
        @pl.when(on)
        def _():
            pltpu.make_async_copy(a, b, s).start()
    for t, sends in ((0, (s0, s1)), (1, (s2, s3))):
        for j, send in enumerate(sends):
            code = table[j, t]

            @pl.when((code >= 0) & (code < half))
            def _():
                send[...] = mine[:, rows_at(code, half), :]

            @pl.when((code >= half) & (code < 2 * half))
            def _():
                send[...] = other[:, rows_at(code - half, half), :]
    for on, a, b, s in copies:
        @pl.when(on)
        def _():
            pltpu.make_async_copy(a, b, s).wait()


def step_kernel(table, now, own, take_r, take_l, ring_in, ok, ov, send_r, send_l, ring, out_k, out_v, sem):
    half = own.shape[2]
    ring_rows = ring.shape[2]
    t = now[0]
    copies = []
    for j, take in enumerate((take_r, take_l)):
        code = table[2 + j, t]
        slot = jnp.clip(code // half, 0, CAP - 1)
        row = rows_at(code - slot * half, half)
        final = (code >= 0) & (code < CAP * half)
        copies.append((final, take.at[0], out_k.at[slot, row], sem.at[j, 0]))
        copies.append((final, take.at[1], out_v.at[slot, row], sem.at[j, 1]))
        copies.append((code >= CAP * half, take, ring.at[j, :, rows_at(code - CAP * half, ring_rows)], sem.at[j, 2]))
    run_all(copies)
    copies = []
    for j, send in enumerate((send_r, send_l)):
        code = table[j, t + LAG]
        which = jnp.clip(code // half, 0, 1)
        copies.append((
            (code >= 0) & (code < 2 * half), own.at[which, :, rows_at(code - which * half, half)], send, sem.at[j, 0]
        ))
        copies.append((code >= 2 * half, ring.at[j, :, rows_at(code - 2 * half, ring_rows)], send, sem.at[j, 1]))
    run_all(copies)


def body(
    prompt_keys,
    prompt_values,
    prompt_lengths,
    assignment,
    new_queries,
    incoming_token_keys,
    incoming_token_values,
    stored_keys,
    stored_values,
    resident_lengths,
    resident_queries,
    stored_token_keys,
    stored_token_values,
):
    step_count = resident_queries.shape[0]
    side = lax.axis_index("side")
    me = lax.axis_index("dp")
    dp = lax.axis_size("dp")
    owner = side * dp + me
    request_count = prompt_lengths.shape[0]
    prompt_len, width = prompt_keys.shape[1:]
    query_width = new_queries.shape[2]
    half = prompt_len // 2
    bf16, f32, i32 = jnp.bfloat16, jnp.float32, jnp.int32
    swap = [(0, 1), (1, 0)]

    own_length = lax.dynamic_index_in_dim(prompt_lengths, owner, 0, False)
    halves = jax.ShapeDtypeStruct((2, half, width), bf16)
    mine, away = pl.pallas_call(
        split_kernel,
        out_shape=(halves, halves),
        in_specs=[SM, HBM, HBM],
        out_specs=[VM, VM],
        scratch_shapes=[pltpu.VMEM((2, prompt_len, width), bf16), pltpu.SemaphoreType.DMA((2,))],
        compiler_params=pltpu.CompilerParams(vmem_limit_bytes=16 << 20),
    )(jnp.stack([side, own_length]).astype(i32), prompt_keys[0], prompt_values[0])
    other = lax.ppermute(away, "side", swap)

    most = half // CHUNK
    ring_chunks = 2 * most + 2 * LAG
    steps_max = request_count * most + LAG * dp + 2 * UNROLL + 2 * LAG
    wide = -(-steps_max // 128) * 128
    slots = jax.ShapeDtypeStruct((CAP, half, width), bf16)
    table, out_k, out_v = pl.pallas_call(
        functools.partial(plan_kernel, dp, half, ring_chunks),
        out_shape=(jax.ShapeDtypeStruct((8, wide), i32), slots, slots),
        in_specs=[SM, VM, VM],
        out_specs=[VM, HBM, HBM],
        scratch_shapes=[pltpu.VMEM((half, width), bf16), pltpu.SemaphoreType.DMA((2, CAP))],
    )(
        jnp.stack([side, me]).astype(i32),
        jnp.reshape(prompt_lengths, (1, request_count)),
        jnp.reshape(assignment, (1, request_count)),
    )
    last = table[4, 0]

    chunk = jax.ShapeDtypeStruct((2, CHUNK, width), bf16)
    own_shape = jax.ShapeDtypeStruct((2, 2, half, width), bf16)
    ring_shape = jax.ShapeDtypeStruct((2, 2, ring_chunks * CHUNK, width), bf16)
    s0, s1, s2, s3, own, ring, out_k, out_v = pl.pallas_call(
        first_kernel,
        out_shape=(chunk, chunk, chunk, chunk, own_shape, ring_shape, slots, slots),
        in_specs=[SM, VM, VM, HBM, HBM],
        out_specs=[VM] * 4 + [HBM] * 4,
        scratch_shapes=[pltpu.SemaphoreType.DMA((2, 3))],
        input_output_aliases={3: 6, 4: 7},
        compiler_params=pltpu.CompilerParams(vmem_limit_bytes=16 << 20),
    )(table, mine, other, out_k, out_v)

    to_right = [(i, i + 1) for i in range(dp - 1)]
    to_left = [(i + 1, i) for i in range(dp - 1)]

    def cross(send_r, send_l):
        return lax.ppermute(send_r, "dp", to_right), lax.ppermute(send_l, "dp", to_left)

    def step(t, takes, ring, out_k, out_v):
        return pl.pallas_call(
            step_kernel,
            out_shape=(chunk, chunk, ring_shape, slots, slots),
            in_specs=[SM, SM, HBM, VM, VM, HBM, HBM, HBM],
            out_specs=[VM, VM, HBM, HBM, HBM],
            scratch_shapes=[pltpu.SemaphoreType.DMA((2, 3))],
            input_output_aliases={5: 2, 6: 3, 7: 4},
            compiler_params=pltpu.CompilerParams(vmem_limit_bytes=16 << 20),
        )(table, jnp.reshape(t, (1,)), own, *takes, ring, out_k, out_v)

    def turn(state):
        t, a, b, ring, out_k, out_v = state
        for i in range(UNROLL):
            got = cross(*a)
            new_r, new_l, ring, out_k, out_v = step(t + i, got, ring, out_k, out_v)
            a, b = b, (new_r, new_l)
        return t + UNROLL, a, b, ring, out_k, out_v

    state = turn((jnp.zeros((), i32), (s0, s1), (s2, s3), ring, out_k, out_v))

    tied = lax.optimization_barrier((s0, new_queries, resident_queries))
    nq, rq = tied[1], tied[2]
    info = jnp.stack([resident_lengths[0], side * stored_keys.shape[1], side, own_length, owner]).astype(i32)
    own_query = lax.dynamic_index_in_dim(nq, owner, 1, False)
    own_tk = lax.dynamic_index_in_dim(incoming_token_keys, owner, 1, False)
    own_tv = lax.dynamic_index_in_dim(incoming_token_values, owner, 1, False)
    rows = step_count * query_width // HEAD_WIDTH
    rows_kv = step_count * query_width // width
    part, own_out = pl.pallas_call(
        attention_kernel,
        out_shape=(
            jax.ShapeDtypeStruct((rows, 3 * HEAD_WIDTH), f32),
            jax.ShapeDtypeStruct((rows, HEAD_WIDTH), f32),
        ),
        in_specs=[SM] + [VM] * 10,
        out_specs=[VM, VM],
        scratch_shapes=[pltpu.VMEM((rows_kv, HEAD_WIDTH), f32)],
        compiler_params=pltpu.CompilerParams(vmem_limit_bytes=32 << 20),
    )(
        info,
        rq[:, 0], stored_keys[0], stored_values[0], stored_token_keys[:, 0], stored_token_values[:, 0],
        own_query, prompt_keys[0], prompt_values[0], own_tk, own_tv,
    )
    part_other = lax.ppermute(part, "side", swap)
    everyone = gather_outputs(own_out, dp)
    state = lax.while_loop(lambda state: state[0] < last, turn, state)
    resident_out, new_out = pl.pallas_call(
        functools.partial(finish_kernel, dp, step_count),
        out_shape=(
            jax.ShapeDtypeStruct((step_count, 1, query_width), bf16),
            jax.ShapeDtypeStruct((step_count, request_count, query_width), bf16),
        ),
        in_specs=[SM] + [VM] * 3,
        out_specs=[VM, VM],
        scratch_shapes=[pltpu.VMEM((rows, HEAD_WIDTH), f32)],
    )(jnp.stack([side, me]).astype(i32), part, part_other, everyone)
    return (resident_out, new_out, state[4], state[5])


def solution(mesh):
    placed = (
        P(("side", "dp"), None, "tp"),
        P(("side", "dp"), None, "tp"),
        P(),
        P(),
        P(None, None, "tp"),
        P(None, None, "tp"),
        P(None, None, "tp"),
        P("dp", "side", "tp"),
        P("dp", "side", "tp"),
        P("dp"),
        P(None, "dp", "tp"),
        P(None, "dp", "tp"),
        P(None, "dp", "tp"),
    )
    return jax.shard_map(
        body,
        mesh=mesh,
        in_specs=placed,
        out_specs=(
            P(None, "dp", "tp"),
            P(None, None, "tp"),
            P("dp", "side", "tp"),
            P("dp", "side", "tp"),
        ),
        check_vma=False,
    )
```

```python
import functools

import jax
import jax.numpy as jnp
from jax import lax
from jax.experimental import pallas as pl
from jax.experimental.pallas import tpu as pltpu
from jax.sharding import PartitionSpec as P

HEAD_WIDTH = 128
CAP = 4
UNIT = 128
PER = 4
MESSAGE = UNIT * PER
PEEL = 4
TURN = 2
LAG = 2
LOW = -1e30

HBM = pl.BlockSpec(memory_space=pltpu.HBM)
VM = pl.BlockSpec(memory_space=pltpu.VMEM)
SM = pl.BlockSpec(memory_space=pltpu.SMEM)


def attend(q, q_rows, k_ref, v_ref, tk, tv, first, length, tokens_on, emit):
    steps = q.shape[0]
    keys, width = k_ref.shape
    heads_kv = width // HEAD_WIDTH
    members = q.shape[1] // width
    rows = members * steps
    scale = HEAD_WIDTH ** -0.5
    for kv in range(heads_kv):
        lanes = slice(kv * HEAD_WIDTH, (kv + 1) * HEAD_WIDTH)
        for g in range(members):
            at = (kv * members + g) * HEAD_WIDTH
            q_rows[g * steps:(g + 1) * steps, :] = q[:, at:at + HEAD_WIDTH]
        q32 = q_rows[...]
        scores = lax.dot_general(
            q32.astype(jnp.bfloat16), k_ref[:, lanes], (((1,), (1,)), ((), ())), preferred_element_type=jnp.float32
        ) * scale
        usable = first + lax.broadcasted_iota(jnp.int32, (rows, keys), 1) < length
        scores = jnp.where(usable, scores, LOW)
        row_step = lax.rem(lax.broadcasted_iota(jnp.int32, (rows, 1), 0), steps)
        top = jnp.max(scores, axis=1, keepdims=True)
        extra = []
        for n in range(steps):
            s = jnp.sum(q32 * tk[n:n + 1, lanes], axis=1, keepdims=True) * scale
            on = (row_step >= n) & tokens_on
            s = jnp.where(on, s, LOW)
            extra.append((on, s))
            top = jnp.maximum(top, s)
        weight = jnp.where(usable, jnp.exp(scores - top), 0.0)
        total = jnp.sum(weight, axis=1, keepdims=True)
        acc = lax.dot_general(
            weight.astype(jnp.bfloat16), v_ref[:, lanes], (((1,), (0,)), ((), ())), preferred_element_type=jnp.float32
        )
        for n, (on, s) in enumerate(extra):
            w = jnp.where(on, jnp.exp(s - top), 0.0)
            total = total + w
            acc = acc + w.astype(jnp.bfloat16).astype(jnp.float32) * tv[n:n + 1, lanes]
        emit(kv, top, total, acc)


def attention_kernel(
    dp, resident_length, lengths, rq, rk, rv, rtk, rtv, nq, nk, nv, ntk, ntv, part, own_out, q_rows
):
    side = lax.axis_index("side")
    owner = side * dp + lax.axis_index("dp")
    steps = rq.shape[0]
    keys, width = rk.shape
    rows = steps * rq.shape[1] // width
    f32 = jnp.float32

    def emit_part(kv, top, total, acc):
        at = slice(kv * rows, (kv + 1) * rows)
        part[at, 0:HEAD_WIDTH] = acc
        part[at, HEAD_WIDTH:2 * HEAD_WIDTH] = jnp.broadcast_to(top, (rows, HEAD_WIDTH))
        part[at, 2 * HEAD_WIDTH:] = jnp.broadcast_to(total, (rows, HEAD_WIDTH))

    attend(
        rq[...].astype(f32), q_rows, rk, rv, rtk[...].astype(f32), rtv[...].astype(f32),
        side * keys, resident_length[0], side == 1, emit_part,
    )

    def own(ref):
        picked = []
        for n in range(steps):
            block = ref[n].astype(f32)
            here = lax.broadcasted_iota(jnp.int32, block.shape, 0) == owner
            picked.append(jnp.sum(jnp.where(here, block, 0.0), axis=0, keepdims=True))
        return jnp.concatenate(picked, axis=0)

    def emit_out(kv, top, total, acc):
        own_out[kv * rows:(kv + 1) * rows, :] = acc / total

    attend(own(nq), q_rows, nk, nv, own(ntk), own(ntv), 0, lengths[owner], side >= 0, emit_out)


def finish_kernel(dp, steps, a, b, everyone, resident, new, o_rows):
    w = HEAD_WIDTH
    heads = resident.shape[1] // w
    top = jnp.maximum(a[:, w:2 * w], b[:, w:2 * w])
    ga = jnp.exp(a[:, w:2 * w] - top)
    gb = jnp.exp(b[:, w:2 * w] - top)
    o_rows[...] = (a[:, 0:w] * ga + b[:, 0:w] * gb) / (a[:, 2 * w:] * ga + b[:, 2 * w:] * gb)
    for h in range(heads):
        resident[:, h * w:(h + 1) * w] = o_rows[h * steps:(h + 1) * steps, :].astype(resident.dtype)
    side, me = lax.axis_index("side"), lax.axis_index("dp")
    count = everyone.shape[0]
    order = []
    for r in range(count):
        far = lax.bitwise_xor(me, r % dp) if dp & (dp - 1) == 0 else lax.rem(me - r % dp + dp, dp)
        order.append(far * 2 + lax.bitwise_xor(side, r // dp))
    at_row = lax.broadcasted_iota(jnp.int32, (count, w), 0)
    for n in range(steps):
        for h in range(heads):
            k = h * steps + n
            block = jnp.zeros((count, w), jnp.float32)
            for r in range(count):
                block = jnp.where(at_row == r, everyone[order[r], k:k + 1, :], block)
            new[n, :, h * w:(h + 1) * w] = block.astype(new.dtype)


def run_all(copies, start=True, wait=True):
    for on, a, b, sem in copies if start else ():
        @pl.when(on)
        def _():
            pltpu.make_async_copy(a, b, sem).start()
    for on, a, b, sem in copies if wait else ():
        @pl.when(on)
        def _():
            pltpu.make_async_copy(a, b, sem).wait()


def units_at(start, limit):
    return pl.ds(pl.multiple_of(jnp.clip(start, 0, limit - UNIT), UNIT), UNIT)


def last_unit(length):
    return (length + UNIT - 1) // UNIT * UNIT - UNIT


def mask_edge(j, length, keys, values, edge, stage, sem):
    first = last_unit(length)
    copies = [
        pltpu.make_async_copy(a.at[units_at(first, a.shape[0])], stage.at[i], sem.at[i])
        for i, a in enumerate((keys, values))
    ]
    for copy in copies:
        copy.start()
    row = lax.broadcasted_iota(jnp.int32, stage.shape[1:], 0)
    for i, copy in enumerate(copies):
        copy.wait()
        edge[j, i] = jnp.where(first + row < length, stage[i], jnp.zeros_like(stage[i]))


def plan_kernel(dp, half, ring_units, scalar_lengths, lengths, goal, keys, values, table, edge, out_k, out_v, blank, stage, fill_sem, sem):
    blank[...] = jnp.zeros_like(blank)
    fills = [
        pltpu.make_async_copy(blank, out.at[slot], fill_sem.at[i, slot])
        for i, out in enumerate((out_k, out_v)) for slot in range(CAP)
    ]
    for fill in fills:
        fill.start()
    side, me = lax.axis_index("side"), lax.axis_index("dp")
    mask_edge(0, scalar_lengths[side * dp + me], keys, values, edge, stage, sem)
    edge[1] = jnp.zeros_like(edge[1])
    f32 = jnp.float32
    full = 2 * half
    count = lengths.shape[1]
    wide = table.shape[1]
    id_row = lax.broadcasted_iota(jnp.int32, (count, count), 1).astype(f32)
    id_col = lax.broadcasted_iota(jnp.int32, (count, count), 0).astype(f32)
    eye = id_row == id_col

    def col(row):
        return jnp.sum(jnp.where(eye, jnp.broadcast_to(row, (count, count)), 0.0), axis=1, keepdims=True)

    ids = id_row[0:1]
    late = jnp.where(ids >= dp, 1.0, 0.0)
    src0 = ids - dp * late
    goal0 = goal[...].astype(f32)
    side_f, me_f = side.astype(f32), me.astype(f32)
    units = jnp.floor((lengths[...].astype(f32) + (UNIT - 1)) * (1.0 / UNIT))
    units_col, late_col, goal0_col, src0_col = col(units), col(late), col(goal0), col(src0)
    slot = jnp.sum(jnp.where((goal0_col == goal0) & (id_col < id_row), 1.0, 0.0), axis=0, keepdims=True)
    slot_col = col(slot)
    time = lax.broadcasted_iota(jnp.int32, (1, wide), 1).astype(f32)
    here_col = jnp.where(late_col == side_f, 0.0, 1.0)
    steps = jnp.zeros((1, 1), f32)
    for flip in (False, True):
        turned = (lambda x: dp - 1 - x) if flip else (lambda x: x)
        s, g, m, s_col, g_col = turned(src0), turned(goal0), turned(me_f), turned(src0_col), turned(goal0_col)
        ahead = (g_col > g) | ((g_col == g) & ((s_col > s) | ((s_col == s) & (id_col < id_row))))
        crosses, bases, starts = [], [], []
        for d in range(dp - 1):
            cross = (s <= d) & (g > d)
            base = jnp.sum(jnp.where(ahead & (s_col <= d) & (g_col > d), units_col, 0.0), axis=0, keepdims=True)
            load = jnp.sum(jnp.where(cross, units, 0.0), axis=1, keepdims=True)
            start = jnp.zeros((1, 1), f32)
            if d > 0:
                lead = jnp.floor((base - bases[-1]) * (1.0 / PER))
                gap = jnp.where(cross & crosses[-1], starts[-1] + LAG - lead, 0.0)
                start = jnp.maximum(jnp.max(gap, axis=1, keepdims=True), 0.0)
            steps = jnp.maximum(steps, jnp.where(load > 0, jnp.floor((load + (PER - 1)) * (1.0 / PER)) + start, 0.0))
            crosses.append(cross)
            bases.append(base)
            starts.append(start)

        def at(link):
            base, start, used = jnp.zeros((1, count), f32), jnp.zeros((1, 1), f32), jnp.zeros((1, count), f32)
            for d in range(dp - 1):
                base = jnp.where(link == d, bases[d], base)
                start = jnp.where(link == d, starts[d], start)
                used = jnp.where(link == d, jnp.where(crosses[d], units, 0.0), used)
            return col(base), start * PER, col(used)

        def ring_row(p):
            return (p - ring_units * jnp.floor((p + 0.5) * (1.0 / ring_units))) * UNIT

        def pick(hit, value):
            return (jnp.sum(jnp.where(hit, value + 1.0, 0.0), axis=0, keepdims=True) - 1.0).astype(jnp.int32)

        base, start, used = at(m)
        p = time - start
        c = p - base
        hit = (c >= 0) & (c < used)
        own = jnp.where(
            c == units_col - 1.0, 2 * full + ring_units * UNIT + here_col * UNIT, here_col * full + c * UNIT
        )
        r = 3 if flip else 0
        table[r:r + 1, :] = pick(hit, jnp.where(s_col == m, own, 2 * full + ring_row(p)))
        here, start, used = at(m - 1)
        c = time - start - here
        hit = (c >= 0) & (c < used)
        r = 2 if flip else 1
        table[r:r + 1, :] = pick(
            hit, jnp.where(g_col == m, slot_col * full + c * UNIT, CAP * full + ring_row(base + c))
        )
    stay = jnp.where((src0 == me_f) & (goal0 == me_f), slot + 1.0, 0.0)
    home = [
        jnp.sum(jnp.where(late == which, stay, 0.0), axis=1, keepdims=True) - 1.0 for which in (side_f, 1.0 - side_f)
    ]
    last = jnp.where(time == 0, steps, jnp.where(time == 1, home[0], home[1]))
    table[4:5, :] = last.astype(jnp.int32)
    table[5:8, :] = jnp.zeros((3, wide), jnp.int32)
    for fill in fills:
        fill.wait()


def send_copies(table, t, side, sources, edge, ring, ring_rows, send, sem):
    full = sources[0].shape[0]
    copies = []
    for i in range(PER):
        code = table[3 * side, t * PER + i]
        to = pl.ds(i * UNIT, UNIT)
        for j in range(2):
            here = (code >= j * full) & (code < (j + 1) * full)
            for n in range(2):
                copies.append((
                    here, sources[2 * j + n].at[units_at(code - j * full, full)], send.at[n, to], sem.at[i, n]
                ))
        last = code >= 2 * full + ring_rows
        which = jnp.clip((code - 2 * full - ring_rows) // UNIT, 0, 1)
        copies.append((last, edge.at[which], send.at[:, to], sem.at[i, 0]))
        if ring is not None:
            copies.append((
                (code >= 2 * full) & (code < 2 * full + ring_rows),
                ring.at[:, units_at(code - 2 * full, ring_rows)], send.at[:, to], sem.at[i, 0],
            ))
    return copies


def take_copies(table, t, row, side, take, out_k, out_v, sem):
    half = out_k.shape[1]
    full = 2 * half
    copies = []
    for i in range(PER):
        code = table[row, t * PER + i]
        slot = jnp.clip(code // full, 0, CAP - 1)
        position = code - slot * full - side * half
        final = (code >= 0) & (code < CAP * full) & (position >= 0) & (position < half)
        for n, out in enumerate((out_k, out_v)):
            copies.append((
                final, take.at[n, pl.ds(i * UNIT, UNIT)], out.at[slot, units_at(position, half)], sem.at[i, n]
            ))
    return copies


def first_kernel(dp, ring_rows, table, lengths, pk, pv, xk, xv, edge_in, send_0, send_1, edge, ring, stage, sem, sem_0, sem_1):
    side, me = lax.axis_index("side"), lax.axis_index("dp")
    edge[0] = edge_in[0]
    mask_edge(1, lengths[(1 - side) * dp + me], xk, xv, edge, stage, sem)
    copies = (
        send_copies(table, 0, side, (pk, pv, xk, xv), edge, None, ring_rows, send_0, sem_0)
        + send_copies(table, 1, side, (pk, pv, xk, xv), edge, None, ring_rows, send_1, sem_1)
    )
    run_all(copies)


def home_kernel(dp, table, lengths, pk, pv, xk, xv, edge, ok, ov, out_k, out_v, sem):
    side, me = lax.axis_index("side"), lax.axis_index("dp")
    half = out_k.shape[1]
    full = 2 * half
    for j, (keys, values) in enumerate(((pk, pv), (xk, xv))):
        slot = table[4, 1 + j]
        to = jnp.clip(slot, 0, CAP - 1)
        length = lengths[lax.bitwise_xor(side, j) * dp + me]
        last = last_unit(length)
        copies = []
        for u in range(half // UNIT):
            first = side * half + u * UNIT
            rows = pl.ds(u * UNIT, UNIT)
            for n, (a, out) in enumerate(((keys, out_k), (values, out_v))):
                copies.append(((slot >= 0) & (first < last), a.at[units_at(first, full)], out.at[to, rows], sem.at[u, n]))
                copies.append(((slot >= 0) & (first == last), edge.at[j, n], out.at[to, rows], sem.at[u, n]))
        run_all(copies)


def step_kernel(
    table, now, pk, pv, xk, xv, edge, got, mirrored, ring_in, ok, ov,
    send, ring, out_k, out_v, ring_sem, got_sem, mirror_sem, send_sem,
):
    side = lax.axis_index("side")
    full = pk.shape[0]
    ring_rows = ring.shape[1]
    t = now[0]
    hops = []
    for i in range(PER):
        code = table[1 + side, t * PER + i] - CAP * full
        hops.append((code >= 0, got.at[:, pl.ds(i * UNIT, UNIT)], ring.at[:, units_at(code, ring_rows)], ring_sem.at[i]))
    run_all(hops, wait=False)
    ends = take_copies(table, t, 1 + side, side, got, out_k, out_v, got_sem)
    before = jnp.maximum(t - 1, 0)
    ends += [
        (on & (t > 0), a, b, s)
        for on, a, b, s in take_copies(table, before, 2 - side, side, mirrored, out_k, out_v, mirror_sem)
    ]
    run_all(ends, wait=False)
    run_all(hops, start=False)
    run_all(send_copies(table, t + LAG, side, (pk, pv, xk, xv), edge, ring, ring_rows, send, send_sem))
    run_all(ends, start=False)


def last_kernel(table, now, mirrored, ok, ov, out_k, out_v, sem):
    side = lax.axis_index("side")
    run_all(take_copies(table, now[0] - 1, 2 - side, side, mirrored, out_k, out_v, sem))


def gather_outputs(own, dp, hold):
    block = jnp.stack([own, lax.ppermute(own, "side", [(0, 1), (1, 0)])])
    if dp & (dp - 1):
        rest = [lax.ppermute(block, "dp", [(i, (i + x) % dp) for i in range(dp)]) for x in range(1, dp)]
        return jnp.concatenate([block] + rest)
    reach = 1
    while reach < dp:
        got = lax.ppermute(block, "dp", [(i, i ^ reach) for i in range(dp)])
        block, got = hold(reach, (block, got))
        block = jnp.concatenate([block, got])
        reach *= 2
    return block


def body(
    prompt_keys,
    prompt_values,
    prompt_lengths,
    assignment,
    new_queries,
    incoming_token_keys,
    incoming_token_values,
    stored_keys,
    stored_values,
    resident_lengths,
    resident_queries,
    stored_token_keys,
    stored_token_values,
):
    step_count = resident_queries.shape[0]
    dp = lax.axis_size("dp")
    request_count = prompt_lengths.shape[0]
    full, width = prompt_keys.shape[1:]
    query_width = new_queries.shape[2]
    half = full // 2
    bf16, f32, i32 = jnp.bfloat16, jnp.float32, jnp.int32
    swap = [(0, 1), (1, 0)]
    shape = jax.ShapeDtypeStruct
    dma = pltpu.SemaphoreType.DMA
    roomy = pltpu.CompilerParams(vmem_limit_bytes=16 << 20)

    pk, pv = prompt_keys[0], prompt_values[0]
    xk, xv = lax.ppermute(pk, "side", swap), lax.ppermute(pv, "side", swap)

    most = full // UNIT
    ring_units = 2 * most + (LAG + 1) * PER
    steps_max = -(-request_count * most // PER) + LAG * dp + PEEL + TURN + LAG
    wide = -(-steps_max * PER // 128) * 128
    slots = shape((CAP, half, width), bf16)
    edges = shape((2, 2, UNIT, width), bf16)
    table, edge, out_k, out_v = pl.pallas_call(
        functools.partial(plan_kernel, dp, half, ring_units),
        out_shape=(shape((8, wide), i32), edges, slots, slots),
        in_specs=[SM, VM, VM, HBM, HBM],
        out_specs=[VM, VM, HBM, HBM],
        scratch_shapes=[
            pltpu.VMEM((half, width), bf16), pltpu.VMEM((2, UNIT, width), bf16), dma((2, CAP)), dma((2,)),
        ],
        compiler_params=roomy,
    )(
        prompt_lengths,
        jnp.reshape(prompt_lengths, (1, request_count)),
        jnp.reshape(assignment, (1, request_count)),
        pk, pv,
    )
    last = table[4, 0]

    message = shape((2, MESSAGE, width), bf16)
    ring_shape = shape((2, ring_units * UNIT, width), bf16)
    first, second, edge, ring = pl.pallas_call(
        functools.partial(first_kernel, dp, ring_units * UNIT),
        out_shape=(message, message, edges, ring_shape),
        in_specs=[SM, SM, HBM, HBM, HBM, HBM, VM],
        out_specs=[VM, VM, VM, HBM],
        scratch_shapes=[pltpu.VMEM((2, UNIT, width), bf16), dma((2,)), dma((PER, 2)), dma((PER, 2))],
        compiler_params=roomy,
    )(table, prompt_lengths, pk, pv, xk, xv, edge)

    rows = step_count * query_width // HEAD_WIDTH
    part, own_out = pl.pallas_call(
        functools.partial(attention_kernel, dp),
        out_shape=(shape((rows, 3 * HEAD_WIDTH), f32), shape((rows, HEAD_WIDTH), f32)),
        in_specs=[SM, SM] + [VM] * 10,
        out_specs=[VM, VM],
        scratch_shapes=[pltpu.VMEM((step_count * query_width // width, HEAD_WIDTH), f32)],
        compiler_params=roomy,
    )(
        resident_lengths, prompt_lengths,
        resident_queries[:, 0], stored_keys[0], stored_values[0], stored_token_keys[:, 0], stored_token_values[:, 0],
        new_queries, pk, pv, incoming_token_keys, incoming_token_values,
    )

    hops = [(i, i + 1) for i in range(dp - 1)] + [(dp + i + 1, dp + i) for i in range(dp - 1)]

    def cross(send):
        return lax.ppermute(send, ("side", "dp"), hops)

    def mirror(got):
        return lax.ppermute(got, "side", swap)

    def place(t, got, mirrored, ring, out_k, out_v):
        return pl.pallas_call(
            step_kernel,
            out_shape=(message, ring_shape, slots, slots),
            in_specs=[SM, SM, HBM, HBM, HBM, HBM, VM, VM, VM, HBM, HBM, HBM],
            out_specs=[VM, HBM, HBM, HBM],
            scratch_shapes=[dma((PER,)), dma((PER, 2)), dma((PER, 2)), dma((PER, 2))],
            input_output_aliases={9: 1, 10: 2, 11: 3},
            compiler_params=roomy,
        )(table, jnp.reshape(t, (1,)), pk, pv, xk, xv, edge, got, mirrored, ring, out_k, out_v)

    def steps(count, state, marks=None):
        t, a, b, mirrored, ring, out_k, out_v = state
        for i in range(count):
            got = cross(a)
            a, (new, ring, out_k, out_v) = b, place(t + i, got, mirrored, ring, out_k, out_v)
            b, mirrored = new, mirror(got)
            if marks is not None:
                marks.append(new)
        return t + count, a, b, mirrored, ring, out_k, out_v

    tied = lax.optimization_barrier((table, first))
    out_k, out_v = pl.pallas_call(
        functools.partial(home_kernel, dp),
        out_shape=(slots, slots),
        in_specs=[SM, SM, HBM, HBM, HBM, HBM, VM, HBM, HBM],
        out_specs=[HBM, HBM],
        scratch_shapes=[dma((half // UNIT, 2))],
        input_output_aliases={7: 0, 8: 1},
    )(tied[0], prompt_lengths, pk, pv, xk, xv, edge, out_k, out_v)

    marks = []
    state = steps(PEEL, (jnp.zeros((), i32), first, second, second, ring, out_k, out_v), marks)

    part_other = lax.ppermute(part, "side", swap)
    everyone = gather_outputs(
        own_out, dp, lambda reach, pair: lax.optimization_barrier((*pair, marks[min(reach, PEEL) - 1]))[:2]
    )
    resident_out, new_out = pl.pallas_call(
        functools.partial(finish_kernel, dp, step_count),
        out_shape=(shape((step_count, query_width), bf16), shape((step_count, request_count, query_width), bf16)),
        in_specs=[VM] * 3,
        out_specs=[VM, VM],
        scratch_shapes=[pltpu.VMEM((rows, HEAD_WIDTH), f32)],
    )(part, part_other, everyone)

    t, _, _, mirrored, _, out_k, out_v = lax.while_loop(
        lambda state: state[0] < last, functools.partial(steps, TURN), state
    )
    out_k, out_v = pl.pallas_call(
        last_kernel,
        out_shape=(slots, slots),
        in_specs=[SM, SM, VM, HBM, HBM],
        out_specs=[HBM, HBM],
        scratch_shapes=[dma((PER, 2))],
        input_output_aliases={3: 0, 4: 1},
        compiler_params=roomy,
    )(table, jnp.reshape(t, (1,)), mirrored, out_k, out_v)
    return (resident_out[:, None, :], new_out, out_k, out_v)


def solution(mesh):
    placed = (
        P(("side", "dp"), None, "tp"),
        P(("side", "dp"), None, "tp"),
        P(),
        P(),
        P(None, None, "tp"),
        P(None, None, "tp"),
        P(None, None, "tp"),
        P("dp", "side", "tp"),
        P("dp", "side", "tp"),
        P("dp"),
        P(None, "dp", "tp"),
        P(None, "dp", "tp"),
        P(None, "dp", "tp"),
    )
    return jax.shard_map(
        body,
        mesh=mesh,
        in_specs=placed,
        out_specs=(
            P(None, "dp", "tp"),
            P(None, None, "tp"),
            P("dp", "side", "tp"),
            P("dp", "side", "tp"),
        ),
        check_vma=False,
    )
```

```python
import functools

import jax
import jax.numpy as jnp
from jax import lax
from jax.experimental import pallas as pl
from jax.experimental.pallas import tpu as pltpu
from jax.sharding import PartitionSpec as P

HEAD_WIDTH = 128
CAP = 4
UNIT = 128
PER = 4
MESSAGE = UNIT * PER
PEEL = 4
ENDS = (0, 1, 2, 3, 4, 5, 6, 7, 8, 10, 12, 14, 16)
TURN = 2
LAG = 2
LOW = -1e30

HBM = pl.BlockSpec(memory_space=pltpu.HBM)
VM = pl.BlockSpec(memory_space=pltpu.VMEM)
SM = pl.BlockSpec(memory_space=pltpu.SMEM)


def attend(q, q_rows, k_ref, v_ref, tk, tv, first, length, tokens_on, emit):
    steps = q.shape[0]
    keys, width = k_ref.shape
    heads_kv = width // HEAD_WIDTH
    members = q.shape[1] // width
    rows = members * steps
    scale = HEAD_WIDTH ** -0.5
    for kv in range(heads_kv):
        lanes = slice(kv * HEAD_WIDTH, (kv + 1) * HEAD_WIDTH)
        for g in range(members):
            at = (kv * members + g) * HEAD_WIDTH
            q_rows[g * steps:(g + 1) * steps, :] = q[:, at:at + HEAD_WIDTH]
        q32 = q_rows[...]
        scores = lax.dot_general(
            q32.astype(jnp.bfloat16), k_ref[:, lanes], (((1,), (1,)), ((), ())), preferred_element_type=jnp.float32
        ) * scale
        usable = first + lax.broadcasted_iota(jnp.int32, (rows, keys), 1) < length
        scores = jnp.where(usable, scores, LOW)
        row_step = lax.rem(lax.broadcasted_iota(jnp.int32, (rows, 1), 0), steps)
        top = jnp.max(scores, axis=1, keepdims=True)
        extra = []
        for n in range(steps):
            s = jnp.sum(q32 * tk[n:n + 1, lanes], axis=1, keepdims=True) * scale
            on = (row_step >= n) & tokens_on
            s = jnp.where(on, s, LOW)
            extra.append((on, s))
            top = jnp.maximum(top, s)
        weight = jnp.where(usable, jnp.exp(scores - top), 0.0)
        total = jnp.sum(weight, axis=1, keepdims=True)
        acc = lax.dot_general(
            weight.astype(jnp.bfloat16), v_ref[:, lanes], (((1,), (0,)), ((), ())), preferred_element_type=jnp.float32
        )
        for n, (on, s) in enumerate(extra):
            w = jnp.where(on, jnp.exp(s - top), 0.0)
            total = total + w
            acc = acc + w.astype(jnp.bfloat16).astype(jnp.float32) * tv[n:n + 1, lanes]
        emit(kv, top, total, acc)


def attention_kernel(
    dp, resident_length, lengths, rq, rk, rv, rtk, rtv, nq, nk, nv, ntk, ntv, part, own_out, q_rows
):
    side = lax.axis_index("side")
    owner = side * dp + lax.axis_index("dp")
    steps = rq.shape[0]
    keys, width = rk.shape
    rows = steps * rq.shape[1] // width
    f32 = jnp.float32

    def emit_part(kv, top, total, acc):
        at = slice(kv * rows, (kv + 1) * rows)
        part[at, 0:HEAD_WIDTH] = acc
        part[at, HEAD_WIDTH:2 * HEAD_WIDTH] = jnp.broadcast_to(top, (rows, HEAD_WIDTH))
        part[at, 2 * HEAD_WIDTH:] = jnp.broadcast_to(total, (rows, HEAD_WIDTH))

    attend(
        rq[...].astype(f32), q_rows, rk, rv, rtk[...].astype(f32), rtv[...].astype(f32),
        side * keys, resident_length[0], side == 1, emit_part,
    )

    def own(ref):
        picked = []
        for n in range(steps):
            block = ref[n].astype(f32)
            here = lax.broadcasted_iota(jnp.int32, block.shape, 0) == owner
            picked.append(jnp.sum(jnp.where(here, block, 0.0), axis=0, keepdims=True))
        return jnp.concatenate(picked, axis=0)

    def emit_out(kv, top, total, acc):
        own_out[kv * rows:(kv + 1) * rows, :] = acc / total

    attend(own(nq), q_rows, nk, nv, own(ntk), own(ntv), 0, lengths[owner], side >= 0, emit_out)


def finish_kernel(dp, steps, a, b, everyone, resident, new, o_rows):
    w = HEAD_WIDTH
    heads = resident.shape[1] // w
    top = jnp.maximum(a[:, w:2 * w], b[:, w:2 * w])
    ga = jnp.exp(a[:, w:2 * w] - top)
    gb = jnp.exp(b[:, w:2 * w] - top)
    o_rows[...] = (a[:, 0:w] * ga + b[:, 0:w] * gb) / (a[:, 2 * w:] * ga + b[:, 2 * w:] * gb)
    for h in range(heads):
        resident[:, h * w:(h + 1) * w] = o_rows[h * steps:(h + 1) * steps, :].astype(resident.dtype)
    side, me = lax.axis_index("side"), lax.axis_index("dp")
    count = everyone.shape[0]
    order = []
    for r in range(count):
        far = lax.bitwise_xor(me, r % dp) if dp & (dp - 1) == 0 else lax.rem(me - r % dp + dp, dp)
        order.append(far * 2 + lax.bitwise_xor(side, r // dp))
    at_row = lax.broadcasted_iota(jnp.int32, (count, w), 0)
    for n in range(steps):
        for h in range(heads):
            k = h * steps + n
            block = jnp.zeros((count, w), jnp.float32)
            for r in range(count):
                block = jnp.where(at_row == r, everyone[order[r], k:k + 1, :], block)
            new[n, :, h * w:(h + 1) * w] = block.astype(new.dtype)


def units_at(start):
    return pl.ds(pl.multiple_of(start, UNIT), UNIT)


def last_unit(length):
    return (length + UNIT - 1) // UNIT * UNIT - UNIT


def mask_unit(ref, first, length):
    row = lax.broadcasted_iota(jnp.int32, (UNIT, ref.shape[1]), 0)
    block = ref[units_at(first), :]
    ref[units_at(first), :] = jnp.where(first + row < length, block, jnp.zeros_like(block))


def plan_kernel(dp, half, ring_units, lengths, goal, table, out_k, out_v, blank, fill_sem):
    blank[...] = jnp.zeros_like(blank)
    fills = [
        pltpu.make_async_copy(blank, out.at[pl.ds(slot * half, half)], fill_sem.at[i, slot])
        for i, out in enumerate((out_k, out_v)) for slot in range(CAP)
    ]
    for fill in fills:
        fill.start()
    side, me = lax.axis_index("side"), lax.axis_index("dp")
    f32 = jnp.float32
    full = 2 * half
    count = lengths.shape[1]
    wide = table.shape[1]
    id_row = lax.broadcasted_iota(jnp.int32, (count, count), 1).astype(f32)
    id_col = lax.broadcasted_iota(jnp.int32, (count, count), 0).astype(f32)
    eye = id_row == id_col

    def col(row):
        return jnp.sum(jnp.where(eye, jnp.broadcast_to(row, (count, count)), 0.0), axis=1, keepdims=True)

    ids = id_row[0:1]
    late = jnp.where(ids >= dp, 1.0, 0.0)
    src0 = ids - dp * late
    goal0 = goal[...].astype(f32)
    side_f, me_f = side.astype(f32), me.astype(f32)
    units = jnp.floor((lengths[...].astype(f32) + (UNIT - 1)) * (1.0 / UNIT))
    units_col, late_col, goal0_col, src0_col = col(units), col(late), col(goal0), col(src0)
    slot = jnp.sum(jnp.where((goal0_col == goal0) & (id_col < id_row), 1.0, 0.0), axis=0, keepdims=True)
    slot_col = col(slot)
    time = lax.broadcasted_iota(jnp.int32, (1, wide), 1).astype(f32)
    here_col = jnp.where(late_col == side_f, 0.0, 1.0)
    steps = jnp.zeros((1, 1), f32)
    sends, passes, ends = [], [], []
    for flip in (False, True):
        turned = (lambda x: dp - 1 - x) if flip else (lambda x: x)
        s, g, m, s_col, g_col = turned(src0), turned(goal0), turned(me_f), turned(src0_col), turned(goal0_col)
        ahead = (g_col > g) | ((g_col == g) & ((s_col > s) | ((s_col == s) & (id_col < id_row))))
        crosses, bases, starts = [], [], []
        for d in range(dp - 1):
            cross = (s <= d) & (g > d)
            base = jnp.sum(jnp.where(ahead & (s_col <= d) & (g_col > d), units_col, 0.0), axis=0, keepdims=True)
            load = jnp.sum(jnp.where(cross, units, 0.0), axis=1, keepdims=True)
            start = jnp.zeros((1, 1), f32)
            if d > 0:
                lead = jnp.floor((base - bases[-1]) * (1.0 / PER))
                gap = jnp.where(cross & crosses[-1], starts[-1] + LAG - lead, 0.0)
                start = jnp.maximum(jnp.max(gap, axis=1, keepdims=True), 0.0)
            steps = jnp.maximum(steps, jnp.where(load > 0, jnp.floor((load + (PER - 1)) * (1.0 / PER)) + start, 0.0))
            crosses.append(cross)
            bases.append(base)
            starts.append(start)

        def at(link):
            base, start, used = jnp.zeros((1, count), f32), jnp.zeros((1, 1), f32), jnp.zeros((1, count), f32)
            for d in range(dp - 1):
                base = jnp.where(link == d, bases[d], base)
                start = jnp.where(link == d, starts[d], start)
                used = jnp.where(link == d, jnp.where(crosses[d], units, 0.0), used)
            return col(base), start * PER, col(used)

        def ring_row(p):
            return (p - ring_units * jnp.floor((p + 0.5) * (1.0 / ring_units))) * UNIT

        def pick(hit, value):
            return jnp.sum(jnp.where(hit, value + 1.0, 0.0), axis=0, keepdims=True) - 1.0

        base, start, used = at(m)
        p = time - start
        c = p - base
        hit = (c >= 0) & (c < used)
        sends.append(jnp.maximum(pick(hit, jnp.where(s_col == m, here_col * full + c * UNIT, 2 * full + ring_row(p))), 0.0))
        here, start, used = at(m - 1)
        c = time - start - here
        hit = (c >= 0) & (c < used)
        passes.append(pick(hit & (g_col != m), 2 * full + ring_row(base + c)))
        row = c * UNIT - half * side_f
        ends.append(pick(hit & (g_col == m) & (row >= 0) & (row < half), slot_col * half + row))
    right = side_f == 0.0
    for r, row in enumerate((
        jnp.where(right, sends[0], sends[1]), jnp.where(right, passes[0], passes[1]),
        jnp.where(right, ends[0], ends[1]), jnp.where(right, ends[1], ends[0]),
    )):
        table[r:r + 1, :] = row.astype(jnp.int32)
    stay = jnp.where((src0 == me_f) & (goal0 == me_f), slot + 1.0, 0.0)
    home = [
        jnp.sum(jnp.where(late == which, stay, 0.0), axis=1, keepdims=True) - 1.0 for which in (side_f, 1.0 - side_f)
    ]
    last = jnp.where(time == 0, steps, jnp.where(time == 1, home[0], home[1]))
    table[4:5, :] = last.astype(jnp.int32)
    table[5:8, :] = jnp.zeros((3, wide), jnp.int32)
    for fill in fills:
        fill.wait()


def first_kernel(dp, table, lengths, pk, pv, xk, xv, send_0, send_1, edge, sem, sem_0, sem_1):
    side, me = lax.axis_index("side"), lax.axis_index("dp")
    full = pk.shape[0]
    sources = ((pk, pv), (xk, xv))
    length = [lengths[which * dp + me] for which in (side, 1 - side)]
    last = [last_unit(x) for x in length]
    masked = [
        pltpu.make_async_copy(a.at[units_at(last[j])], edge.at[j, n], sem.at[j, n])
        for j in range(2) for n, a in enumerate(sources[j])
    ]
    for copy in masked:
        copy.start()
    for t, send, done in ((0, send_0, sem_0), (1, send_1, sem_1)):
        for i in range(PER):
            code = table[0, t * PER + i]
            for j in range(2):
                row = code - j * full

                @pl.when((row >= 0) & (row < full) & (row != last[j]))
                def _():
                    for n in range(2):
                        pltpu.make_async_copy(
                            sources[j][n].at[units_at(row)], send.at[n, pl.ds(i * UNIT, UNIT)], done.at[i, n]
                        ).start()
    for copy in masked:
        copy.wait()
    for j in range(2):
        for n in range(2):
            mask_unit(edge.at[j, n], 0, length[j] - last[j])
    for t, send, done in ((0, send_0, sem_0), (1, send_1, sem_1)):
        for i in range(PER):
            code = table[0, t * PER + i]
            to = pl.ds(i * UNIT, UNIT)
            at_edge = [code == j * full + last[j] for j in range(2)]
            for j in range(2):
                @pl.when(at_edge[j])
                def _():
                    send[:, to, :] = edge[j]

            @pl.when(jnp.logical_not(at_edge[0] | at_edge[1]) & (code < 2 * full))
            def _():
                for n in range(2):
                    pltpu.make_async_copy(pk.at[pl.ds(0, UNIT)], send.at[n, to], done.at[i, n]).wait()


def pool_kernel(dp, table, lengths, pk, pv, xk, xv, ok, ov, pool, out_k, out_v, stage, load_sem, pool_sem, home_sem):
    side, me = lax.axis_index("side"), lax.axis_index("dp")
    full = pk.shape[0]
    half = full // 2
    loads = [
        pltpu.make_async_copy(a, stage.at[j, n], load_sem.at[j, n])
        for j, pair in enumerate(((pk, pv), (xk, xv))) for n, a in enumerate(pair)
    ]
    for copy in loads:
        copy.start()
    stores, homes = [], []
    for j in range(2):
        length = lengths[lax.bitwise_xor(side, j) * dp + me]
        last = last_unit(length)
        for n in range(2):
            loads[2 * j + n].wait()
            mask_unit(stage.at[j, n], last, length)
        store = pltpu.make_async_copy(stage.at[j], pool.at[:, pl.ds(j * full, full)], pool_sem.at[j])
        store.start()
        stores.append(store)
        slot = table[4, 1 + j]
        count = jnp.where(slot >= 0, jnp.clip((last + UNIT - side * half) // UNIT, 0, half // UNIT), 0)

        def home(u, wait, j=j, slot=slot):
            for n, out in enumerate((out_k, out_v)):
                copy = pltpu.make_async_copy(
                    stage.at[j, n, units_at(side * half + u * UNIT)], out.at[units_at(slot * half + u * UNIT)],
                    home_sem.at[j, n, u],
                )
                copy.wait() if wait else copy.start()

        pl.loop(0, count)(functools.partial(home, wait=False))
        homes.append((count, home))
    for count, home in homes:
        pl.loop(0, count)(functools.partial(home, wait=True))
    for store in stores:
        store.wait()


def end_copies(table, t, row, take, out_k, out_v, sem):
    copies = []
    for i in range(PER):
        code = table[row, t * PER + i]
        to = units_at(jnp.maximum(code, 0))
        copies.append((code >= 0, [
            pltpu.make_async_copy(take.at[n, pl.ds(i * UNIT, UNIT)], out.at[to], sem.at[i, n])
            for n, out in enumerate((out_k, out_v))
        ]))
    return copies


def when_all(copies, act):
    for on, group in copies:
        @pl.when(on)
        def _():
            for copy in group:
                act(copy)


def step_kernel(
    table, now, got, mirrored, pool_in, ok, ov, send, pool, out_k, out_v, pass_sem, got_sem, mirror_sem, send_sem
):
    t = now[0]
    passes = []
    for i in range(PER):
        code = table[1, t * PER + i]
        to = pool.at[:, units_at(jnp.maximum(code, 0))]
        passes.append((code >= 0, [pltpu.make_async_copy(got.at[:, pl.ds(i * UNIT, UNIT)], to, pass_sem.at[i])]))
    when_all(passes, lambda copy: copy.start())
    ends = end_copies(table, t, 2, got, out_k, out_v, got_sem)
    if mirrored is not None:
        ends += end_copies(table, t - 1, 3, mirrored, out_k, out_v, mirror_sem)
    when_all(ends, lambda copy: copy.start())
    when_all(passes, lambda copy: copy.wait())
    if send is not None:
        lay = [
            pltpu.make_async_copy(
                pool.at[:, units_at(table[0, (t + LAG) * PER + i])], send.at[:, pl.ds(i * UNIT, UNIT)], send_sem.at[i]
            )
            for i in range(PER)
        ]
        for copy in lay:
            copy.start()
        for copy in lay:
            copy.wait()
    when_all(ends, lambda copy: copy.wait())


def last_kernel(table, now, mirrored, ok, ov, out_k, out_v, sem):
    ends = end_copies(table, now[0] - 1, 3, mirrored, out_k, out_v, sem)
    when_all(ends, lambda copy: copy.start())
    when_all(ends, lambda copy: copy.wait())


def gather_outputs(own, dp, hold):
    block = jnp.stack([own, lax.ppermute(own, "side", [(0, 1), (1, 0)])])
    if dp & (dp - 1):
        rest = [lax.ppermute(block, "dp", [(i, (i + x) % dp) for i in range(dp)]) for x in range(1, dp)]
        return jnp.concatenate([block] + rest)
    reach = 1
    while reach < dp:
        got = lax.ppermute(block, "dp", [(i, i ^ reach) for i in range(dp)])
        block, got = hold(reach, (block, got))
        block = jnp.concatenate([block, got])
        reach *= 2
    return block


def body(
    prompt_keys,
    prompt_values,
    prompt_lengths,
    assignment,
    new_queries,
    incoming_token_keys,
    incoming_token_values,
    stored_keys,
    stored_values,
    resident_lengths,
    resident_queries,
    stored_token_keys,
    stored_token_values,
):
    step_count = resident_queries.shape[0]
    dp = lax.axis_size("dp")
    request_count = prompt_lengths.shape[0]
    full, width = prompt_keys.shape[1:]
    query_width = new_queries.shape[2]
    half = full // 2
    bf16, f32, i32 = jnp.bfloat16, jnp.float32, jnp.int32
    swap = [(0, 1), (1, 0)]
    shape = jax.ShapeDtypeStruct
    dma = pltpu.SemaphoreType.DMA
    roomy = pltpu.CompilerParams(vmem_limit_bytes=16 << 20)

    pk, pv = prompt_keys[0], prompt_values[0]
    xk, xv = lax.ppermute(pk, "side", swap), lax.ppermute(pv, "side", swap)

    most = full // UNIT
    ring_units = 2 * most + (LAG + 1) * PER
    steps_max = -(-request_count * most // PER) + LAG * dp + PEEL + TURN + LAG
    wide = -(-steps_max * PER // 128) * 128
    slots = shape((CAP * half, width), bf16)
    table, out_k, out_v = pl.pallas_call(
        functools.partial(plan_kernel, dp, half, ring_units),
        out_shape=(shape((8, wide), i32), slots, slots),
        in_specs=[VM, VM],
        out_specs=[VM, HBM, HBM],
        scratch_shapes=[pltpu.VMEM((half, width), bf16), dma((2, CAP))],
        compiler_params=roomy,
    )(jnp.reshape(prompt_lengths, (1, request_count)), jnp.reshape(assignment, (1, request_count)))
    last = table[4, 0]

    message = shape((2, MESSAGE, width), bf16)
    pool_shape = shape((2, 2 * full + ring_units * UNIT, width), bf16)
    first, second = pl.pallas_call(
        functools.partial(first_kernel, dp),
        out_shape=(message, message),
        in_specs=[SM, SM, HBM, HBM, HBM, HBM],
        out_specs=[VM, VM],
        scratch_shapes=[pltpu.VMEM((2, 2, UNIT, width), bf16), dma((2, 2)), dma((PER, 2)), dma((PER, 2))],
        compiler_params=roomy,
    )(table, prompt_lengths, pk, pv, xk, xv)

    tied = lax.optimization_barrier((table, first))
    pool, out_k, out_v = pl.pallas_call(
        functools.partial(pool_kernel, dp),
        out_shape=(pool_shape, slots, slots),
        in_specs=[SM, SM] + [HBM] * 6,
        out_specs=[HBM] * 3,
        scratch_shapes=[
            pltpu.VMEM((2, 2, full, width), bf16), dma((2, 2)), dma((2,)), dma((2, 2, half // UNIT)),
        ],
        input_output_aliases={6: 1, 7: 2},
        compiler_params=roomy,
    )(tied[0], prompt_lengths, pk, pv, xk, xv, out_k, out_v)

    rows = step_count * query_width // HEAD_WIDTH
    part, own_out = pl.pallas_call(
        functools.partial(attention_kernel, dp),
        out_shape=(shape((rows, 3 * HEAD_WIDTH), f32), shape((rows, HEAD_WIDTH), f32)),
        in_specs=[SM, SM] + [VM] * 10,
        out_specs=[VM, VM],
        scratch_shapes=[pltpu.VMEM((step_count * query_width // width, HEAD_WIDTH), f32)],
        compiler_params=roomy,
    )(
        resident_lengths, prompt_lengths,
        resident_queries[:, 0], stored_keys[0], stored_values[0], stored_token_keys[:, 0], stored_token_values[:, 0],
        new_queries, pk, pv, incoming_token_keys, incoming_token_values,
    )

    hops = [(i, i + 1) for i in range(dp - 1)] + [(dp + i + 1, dp + i) for i in range(dp - 1)]

    def cross(send):
        return lax.ppermute(send, ("side", "dp"), hops)

    def mirror(got):
        return lax.ppermute(got, "side", swap)

    def place(t, got, mirrored, pool, out_k, out_v, lay):
        news = [message] if lay else []
        first_kept = len(news)
        mirrors = [] if mirrored is None else [mirrored]

        def kernel(table, now, got, *refs):
            refs = list(refs)
            mirrored = refs.pop(0) if mirrors else None
            send = refs.pop(3) if lay else None
            step_kernel(table, now, got, mirrored, *refs[:3], send, *refs[3:])

        kept = 3 + len(mirrors)
        outs = pl.pallas_call(
            kernel,
            out_shape=(*news, pool_shape, slots, slots),
            in_specs=[SM, SM, VM] + [VM] * len(mirrors) + [HBM] * 3,
            out_specs=[VM] * len(news) + [HBM] * 3,
            scratch_shapes=[dma((PER,)), dma((PER, 2)), dma((PER, 2)), dma((PER,))],
            input_output_aliases={kept + i: first_kept + i for i in range(3)},
            compiler_params=roomy,
        )(table, jnp.full((1,), t, i32), got, *mirrors, pool, out_k, out_v)
        return outs if lay else (None, *outs)

    def finish(t, mirrored, out_k, out_v):
        return pl.pallas_call(
            last_kernel,
            out_shape=(slots, slots),
            in_specs=[SM, SM, VM, HBM, HBM],
            out_specs=[HBM, HBM],
            scratch_shapes=[dma((PER, 2))],
            input_output_aliases={3: 0, 4: 1},
            compiler_params=roomy,
        )(table, jnp.full((1,), t, i32), mirrored, out_k, out_v)

    marks = []
    a, b, mirrored = first, second, None
    for t in range(PEEL - 1):
        got = cross(a)
        new, pool, out_k, out_v = place(t, got, mirrored, pool, out_k, out_v, True)
        a, b, mirrored = b, new, mirror(got)
        marks.append(new)
    got, a = cross(a), b

    def rest(count, looped, got, a, mirrored, pool, out_k, out_v):
        for t in range(PEEL - 1, PEEL + count):
            more = t < PEEL + count - 1
            if more:
                coming = cross(a)
            b, pool, out_k, out_v = place(t, got, mirrored, pool, out_k, out_v, t + LAG < PEEL + count or looped)
            mirrored = mirror(got)
            if more or looped:
                got, a, spare = coming if more else None, b, a
        end = PEEL + count
        if looped:
            def turn(state):
                t, a, b, mirrored, pool, out_k, out_v = state
                for i in range(TURN):
                    got = cross(a)
                    new, pool, out_k, out_v = place(t + i, got, mirrored, pool, out_k, out_v, True)
                    a, b, mirrored = b, new, mirror(got)
                return t + TURN, a, b, mirrored, pool, out_k, out_v

            state = (jnp.asarray(end, i32), spare, a, mirrored, pool, out_k, out_v)
            end, _, _, mirrored, pool, out_k, out_v = lax.while_loop(lambda state: state[0] < last, turn, state)
        return finish(end, mirrored, out_k, out_v)

    crowd = max(min(2 * (d + 1), CAP * (dp - 1 - d)) for d in range(dp - 1))
    most_left = max(-(-crowd * most // PER) + LAG * (dp - 2) - PEEL, 0)
    counts = [n for n in ENDS if n < most_left] + [min([n for n in ENDS if n >= most_left], default=ENDS[-1])]
    branches = [functools.partial(rest, n, n < most_left and n == counts[-1]) for n in counts]
    left = last - PEEL
    which = sum((left > n).astype(i32) for n in counts[:-1])
    out_k, out_v = lax.switch(which, branches, got, a, mirrored, pool, out_k, out_v)

    part_other = lax.ppermute(part, "side", swap)
    everyone = gather_outputs(
        own_out, dp, lambda reach, pair: lax.optimization_barrier((*pair, marks[min(reach.bit_length(), len(marks)) - 1]))[:2]
    )
    resident_out, new_out = pl.pallas_call(
        functools.partial(finish_kernel, dp, step_count),
        out_shape=(shape((step_count, query_width), bf16), shape((step_count, request_count, query_width), bf16)),
        in_specs=[VM] * 3,
        out_specs=[VM, VM],
        scratch_shapes=[pltpu.VMEM((rows, HEAD_WIDTH), f32)],
    )(part, part_other, everyone)

    out_k, out_v = (out.reshape(CAP, half, width) for out in (out_k, out_v))
    return (resident_out[:, None, :], new_out, out_k, out_v)


def solution(mesh):
    placed = (
        P(("side", "dp"), None, "tp"),
        P(("side", "dp"), None, "tp"),
        P(),
        P(),
        P(None, None, "tp"),
        P(None, None, "tp"),
        P(None, None, "tp"),
        P("dp", "side", "tp"),
        P("dp", "side", "tp"),
        P("dp"),
        P(None, "dp", "tp"),
        P(None, "dp", "tp"),
        P(None, "dp", "tp"),
    )
    return jax.shard_map(
        body,
        mesh=mesh,
        in_specs=placed,
        out_specs=(
            P(None, "dp", "tp"),
            P(None, None, "tp"),
            P("dp", "side", "tp"),
            P("dp", "side", "tp"),
        ),
        check_vma=False,
    )
```

```python
import functools

import jax
import jax.numpy as jnp
from jax import lax
from jax.experimental import pallas as pl
from jax.experimental.pallas import tpu as pltpu
from jax.sharding import PartitionSpec as P

HEAD_WIDTH = 128
CAP = 4
UNIT = 128
PER = 6
MESSAGE = UNIT * PER
PEEL = 5
TURNS = (4, 2, 1)
LAG = 2
LOW = -1e30

HBM = pl.BlockSpec(memory_space=pltpu.HBM)
VM = pl.BlockSpec(memory_space=pltpu.VMEM)
SM = pl.BlockSpec(memory_space=pltpu.SMEM)


def attend(q, q_rows, k_ref, v_ref, tk, tv, first, length, tokens_on, emit):
    steps = q.shape[0]
    keys, width = k_ref.shape
    heads_kv = width // HEAD_WIDTH
    members = q.shape[1] // width
    rows = members * steps
    scale = HEAD_WIDTH ** -0.5
    for kv in range(heads_kv):
        lanes = slice(kv * HEAD_WIDTH, (kv + 1) * HEAD_WIDTH)
        for g in range(members):
            at = (kv * members + g) * HEAD_WIDTH
            q_rows[g * steps:(g + 1) * steps, :] = q[:, at:at + HEAD_WIDTH]
        q32 = q_rows[...]
        scores = lax.dot_general(
            q32.astype(jnp.bfloat16), k_ref[:, lanes], (((1,), (1,)), ((), ())), preferred_element_type=jnp.float32
        ) * scale
        usable = first + lax.broadcasted_iota(jnp.int32, (rows, keys), 1) < length
        scores = jnp.where(usable, scores, LOW)
        row_step = lax.rem(lax.broadcasted_iota(jnp.int32, (rows, 1), 0), steps)
        top = jnp.max(scores, axis=1, keepdims=True)
        extra = []
        for n in range(steps):
            s = jnp.sum(q32 * tk[n:n + 1, lanes], axis=1, keepdims=True) * scale
            on = (row_step >= n) & tokens_on
            s = jnp.where(on, s, LOW)
            extra.append((on, s))
            top = jnp.maximum(top, s)
        weight = jnp.where(usable, jnp.exp(scores - top), 0.0)
        total = jnp.sum(weight, axis=1, keepdims=True)
        acc = lax.dot_general(
            weight.astype(jnp.bfloat16), v_ref[:, lanes], (((1,), (0,)), ((), ())), preferred_element_type=jnp.float32
        )
        for n, (on, s) in enumerate(extra):
            w = jnp.where(on, jnp.exp(s - top), 0.0)
            total = total + w
            acc = acc + w.astype(jnp.bfloat16).astype(jnp.float32) * tv[n:n + 1, lanes]
        emit(kv, top, total, acc)


def attention_kernel(
    dp, resident_length, lengths, rq, rk, rv, rtk, rtv, nq, nk, nv, ntk, ntv, part, own_out, q_rows
):
    side = lax.axis_index("side")
    owner = side * dp + lax.axis_index("dp")
    steps = rq.shape[0]
    keys, width = rk.shape
    rows = steps * rq.shape[1] // width
    f32 = jnp.float32

    def emit_part(kv, top, total, acc):
        at = slice(kv * rows, (kv + 1) * rows)
        part[at, 0:HEAD_WIDTH] = acc
        part[at, HEAD_WIDTH:2 * HEAD_WIDTH] = jnp.broadcast_to(top, (rows, HEAD_WIDTH))
        part[at, 2 * HEAD_WIDTH:] = jnp.broadcast_to(total, (rows, HEAD_WIDTH))

    attend(
        rq[...].astype(f32), q_rows, rk, rv, rtk[...].astype(f32), rtv[...].astype(f32),
        side * keys, resident_length[0], side == 1, emit_part,
    )

    def own(ref):
        picked = []
        for n in range(steps):
            block = ref[n].astype(f32)
            here = lax.broadcasted_iota(jnp.int32, block.shape, 0) == owner
            picked.append(jnp.sum(jnp.where(here, block, 0.0), axis=0, keepdims=True))
        return jnp.concatenate(picked, axis=0)

    def emit_out(kv, top, total, acc):
        own_out[kv * rows:(kv + 1) * rows, :] = acc / total

    attend(own(nq), q_rows, nk, nv, own(ntk), own(ntv), 0, lengths[owner], side >= 0, emit_out)


def finish_kernel(dp, steps, a, b, everyone, resident, new, o_rows):
    w = HEAD_WIDTH
    heads = resident.shape[1] // w
    top = jnp.maximum(a[:, w:2 * w], b[:, w:2 * w])
    ga = jnp.exp(a[:, w:2 * w] - top)
    gb = jnp.exp(b[:, w:2 * w] - top)
    o_rows[...] = (a[:, 0:w] * ga + b[:, 0:w] * gb) / (a[:, 2 * w:] * ga + b[:, 2 * w:] * gb)
    for h in range(heads):
        resident[:, h * w:(h + 1) * w] = o_rows[h * steps:(h + 1) * steps, :].astype(resident.dtype)
    side, me = lax.axis_index("side"), lax.axis_index("dp")
    count = everyone.shape[0]
    order = []
    for r in range(count):
        far = lax.bitwise_xor(me, r % dp) if dp & (dp - 1) == 0 else lax.rem(me - r % dp + dp, dp)
        order.append(far * 2 + lax.bitwise_xor(side, r // dp))
    at_row = lax.broadcasted_iota(jnp.int32, (count, w), 0)
    for n in range(steps):
        for h in range(heads):
            k = h * steps + n
            block = jnp.zeros((count, w), jnp.float32)
            for r in range(count):
                block = jnp.where(at_row == r, everyone[order[r], k:k + 1, :], block)
            new[n, :, h * w:(h + 1) * w] = block.astype(new.dtype)


def units_at(start):
    return pl.ds(pl.multiple_of(start, UNIT), UNIT)


def last_unit(length):
    return (length + UNIT - 1) // UNIT * UNIT - UNIT


def mask_unit(ref, first, length):
    row = lax.broadcasted_iota(jnp.int32, (UNIT, ref.shape[1]), 0)
    block = ref[units_at(first), :]
    ref[units_at(first), :] = jnp.where(first + row < length, block, jnp.zeros_like(block))


def plan_kernel(dp, half, ring_units, lengths, goal, table, out_k, out_v, blank, fill_sem):
    blank[...] = jnp.zeros_like(blank)
    fills = [
        pltpu.make_async_copy(blank, out.at[pl.ds(slot * half, half)], fill_sem.at[i, slot])
        for i, out in enumerate((out_k, out_v)) for slot in range(CAP)
    ]
    for fill in fills:
        fill.start()
    side, me = lax.axis_index("side"), lax.axis_index("dp")
    f32 = jnp.float32
    full = 2 * half
    count = lengths.shape[0]
    wide = table.shape[1]
    id_row = lax.broadcasted_iota(jnp.int32, (count, count), 1).astype(f32)
    id_col = lax.broadcasted_iota(jnp.int32, (count, count), 0).astype(f32)
    eye = id_row == id_col

    def col(row):
        return jnp.sum(jnp.where(eye, jnp.broadcast_to(row, (count, count)), 0.0), axis=1, keepdims=True)

    def spread(scalars):
        row = jnp.zeros((1, count), jnp.int32)
        lane = lax.broadcasted_iota(jnp.int32, (1, count), 1)
        for r in range(count):
            row = jnp.where(lane == r, scalars[r], row)
        return row.astype(f32)

    ids = id_row[0:1]
    late = jnp.where(ids >= dp, 1.0, 0.0)
    src0 = ids - dp * late
    goal0 = spread(goal)
    side_f, me_f = side.astype(f32), me.astype(f32)
    units = jnp.floor((spread(lengths) + (UNIT - 1)) * (1.0 / UNIT))
    units_col, late_col, goal0_col, src0_col = col(units), col(late), col(goal0), col(src0)
    slot = jnp.sum(jnp.where((goal0_col == goal0) & (id_col < id_row), 1.0, 0.0), axis=0, keepdims=True)
    slot_col = col(slot)
    time = lax.broadcasted_iota(jnp.int32, (1, wide), 1).astype(f32)
    here_col = jnp.where(late_col == side_f, 0.0, 1.0)
    steps = jnp.zeros((1, 1), f32)
    sends, passes, ends = [], [], []
    for flip in (False, True):
        turned = (lambda x: dp - 1 - x) if flip else (lambda x: x)
        s, g, m, s_col, g_col = turned(src0), turned(goal0), turned(me_f), turned(src0_col), turned(goal0_col)
        ahead = (g_col > g) | ((g_col == g) & ((s_col > s) | ((s_col == s) & (id_col < id_row))))
        crosses, bases, starts = [], [], []
        for d in range(dp - 1):
            cross = (s <= d) & (g > d)
            base = jnp.sum(jnp.where(ahead & (s_col <= d) & (g_col > d), units_col, 0.0), axis=0, keepdims=True)
            load = jnp.sum(jnp.where(cross, units, 0.0), axis=1, keepdims=True)
            start = jnp.zeros((1, 1), f32)
            if d > 0:
                lead = jnp.floor((base - bases[-1]) * (1.0 / PER))
                gap = jnp.where(cross & crosses[-1], starts[-1] + LAG - lead, 0.0)
                start = jnp.maximum(jnp.max(gap, axis=1, keepdims=True), 0.0)
            steps = jnp.maximum(steps, jnp.where(load > 0, jnp.floor((load + (PER - 1)) * (1.0 / PER)) + start, 0.0))
            crosses.append(cross)
            bases.append(base)
            starts.append(start)

        def at(link):
            base, start, used = jnp.zeros((1, count), f32), jnp.zeros((1, 1), f32), jnp.zeros((1, count), f32)
            for d in range(dp - 1):
                base = jnp.where(link == d, bases[d], base)
                start = jnp.where(link == d, starts[d], start)
                used = jnp.where(link == d, jnp.where(crosses[d], units, 0.0), used)
            return col(base), start * PER, col(used)

        def ring_row(p):
            return (p - ring_units * jnp.floor((p + 0.5) * (1.0 / ring_units))) * UNIT

        def pick(hit, value):
            return jnp.sum(jnp.where(hit, value + 1.0, 0.0), axis=0, keepdims=True) - 1.0

        base, start, used = at(m)
        p = time - start
        c = p - base
        hit = (c >= 0) & (c < used)
        sends.append(jnp.maximum(pick(hit, jnp.where(s_col == m, here_col * full + c * UNIT, 2 * full + ring_row(p))), 0.0))
        here, start, used = at(m - 1)
        c = time - start - here
        hit = (c >= 0) & (c < used)
        passes.append(pick(hit & (g_col != m), 2 * full + ring_row(base + c)))
        row = c * UNIT - half * side_f
        ends.append(pick(hit & (g_col == m) & (row >= 0) & (row < half), slot_col * half + row))
    right = side_f == 0.0
    for r, row in enumerate((
        jnp.where(right, sends[0], sends[1]), jnp.where(right, passes[0], passes[1]),
        jnp.where(right, ends[0], ends[1]), jnp.where(right, ends[1], ends[0]),
    )):
        table[r:r + 1, :] = row.astype(jnp.int32)
    stay = jnp.where((src0 == me_f) & (goal0 == me_f), slot + 1.0, 0.0)
    home = [
        jnp.sum(jnp.where(late == which, stay, 0.0), axis=1, keepdims=True) - 1.0 for which in (side_f, 1.0 - side_f)
    ]
    last = jnp.where(time == 0, steps, jnp.where(time == 1, home[0], home[1]))
    table[4:5, :] = last.astype(jnp.int32)
    table[5:8, :] = jnp.zeros((3, wide), jnp.int32)
    for fill in fills:
        fill.wait()


def first_kernel(dp, t, table, lengths, pk, pv, xk, xv, send, edge, sem, done):
    side, me = lax.axis_index("side"), lax.axis_index("dp")
    full = pk.shape[0]
    sources = ((pk, pv), (xk, xv))
    length = [lengths[which * dp + me] for which in (side, 1 - side)]
    last = [last_unit(x) for x in length]
    masked = [
        pltpu.make_async_copy(a.at[units_at(last[j])], edge.at[j, n], sem.at[j, n])
        for j in range(2) for n, a in enumerate(sources[j])
    ]
    for copy in masked:
        copy.start()
    codes = [table[0, t * PER + i] for i in range(PER)]
    for i, code in enumerate(codes):
        for j in range(2):
            row = code - j * full

            @pl.when((row >= 0) & (row < full))
            def _():
                for n in range(2):
                    pltpu.make_async_copy(
                        sources[j][n].at[units_at(row)], send.at[n, pl.ds(i * UNIT, UNIT)], done.at[i, n]
                    ).start()
    for copy in masked:
        copy.wait()
    for j in range(2):
        for n in range(2):
            mask_unit(edge.at[j, n], 0, length[j] - last[j])
    for i, code in enumerate(codes):
        @pl.when(code < 2 * full)
        def _():
            for n in range(2):
                pltpu.make_async_copy(pk.at[pl.ds(0, UNIT)], send.at[n, pl.ds(i * UNIT, UNIT)], done.at[i, n]).wait()
    for i, code in enumerate(codes):
        for j in range(2):
            @pl.when(code == j * full + last[j])
            def _():
                send[:, i * UNIT:(i + 1) * UNIT, :] = edge[j]


def pool_kernel(dp, table, lengths, pk, pv, xk, xv, ok, ov, pool, out_k, out_v, stage, load_sem, pool_sem, home_sem):
    side, me = lax.axis_index("side"), lax.axis_index("dp")
    full = pk.shape[0]
    half = full // 2
    loads = [
        pltpu.make_async_copy(a, stage.at[j, n], load_sem.at[j, n])
        for j, pair in enumerate(((pk, pv), (xk, xv))) for n, a in enumerate(pair)
    ]
    for copy in loads:
        copy.start()
    stores, homes = [], []
    for j in range(2):
        length = lengths[lax.bitwise_xor(side, j) * dp + me]
        last = last_unit(length)
        for n in range(2):
            loads[2 * j + n].wait()
            mask_unit(stage.at[j, n], last, length)
        store = pltpu.make_async_copy(stage.at[j], pool.at[:, pl.ds(j * full, full)], pool_sem.at[j])
        store.start()
        stores.append(store)
        slot = table[4, 1 + j]
        count = jnp.where(slot >= 0, jnp.clip((last + UNIT - side * half) // UNIT, 0, half // UNIT), 0)

        def home(u, wait, j=j, slot=slot):
            for n, out in enumerate((out_k, out_v)):
                copy = pltpu.make_async_copy(
                    stage.at[j, n, units_at(side * half + u * UNIT)], out.at[units_at(slot * half + u * UNIT)],
                    home_sem.at[j, n, u],
                )
                copy.wait() if wait else copy.start()

        pl.loop(0, count)(functools.partial(home, wait=False))
        homes.append((count, home))
    for count, home in homes:
        pl.loop(0, count)(functools.partial(home, wait=True))
    for store in stores:
        store.wait()


def end_copies(table, t, row, take, out_k, out_v, sem):
    copies = []
    for i in range(PER):
        code = table[row, t * PER + i]
        to = units_at(jnp.maximum(code, 0))
        copies.append((code >= 0, [
            pltpu.make_async_copy(take.at[n, pl.ds(i * UNIT, UNIT)], out.at[to], sem.at[i, n])
            for n, out in enumerate((out_k, out_v))
        ]))
    return copies


def when_all(copies, act):
    for on, group in copies:
        @pl.when(on)
        def _():
            for copy in group:
                act(copy)


def step_kernel(
    table, now, got, mirrored, pool_in, ok, ov, send, pool, out_k, out_v, pass_sem, got_sem, mirror_sem, send_sem
):
    t = now[0]
    passes = []
    for i in range(PER):
        code = table[1, t * PER + i]
        to = pool.at[:, units_at(jnp.maximum(code, 0))]
        passes.append((code >= 0, [pltpu.make_async_copy(got.at[:, pl.ds(i * UNIT, UNIT)], to, pass_sem.at[i])]))
    when_all(passes, lambda copy: copy.start())
    ends = end_copies(table, t, 2, got, out_k, out_v, got_sem)
    if mirrored is not None:
        ends += end_copies(table, t - 1, 3, mirrored, out_k, out_v, mirror_sem)
    when_all(ends, lambda copy: copy.start())
    when_all(passes, lambda copy: copy.wait())
    if send is not None:
        lay = [
            pltpu.make_async_copy(
                pool.at[:, units_at(table[0, (t + LAG) * PER + i])], send.at[:, pl.ds(i * UNIT, UNIT)], send_sem.at[i]
            )
            for i in range(PER)
        ]
        for copy in lay:
            copy.start()
        for copy in lay:
            copy.wait()
    when_all(ends, lambda copy: copy.wait())


def last_kernel(table, now, mirrored, ok, ov, out_k, out_v, sem):
    ends = end_copies(table, now[0] - 1, 3, mirrored, out_k, out_v, sem)
    when_all(ends, lambda copy: copy.start())
    when_all(ends, lambda copy: copy.wait())


def gather_stages(own, dp):
    block = jnp.stack([own, lax.ppermute(own, "side", [(0, 1), (1, 0)])])
    if dp & (dp - 1):
        rest = [lax.ppermute(block, "dp", [(i, (i + x) % dp) for i in range(dp)]) for x in range(1, dp)]
        yield jnp.concatenate([block] + (yield rest))
    else:
        for stage in range(dp.bit_length() - 1):
            got = yield lax.ppermute(block, "dp", [(i, i ^ (1 << stage)) for i in range(dp)])
            block = jnp.concatenate([block, got])
            yield block


def body(
    prompt_keys,
    prompt_values,
    prompt_lengths,
    assignment,
    new_queries,
    incoming_token_keys,
    incoming_token_values,
    stored_keys,
    stored_values,
    resident_lengths,
    resident_queries,
    stored_token_keys,
    stored_token_values,
):
    step_count = resident_queries.shape[0]
    dp = lax.axis_size("dp")
    request_count = prompt_lengths.shape[0]
    full, width = prompt_keys.shape[1:]
    query_width = new_queries.shape[2]
    half = full // 2
    bf16, f32, i32 = jnp.bfloat16, jnp.float32, jnp.int32
    swap = [(0, 1), (1, 0)]
    shape = jax.ShapeDtypeStruct
    dma = pltpu.SemaphoreType.DMA
    roomy = pltpu.CompilerParams(vmem_limit_bytes=16 << 20)

    pk, pv = prompt_keys[0], prompt_values[0]
    xk, xv = lax.ppermute(pk, "side", swap), lax.ppermute(pv, "side", swap)

    most = full // UNIT
    ring_units = 2 * most + (LAG + 1) * PER
    steps_max = -(-request_count * most // PER) + LAG * dp + PEEL + max(TURNS) + LAG
    wide = -(-steps_max * PER // 128) * 128
    slots = shape((CAP * half, width), bf16)
    table, out_k, out_v = pl.pallas_call(
        functools.partial(plan_kernel, dp, half, ring_units),
        out_shape=(shape((8, wide), i32), slots, slots),
        in_specs=[SM, SM],
        out_specs=[VM, HBM, HBM],
        scratch_shapes=[pltpu.VMEM((half, width), bf16), dma((2, CAP))],
        compiler_params=roomy,
    )(prompt_lengths, jnp.reshape(assignment, (request_count,)))
    last = table[4, 0]

    message = shape((2, MESSAGE, width), bf16)
    pool_shape = shape((2, 2 * full + ring_units * UNIT, width), bf16)

    def lay_first(t, table):
        return pl.pallas_call(
            functools.partial(first_kernel, dp, t),
            out_shape=message,
            in_specs=[SM, SM, HBM, HBM, HBM, HBM],
            out_specs=VM,
            scratch_shapes=[pltpu.VMEM((2, 2, UNIT, width), bf16), dma((2, 2)), dma((PER, 2))],
            compiler_params=pltpu.CompilerParams(vmem_limit_bytes=56 << 20),
        )(table, prompt_lengths, pk, pv, xk, xv)

    first = lay_first(0, table)
    second = lay_first(1, lax.optimization_barrier((table, first))[0])

    held = lax.optimization_barrier((new_queries, second))[0]
    rows = step_count * query_width // HEAD_WIDTH
    part, own_out = pl.pallas_call(
        functools.partial(attention_kernel, dp),
        out_shape=(shape((rows, 3 * HEAD_WIDTH), f32), shape((rows, HEAD_WIDTH), f32)),
        in_specs=[SM, SM] + [VM] * 10,
        out_specs=[VM, VM],
        scratch_shapes=[pltpu.VMEM((step_count * query_width // width, HEAD_WIDTH), f32)],
        compiler_params=roomy,
    )(
        resident_lengths, prompt_lengths,
        resident_queries[:, 0], stored_keys[0], stored_values[0], stored_token_keys[:, 0], stored_token_values[:, 0],
        held, pk, pv, incoming_token_keys, incoming_token_values,
    )

    tied = lax.optimization_barrier((table, second, own_out))
    pool, out_k, out_v = pl.pallas_call(
        functools.partial(pool_kernel, dp),
        out_shape=(pool_shape, slots, slots),
        in_specs=[SM, SM] + [HBM] * 6,
        out_specs=[HBM] * 3,
        scratch_shapes=[
            pltpu.VMEM((2, 2, full, width), bf16), dma((2, 2)), dma((2,)), dma((2, 2, half // UNIT)),
        ],
        input_output_aliases={6: 1, 7: 2},
        compiler_params=roomy,
    )(tied[0], prompt_lengths, pk, pv, xk, xv, out_k, out_v)

    hops = [(i, i + 1) for i in range(dp - 1)] + [(dp + i + 1, dp + i) for i in range(dp - 1)]

    def cross(send):
        return lax.ppermute(send, ("side", "dp"), hops)

    def mirror(got):
        return lax.ppermute(got, "side", swap)

    def place(t, got, mirrored, pool, out_k, out_v, lay):
        news = [message] if lay else []
        first_kept = len(news)
        mirrors = [] if mirrored is None else [mirrored]

        def kernel(table, now, got, *refs):
            refs = list(refs)
            mirrored = refs.pop(0) if mirrors else None
            send = refs.pop(3) if lay else None
            step_kernel(table, now, got, mirrored, *refs[:3], send, *refs[3:])

        kept = 3 + len(mirrors)
        outs = pl.pallas_call(
            kernel,
            out_shape=(*news, pool_shape, slots, slots),
            in_specs=[SM, SM, VM] + [VM] * len(mirrors) + [HBM] * 3,
            out_specs=[VM] * len(news) + [HBM] * 3,
            scratch_shapes=[dma((PER,)), dma((PER, 2)), dma((PER, 2)), dma((PER,))],
            input_output_aliases={kept + i: first_kept + i for i in range(3)},
            compiler_params=roomy,
        )(table, jnp.full((1,), t, i32), got, *mirrors, pool, out_k, out_v)
        return outs if lay else (None, *outs)

    def finish(t, mirrored, out_k, out_v):
        return pl.pallas_call(
            last_kernel,
            out_shape=(slots, slots),
            in_specs=[SM, SM, VM, HBM, HBM],
            out_specs=[HBM, HBM],
            scratch_shapes=[dma((PER, 2))],
            input_output_aliases={3: 0, 4: 1},
            compiler_params=roomy,
        )(table, jnp.full((1,), t, i32), mirrored, out_k, out_v)

    def advance(count, state, beside=None):
        t, got, a, mirrored, pool, out_k, out_v = state
        for i in range(count):
            coming = cross(a)
            if beside is not None:
                got = beside(i, got, a)
            a, pool, out_k, out_v = place(t + i, got, mirrored, pool, out_k, out_v, True)
            got, mirrored = coming, mirror(got)
        return t + count, got, a, mirrored, pool, out_k, out_v

    part_other = lax.ppermute(part, "side", swap)
    stages = gather_stages(own_out, dp)
    small = [part_other, next(stages)]

    def beside(i, got, a):
        if i % 2 == 0:
            return got
        tied, small[0] = lax.optimization_barrier((small[1], small[0], a))[:2]
        block = stages.send(tied)
        small[1] = block
        for arrived in stages:
            if i < PEEL - 2:
                small[1] = arrived
                break
            block = small[1] = stages.send(arrived)
        return lax.optimization_barrier((got, block))[0]

    second = lax.optimization_barrier((second, own_out, pool))[0]
    state = advance(PEEL - 1, (0, cross(first), second, None, pool, out_k, out_v), beside)
    part_other, everyone = small

    state = (jnp.asarray(state[0], i32), *state[1:])
    for count in TURNS:
        state = lax.while_loop(
            lambda state, count=count: state[0] + count < last, functools.partial(advance, count), state
        )
    t, got, _, mirrored, pool, out_k, out_v = state
    _, _, out_k, out_v = place(t, got, mirrored, pool, out_k, out_v, False)
    out_k, out_v = finish(t + 1, mirror(got), out_k, out_v)

    part, part_other, everyone, _ = lax.optimization_barrier((part, part_other, everyone, t))
    resident_out, new_out = pl.pallas_call(
        functools.partial(finish_kernel, dp, step_count),
        out_shape=(shape((step_count, query_width), bf16), shape((step_count, request_count, query_width), bf16)),
        in_specs=[VM] * 3,
        out_specs=[VM, VM],
        scratch_shapes=[pltpu.VMEM((rows, HEAD_WIDTH), f32)],
    )(part, part_other, everyone)
    out_k, out_v = (out.reshape(CAP, half, width) for out in (out_k, out_v))
    return (resident_out[:, None, :], new_out, out_k, out_v)


def solution(mesh):
    placed = (
        P(("side", "dp"), None, "tp"),
        P(("side", "dp"), None, "tp"),
        P(),
        P(),
        P(None, None, "tp"),
        P(None, None, "tp"),
        P(None, None, "tp"),
        P("dp", "side", "tp"),
        P("dp", "side", "tp"),
        P("dp"),
        P(None, "dp", "tp"),
        P(None, "dp", "tp"),
        P(None, "dp", "tp"),
    )
    return jax.shard_map(
        body,
        mesh=mesh,
        in_specs=placed,
        out_specs=(
            P(None, "dp", "tp"),
            P(None, None, "tp"),
            P("dp", "side", "tp"),
            P("dp", "side", "tp"),
        ),
        check_vma=False,
    )
```

```python
import functools

import jax
import jax.numpy as jnp
from jax import lax
from jax.experimental import pallas as pl
from jax.experimental.pallas import tpu as pltpu
from jax.sharding import PartitionSpec as P

HEAD_WIDTH = 128
CAP = 4
UNIT = 128
PER = 6
MESSAGE = UNIT * PER
PEEL = 5
TURNS = (3, 1)
LAG = 2
LOW = -1e30

HBM = pl.BlockSpec(memory_space=pltpu.HBM)
VM = pl.BlockSpec(memory_space=pltpu.VMEM)
SM = pl.BlockSpec(memory_space=pltpu.SMEM)


def attend(q, q_rows, k_ref, v_ref, tk, tv, first, length, tokens_on, emit):
    steps = q.shape[0]
    keys, width = k_ref.shape
    heads_kv = width // HEAD_WIDTH
    members = q.shape[1] // width
    rows = members * steps
    scale = HEAD_WIDTH ** -0.5
    for kv in range(heads_kv):
        lanes = slice(kv * HEAD_WIDTH, (kv + 1) * HEAD_WIDTH)
        for g in range(members):
            at = (kv * members + g) * HEAD_WIDTH
            q_rows[g * steps:(g + 1) * steps, :] = q[:, at:at + HEAD_WIDTH]
        q32 = q_rows[...]
        scores = lax.dot_general(
            q32.astype(jnp.bfloat16), k_ref[:, lanes], (((1,), (1,)), ((), ())), preferred_element_type=jnp.float32
        ) * scale
        usable = first + lax.broadcasted_iota(jnp.int32, (rows, keys), 1) < length
        scores = jnp.where(usable, scores, LOW)
        row_step = lax.rem(lax.broadcasted_iota(jnp.int32, (rows, 1), 0), steps)
        top = jnp.max(scores, axis=1, keepdims=True)
        extra = []
        for n in range(steps):
            s = jnp.sum(q32 * tk[n:n + 1, lanes], axis=1, keepdims=True) * scale
            on = (row_step >= n) & tokens_on
            s = jnp.where(on, s, LOW)
            extra.append((on, s))
            top = jnp.maximum(top, s)
        weight = jnp.where(usable, jnp.exp(scores - top), 0.0)
        total = jnp.sum(weight, axis=1, keepdims=True)
        acc = lax.dot_general(
            weight.astype(jnp.bfloat16), v_ref[:, lanes], (((1,), (0,)), ((), ())), preferred_element_type=jnp.float32
        )
        for n, (on, s) in enumerate(extra):
            w = jnp.where(on, jnp.exp(s - top), 0.0)
            total = total + w
            acc = acc + w.astype(jnp.bfloat16).astype(jnp.float32) * tv[n:n + 1, lanes]
        emit(kv, top, total, acc)


def attention_kernel(
    dp, resident_length, lengths, rq, rk, rv, rtk, rtv, nq, nk, nv, ntk, ntv, part, own_out, q_rows
):
    side = lax.axis_index("side")
    owner = side * dp + lax.axis_index("dp")
    steps = rq.shape[0]
    keys, width = rk.shape
    rows = steps * rq.shape[1] // width
    f32 = jnp.float32

    def emit_part(kv, top, total, acc):
        at = slice(kv * rows, (kv + 1) * rows)
        part[at, 0:HEAD_WIDTH] = acc
        part[at, HEAD_WIDTH:2 * HEAD_WIDTH] = jnp.broadcast_to(top, (rows, HEAD_WIDTH))
        part[at, 2 * HEAD_WIDTH:] = jnp.broadcast_to(total, (rows, HEAD_WIDTH))

    attend(
        rq[...].astype(f32), q_rows, rk, rv, rtk[...].astype(f32), rtv[...].astype(f32),
        side * keys, resident_length[0], side == 1, emit_part,
    )

    def own(ref):
        picked = []
        for n in range(steps):
            block = ref[n].astype(f32)
            here = lax.broadcasted_iota(jnp.int32, block.shape, 0) == owner
            picked.append(jnp.sum(jnp.where(here, block, 0.0), axis=0, keepdims=True))
        return jnp.concatenate(picked, axis=0)

    def emit_out(kv, top, total, acc):
        own_out[kv * rows:(kv + 1) * rows, :] = acc / total

    attend(own(nq), q_rows, nk, nv, own(ntk), own(ntv), 0, lengths[owner], side >= 0, emit_out)


def finish_kernel(dp, steps, a, b, everyone, resident, new, o_rows):
    w = HEAD_WIDTH
    heads = resident.shape[1] // w
    top = jnp.maximum(a[:, w:2 * w], b[:, w:2 * w])
    ga = jnp.exp(a[:, w:2 * w] - top)
    gb = jnp.exp(b[:, w:2 * w] - top)
    o_rows[...] = (a[:, 0:w] * ga + b[:, 0:w] * gb) / (a[:, 2 * w:] * ga + b[:, 2 * w:] * gb)
    for h in range(heads):
        resident[:, h * w:(h + 1) * w] = o_rows[h * steps:(h + 1) * steps, :].astype(resident.dtype)
    side, me = lax.axis_index("side"), lax.axis_index("dp")
    count = everyone.shape[0]
    order = []
    for r in range(count):
        far = lax.bitwise_xor(me, r % dp) if dp & (dp - 1) == 0 else lax.rem(me - r % dp + dp, dp)
        order.append(far * 2 + lax.bitwise_xor(side, r // dp))
    at_row = lax.broadcasted_iota(jnp.int32, (count, w), 0)
    for n in range(steps):
        for h in range(heads):
            k = h * steps + n
            block = jnp.zeros((count, w), jnp.float32)
            for r in range(count):
                block = jnp.where(at_row == r, everyone[order[r], k:k + 1, :], block)
            new[n, :, h * w:(h + 1) * w] = block.astype(new.dtype)


def units_at(start):
    return pl.ds(pl.multiple_of(start, UNIT), UNIT)


def last_unit(length):
    return (length + UNIT - 1) // UNIT * UNIT - UNIT


def mask_unit(ref, first, length):
    row = lax.broadcasted_iota(jnp.int32, (UNIT, ref.shape[1]), 0)
    block = ref[units_at(first), :]
    ref[units_at(first), :] = jnp.where(first + row < length, block, jnp.zeros_like(block))


def plan_kernel(dp, half, ring_units, lengths, goal, table, out_k, out_v, blank, fill_sem):
    blank[...] = jnp.zeros_like(blank)
    fills = [
        pltpu.make_async_copy(blank, out.at[pl.ds(slot * half, half)], fill_sem.at[i, slot])
        for i, out in enumerate((out_k, out_v)) for slot in range(CAP)
    ]
    for fill in fills:
        fill.start()
    side, me = lax.axis_index("side"), lax.axis_index("dp")
    f32 = jnp.float32
    full = 2 * half
    count = lengths.shape[0]
    wide = table.shape[1]
    id_row = lax.broadcasted_iota(jnp.int32, (count, count), 1).astype(f32)
    id_col = lax.broadcasted_iota(jnp.int32, (count, count), 0).astype(f32)
    eye = id_row == id_col

    def col(row):
        return jnp.sum(jnp.where(eye, jnp.broadcast_to(row, (count, count)), 0.0), axis=1, keepdims=True)

    def spread(scalars):
        row = jnp.zeros((1, count), jnp.int32)
        lane = lax.broadcasted_iota(jnp.int32, (1, count), 1)
        for r in range(count):
            row = jnp.where(lane == r, scalars[r], row)
        return row.astype(f32)

    ids = id_row[0:1]
    late = jnp.where(ids >= dp, 1.0, 0.0)
    src0 = ids - dp * late
    goal0 = spread(goal)
    side_f, me_f = side.astype(f32), me.astype(f32)
    units = jnp.floor((spread(lengths) + (UNIT - 1)) * (1.0 / UNIT))
    units_col, late_col, goal0_col, src0_col = col(units), col(late), col(goal0), col(src0)
    slot = jnp.sum(jnp.where((goal0_col == goal0) & (id_col < id_row), 1.0, 0.0), axis=0, keepdims=True)
    slot_col = col(slot)
    time = lax.broadcasted_iota(jnp.int32, (1, wide), 1).astype(f32)
    here_col = jnp.where(late_col == side_f, 0.0, 1.0)
    steps = jnp.zeros((1, 1), f32)
    sends, passes, ends = [], [], []
    for flip in (False, True):
        turned = (lambda x: dp - 1 - x) if flip else (lambda x: x)
        s, g, m, s_col, g_col = turned(src0), turned(goal0), turned(me_f), turned(src0_col), turned(goal0_col)
        ahead = (g_col > g) | ((g_col == g) & ((s_col > s) | ((s_col == s) & (id_col < id_row))))
        crosses, bases, starts = [], [], []
        for d in range(dp - 1):
            cross = (s <= d) & (g > d)
            base = jnp.sum(jnp.where(ahead & (s_col <= d) & (g_col > d), units_col, 0.0), axis=0, keepdims=True)
            load = jnp.sum(jnp.where(cross, units, 0.0), axis=1, keepdims=True)
            start = jnp.zeros((1, 1), f32)
            if d > 0:
                lead = jnp.floor((base - bases[-1]) * (1.0 / PER))
                gap = jnp.where(cross & crosses[-1], starts[-1] + LAG - lead, 0.0)
                start = jnp.maximum(jnp.max(gap, axis=1, keepdims=True), 0.0)
            steps = jnp.maximum(steps, jnp.where(load > 0, jnp.floor((load + (PER - 1)) * (1.0 / PER)) + start, 0.0))
            crosses.append(cross)
            bases.append(base)
            starts.append(start)

        def at(link):
            base, start, used = jnp.zeros((1, count), f32), jnp.zeros((1, 1), f32), jnp.zeros((1, count), f32)
            for d in range(dp - 1):
                base = jnp.where(link == d, bases[d], base)
                start = jnp.where(link == d, starts[d], start)
                used = jnp.where(link == d, jnp.where(crosses[d], units, 0.0), used)
            return col(base), start * PER, col(used)

        def ring_row(p):
            return (p - ring_units * jnp.floor((p + 0.5) * (1.0 / ring_units))) * UNIT

        def pick(hit, value):
            return jnp.sum(jnp.where(hit, value + 1.0, 0.0), axis=0, keepdims=True) - 1.0

        base, start, used = at(m)
        p = time - start
        c = p - base
        hit = (c >= 0) & (c < used)
        sends.append(jnp.maximum(pick(hit, jnp.where(s_col == m, here_col * full + c * UNIT, 2 * full + ring_row(p))), 0.0))
        here, start, used = at(m - 1)
        c = time - start - here
        hit = (c >= 0) & (c < used)
        passes.append(pick(hit & (g_col != m), 2 * full + ring_row(base + c)))
        row = c * UNIT - half * side_f
        ends.append(pick(hit & (g_col == m) & (row >= 0) & (row < half), slot_col * half + row))
    right = side_f == 0.0
    for r, row in enumerate((
        jnp.where(right, sends[0], sends[1]), jnp.where(right, passes[0], passes[1]),
        jnp.where(right, ends[0], ends[1]), jnp.where(right, ends[1], ends[0]),
    )):
        table[r:r + 1, :] = row.astype(jnp.int32)
    stay = jnp.where((src0 == me_f) & (goal0 == me_f), slot + 1.0, 0.0)
    home = [
        jnp.sum(jnp.where(late == which, stay, 0.0), axis=1, keepdims=True) - 1.0 for which in (side_f, 1.0 - side_f)
    ]
    last = jnp.where(time == 0, steps, jnp.where(time == 1, home[0], home[1]))
    table[4:5, :] = last.astype(jnp.int32)
    table[5:8, :] = jnp.zeros((3, wide), jnp.int32)
    for fill in fills:
        fill.wait()


def first_kernel(dp, table, lengths, pk, pv, xk, xv, send):
    side, me = lax.axis_index("side"), lax.axis_index("dp")
    full = pk.shape[0]
    for j, pair in enumerate(((pk, pv), (xk, xv))):
        length = lengths[lax.bitwise_xor(side, j) * dp + me]
        last = last_unit(length)
        for i in range(PER):
            row = table[0, i] - j * full

            @pl.when((row >= 0) & (row < full))
            def _():
                for n in range(2):
                    send[n, i * UNIT:(i + 1) * UNIT, :] = pair[n][units_at(row), :]

            @pl.when(row == last)
            def _():
                for n in range(2):
                    mask_unit(send.at[n, i * UNIT:(i + 1) * UNIT], 0, length - last)


def pool_kernel(
    dp, table, lengths, pk, pv, xk, xv, ok, ov, pool, send, out_k, out_v, stage, load_sem, pool_sem, home_sem
):
    side, me = lax.axis_index("side"), lax.axis_index("dp")
    full = pk.shape[0]
    half = full // 2
    loads = [
        pltpu.make_async_copy(a, stage.at[j, n], load_sem.at[j, n])
        for j, pair in enumerate(((pk, pv), (xk, xv))) for n, a in enumerate(pair)
    ]
    for copy in loads:
        copy.start()
    stores, homes = [], []
    for j in range(2):
        length = lengths[lax.bitwise_xor(side, j) * dp + me]
        last = last_unit(length)
        for n in range(2):
            loads[2 * j + n].wait()
            mask_unit(stage.at[j, n], last, length)
        store = pltpu.make_async_copy(stage.at[j], pool.at[:, pl.ds(j * full, full)], pool_sem.at[j])
        store.start()
        stores.append(store)
        slot = table[4, 1 + j]
        count = jnp.where(slot >= 0, jnp.clip((last + UNIT - side * half) // UNIT, 0, half // UNIT), 0)

        def home(u, wait, j=j, slot=slot):
            for n, out in enumerate((out_k, out_v)):
                copy = pltpu.make_async_copy(
                    stage.at[j, n, units_at(side * half + u * UNIT)], out.at[units_at(slot * half + u * UNIT)],
                    home_sem.at[j, n, u],
                )
                copy.wait() if wait else copy.start()

        pl.loop(0, count)(functools.partial(home, wait=False))
        homes.append((count, home))
    for i in range(PER):
        code = table[0, PER + i]
        j = jnp.clip(code // full, 0, 1)
        row = jnp.clip(code - j * full, 0, full - UNIT)
        for n in range(2):
            send[n, i * UNIT:(i + 1) * UNIT, :] = stage[j, n, units_at(row), :]
    for count, home in homes:
        pl.loop(0, count)(functools.partial(home, wait=True))
    for store in stores:
        store.wait()


def end_copies(table, t, row, take, out_k, out_v, sem):
    copies = []
    for i in range(PER):
        code = table[row, t * PER + i]
        to = units_at(jnp.maximum(code, 0))
        copies.append((code >= 0, [
            pltpu.make_async_copy(take.at[n, pl.ds(i * UNIT, UNIT)], out.at[to], sem.at[i, n])
            for n, out in enumerate((out_k, out_v))
        ]))
    return copies


def when_all(copies, act):
    @pl.when(functools.reduce(jnp.logical_or, [on for on, _ in copies]))
    def _():
        for on, group in copies:
            @pl.when(on)
            def _():
                for copy in group:
                    act(copy)


def step_kernel(
    table, now, got, mirrored, pool_in, ok, ov, send, pool, out_k, out_v, pass_sem, got_sem, mirror_sem, send_sem
):
    t = now[0]
    passes = []
    for i in range(PER):
        code = table[1, t * PER + i]
        to = pool.at[:, units_at(jnp.maximum(code, 0))]
        passes.append((code >= 0, [pltpu.make_async_copy(got.at[:, pl.ds(i * UNIT, UNIT)], to, pass_sem.at[i])]))
    when_all(passes, lambda copy: copy.start())
    ends = [end_copies(table, t, 2, got, out_k, out_v, got_sem)]
    if mirrored is not None:
        ends.append(end_copies(table, t - 1, 3, mirrored, out_k, out_v, mirror_sem))
    for copies in ends:
        when_all(copies, lambda copy: copy.start())
    when_all(passes, lambda copy: copy.wait())
    if send is not None:
        lay = [
            pltpu.make_async_copy(
                pool.at[:, units_at(table[0, (t + LAG) * PER + i])], send.at[:, pl.ds(i * UNIT, UNIT)], send_sem.at[i]
            )
            for i in range(PER)
        ]
        for copy in lay:
            copy.start()
        for copy in lay:
            copy.wait()
    for copies in ends:
        when_all(copies, lambda copy: copy.wait())


def last_kernel(table, now, mirrored, ok, ov, out_k, out_v, sem):
    ends = end_copies(table, now[0] - 1, 3, mirrored, out_k, out_v, sem)
    when_all(ends, lambda copy: copy.start())
    when_all(ends, lambda copy: copy.wait())


def gather_stages(own, dp):
    block = jnp.stack([own, lax.ppermute(own, "side", [(0, 1), (1, 0)])])
    if dp & (dp - 1):
        rest = [lax.ppermute(block, "dp", [(i, (i + x) % dp) for i in range(dp)]) for x in range(1, dp)]
        yield jnp.concatenate([block] + (yield rest))
    else:
        for stage in range(dp.bit_length() - 1):
            got = yield lax.ppermute(block, "dp", [(i, i ^ (1 << stage)) for i in range(dp)])
            block = jnp.concatenate([block, got])
            yield block


def body(
    prompt_keys,
    prompt_values,
    prompt_lengths,
    assignment,
    new_queries,
    incoming_token_keys,
    incoming_token_values,
    stored_keys,
    stored_values,
    resident_lengths,
    resident_queries,
    stored_token_keys,
    stored_token_values,
):
    step_count = resident_queries.shape[0]
    dp = lax.axis_size("dp")
    request_count = prompt_lengths.shape[0]
    full, width = prompt_keys.shape[1:]
    query_width = new_queries.shape[2]
    half = full // 2
    bf16, f32, i32 = jnp.bfloat16, jnp.float32, jnp.int32
    swap = [(0, 1), (1, 0)]
    shape = jax.ShapeDtypeStruct
    dma = pltpu.SemaphoreType.DMA
    roomy = pltpu.CompilerParams(vmem_limit_bytes=16 << 20)

    pk, pv = prompt_keys[0], prompt_values[0]
    xk, xv = lax.ppermute(pk, "side", swap), lax.ppermute(pv, "side", swap)

    most = full // UNIT
    ring_units = 2 * most + (LAG + 1) * PER
    steps_max = -(-request_count * most // PER) + LAG * dp + PEEL + max(TURNS) + LAG
    wide = -(-steps_max * PER // 128) * 128
    slots = shape((CAP * half, width), bf16)
    table, out_k, out_v = pl.pallas_call(
        functools.partial(plan_kernel, dp, half, ring_units),
        out_shape=(shape((8, wide), i32), slots, slots),
        in_specs=[SM, SM],
        out_specs=[VM, HBM, HBM],
        scratch_shapes=[pltpu.VMEM((half, width), bf16), dma((2, CAP))],
        compiler_params=roomy,
    )(prompt_lengths, jnp.reshape(assignment, (request_count,)))
    last = table[4, 0]

    message = shape((2, MESSAGE, width), bf16)
    pool_shape = shape((2, 2 * full + ring_units * UNIT, width), bf16)
    first = pl.pallas_call(
        functools.partial(first_kernel, dp),
        out_shape=message,
        in_specs=[SM, SM] + [VM] * 4,
        out_specs=VM,
        compiler_params=roomy,
    )(table, prompt_lengths, pk, pv, xk, xv)

    held = lax.optimization_barrier((new_queries, first))[0]
    rows = step_count * query_width // HEAD_WIDTH
    part, own_out = pl.pallas_call(
        functools.partial(attention_kernel, dp),
        out_shape=(shape((rows, 3 * HEAD_WIDTH), f32), shape((rows, HEAD_WIDTH), f32)),
        in_specs=[SM, SM] + [VM] * 10,
        out_specs=[VM, VM],
        scratch_shapes=[pltpu.VMEM((step_count * query_width // width, HEAD_WIDTH), f32)],
        compiler_params=roomy,
    )(
        resident_lengths, prompt_lengths,
        resident_queries[:, 0], stored_keys[0], stored_values[0], stored_token_keys[:, 0], stored_token_values[:, 0],
        held, pk, pv, incoming_token_keys, incoming_token_values,
    )

    tied = lax.optimization_barrier((table, first))
    pool, second, out_k, out_v = pl.pallas_call(
        functools.partial(pool_kernel, dp),
        out_shape=(pool_shape, message, slots, slots),
        in_specs=[SM, SM] + [HBM] * 6,
        out_specs=[HBM, VM, HBM, HBM],
        scratch_shapes=[
            pltpu.VMEM((2, 2, full, width), bf16), dma((2, 2)), dma((2,)), dma((2, 2, half // UNIT)),
        ],
        input_output_aliases={6: 2, 7: 3},
        compiler_params=roomy,
    )(tied[0], prompt_lengths, pk, pv, xk, xv, out_k, out_v)

    hops = [(i, i + 1) for i in range(dp - 1)] + [(dp + i + 1, dp + i) for i in range(dp - 1)]

    def cross(send):
        return lax.ppermute(send, ("side", "dp"), hops)

    def mirror(got):
        return lax.ppermute(got, "side", swap)

    def place(t, got, mirrored, pool, out_k, out_v, lay):
        news = [message] if lay else []
        first_kept = len(news)
        mirrors = [] if mirrored is None else [mirrored]

        def kernel(table, now, got, *refs):
            refs = list(refs)
            mirrored = refs.pop(0) if mirrors else None
            send = refs.pop(3) if lay else None
            step_kernel(table, now, got, mirrored, *refs[:3], send, *refs[3:])

        kept = 3 + len(mirrors)
        outs = pl.pallas_call(
            kernel,
            out_shape=(*news, pool_shape, slots, slots),
            in_specs=[SM, SM, VM] + [VM] * len(mirrors) + [HBM] * 3,
            out_specs=[VM] * len(news) + [HBM] * 3,
            scratch_shapes=[dma((PER,)), dma((PER, 2)), dma((PER, 2)), dma((PER,))],
            input_output_aliases={kept + i: first_kept + i for i in range(3)},
            compiler_params=roomy,
        )(table, jnp.full((1,), t, i32), got, *mirrors, pool, out_k, out_v)
        return outs if lay else (None, *outs)

    def finish(t, mirrored, out_k, out_v):
        return pl.pallas_call(
            last_kernel,
            out_shape=(slots, slots),
            in_specs=[SM, SM, VM, HBM, HBM],
            out_specs=[HBM, HBM],
            scratch_shapes=[dma((PER, 2))],
            input_output_aliases={3: 0, 4: 1},
            compiler_params=roomy,
        )(table, jnp.full((1,), t, i32), mirrored, out_k, out_v)

    def advance(count, state, beside=None):
        t, got, a, mirrored, pool, out_k, out_v = state
        for i in range(count):
            coming = cross(a)
            if beside is not None:
                got = beside(i, got, a)
            a, pool, out_k, out_v = place(t + i, got, mirrored, pool, out_k, out_v, True)
            got, mirrored = coming, mirror(got)
        return t + count, got, a, mirrored, pool, out_k, out_v

    part_other = lax.ppermute(part, "side", swap)
    stages = gather_stages(own_out, dp)
    small = [part_other, next(stages)]

    def beside(i, got, a):
        if i % 2 == 0:
            return got
        tied, small[0] = lax.optimization_barrier((small[1], small[0], a))[:2]
        block = stages.send(tied)
        small[1] = block
        for arrived in stages:
            if i < PEEL - 2:
                small[1] = arrived
                break
            block = small[1] = stages.send(arrived)
        return lax.optimization_barrier((got, block))[0]

    second = lax.optimization_barrier((second, own_out))[0]
    state = advance(PEEL - 1, (0, cross(first), second, None, pool, out_k, out_v), beside)
    part_other, everyone = small

    resident_out, new_out = pl.pallas_call(
        functools.partial(finish_kernel, dp, step_count),
        out_shape=(shape((step_count, query_width), bf16), shape((step_count, request_count, query_width), bf16)),
        in_specs=[VM] * 3,
        out_specs=[VM, VM],
        scratch_shapes=[pltpu.VMEM((rows, HEAD_WIDTH), f32)],
    )(part, part_other, everyone)
    resident_out, new_out, a = lax.optimization_barrier((resident_out, new_out, state[2]))
    state = (jnp.asarray(state[0], i32), state[1], a, *state[3:])
    for count in TURNS:
        state = lax.while_loop(
            lambda state, count=count: state[0] + count < last, functools.partial(advance, count), state
        )
    t, got, _, mirrored, pool, out_k, out_v = state
    _, _, out_k, out_v = place(t, got, mirrored, pool, out_k, out_v, False)
    out_k, out_v = finish(t + 1, mirror(got), out_k, out_v)

    out_k, out_v = (out.reshape(CAP, half, width) for out in (out_k, out_v))
    return (resident_out[:, None, :], new_out, out_k, out_v)


def solution(mesh):
    placed = (
        P(("side", "dp"), None, "tp"),
        P(("side", "dp"), None, "tp"),
        P(),
        P(),
        P(None, None, "tp"),
        P(None, None, "tp"),
        P(None, None, "tp"),
        P("dp", "side", "tp"),
        P("dp", "side", "tp"),
        P("dp"),
        P(None, "dp", "tp"),
        P(None, "dp", "tp"),
        P(None, "dp", "tp"),
    )
    return jax.shard_map(
        body,
        mesh=mesh,
        in_specs=placed,
        out_specs=(
            P(None, "dp", "tp"),
            P(None, None, "tp"),
            P("dp", "side", "tp"),
            P("dp", "side", "tp"),
        ),
        check_vma=False,
    )
```

```python
import functools

import jax
import jax.numpy as jnp
from jax import lax
from jax.experimental import pallas as pl
from jax.experimental.pallas import tpu as pltpu
from jax.sharding import PartitionSpec as P

HEAD_WIDTH = 128
CAP = 4
UNIT = 128
PER = 6
MESSAGE = UNIT * PER
PEEL = 6
ENDS = (0, 1, 2, 4, 9)
TURN = 3
LAG = 2
LOW = -1e30

HBM = pl.BlockSpec(memory_space=pltpu.HBM)
VM = pl.BlockSpec(memory_space=pltpu.VMEM)
SM = pl.BlockSpec(memory_space=pltpu.SMEM)


def attend(q, q_rows, k_ref, v_ref, tk, tv, first, length, tokens_on, emit):
    steps = q.shape[0]
    keys, width = k_ref.shape
    heads_kv = width // HEAD_WIDTH
    members = q.shape[1] // width
    rows = members * steps
    scale = HEAD_WIDTH ** -0.5
    for kv in range(heads_kv):
        lanes = slice(kv * HEAD_WIDTH, (kv + 1) * HEAD_WIDTH)
        for g in range(members):
            at = (kv * members + g) * HEAD_WIDTH
            q_rows[g * steps:(g + 1) * steps, :] = q[:, at:at + HEAD_WIDTH]
        q32 = q_rows[...]
        scores = lax.dot_general(
            q32.astype(jnp.bfloat16), k_ref[:, lanes], (((1,), (1,)), ((), ())), preferred_element_type=jnp.float32
        ) * scale
        usable = first + lax.broadcasted_iota(jnp.int32, (rows, keys), 1) < length
        scores = jnp.where(usable, scores, LOW)
        row_step = lax.rem(lax.broadcasted_iota(jnp.int32, (rows, 1), 0), steps)
        top = jnp.max(scores, axis=1, keepdims=True)
        extra = []
        for n in range(steps):
            s = jnp.sum(q32 * tk[n:n + 1, lanes], axis=1, keepdims=True) * scale
            on = (row_step >= n) & tokens_on
            s = jnp.where(on, s, LOW)
            extra.append((on, s))
            top = jnp.maximum(top, s)
        weight = jnp.where(usable, jnp.exp(scores - top), 0.0)
        total = jnp.sum(weight, axis=1, keepdims=True)
        acc = lax.dot_general(
            weight.astype(jnp.bfloat16), v_ref[:, lanes], (((1,), (0,)), ((), ())), preferred_element_type=jnp.float32
        )
        for n, (on, s) in enumerate(extra):
            w = jnp.where(on, jnp.exp(s - top), 0.0)
            total = total + w
            acc = acc + w.astype(jnp.bfloat16).astype(jnp.float32) * tv[n:n + 1, lanes]
        emit(kv, top, total, acc)


def attention_kernel(
    dp, resident_length, lengths, rq, rk, rv, rtk, rtv, nq, nk, nv, ntk, ntv, part, own_out, q_rows
):
    side = lax.axis_index("side")
    owner = side * dp + lax.axis_index("dp")
    steps = rq.shape[0]
    keys, width = rk.shape
    rows = steps * rq.shape[1] // width
    f32 = jnp.float32

    def emit_part(kv, top, total, acc):
        at = slice(kv * rows, (kv + 1) * rows)
        part[at, 0:HEAD_WIDTH] = acc
        part[at, HEAD_WIDTH:2 * HEAD_WIDTH] = jnp.broadcast_to(top, (rows, HEAD_WIDTH))
        part[at, 2 * HEAD_WIDTH:] = jnp.broadcast_to(total, (rows, HEAD_WIDTH))

    attend(
        rq[...].astype(f32), q_rows, rk, rv, rtk[...].astype(f32), rtv[...].astype(f32),
        side * keys, resident_length[0], side == 1, emit_part,
    )

    def own(ref):
        picked = []
        for n in range(steps):
            block = ref[n].astype(f32)
            here = lax.broadcasted_iota(jnp.int32, block.shape, 0) == owner
            picked.append(jnp.sum(jnp.where(here, block, 0.0), axis=0, keepdims=True))
        return jnp.concatenate(picked, axis=0)

    def emit_out(kv, top, total, acc):
        own_out[kv * rows:(kv + 1) * rows, :] = acc / total

    attend(own(nq), q_rows, nk, nv, own(ntk), own(ntv), 0, lengths[owner], side >= 0, emit_out)


def finish_kernel(dp, steps, a, b, everyone, resident, new, o_rows):
    w = HEAD_WIDTH
    heads = resident.shape[1] // w
    top = jnp.maximum(a[:, w:2 * w], b[:, w:2 * w])
    ga = jnp.exp(a[:, w:2 * w] - top)
    gb = jnp.exp(b[:, w:2 * w] - top)
    o_rows[...] = (a[:, 0:w] * ga + b[:, 0:w] * gb) / (a[:, 2 * w:] * ga + b[:, 2 * w:] * gb)
    for h in range(heads):
        resident[:, h * w:(h + 1) * w] = o_rows[h * steps:(h + 1) * steps, :].astype(resident.dtype)
    side, me = lax.axis_index("side"), lax.axis_index("dp")
    count = everyone.shape[0]
    order = []
    for r in range(count):
        far = lax.bitwise_xor(me, r % dp) if dp & (dp - 1) == 0 else lax.rem(me - r % dp + dp, dp)
        order.append(far * 2 + lax.bitwise_xor(side, r // dp))
    at_row = lax.broadcasted_iota(jnp.int32, (count, w), 0)
    for n in range(steps):
        for h in range(heads):
            k = h * steps + n
            block = jnp.zeros((count, w), jnp.float32)
            for r in range(count):
                block = jnp.where(at_row == r, everyone[order[r], k:k + 1, :], block)
            new[n, :, h * w:(h + 1) * w] = block.astype(new.dtype)


def units_at(start):
    return pl.ds(pl.multiple_of(start, UNIT), UNIT)


def last_unit(length):
    return (length + UNIT - 1) // UNIT * UNIT - UNIT


def mask_unit(ref, first, length):
    row = lax.broadcasted_iota(jnp.int32, (UNIT, ref.shape[1]), 0)
    block = ref[units_at(first), :]
    ref[units_at(first), :] = jnp.where(first + row < length, block, jnp.zeros_like(block))


def plan_kernel(dp, half, ring_units, lengths, goal, table, out_k, out_v, blank, fill_sem):
    blank[...] = jnp.zeros_like(blank)
    fills = [
        pltpu.make_async_copy(blank, out.at[pl.ds(slot * half, half)], fill_sem.at[i, slot])
        for i, out in enumerate((out_k, out_v)) for slot in range(CAP)
    ]
    for fill in fills:
        fill.start()
    side, me = lax.axis_index("side"), lax.axis_index("dp")
    f32 = jnp.float32
    full = 2 * half
    count = lengths.shape[0]
    wide = table.shape[1]
    id_row = lax.broadcasted_iota(jnp.int32, (count, count), 1).astype(f32)
    id_col = lax.broadcasted_iota(jnp.int32, (count, count), 0).astype(f32)
    eye = id_row == id_col

    def col(row):
        return jnp.sum(jnp.where(eye, jnp.broadcast_to(row, (count, count)), 0.0), axis=1, keepdims=True)

    def spread(scalars):
        row = jnp.zeros((1, count), jnp.int32)
        lane = lax.broadcasted_iota(jnp.int32, (1, count), 1)
        for r in range(count):
            row = jnp.where(lane == r, scalars[r], row)
        return row.astype(f32)

    ids = id_row[0:1]
    late = jnp.where(ids >= dp, 1.0, 0.0)
    src0 = ids - dp * late
    goal0 = spread(goal)
    side_f, me_f = side.astype(f32), me.astype(f32)
    units = jnp.floor((spread(lengths) + (UNIT - 1)) * (1.0 / UNIT))
    units_col, late_col, goal0_col, src0_col = col(units), col(late), col(goal0), col(src0)
    slot = jnp.sum(jnp.where((goal0_col == goal0) & (id_col < id_row), 1.0, 0.0), axis=0, keepdims=True)
    slot_col = col(slot)
    time = lax.broadcasted_iota(jnp.int32, (1, wide), 1).astype(f32)
    here_col = jnp.where(late_col == side_f, 0.0, 1.0)
    steps = jnp.zeros((1, 1), f32)
    sends, passes, ends = [], [], []
    for flip in (False, True):
        turned = (lambda x: dp - 1 - x) if flip else (lambda x: x)
        s, g, m, s_col, g_col = turned(src0), turned(goal0), turned(me_f), turned(src0_col), turned(goal0_col)
        ahead = (g_col > g) | ((g_col == g) & ((s_col > s) | ((s_col == s) & (id_col < id_row))))
        crosses, bases, starts = [], [], []
        for d in range(dp - 1):
            cross = (s <= d) & (g > d)
            base = jnp.sum(jnp.where(ahead & (s_col <= d) & (g_col > d), units_col, 0.0), axis=0, keepdims=True)
            load = jnp.sum(jnp.where(cross, units, 0.0), axis=1, keepdims=True)
            start = jnp.zeros((1, 1), f32)
            if d > 0:
                lead = jnp.floor((base - bases[-1]) * (1.0 / PER))
                gap = jnp.where(cross & crosses[-1], starts[-1] + LAG - lead, 0.0)
                start = jnp.maximum(jnp.max(gap, axis=1, keepdims=True), 0.0)
            steps = jnp.maximum(steps, jnp.where(load > 0, jnp.floor((load + (PER - 1)) * (1.0 / PER)) + start, 0.0))
            crosses.append(cross)
            bases.append(base)
            starts.append(start)

        def at(link):
            base, start, used = jnp.zeros((1, count), f32), jnp.zeros((1, 1), f32), jnp.zeros((1, count), f32)
            for d in range(dp - 1):
                base = jnp.where(link == d, bases[d], base)
                start = jnp.where(link == d, starts[d], start)
                used = jnp.where(link == d, jnp.where(crosses[d], units, 0.0), used)
            return col(base), start * PER, col(used)

        def ring_row(p):
            return (p - ring_units * jnp.floor((p + 0.5) * (1.0 / ring_units))) * UNIT

        def pick(hit, value):
            return jnp.sum(jnp.where(hit, value + 1.0, 0.0), axis=0, keepdims=True) - 1.0

        base, start, used = at(m)
        p = time - start
        c = p - base
        hit = (c >= 0) & (c < used)
        sends.append(jnp.maximum(pick(hit, jnp.where(s_col == m, here_col * full + c * UNIT, 2 * full + ring_row(p))), 0.0))
        here, start, used = at(m - 1)
        c = time - start - here
        hit = (c >= 0) & (c < used)
        passes.append(pick(hit & (g_col != m), 2 * full + ring_row(base + c)))
        row = c * UNIT - half * side_f
        ends.append(pick(hit & (g_col == m) & (row >= 0) & (row < half), slot_col * half + row))
    right = side_f == 0.0
    for r, row in enumerate((
        jnp.where(right, sends[0], sends[1]), jnp.where(right, passes[0], passes[1]),
        jnp.where(right, ends[0], ends[1]), jnp.where(right, ends[1], ends[0]),
    )):
        table[r:r + 1, :] = row.astype(jnp.int32)
    stay = jnp.where((src0 == me_f) & (goal0 == me_f), slot + 1.0, 0.0)
    home = [
        jnp.sum(jnp.where(late == which, stay, 0.0), axis=1, keepdims=True) - 1.0 for which in (side_f, 1.0 - side_f)
    ]
    last = jnp.where(time == 0, steps, jnp.where(time == 1, home[0], home[1]))
    table[4:5, :] = last.astype(jnp.int32)
    table[5:8, :] = jnp.zeros((3, wide), jnp.int32)
    for fill in fills:
        fill.wait()


def first_kernel(dp, table, lengths, pk, pv, xk, xv, send, sem):
    side, me = lax.axis_index("side"), lax.axis_index("dp")
    full = pk.shape[0]
    codes = [table[0, i] for i in range(PER)]
    at = [slice(i * UNIT, (i + 1) * UNIT) for i in range(PER)]

    def own_copies(i):
        row = units_at(jnp.minimum(codes[i], full - UNIT))
        return [pltpu.make_async_copy(a.at[row], send.at[n, at[i]], sem.at[i, n]) for n, a in enumerate((pk, pv))]

    for i in range(PER):
        @pl.when(codes[i] < full)
        def _():
            for copy in own_copies(i):
                copy.start()
    for i in range(PER):
        @pl.when((codes[i] >= full) & (codes[i] < 2 * full))
        def _():
            for n, a in enumerate((xk, xv)):
                send[n, at[i], :] = a[units_at(codes[i] - full), :]
    for i in range(PER):
        @pl.when(codes[i] < full)
        def _():
            for copy in own_copies(i):
                copy.wait()
    for j in range(2):
        length = lengths[lax.bitwise_xor(side, j) * dp + me]
        last = last_unit(length)
        for i in range(PER):
            @pl.when(codes[i] == j * full + last)
            def _():
                for n in range(2):
                    mask_unit(send.at[n, at[i]], 0, length - last)


def pool_kernel(
    dp, table, lengths, pk, pv, xk, xv, ok, ov, pool, send, out_k, out_v, stage, load_sem, pool_sem, home_sem
):
    side, me = lax.axis_index("side"), lax.axis_index("dp")
    full = xk.shape[0]
    half = full // 2
    loads = [
        pltpu.make_async_copy(a, stage.at[j, n], load_sem.at[j, n])
        for j, pair in enumerate(((pk, pv), (xk, xv))) for n, a in enumerate(pair)
    ]
    for copy in loads:
        copy.start()
    stores, homes = [], []
    for j in range(2):
        length = lengths[lax.bitwise_xor(side, j) * dp + me]
        last = last_unit(length)
        for n in range(2):
            loads[2 * j + n].wait()
            mask_unit(stage.at[j, n], last, length)
        store = pltpu.make_async_copy(stage.at[j], pool.at[:, pl.ds(j * full, full)], pool_sem.at[j])
        store.start()
        stores.append(store)
        slot = table[4, 1 + j]
        count = jnp.where(slot >= 0, jnp.clip((last + UNIT - side * half) // UNIT, 0, half // UNIT), 0)

        def home(u, wait, j=j, slot=slot):
            for n, out in enumerate((out_k, out_v)):
                copy = pltpu.make_async_copy(
                    stage.at[j, n, units_at(side * half + u * UNIT)], out.at[units_at(slot * half + u * UNIT)],
                    home_sem.at[j, n, u],
                )
                copy.wait() if wait else copy.start()

        pl.loop(0, count)(functools.partial(home, wait=False))
        homes.append((count, home))
    for i in range(PER):
        code = table[0, PER + i]
        j = jnp.clip(code // full, 0, 1)
        row = jnp.clip(code - j * full, 0, full - UNIT)
        for n in range(2):
            send[n, i * UNIT:(i + 1) * UNIT, :] = stage[j, n, units_at(row), :]
    for count, home in homes:
        pl.loop(0, count)(functools.partial(home, wait=True))
    for store in stores:
        store.wait()


def end_copies(table, t, row, take, out_k, out_v, sem):
    copies = []
    for i in range(PER):
        code = table[row, t * PER + i]
        to = units_at(jnp.maximum(code, 0))
        copies.append((code >= 0, [
            pltpu.make_async_copy(take.at[n, pl.ds(i * UNIT, UNIT)], out.at[to], sem.at[i, n])
            for n, out in enumerate((out_k, out_v))
        ]))
    return copies


def when_all(copies, act):
    @pl.when(functools.reduce(jnp.logical_or, [on for on, _ in copies]))
    def _():
        for on, group in copies:
            @pl.when(on)
            def _():
                for copy in group:
                    act(copy)


def step_kernel(
    table, now, got, mirrored, pool_in, ok, ov, send, pool, out_k, out_v, pass_sem, got_sem, mirror_sem, send_sem
):
    t = now[0]
    passes = []
    for i in range(PER):
        code = table[1, t * PER + i]
        to = pool.at[:, units_at(jnp.maximum(code, 0))]
        passes.append((code >= 0, [pltpu.make_async_copy(got.at[:, pl.ds(i * UNIT, UNIT)], to, pass_sem.at[i])]))
    when_all(passes, lambda copy: copy.start())
    ends = [end_copies(table, t, 2, got, out_k, out_v, got_sem)]
    if mirrored is not None:
        ends.append(end_copies(table, t - 1, 3, mirrored, out_k, out_v, mirror_sem))
    for copies in ends:
        when_all(copies, lambda copy: copy.start())
    when_all(passes, lambda copy: copy.wait())
    if send is not None:
        lay = [
            pltpu.make_async_copy(
                pool.at[:, units_at(table[0, (t + LAG) * PER + i])], send.at[:, pl.ds(i * UNIT, UNIT)], send_sem.at[i]
            )
            for i in range(PER)
        ]
        for copy in lay:
            copy.start()
        for copy in lay:
            copy.wait()
    for copies in ends:
        when_all(copies, lambda copy: copy.wait())


def last_kernel(table, now, mirrored, ok, ov, out_k, out_v, sem):
    ends = end_copies(table, now[0] - 1, 3, mirrored, out_k, out_v, sem)
    when_all(ends, lambda copy: copy.start())
    when_all(ends, lambda copy: copy.wait())


def gather_stages(own, dp):
    block = jnp.stack([own, lax.ppermute(own, "side", [(0, 1), (1, 0)])])
    yield block
    if dp & (dp - 1):
        rest = [lax.ppermute(block, "dp", [(i, (i + x) % dp) for i in range(dp)]) for x in range(1, dp)]
        yield jnp.concatenate([block] + (yield rest))
    else:
        for stage in range(dp.bit_length() - 1):
            got = yield lax.ppermute(block, "dp", [(i, i ^ (1 << stage)) for i in range(dp)])
            block = jnp.concatenate([block, got])
            yield block


def body(
    prompt_keys,
    prompt_values,
    prompt_lengths,
    assignment,
    new_queries,
    incoming_token_keys,
    incoming_token_values,
    stored_keys,
    stored_values,
    resident_lengths,
    resident_queries,
    stored_token_keys,
    stored_token_values,
):
    step_count = resident_queries.shape[0]
    dp = lax.axis_size("dp")
    request_count = prompt_lengths.shape[0]
    full, width = prompt_keys.shape[1:]
    query_width = new_queries.shape[2]
    half = full // 2
    bf16, f32, i32 = jnp.bfloat16, jnp.float32, jnp.int32
    swap = [(0, 1), (1, 0)]
    shape = jax.ShapeDtypeStruct
    dma = pltpu.SemaphoreType.DMA
    roomy = pltpu.CompilerParams(vmem_limit_bytes=16 << 20)
    wide_open = pltpu.CompilerParams(vmem_limit_bytes=58 << 20)

    pk, pv = prompt_keys[0], prompt_values[0]
    xk, xv = lax.ppermute(pk, "side", swap), lax.ppermute(pv, "side", swap)

    most = full // UNIT
    ring_units = 2 * most + (LAG + 1) * PER
    steps_max = -(-request_count * most // PER) + LAG * dp + PEEL + ENDS[-1] + LAG
    wide = -(-steps_max * PER // 128) * 128
    slots = shape((CAP * half, width), bf16)
    table, out_k, out_v = pl.pallas_call(
        functools.partial(plan_kernel, dp, half, ring_units),
        out_shape=(shape((8, wide), i32), slots, slots),
        in_specs=[SM, SM],
        out_specs=[VM, HBM, HBM],
        scratch_shapes=[pltpu.VMEM((half, width), bf16), dma((2, CAP))],
        compiler_params=wide_open,
    )(prompt_lengths, jnp.reshape(assignment, (request_count,)))
    last = table[4, 0]

    message = shape((2, MESSAGE, width), bf16)
    pool_shape = shape((2, 2 * full + ring_units * UNIT, width), bf16)
    first = pl.pallas_call(
        functools.partial(first_kernel, dp),
        out_shape=message,
        in_specs=[SM, SM, HBM, HBM, VM, VM],
        out_specs=VM,
        scratch_shapes=[dma((PER, 2))],
        compiler_params=wide_open,
    )(table, prompt_lengths, pk, pv, xk, xv)

    held = lax.optimization_barrier((new_queries, first))[0]
    rows = step_count * query_width // HEAD_WIDTH
    part, own_out = pl.pallas_call(
        functools.partial(attention_kernel, dp),
        out_shape=(shape((rows, 3 * HEAD_WIDTH), f32), shape((rows, HEAD_WIDTH), f32)),
        in_specs=[SM, SM] + [VM] * 10,
        out_specs=[VM, VM],
        scratch_shapes=[pltpu.VMEM((step_count * query_width // width, HEAD_WIDTH), f32)],
        compiler_params=roomy,
    )(
        resident_lengths, prompt_lengths,
        resident_queries[:, 0], stored_keys[0], stored_values[0], stored_token_keys[:, 0], stored_token_values[:, 0],
        held, pk, pv, incoming_token_keys, incoming_token_values,
    )

    tied = lax.optimization_barrier((table, first))
    pool, second, out_k, out_v = pl.pallas_call(
        functools.partial(pool_kernel, dp),
        out_shape=(pool_shape, message, slots, slots),
        in_specs=[SM, SM, HBM, HBM, VM, VM, HBM, HBM],
        out_specs=[HBM, VM, HBM, HBM],
        scratch_shapes=[
            pltpu.VMEM((2, 2, full, width), bf16), dma((2, 2)), dma((2,)), dma((2, 2, half // UNIT)),
        ],
        input_output_aliases={6: 2, 7: 3},
        compiler_params=roomy,
    )(tied[0], prompt_lengths, pk, pv, xk, xv, out_k, out_v)

    hops = [(i, i + 1) for i in range(dp - 1)] + [(dp + i + 1, dp + i) for i in range(dp - 1)]

    def cross(send):
        return lax.ppermute(send, ("side", "dp"), hops)

    def mirror(got):
        return lax.ppermute(got, "side", swap)

    def place(t, got, mirrored, pool, out_k, out_v, lay):
        news = [message] if lay else []
        first_kept = len(news)
        mirrors = [] if mirrored is None else [mirrored]

        def kernel(table, now, got, *refs):
            refs = list(refs)
            mirrored = refs.pop(0) if mirrors else None
            send = refs.pop(3) if lay else None
            step_kernel(table, now, got, mirrored, *refs[:3], send, *refs[3:])

        kept = 3 + len(mirrors)
        outs = pl.pallas_call(
            kernel,
            out_shape=(*news, pool_shape, slots, slots),
            in_specs=[SM, SM, VM] + [VM] * len(mirrors) + [HBM] * 3,
            out_specs=[VM] * len(news) + [HBM] * 3,
            scratch_shapes=[dma((PER,)), dma((PER, 2)), dma((PER, 2)), dma((PER,))],
            input_output_aliases={kept + i: first_kept + i for i in range(3)},
            compiler_params=roomy,
        )(table, jnp.full((1,), t, i32), got, *mirrors, pool, out_k, out_v)
        return outs if lay else (None, *outs)

    def finish(t, mirrored, out_k, out_v):
        return pl.pallas_call(
            last_kernel,
            out_shape=(slots, slots),
            in_specs=[SM, SM, VM, HBM, HBM],
            out_specs=[HBM, HBM],
            scratch_shapes=[dma((PER, 2))],
            input_output_aliases={3: 0, 4: 1},
            compiler_params=roomy,
        )(table, jnp.full((1,), t, i32), mirrored, out_k, out_v)

    def advance(count, state, beside=None):
        t, got, a, mirrored, pool, out_k, out_v = state
        for i in range(count):
            coming = cross(a)
            if beside is not None:
                got = beside(i, got, a)
            a, pool, out_k, out_v = place(t + i, got, mirrored, pool, out_k, out_v, True)
            got, mirrored = coming, mirror(got)
        return t + count, got, a, mirrored, pool, out_k, out_v

    small = {}

    def beside(i, got, a):
        if i == 1:
            here, kept, _ = lax.optimization_barrier((own_out, part, a))
            small["part"] = lax.ppermute(kept, "side", swap)
            small["stages"] = gather_stages(here, dp)
            small["rows"] = next(small["stages"])
            small["arrived"] = next(small["stages"], None)
        elif small.get("arrived") is not None:
            arrived = lax.optimization_barrier((small["arrived"], a))[0]
            small["rows"] = small["stages"].send(arrived)
            small["arrived"] = next(small["stages"], None)
            while i == PEEL - 2 and small["arrived"] is not None:
                small["rows"] = small["stages"].send(small["arrived"])
                small["arrived"] = next(small["stages"], None)
        else:
            return got
        return lax.optimization_barrier((got, small["rows"]))[0]

    state = advance(PEEL - 1, (0, cross(first), second, None, pool, out_k, out_v), beside)
    part_other, everyone = small["part"], small["rows"]
    resident_out, new_out = pl.pallas_call(
        functools.partial(finish_kernel, dp, step_count),
        out_shape=(shape((step_count, query_width), bf16), shape((step_count, request_count, query_width), bf16)),
        in_specs=[VM] * 3,
        out_specs=[VM, VM],
        scratch_shapes=[pltpu.VMEM((rows, HEAD_WIDTH), f32)],
    )(part, part_other, everyone)
    resident_out, new_out, a = lax.optimization_barrier((resident_out, new_out, state[2]))
    t, got, _, mirrored, pool, out_k, out_v = state
    left = jnp.maximum(last - PEEL, 0)
    crowd = max(min(2 * (d + 1), CAP * (dp - 1 - d)) for d in range(dp - 1))
    if -(-crowd * most // PER) + LAG * (dp - 2) > PEEL + ENDS[-1]:
        left, (t, got, a, mirrored, pool, out_k, out_v) = lax.while_loop(
            lambda state: state[0] > ENDS[-1],
            lambda state: (state[0] - TURN, advance(TURN, state[1])),
            (left, (jnp.asarray(t, i32), got, a, mirrored, pool, out_k, out_v)),
        )

    def end(count, state):
        _, pool, out_k, out_v = state
        now = [got, a, mirrored]
        for i in range(count + 1):
            arrived, message, passed = now
            coming = cross(message) if i < count else None
            message, pool, out_k, out_v = place(t + i, arrived, passed, pool, out_k, out_v, i + 1 < count)
            now = [coming, message, mirror(arrived)]
        out_k, out_v = finish(t + count + 1, now[2], out_k, out_v)
        return jnp.full((), -1, i32), pool, out_k, out_v

    state = (left, pool, out_k, out_v)
    for lower, count in zip((-1, *ENDS), ENDS):
        state = lax.while_loop(
            lambda state, lower=lower, count=count: (state[0] > lower) & (state[0] <= count),
            functools.partial(end, count), state,
        )
    _, _, out_k, out_v = state
    out_k, out_v = (out.reshape(CAP, half, width) for out in (out_k, out_v))
    return (resident_out[:, None, :], new_out, out_k, out_v)


def solution(mesh):
    placed = (
        P(("side", "dp"), None, "tp"),
        P(("side", "dp"), None, "tp"),
        P(),
        P(),
        P(None, None, "tp"),
        P(None, None, "tp"),
        P(None, None, "tp"),
        P("dp", "side", "tp"),
        P("dp", "side", "tp"),
        P("dp"),
        P(None, "dp", "tp"),
        P(None, "dp", "tp"),
        P(None, "dp", "tp"),
    )
    return jax.shard_map(
        body,
        mesh=mesh,
        in_specs=placed,
        out_specs=(
            P(None, "dp", "tp"),
            P(None, None, "tp"),
            P("dp", "side", "tp"),
            P("dp", "side", "tp"),
        ),
        check_vma=False,
    )
```

```python
import functools

import jax
import jax.numpy as jnp
from jax import lax
from jax.experimental import pallas as pl
from jax.experimental.pallas import tpu as pltpu
from jax.sharding import PartitionSpec as P

HEAD_WIDTH = 128
CAP = 4
UNIT = 128
PER = 6
MESSAGE = UNIT * PER
PEEL = 6
ENDS = (0, 1, 2, 3, 4, 5, 7, 9)
TURN = 3
LAG = 2
LOW = -1e30

HBM = pl.BlockSpec(memory_space=pltpu.HBM)
VM = pl.BlockSpec(memory_space=pltpu.VMEM)
SM = pl.BlockSpec(memory_space=pltpu.SMEM)


def attend(q, q_rows, k_ref, v_ref, tk, tv, first, length, tokens_on, emit):
    steps = q.shape[0]
    keys, width = k_ref.shape
    heads_kv = width // HEAD_WIDTH
    members = q.shape[1] // width
    rows = members * steps
    scale = HEAD_WIDTH ** -0.5
    for kv in range(heads_kv):
        lanes = slice(kv * HEAD_WIDTH, (kv + 1) * HEAD_WIDTH)
        for g in range(members):
            at = (kv * members + g) * HEAD_WIDTH
            q_rows[g * steps:(g + 1) * steps, :] = q[:, at:at + HEAD_WIDTH]
        q32 = q_rows[...]
        scores = lax.dot_general(
            q32.astype(jnp.bfloat16), k_ref[:, lanes], (((1,), (1,)), ((), ())), preferred_element_type=jnp.float32
        ) * scale
        usable = first + lax.broadcasted_iota(jnp.int32, (rows, keys), 1) < length
        scores = jnp.where(usable, scores, LOW)
        row_step = lax.rem(lax.broadcasted_iota(jnp.int32, (rows, 1), 0), steps)
        top = jnp.max(scores, axis=1, keepdims=True)
        extra = []
        for n in range(steps):
            s = jnp.sum(q32 * tk[n:n + 1, lanes], axis=1, keepdims=True) * scale
            on = (row_step >= n) & tokens_on
            s = jnp.where(on, s, LOW)
            extra.append((on, s))
            top = jnp.maximum(top, s)
        weight = jnp.where(usable, jnp.exp(scores - top), 0.0)
        total = jnp.sum(weight, axis=1, keepdims=True)
        acc = lax.dot_general(
            weight.astype(jnp.bfloat16), v_ref[:, lanes], (((1,), (0,)), ((), ())), preferred_element_type=jnp.float32
        )
        for n, (on, s) in enumerate(extra):
            w = jnp.where(on, jnp.exp(s - top), 0.0)
            total = total + w
            acc = acc + w.astype(jnp.bfloat16).astype(jnp.float32) * tv[n:n + 1, lanes]
        emit(kv, top, total, acc)


def attention_kernel(
    dp, resident_length, lengths, rq, rk, rv, rtk, rtv, nq, nk, nv, ntk, ntv, part, own_out, q_rows
):
    side = lax.axis_index("side")
    owner = side * dp + lax.axis_index("dp")
    steps = rq.shape[0]
    keys, width = rk.shape
    rows = steps * rq.shape[1] // width
    f32 = jnp.float32

    def emit_part(kv, top, total, acc):
        at = slice(kv * rows, (kv + 1) * rows)
        part[at, 0:HEAD_WIDTH] = acc
        part[at, HEAD_WIDTH:2 * HEAD_WIDTH] = jnp.broadcast_to(top, (rows, HEAD_WIDTH))
        part[at, 2 * HEAD_WIDTH:] = jnp.broadcast_to(total, (rows, HEAD_WIDTH))

    attend(
        rq[...].astype(f32), q_rows, rk, rv, rtk[...].astype(f32), rtv[...].astype(f32),
        side * keys, resident_length[0], side == 1, emit_part,
    )

    def own(ref):
        picked = []
        for n in range(steps):
            block = ref[n].astype(f32)
            here = lax.broadcasted_iota(jnp.int32, block.shape, 0) == owner
            picked.append(jnp.sum(jnp.where(here, block, 0.0), axis=0, keepdims=True))
        return jnp.concatenate(picked, axis=0)

    def emit_out(kv, top, total, acc):
        own_out[kv * rows:(kv + 1) * rows, :] = acc / total

    attend(own(nq), q_rows, nk, nv, own(ntk), own(ntv), 0, lengths[owner], side >= 0, emit_out)


def finish_kernel(dp, steps, a, b, everyone, resident, new, o_rows):
    w = HEAD_WIDTH
    heads = resident.shape[1] // w
    top = jnp.maximum(a[:, w:2 * w], b[:, w:2 * w])
    ga = jnp.exp(a[:, w:2 * w] - top)
    gb = jnp.exp(b[:, w:2 * w] - top)
    o_rows[...] = (a[:, 0:w] * ga + b[:, 0:w] * gb) / (a[:, 2 * w:] * ga + b[:, 2 * w:] * gb)
    for h in range(heads):
        resident[:, h * w:(h + 1) * w] = o_rows[h * steps:(h + 1) * steps, :].astype(resident.dtype)
    side, me = lax.axis_index("side"), lax.axis_index("dp")
    count = everyone.shape[0]
    order = []
    for r in range(count):
        far = lax.bitwise_xor(me, r % dp) if dp & (dp - 1) == 0 else lax.rem(me - r % dp + dp, dp)
        order.append(far * 2 + lax.bitwise_xor(side, r // dp))
    at_row = lax.broadcasted_iota(jnp.int32, (count, w), 0)
    for n in range(steps):
        for h in range(heads):
            k = h * steps + n
            block = jnp.zeros((count, w), jnp.float32)
            for r in range(count):
                block = jnp.where(at_row == r, everyone[order[r], k:k + 1, :], block)
            new[n, :, h * w:(h + 1) * w] = block.astype(new.dtype)


def units_at(start):
    return pl.ds(pl.multiple_of(start, UNIT), UNIT)


def last_unit(length):
    return (length + UNIT - 1) // UNIT * UNIT - UNIT


def mask_unit(ref, first, length):
    row = lax.broadcasted_iota(jnp.int32, (UNIT, ref.shape[1]), 0)
    block = ref[units_at(first), :]
    ref[units_at(first), :] = jnp.where(first + row < length, block, jnp.zeros_like(block))


def plan_kernel(dp, half, ring_units, lengths, goal, pk, pv, table):
    side, me = lax.axis_index("side"), lax.axis_index("dp")
    f32 = jnp.float32
    full = 2 * half
    count = lengths.shape[0]
    wide = table.shape[1]
    id_row = lax.broadcasted_iota(jnp.int32, (count, count), 1).astype(f32)
    id_col = lax.broadcasted_iota(jnp.int32, (count, count), 0).astype(f32)
    eye = id_row == id_col

    def col(row):
        return jnp.sum(jnp.where(eye, jnp.broadcast_to(row, (count, count)), 0.0), axis=1, keepdims=True)

    def spread(scalars):
        row = jnp.zeros((1, count), jnp.int32)
        lane = lax.broadcasted_iota(jnp.int32, (1, count), 1)
        for r in range(count):
            row = jnp.where(lane == r, scalars[r], row)
        return row.astype(f32)

    ids = id_row[0:1]
    late = jnp.where(ids >= dp, 1.0, 0.0)
    src0 = ids - dp * late
    goal0 = spread(goal)
    side_f, me_f = side.astype(f32), me.astype(f32)
    units = jnp.floor((spread(lengths) + (UNIT - 1)) * (1.0 / UNIT))
    units_col, late_col, goal0_col, src0_col = col(units), col(late), col(goal0), col(src0)
    slot = jnp.sum(jnp.where((goal0_col == goal0) & (id_col < id_row), 1.0, 0.0), axis=0, keepdims=True)
    slot_col = col(slot)
    time = lax.broadcasted_iota(jnp.int32, (1, wide), 1).astype(f32)
    here_col = jnp.where(late_col == side_f, 0.0, 1.0)
    steps = jnp.zeros((1, 1), f32)
    sends, passes, ends = [], [], []
    for flip in (False, True):
        turned = (lambda x: dp - 1 - x) if flip else (lambda x: x)
        s, g, m, s_col, g_col = turned(src0), turned(goal0), turned(me_f), turned(src0_col), turned(goal0_col)
        ahead = (g_col > g) | ((g_col == g) & ((s_col > s) | ((s_col == s) & (id_col < id_row))))
        crosses, bases, starts = [], [], []
        for d in range(dp - 1):
            cross = (s <= d) & (g > d)
            base = jnp.sum(jnp.where(ahead & (s_col <= d) & (g_col > d), units_col, 0.0), axis=0, keepdims=True)
            load = jnp.sum(jnp.where(cross, units, 0.0), axis=1, keepdims=True)
            start = jnp.zeros((1, 1), f32)
            if d > 0:
                lead = jnp.floor((base - bases[-1]) * (1.0 / PER))
                gap = jnp.where(cross & crosses[-1], starts[-1] + LAG - lead, 0.0)
                start = jnp.maximum(jnp.max(gap, axis=1, keepdims=True), 0.0)
            steps = jnp.maximum(steps, jnp.where(load > 0, jnp.floor((load + (PER - 1)) * (1.0 / PER)) + start, 0.0))
            crosses.append(cross)
            bases.append(base)
            starts.append(start)

        def at(link):
            base, start, used = jnp.zeros((1, count), f32), jnp.zeros((1, 1), f32), jnp.zeros((1, count), f32)
            for d in range(dp - 1):
                base = jnp.where(link == d, bases[d], base)
                start = jnp.where(link == d, starts[d], start)
                used = jnp.where(link == d, jnp.where(crosses[d], units, 0.0), used)
            return col(base), start * PER, col(used)

        def ring_row(p):
            return (p - ring_units * jnp.floor((p + 0.5) * (1.0 / ring_units))) * UNIT

        def pick(hit, value):
            return jnp.sum(jnp.where(hit, value + 1.0, 0.0), axis=0, keepdims=True) - 1.0

        base, start, used = at(m)
        p = time - start
        c = p - base
        hit = (c >= 0) & (c < used)
        sends.append(jnp.maximum(pick(hit, jnp.where(s_col == m, here_col * full + c * UNIT, 2 * full + ring_row(p))), 0.0))
        here, start, used = at(m - 1)
        c = time - start - here
        hit = (c >= 0) & (c < used)
        passes.append(pick(hit & (g_col != m), 2 * full + ring_row(base + c)))
        row = c * UNIT - half * side_f
        ends.append(pick(hit & (g_col == m) & (row >= 0) & (row < half), slot_col * half + row))
    right = side_f == 0.0
    for r, row in enumerate((
        jnp.where(right, sends[0], sends[1]), jnp.where(right, passes[0], passes[1]),
        jnp.where(right, ends[0], ends[1]), jnp.where(right, ends[1], ends[0]),
    )):
        table[r:r + 1, :] = row.astype(jnp.int32)
    stay = jnp.where((src0 == me_f) & (goal0 == me_f), slot + 1.0, 0.0)
    home = [
        jnp.sum(jnp.where(late == which, stay, 0.0), axis=1, keepdims=True) - 1.0 for which in (side_f, 1.0 - side_f)
    ]
    last = jnp.where(time == 0, steps, jnp.where(time == 1, home[0], home[1]))
    table[4:5, :] = last.astype(jnp.int32)
    table[5:8, :] = jnp.zeros((3, wide), jnp.int32)


def first_kernel(dp, table, lengths, pk, pv, xk, xv, send):
    side, me = lax.axis_index("side"), lax.axis_index("dp")
    full = pk.shape[0]
    for j, pair in enumerate(((pk, pv), (xk, xv))):
        length = lengths[lax.bitwise_xor(side, j) * dp + me]
        last = last_unit(length)
        for i in range(PER):
            row = table[0, i] - j * full

            @pl.when((row >= 0) & (row < full))
            def _():
                for n in range(2):
                    send[n, i * UNIT:(i + 1) * UNIT, :] = pair[n][units_at(row), :]

            @pl.when(row == last)
            def _():
                for n in range(2):
                    mask_unit(send.at[n, i * UNIT:(i + 1) * UNIT], 0, length - last)


def pool_kernel(
    dp, table, lengths, pk, pv, xk, xv, pool, send, out_k, out_v, blank, stage, fill_sem, load_sem, pool_sem, home_sem
):
    side, me = lax.axis_index("side"), lax.axis_index("dp")
    full = xk.shape[0]
    half = full // 2
    loads = [
        pltpu.make_async_copy(a, stage.at[j, n], load_sem.at[j, n])
        for j, pair in enumerate(((pk, pv), (xk, xv))) for n, a in enumerate(pair)
    ]
    for copy in loads:
        copy.start()
    blank[...] = jnp.zeros_like(blank)
    fills = [
        pltpu.make_async_copy(blank, out.at[pl.ds(slot * half, half)], fill_sem.at[i, slot])
        for i, out in enumerate((out_k, out_v)) for slot in range(CAP)
    ]
    for fill in fills:
        fill.start()
    stores, homes = [], []
    for j in range(2):
        length = lengths[lax.bitwise_xor(side, j) * dp + me]
        last = last_unit(length)
        for n in range(2):
            loads[2 * j + n].wait()
            mask_unit(stage.at[j, n], last, length)
        store = pltpu.make_async_copy(stage.at[j], pool.at[:, pl.ds(j * full, full)], pool_sem.at[j])
        store.start()
        stores.append(store)
        slot = table[4, 1 + j]
        count = jnp.where(slot >= 0, jnp.clip((last + UNIT - side * half) // UNIT, 0, half // UNIT), 0)

        def home(u, wait, j=j, slot=slot):
            for n, out in enumerate((out_k, out_v)):
                copy = pltpu.make_async_copy(
                    stage.at[j, n, units_at(side * half + u * UNIT)], out.at[units_at(slot * half + u * UNIT)],
                    home_sem.at[j, n, u],
                )
                copy.wait() if wait else copy.start()

        homes.append((count, home))
    for fill in fills:
        fill.wait()
    for count, home in homes:
        pl.loop(0, count)(functools.partial(home, wait=False))
    for i in range(PER):
        code = table[0, PER + i]
        j = jnp.clip(code // full, 0, 1)
        row = jnp.clip(code - j * full, 0, full - UNIT)
        for n in range(2):
            send[n, i * UNIT:(i + 1) * UNIT, :] = stage[j, n, units_at(row), :]
    for count, home in homes:
        pl.loop(0, count)(functools.partial(home, wait=True))
    for store in stores:
        store.wait()


def end_copies(table, t, row, take, out_k, out_v, sem):
    copies = []
    for i in range(PER):
        code = table[row, t * PER + i]
        to = units_at(jnp.maximum(code, 0))
        copies.append((code >= 0, [
            pltpu.make_async_copy(take.at[n, pl.ds(i * UNIT, UNIT)], out.at[to], sem.at[i, n])
            for n, out in enumerate((out_k, out_v))
        ]))
    return copies


def when_all(copies, act):
    @pl.when(functools.reduce(jnp.logical_or, [on for on, _ in copies]))
    def _():
        for on, group in copies:
            @pl.when(on)
            def _():
                for copy in group:
                    act(copy)


def step_kernel(
    table, now, got, mirrored, pool_in, ok, ov, send, pool, out_k, out_v, pass_sem, got_sem, mirror_sem, send_sem
):
    t = now[0]
    passes = []
    for i in range(PER):
        code = table[1, t * PER + i]
        to = pool.at[:, units_at(jnp.maximum(code, 0))]
        passes.append((code >= 0, [pltpu.make_async_copy(got.at[:, pl.ds(i * UNIT, UNIT)], to, pass_sem.at[i])]))
    when_all(passes, lambda copy: copy.start())
    ends = [end_copies(table, t, 2, got, out_k, out_v, got_sem)]
    if mirrored is not None:
        ends.append(end_copies(table, t - 1, 3, mirrored, out_k, out_v, mirror_sem))
    for copies in ends:
        when_all(copies, lambda copy: copy.start())
    when_all(passes, lambda copy: copy.wait())
    if send is not None:
        lay = [
            pltpu.make_async_copy(
                pool.at[:, units_at(table[0, (t + LAG) * PER + i])], send.at[:, pl.ds(i * UNIT, UNIT)], send_sem.at[i]
            )
            for i in range(PER)
        ]
        for copy in lay:
            copy.start()
        for copy in lay:
            copy.wait()
    for copies in ends:
        when_all(copies, lambda copy: copy.wait())


def last_kernel(table, now, mirrored, ok, ov, out_k, out_v, sem):
    ends = end_copies(table, now[0] - 1, 3, mirrored, out_k, out_v, sem)
    when_all(ends, lambda copy: copy.start())
    when_all(ends, lambda copy: copy.wait())


def gather_stages(own, dp):
    block = jnp.stack([own, lax.ppermute(own, "side", [(0, 1), (1, 0)])])
    yield block
    if dp & (dp - 1):
        rest = [lax.ppermute(block, "dp", [(i, (i + x) % dp) for i in range(dp)]) for x in range(1, dp)]
        yield jnp.concatenate([block] + (yield rest))
    else:
        for stage in range(dp.bit_length() - 1):
            got = yield lax.ppermute(block, "dp", [(i, i ^ (1 << stage)) for i in range(dp)])
            block = jnp.concatenate([block, got])
            yield block


def body(
    prompt_keys,
    prompt_values,
    prompt_lengths,
    assignment,
    new_queries,
    incoming_token_keys,
    incoming_token_values,
    stored_keys,
    stored_values,
    resident_lengths,
    resident_queries,
    stored_token_keys,
    stored_token_values,
):
    step_count = resident_queries.shape[0]
    dp = lax.axis_size("dp")
    request_count = prompt_lengths.shape[0]
    full, width = prompt_keys.shape[1:]
    query_width = new_queries.shape[2]
    half = full // 2
    bf16, f32, i32 = jnp.bfloat16, jnp.float32, jnp.int32
    swap = [(0, 1), (1, 0)]
    shape = jax.ShapeDtypeStruct
    dma = pltpu.SemaphoreType.DMA
    roomy = pltpu.CompilerParams(vmem_limit_bytes=16 << 20)

    pk, pv = prompt_keys[0], prompt_values[0]
    xk, xv = lax.ppermute(pk, "side", swap), lax.ppermute(pv, "side", swap)

    most = full // UNIT
    ring_units = 2 * most + (LAG + 1) * PER
    steps_max = -(-request_count * most // PER) + LAG * dp + PEEL + ENDS[-1] + LAG
    wide = -(-steps_max * PER // 128) * 128
    slots = shape((CAP * half, width), bf16)
    table = pl.pallas_call(
        functools.partial(plan_kernel, dp, half, ring_units),
        out_shape=shape((8, wide), i32),
        in_specs=[SM, SM, VM, VM],
        out_specs=VM,
        compiler_params=roomy,
    )(prompt_lengths, jnp.reshape(assignment, (request_count,)), pk, pv)
    last = table[4, 0]

    message = shape((2, MESSAGE, width), bf16)
    pool_shape = shape((2, 2 * full + ring_units * UNIT, width), bf16)
    first = pl.pallas_call(
        functools.partial(first_kernel, dp),
        out_shape=message,
        in_specs=[SM, SM] + [VM] * 4,
        out_specs=VM,
        compiler_params=roomy,
    )(table, prompt_lengths, pk, pv, xk, xv)

    held = lax.optimization_barrier((new_queries, first))[0]
    rows = step_count * query_width // HEAD_WIDTH
    part, own_out = pl.pallas_call(
        functools.partial(attention_kernel, dp),
        out_shape=(shape((rows, 3 * HEAD_WIDTH), f32), shape((rows, HEAD_WIDTH), f32)),
        in_specs=[SM, SM] + [VM] * 10,
        out_specs=[VM, VM],
        scratch_shapes=[pltpu.VMEM((step_count * query_width // width, HEAD_WIDTH), f32)],
        compiler_params=roomy,
    )(
        resident_lengths, prompt_lengths,
        resident_queries[:, 0], stored_keys[0], stored_values[0], stored_token_keys[:, 0], stored_token_values[:, 0],
        held, pk, pv, incoming_token_keys, incoming_token_values,
    )

    tied = lax.optimization_barrier((table, first))
    pool, second, out_k, out_v = pl.pallas_call(
        functools.partial(pool_kernel, dp),
        out_shape=(pool_shape, message, slots, slots),
        in_specs=[SM, SM] + [VM] * 4,
        out_specs=[HBM, VM, HBM, HBM],
        scratch_shapes=[
            pltpu.VMEM((half, width), bf16), pltpu.VMEM((2, 2, full, width), bf16),
            dma((2, CAP)), dma((2, 2)), dma((2,)), dma((2, 2, half // UNIT)),
        ],
        compiler_params=roomy,
    )(tied[0], prompt_lengths, pk, pv, xk, xv)

    hops = [(i, i + 1) for i in range(dp - 1)] + [(dp + i + 1, dp + i) for i in range(dp - 1)]

    def cross(send):
        return lax.ppermute(send, ("side", "dp"), hops)

    def mirror(got):
        return lax.ppermute(got, "side", swap)

    def place(t, got, mirrored, pool, out_k, out_v, lay):
        news = [message] if lay else []
        first_kept = len(news)
        mirrors = [] if mirrored is None else [mirrored]

        def kernel(table, now, got, *refs):
            refs = list(refs)
            mirrored = refs.pop(0) if mirrors else None
            send = refs.pop(3) if lay else None
            step_kernel(table, now, got, mirrored, *refs[:3], send, *refs[3:])

        kept = 3 + len(mirrors)
        outs = pl.pallas_call(
            kernel,
            out_shape=(*news, pool_shape, slots, slots),
            in_specs=[SM, SM, VM] + [VM] * len(mirrors) + [HBM] * 3,
            out_specs=[VM] * len(news) + [HBM] * 3,
            scratch_shapes=[dma((PER,)), dma((PER, 2)), dma((PER, 2)), dma((PER,))],
            input_output_aliases={kept + i: first_kept + i for i in range(3)},
            compiler_params=roomy,
        )(table, jnp.full((1,), t, i32), got, *mirrors, pool, out_k, out_v)
        return outs if lay else (None, *outs)

    def finish(t, mirrored, out_k, out_v):
        return pl.pallas_call(
            last_kernel,
            out_shape=(slots, slots),
            in_specs=[SM, SM, VM, HBM, HBM],
            out_specs=[HBM, HBM],
            scratch_shapes=[dma((PER, 2))],
            input_output_aliases={3: 0, 4: 1},
            compiler_params=roomy,
        )(table, jnp.full((1,), t, i32), mirrored, out_k, out_v)

    def advance(count, state, beside=None):
        t, got, a, mirrored, pool, out_k, out_v = state
        for i in range(count):
            coming = cross(a)
            if beside is not None:
                got = beside(i, got, a)
            a, pool, out_k, out_v = place(t + i, got, mirrored, pool, out_k, out_v, True)
            got, mirrored = coming, mirror(got)
        return t + count, got, a, mirrored, pool, out_k, out_v

    small = {}

    def beside(i, got, a):
        if i == 1:
            here, kept, _ = lax.optimization_barrier((own_out, part, a))
            small["part"] = lax.ppermute(kept, "side", swap)
            small["stages"] = gather_stages(here, dp)
            small["rows"] = next(small["stages"])
            small["arrived"] = next(small["stages"], None)
        elif i % 2 == 0 and small.get("arrived") is not None:
            arrived = lax.optimization_barrier((small["arrived"], a))[0]
            small["rows"] = small["stages"].send(arrived)
            small["arrived"] = next(small["stages"], None)
            while i >= (PEEL - 2) // 2 * 2 and small["arrived"] is not None:
                small["rows"] = small["stages"].send(small["arrived"])
                small["arrived"] = next(small["stages"], None)
        else:
            return got
        return lax.optimization_barrier((got, small["rows"]))[0]

    second = lax.optimization_barrier((second, own_out))[0]
    state = advance(PEEL - 1, (0, cross(first), second, None, pool, out_k, out_v), beside)
    part_other, everyone = small["part"], small["rows"]
    resident_out, new_out = pl.pallas_call(
        functools.partial(finish_kernel, dp, step_count),
        out_shape=(shape((step_count, query_width), bf16), shape((step_count, request_count, query_width), bf16)),
        in_specs=[VM] * 3,
        out_specs=[VM, VM],
        scratch_shapes=[pltpu.VMEM((rows, HEAD_WIDTH), f32)],
    )(part, part_other, everyone)
    resident_out, new_out, a = lax.optimization_barrier((resident_out, new_out, state[2]))
    t, got, _, mirrored, pool, out_k, out_v = state
    left = jnp.maximum(last - PEEL, 0)
    crowd = max(min(2 * (d + 1), CAP * (dp - 1 - d)) for d in range(dp - 1))
    if -(-crowd * most // PER) + LAG * (dp - 2) > PEEL + ENDS[-1]:
        left, (t, got, a, mirrored, pool, out_k, out_v) = lax.while_loop(
            lambda state: state[0] > ENDS[-1],
            lambda state: (state[0] - TURN, advance(TURN, state[1])),
            (left, (jnp.asarray(t, i32), got, a, mirrored, pool, out_k, out_v)),
        )

    def end(count, state):
        _, pool, out_k, out_v = state
        now = [got, a, mirrored]
        for i in range(count + 1):
            arrived, message, passed = now
            coming = cross(message) if i < count else None
            message, pool, out_k, out_v = place(t + i, arrived, passed, pool, out_k, out_v, i + 1 < count)
            now = [coming, message, mirror(arrived)]
        out_k, out_v = finish(t + count + 1, now[2], out_k, out_v)
        return jnp.full((), -1, i32), pool, out_k, out_v

    state = (left, pool, out_k, out_v)
    for lower, count in zip((-1, *ENDS), ENDS):
        state = lax.while_loop(
            lambda state, lower=lower, count=count: (state[0] > lower) & (state[0] <= count),
            functools.partial(end, count), state,
        )
    _, _, out_k, out_v = state
    out_k, out_v = (out.reshape(CAP, half, width) for out in (out_k, out_v))
    return (resident_out[:, None, :], new_out, out_k, out_v)


def solution(mesh):
    placed = (
        P(("side", "dp"), None, "tp"),
        P(("side", "dp"), None, "tp"),
        P(),
        P(),
        P(None, None, "tp"),
        P(None, None, "tp"),
        P(None, None, "tp"),
        P("dp", "side", "tp"),
        P("dp", "side", "tp"),
        P("dp"),
        P(None, "dp", "tp"),
        P(None, "dp", "tp"),
        P(None, "dp", "tp"),
    )
    return jax.shard_map(
        body,
        mesh=mesh,
        in_specs=placed,
        out_specs=(
            P(None, "dp", "tp"),
            P(None, None, "tp"),
            P("dp", "side", "tp"),
            P("dp", "side", "tp"),
        ),
        check_vma=False,
    )
```

```python
import functools

import jax
import jax.numpy as jnp
from jax import lax
from jax.experimental import pallas as pl
from jax.experimental.pallas import tpu as pltpu
from jax.sharding import PartitionSpec as P

HEAD_WIDTH = 128
CAP = 4
UNIT = 128
PER = 6
MESSAGE = UNIT * PER
PEEL = 6
ENDS = (0, 1, 2, 3, 4, 5, 7, 9)
TURN = 3
LAG = 2
LOW = -1e30

HBM = pl.BlockSpec(memory_space=pltpu.HBM)
VM = pl.BlockSpec(memory_space=pltpu.VMEM)
SM = pl.BlockSpec(memory_space=pltpu.SMEM)


def attend(q, q_rows, k_ref, v_ref, tk, tv, first, length, tokens_on, emit):
    steps = q.shape[0]
    keys, width = k_ref.shape
    heads_kv = width // HEAD_WIDTH
    members = q.shape[1] // width
    rows = members * steps
    scale = HEAD_WIDTH ** -0.5
    for kv in range(heads_kv):
        lanes = slice(kv * HEAD_WIDTH, (kv + 1) * HEAD_WIDTH)
        for g in range(members):
            at = (kv * members + g) * HEAD_WIDTH
            q_rows[g * steps:(g + 1) * steps, :] = q[:, at:at + HEAD_WIDTH]
        q32 = q_rows[...]
        scores = lax.dot_general(
            q32.astype(jnp.bfloat16), k_ref[:, lanes], (((1,), (1,)), ((), ())), preferred_element_type=jnp.float32
        ) * scale
        usable = first + lax.broadcasted_iota(jnp.int32, (rows, keys), 1) < length
        scores = jnp.where(usable, scores, LOW)
        row_step = lax.rem(lax.broadcasted_iota(jnp.int32, (rows, 1), 0), steps)
        top = jnp.max(scores, axis=1, keepdims=True)
        extra = []
        for n in range(steps):
            s = jnp.sum(q32 * tk[n:n + 1, lanes], axis=1, keepdims=True) * scale
            on = (row_step >= n) & tokens_on
            s = jnp.where(on, s, LOW)
            extra.append((on, s))
            top = jnp.maximum(top, s)
        weight = jnp.where(usable, jnp.exp(scores - top), 0.0)
        total = jnp.sum(weight, axis=1, keepdims=True)
        acc = lax.dot_general(
            weight.astype(jnp.bfloat16), v_ref[:, lanes], (((1,), (0,)), ((), ())), preferred_element_type=jnp.float32
        )
        for n, (on, s) in enumerate(extra):
            w = jnp.where(on, jnp.exp(s - top), 0.0)
            total = total + w
            acc = acc + w.astype(jnp.bfloat16).astype(jnp.float32) * tv[n:n + 1, lanes]
        emit(kv, top, total, acc)


def attention_kernel(
    dp, resident_length, lengths, rq, rk, rv, rtk, rtv, nq, nk, nv, ntk, ntv, part, own_out, q_rows
):
    side = lax.axis_index("side")
    owner = side * dp + lax.axis_index("dp")
    steps = rq.shape[0]
    keys, width = rk.shape
    rows = steps * rq.shape[1] // width
    f32 = jnp.float32

    def emit_part(kv, top, total, acc):
        at = slice(kv * rows, (kv + 1) * rows)
        part[at, 0:HEAD_WIDTH] = acc
        part[at, HEAD_WIDTH:2 * HEAD_WIDTH] = jnp.broadcast_to(top, (rows, HEAD_WIDTH))
        part[at, 2 * HEAD_WIDTH:] = jnp.broadcast_to(total, (rows, HEAD_WIDTH))

    attend(
        rq[...].astype(f32), q_rows, rk, rv, rtk[...].astype(f32), rtv[...].astype(f32),
        side * keys, resident_length[0], side == 1, emit_part,
    )

    def own(ref):
        picked = []
        for n in range(steps):
            block = ref[n].astype(f32)
            here = lax.broadcasted_iota(jnp.int32, block.shape, 0) == owner
            picked.append(jnp.sum(jnp.where(here, block, 0.0), axis=0, keepdims=True))
        return jnp.concatenate(picked, axis=0)

    def emit_out(kv, top, total, acc):
        own_out[kv * rows:(kv + 1) * rows, :] = acc / total

    attend(own(nq), q_rows, nk, nv, own(ntk), own(ntv), 0, lengths[owner], side >= 0, emit_out)


def finish_kernel(dp, steps, a, b, everyone, resident, new, o_rows):
    w = HEAD_WIDTH
    heads = resident.shape[1] // w
    top = jnp.maximum(a[:, w:2 * w], b[:, w:2 * w])
    ga = jnp.exp(a[:, w:2 * w] - top)
    gb = jnp.exp(b[:, w:2 * w] - top)
    o_rows[...] = (a[:, 0:w] * ga + b[:, 0:w] * gb) / (a[:, 2 * w:] * ga + b[:, 2 * w:] * gb)
    for h in range(heads):
        resident[:, h * w:(h + 1) * w] = o_rows[h * steps:(h + 1) * steps, :].astype(resident.dtype)
    side, me = lax.axis_index("side"), lax.axis_index("dp")
    count = everyone.shape[0]
    order = []
    for r in range(count):
        far = lax.bitwise_xor(me, r % dp) if dp & (dp - 1) == 0 else lax.rem(me - r % dp + dp, dp)
        order.append(far * 2 + lax.bitwise_xor(side, r // dp))
    at_row = lax.broadcasted_iota(jnp.int32, (count, w), 0)
    for n in range(steps):
        for h in range(heads):
            k = h * steps + n
            block = jnp.zeros((count, w), jnp.float32)
            for r in range(count):
                block = jnp.where(at_row == r, everyone[order[r], k:k + 1, :], block)
            new[n, :, h * w:(h + 1) * w] = block.astype(new.dtype)


def units_at(start):
    return pl.ds(pl.multiple_of(start, UNIT), UNIT)


def last_unit(length):
    return (length + UNIT - 1) // UNIT * UNIT - UNIT


def mask_unit(ref, first, length):
    row = lax.broadcasted_iota(jnp.int32, (UNIT, ref.shape[1]), 0)
    block = ref[units_at(first), :]
    ref[units_at(first), :] = jnp.where(first + row < length, block, jnp.zeros_like(block))


def plan_kernel(dp, half, ring_units, lengths, goal, pk, pv, table):
    side, me = lax.axis_index("side"), lax.axis_index("dp")
    f32 = jnp.float32
    full = 2 * half
    count = lengths.shape[0]
    wide = table.shape[1]
    id_row = lax.broadcasted_iota(jnp.int32, (count, count), 1).astype(f32)
    id_col = lax.broadcasted_iota(jnp.int32, (count, count), 0).astype(f32)
    eye = id_row == id_col

    def col(row):
        return jnp.sum(jnp.where(eye, jnp.broadcast_to(row, (count, count)), 0.0), axis=1, keepdims=True)

    def spread(scalars):
        row = jnp.zeros((1, count), jnp.int32)
        lane = lax.broadcasted_iota(jnp.int32, (1, count), 1)
        for r in range(count):
            row = jnp.where(lane == r, scalars[r], row)
        return row.astype(f32)

    ids = id_row[0:1]
    late = jnp.where(ids >= dp, 1.0, 0.0)
    src0 = ids - dp * late
    goal0 = spread(goal)
    side_f, me_f = side.astype(f32), me.astype(f32)
    units = jnp.floor((spread(lengths) + (UNIT - 1)) * (1.0 / UNIT))
    units_col, late_col, goal0_col, src0_col = col(units), col(late), col(goal0), col(src0)
    slot = jnp.sum(jnp.where((goal0_col == goal0) & (id_col < id_row), 1.0, 0.0), axis=0, keepdims=True)
    slot_col = col(slot)
    time = lax.broadcasted_iota(jnp.int32, (1, wide), 1).astype(f32)
    here_col = jnp.where(late_col == side_f, 0.0, 1.0)
    steps = jnp.zeros((1, 1), f32)
    sends, passes, ends = [], [], []
    for flip in (False, True):
        turned = (lambda x: dp - 1 - x) if flip else (lambda x: x)
        s, g, m, s_col, g_col = turned(src0), turned(goal0), turned(me_f), turned(src0_col), turned(goal0_col)
        crosses, bases, times = [], [], []
        for d in range(dp - 1):
            cross = (s <= d) & (g > d)
            cross_col = (s_col <= d) & (g_col > d)
            ready = jnp.zeros((1, count), f32)
            if d > 0:
                ready = jnp.where(s == d, 0.0, times[-1] + LAG * PER)
            ready_col = col(ready)
            ahead = (ready_col < ready) | (
                (ready_col == ready) & ((g_col > g) | ((g_col == g) & (id_col < id_row)))
            )
            base = jnp.sum(jnp.where(ahead & cross_col, units_col, 0.0), axis=0, keepdims=True)
            slack = jnp.where((ahead | eye) & cross_col, ready_col - col(base), 0.0)
            start = base + jnp.max(slack, axis=0, keepdims=True)
            end = jnp.max(jnp.where(cross, start + units, 0.0), axis=1, keepdims=True)
            steps = jnp.maximum(steps, jnp.floor((end + (PER - 1)) * (1.0 / PER)))
            crosses.append(cross)
            bases.append(base)
            times.append(start)

        def at(link):
            base, start, used = (jnp.zeros((1, count), f32) for _ in range(3))
            for d in range(dp - 1):
                base = jnp.where(link == d, bases[d], base)
                start = jnp.where(link == d, times[d], start)
                used = jnp.where(link == d, jnp.where(crosses[d], units, 0.0), used)
            return col(base), col(start), col(used)

        def ring_row(p):
            return (p - ring_units * jnp.floor((p + 0.5) * (1.0 / ring_units))) * UNIT

        def pick(hit, value):
            return jnp.sum(jnp.where(hit, value + 1.0, 0.0), axis=0, keepdims=True) - 1.0

        base, start, used = at(m)
        c = time - start
        hit = (c >= 0) & (c < used)
        own = here_col * full + c * UNIT
        sends.append(jnp.maximum(pick(hit, jnp.where(s_col == m, own, 2 * full + ring_row(base + c))), 0.0))
        _, start, used = at(m - 1)
        c = time - start
        hit = (c >= 0) & (c < used)
        passes.append(pick(hit & (g_col != m), 2 * full + ring_row(base + c)))
        row = c * UNIT - half * side_f
        ends.append(pick(hit & (g_col == m) & (row >= 0) & (row < half), slot_col * half + row))
    right = side_f == 0.0
    for r, row in enumerate((
        jnp.where(right, sends[0], sends[1]), jnp.where(right, passes[0], passes[1]),
        jnp.where(right, ends[0], ends[1]), jnp.where(right, ends[1], ends[0]),
    )):
        table[r:r + 1, :] = row.astype(jnp.int32)
    stay = jnp.where((src0 == me_f) & (goal0 == me_f), slot + 1.0, 0.0)
    home = [
        jnp.sum(jnp.where(late == which, stay, 0.0), axis=1, keepdims=True) - 1.0 for which in (side_f, 1.0 - side_f)
    ]
    last = jnp.where(time == 0, steps, jnp.where(time == 1, home[0], home[1]))
    table[4:5, :] = last.astype(jnp.int32)
    table[5:8, :] = jnp.zeros((3, wide), jnp.int32)


def first_kernel(dp, table, lengths, pk, pv, xk, xv, send):
    side, me = lax.axis_index("side"), lax.axis_index("dp")
    full = pk.shape[0]
    for j, pair in enumerate(((pk, pv), (xk, xv))):
        length = lengths[lax.bitwise_xor(side, j) * dp + me]
        last = last_unit(length)
        for i in range(PER):
            row = table[0, i] - j * full

            @pl.when((row >= 0) & (row < full))
            def _():
                for n in range(2):
                    send[n, i * UNIT:(i + 1) * UNIT, :] = pair[n][units_at(row), :]

            @pl.when(row == last)
            def _():
                for n in range(2):
                    mask_unit(send.at[n, i * UNIT:(i + 1) * UNIT], 0, length - last)


def pool_kernel(
    dp, table, lengths, pk, pv, xk, xv, pool, send, out_k, out_v, blank, stage, fill_sem, load_sem, pool_sem, home_sem
):
    side, me = lax.axis_index("side"), lax.axis_index("dp")
    full = xk.shape[0]
    half = full // 2
    loads = [
        pltpu.make_async_copy(a, stage.at[j, n], load_sem.at[j, n])
        for j, pair in enumerate(((pk, pv), (xk, xv))) for n, a in enumerate(pair)
    ]
    for copy in loads:
        copy.start()
    blank[...] = jnp.zeros_like(blank)
    fills = [
        pltpu.make_async_copy(blank, out.at[pl.ds(slot * half, half)], fill_sem.at[i, slot])
        for i, out in enumerate((out_k, out_v)) for slot in range(CAP)
    ]
    for fill in fills:
        fill.start()
    stores, homes = [], []
    for j in range(2):
        length = lengths[lax.bitwise_xor(side, j) * dp + me]
        last = last_unit(length)
        for n in range(2):
            loads[2 * j + n].wait()
            mask_unit(stage.at[j, n], last, length)
        store = pltpu.make_async_copy(stage.at[j], pool.at[:, pl.ds(j * full, full)], pool_sem.at[j])
        store.start()
        stores.append(store)
        slot = table[4, 1 + j]
        count = jnp.where(slot >= 0, jnp.clip((last + UNIT - side * half) // UNIT, 0, half // UNIT), 0)

        def home(u, wait, j=j, slot=slot):
            for n, out in enumerate((out_k, out_v)):
                copy = pltpu.make_async_copy(
                    stage.at[j, n, units_at(side * half + u * UNIT)], out.at[units_at(slot * half + u * UNIT)],
                    home_sem.at[j, n, u],
                )
                copy.wait() if wait else copy.start()

        homes.append((count, home))
    for fill in fills:
        fill.wait()
    for count, home in homes:
        pl.loop(0, count)(functools.partial(home, wait=False))
    for i in range(PER):
        code = table[0, PER + i]
        j = jnp.clip(code // full, 0, 1)
        row = jnp.clip(code - j * full, 0, full - UNIT)
        for n in range(2):
            send[n, i * UNIT:(i + 1) * UNIT, :] = stage[j, n, units_at(row), :]
    for count, home in homes:
        pl.loop(0, count)(functools.partial(home, wait=True))
    for store in stores:
        store.wait()


def end_copies(table, t, row, take, out_k, out_v, sem):
    copies = []
    for i in range(PER):
        code = table[row, t * PER + i]
        to = units_at(jnp.maximum(code, 0))
        copies.append((code >= 0, [
            pltpu.make_async_copy(take.at[n, pl.ds(i * UNIT, UNIT)], out.at[to], sem.at[i, n])
            for n, out in enumerate((out_k, out_v))
        ]))
    return copies


def when_all(copies, act):
    @pl.when(functools.reduce(jnp.logical_or, [on for on, _ in copies]))
    def _():
        for on, group in copies:
            @pl.when(on)
            def _():
                for copy in group:
                    act(copy)


def step_kernel(
    table, now, got, mirrored, pool_in, ok, ov, send, pool, out_k, out_v, pass_sem, got_sem, mirror_sem, send_sem
):
    t = now[0]
    passes = []
    for i in range(PER):
        code = table[1, t * PER + i]
        to = pool.at[:, units_at(jnp.maximum(code, 0))]
        passes.append((code >= 0, [pltpu.make_async_copy(got.at[:, pl.ds(i * UNIT, UNIT)], to, pass_sem.at[i])]))
    when_all(passes, lambda copy: copy.start())
    ends = [end_copies(table, t, 2, got, out_k, out_v, got_sem)]
    if mirrored is not None:
        ends.append(end_copies(table, t - 1, 3, mirrored, out_k, out_v, mirror_sem))
    for copies in ends:
        when_all(copies, lambda copy: copy.start())
    when_all(passes, lambda copy: copy.wait())
    if send is not None:
        lay = [
            pltpu.make_async_copy(
                pool.at[:, units_at(table[0, (t + LAG) * PER + i])], send.at[:, pl.ds(i * UNIT, UNIT)], send_sem.at[i]
            )
            for i in range(PER)
        ]
        for copy in lay:
            copy.start()
        for copy in lay:
            copy.wait()
    for copies in ends:
        when_all(copies, lambda copy: copy.wait())


def last_kernel(table, now, mirrored, ok, ov, out_k, out_v, sem):
    ends = end_copies(table, now[0] - 1, 3, mirrored, out_k, out_v, sem)
    when_all(ends, lambda copy: copy.start())
    when_all(ends, lambda copy: copy.wait())


def gather_stages(own, dp):
    block = jnp.stack([own, lax.ppermute(own, "side", [(0, 1), (1, 0)])])
    yield block
    if dp & (dp - 1):
        rest = [lax.ppermute(block, "dp", [(i, (i + x) % dp) for i in range(dp)]) for x in range(1, dp)]
        yield jnp.concatenate([block] + (yield rest))
    else:
        for stage in range(dp.bit_length() - 1):
            reach = 1 << stage
            hops = [(z, z - reach) for z in range(dp) if z & reach] + [
                (dp + z, dp + z + reach) for z in range(dp) if not z & reach
            ]
            came = yield lax.ppermute(block, ("side", "dp"), hops)
            shared = lax.ppermute(came, "side", [(0, 1), (1, 0)])
            shared = shared.reshape(-1, 2, *own.shape)[:, ::-1].reshape(block.shape)
            block = jnp.concatenate([block, came + shared])
            yield block


def body(
    prompt_keys,
    prompt_values,
    prompt_lengths,
    assignment,
    new_queries,
    incoming_token_keys,
    incoming_token_values,
    stored_keys,
    stored_values,
    resident_lengths,
    resident_queries,
    stored_token_keys,
    stored_token_values,
):
    step_count = resident_queries.shape[0]
    dp = lax.axis_size("dp")
    request_count = prompt_lengths.shape[0]
    full, width = prompt_keys.shape[1:]
    query_width = new_queries.shape[2]
    half = full // 2
    bf16, f32, i32 = jnp.bfloat16, jnp.float32, jnp.int32
    swap = [(0, 1), (1, 0)]
    shape = jax.ShapeDtypeStruct
    dma = pltpu.SemaphoreType.DMA
    roomy = pltpu.CompilerParams(vmem_limit_bytes=16 << 20)

    pk, pv = prompt_keys[0], prompt_values[0]
    xk, xv = lax.ppermute(pk, "side", swap), lax.ppermute(pv, "side", swap)

    most = full // UNIT
    ring_units = 2 * most + (LAG + 1) * PER
    steps_max = -(-request_count * most // PER) + LAG * dp + PEEL + ENDS[-1] + LAG
    wide = -(-steps_max * PER // 128) * 128
    slots = shape((CAP * half, width), bf16)
    table = pl.pallas_call(
        functools.partial(plan_kernel, dp, half, ring_units),
        out_shape=shape((8, wide), i32),
        in_specs=[SM, SM, VM, VM],
        out_specs=VM,
        compiler_params=pltpu.CompilerParams(vmem_limit_bytes=58 << 20),
    )(prompt_lengths, jnp.reshape(assignment, (request_count,)), pk, pv)
    last = table[4, 0]

    message = shape((2, MESSAGE, width), bf16)
    pool_shape = shape((2, 2 * full + ring_units * UNIT, width), bf16)
    first = pl.pallas_call(
        functools.partial(first_kernel, dp),
        out_shape=message,
        in_specs=[SM, SM] + [VM] * 4,
        out_specs=VM,
        compiler_params=roomy,
    )(table, prompt_lengths, pk, pv, xk, xv)

    held = lax.optimization_barrier((new_queries, first))[0]
    rows = step_count * query_width // HEAD_WIDTH
    part, own_out = pl.pallas_call(
        functools.partial(attention_kernel, dp),
        out_shape=(shape((rows, 3 * HEAD_WIDTH), f32), shape((rows, HEAD_WIDTH), f32)),
        in_specs=[SM, SM] + [VM] * 10,
        out_specs=[VM, VM],
        scratch_shapes=[pltpu.VMEM((step_count * query_width // width, HEAD_WIDTH), f32)],
        compiler_params=roomy,
    )(
        resident_lengths, prompt_lengths,
        resident_queries[:, 0], stored_keys[0], stored_values[0], stored_token_keys[:, 0], stored_token_values[:, 0],
        held, pk, pv, incoming_token_keys, incoming_token_values,
    )

    tied = lax.optimization_barrier((table, first))
    pool, second, out_k, out_v = pl.pallas_call(
        functools.partial(pool_kernel, dp),
        out_shape=(pool_shape, message, slots, slots),
        in_specs=[SM, SM] + [VM] * 4,
        out_specs=[HBM, VM, HBM, HBM],
        scratch_shapes=[
            pltpu.VMEM((half, width), bf16), pltpu.VMEM((2, 2, full, width), bf16),
            dma((2, CAP)), dma((2, 2)), dma((2,)), dma((2, 2, half // UNIT)),
        ],
        compiler_params=roomy,
    )(tied[0], prompt_lengths, pk, pv, xk, xv)

    hops = [(i, i + 1) for i in range(dp - 1)] + [(dp + i + 1, dp + i) for i in range(dp - 1)]

    def cross(send):
        return lax.ppermute(send, ("side", "dp"), hops)

    def mirror(got):
        return lax.ppermute(got, "side", swap)

    def place(t, got, mirrored, pool, out_k, out_v, lay):
        news = [message] if lay else []
        first_kept = len(news)
        mirrors = [] if mirrored is None else [mirrored]

        def kernel(table, now, got, *refs):
            refs = list(refs)
            mirrored = refs.pop(0) if mirrors else None
            send = refs.pop(3) if lay else None
            step_kernel(table, now, got, mirrored, *refs[:3], send, *refs[3:])

        kept = 3 + len(mirrors)
        outs = pl.pallas_call(
            kernel,
            out_shape=(*news, pool_shape, slots, slots),
            in_specs=[SM, SM, VM] + [VM] * len(mirrors) + [HBM] * 3,
            out_specs=[VM] * len(news) + [HBM] * 3,
            scratch_shapes=[dma((PER,)), dma((PER, 2)), dma((PER, 2)), dma((PER,))],
            input_output_aliases={kept + i: first_kept + i for i in range(3)},
            compiler_params=roomy,
        )(table, jnp.full((1,), t, i32), got, *mirrors, pool, out_k, out_v)
        return outs if lay else (None, *outs)

    def finish(t, mirrored, out_k, out_v):
        return pl.pallas_call(
            last_kernel,
            out_shape=(slots, slots),
            in_specs=[SM, SM, VM, HBM, HBM],
            out_specs=[HBM, HBM],
            scratch_shapes=[dma((PER, 2))],
            input_output_aliases={3: 0, 4: 1},
            compiler_params=roomy,
        )(table, jnp.full((1,), t, i32), mirrored, out_k, out_v)

    def advance(count, state, beside=None):
        t, got, a, mirrored, pool, out_k, out_v = state
        for i in range(count):
            coming = cross(a)
            if beside is not None:
                got = beside(i, got, a)
            a, pool, out_k, out_v = place(t + i, got, mirrored, pool, out_k, out_v, True)
            got, mirrored = coming, mirror(got)
        return t + count, got, a, mirrored, pool, out_k, out_v

    part_other = lax.ppermute(part, "side", swap)
    stages = gather_stages(own_out, dp)
    small = {"rows": next(stages)}
    second, part_other, small["rows"] = lax.optimization_barrier((second, part_other, small["rows"]))
    small["arrived"] = next(stages, None)

    def beside(i, got, a):
        if i % 2 == 0 or small["arrived"] is None:
            return got
        small["rows"] = stages.send(lax.optimization_barrier((small["arrived"], a))[0])
        small["arrived"] = next(stages, None)
        while i >= PEEL - 3 and small["arrived"] is not None:
            small["rows"] = stages.send(small["arrived"])
            small["arrived"] = next(stages, None)
        return lax.optimization_barrier((got, small["rows"]))[0]

    state = advance(PEEL - 1, (0, cross(first), second, None, pool, out_k, out_v), beside)
    everyone = small["rows"]
    resident_out, new_out = pl.pallas_call(
        functools.partial(finish_kernel, dp, step_count),
        out_shape=(shape((step_count, query_width), bf16), shape((step_count, request_count, query_width), bf16)),
        in_specs=[VM] * 3,
        out_specs=[VM, VM],
        scratch_shapes=[pltpu.VMEM((rows, HEAD_WIDTH), f32)],
    )(part, part_other, everyone)
    resident_out, new_out, a = lax.optimization_barrier((resident_out, new_out, state[2]))
    t, got, _, mirrored, pool, out_k, out_v = state
    left = jnp.maximum(last - PEEL, 0)
    crowd = max(min(2 * (d + 1), CAP * (dp - 1 - d)) for d in range(dp - 1))
    if -(-crowd * most // PER) + LAG * (dp - 2) > PEEL + ENDS[-1]:
        left, (t, got, a, mirrored, pool, out_k, out_v) = lax.while_loop(
            lambda state: state[0] > ENDS[-1],
            lambda state: (state[0] - TURN, advance(TURN, state[1])),
            (left, (jnp.asarray(t, i32), got, a, mirrored, pool, out_k, out_v)),
        )

    def end(count, state):
        _, pool, out_k, out_v = state
        now = [got, a, mirrored]
        for i in range(count + 1):
            arrived, message, passed = now
            coming = cross(message) if i < count else None
            message, pool, out_k, out_v = place(t + i, arrived, passed, pool, out_k, out_v, i + 1 < count)
            now = [coming, message, mirror(arrived)]
        out_k, out_v = finish(t + count + 1, now[2], out_k, out_v)
        return jnp.full((), -1, i32), pool, out_k, out_v

    state = (left, pool, out_k, out_v)
    for lower, count in zip((-1, *ENDS), ENDS):
        state = lax.while_loop(
            lambda state, lower=lower, count=count: (state[0] > lower) & (state[0] <= count),
            functools.partial(end, count), state,
        )
    _, _, out_k, out_v = state
    out_k, out_v = (out.reshape(CAP, half, width) for out in (out_k, out_v))
    return (resident_out[:, None, :], new_out, out_k, out_v)


def solution(mesh):
    placed = (
        P(("side", "dp"), None, "tp"),
        P(("side", "dp"), None, "tp"),
        P(),
        P(),
        P(None, None, "tp"),
        P(None, None, "tp"),
        P(None, None, "tp"),
        P("dp", "side", "tp"),
        P("dp", "side", "tp"),
        P("dp"),
        P(None, "dp", "tp"),
        P(None, "dp", "tp"),
        P(None, "dp", "tp"),
    )
    return jax.shard_map(
        body,
        mesh=mesh,
        in_specs=placed,
        out_specs=(
            P(None, "dp", "tp"),
            P(None, None, "tp"),
            P("dp", "side", "tp"),
            P("dp", "side", "tp"),
        ),
        check_vma=False,
    )
```

```python
import functools

import jax
import jax.numpy as jnp
from jax import lax
from jax.experimental import pallas as pl
from jax.experimental.pallas import tpu as pltpu
from jax.sharding import PartitionSpec as P

HEAD_WIDTH = 128
CAP = 4
UNIT = 128
PER = 6
MESSAGE = UNIT * PER
PEEL = 6
ENDS = (0, 1, 2, 3, 4, 5, 7, 9)
TURN = 3
POOL_ROWS = 22528
LAG = 2
LOW = -1e30

HBM = pl.BlockSpec(memory_space=pltpu.HBM)
VM = pl.BlockSpec(memory_space=pltpu.VMEM)
SM = pl.BlockSpec(memory_space=pltpu.SMEM)


def attend(q, q_rows, k_ref, v_ref, tk, tv, first, length, tokens_on, emit):
    steps = q.shape[0]
    keys, width = k_ref.shape
    heads_kv = width // HEAD_WIDTH
    members = q.shape[1] // width
    rows = members * steps
    scale = HEAD_WIDTH ** -0.5
    for kv in range(heads_kv):
        lanes = slice(kv * HEAD_WIDTH, (kv + 1) * HEAD_WIDTH)
        for g in range(members):
            at = (kv * members + g) * HEAD_WIDTH
            q_rows[g * steps:(g + 1) * steps, :] = q[:, at:at + HEAD_WIDTH]
        q32 = q_rows[...]
        scores = lax.dot_general(
            q32.astype(jnp.bfloat16), k_ref[:, lanes], (((1,), (1,)), ((), ())), preferred_element_type=jnp.float32
        ) * scale
        usable = first + lax.broadcasted_iota(jnp.int32, (rows, keys), 1) < length
        scores = jnp.where(usable, scores, LOW)
        row_step = lax.rem(lax.broadcasted_iota(jnp.int32, (rows, 1), 0), steps)
        top = jnp.max(scores, axis=1, keepdims=True)
        extra = []
        for n in range(steps):
            s = jnp.sum(q32 * tk[n:n + 1, lanes], axis=1, keepdims=True) * scale
            on = (row_step >= n) & tokens_on
            s = jnp.where(on, s, LOW)
            extra.append((on, s))
            top = jnp.maximum(top, s)
        weight = jnp.where(usable, jnp.exp(scores - top), 0.0)
        total = jnp.sum(weight, axis=1, keepdims=True)
        acc = lax.dot_general(
            weight.astype(jnp.bfloat16), v_ref[:, lanes], (((1,), (0,)), ((), ())), preferred_element_type=jnp.float32
        )
        for n, (on, s) in enumerate(extra):
            w = jnp.where(on, jnp.exp(s - top), 0.0)
            total = total + w
            acc = acc + w.astype(jnp.bfloat16).astype(jnp.float32) * tv[n:n + 1, lanes]
        emit(kv, top, total, acc)


def attention_kernel(
    dp, resident_length, lengths, rq, rk, rv, rtk, rtv, nq, nk, nv, ntk, ntv, part, own_out, q_rows
):
    side = lax.axis_index("side")
    owner = side * dp + lax.axis_index("dp")
    steps = rq.shape[0]
    keys, width = rk.shape
    rows = steps * rq.shape[1] // width
    f32 = jnp.float32

    def emit_part(kv, top, total, acc):
        at = slice(kv * rows, (kv + 1) * rows)
        part[at, 0:HEAD_WIDTH] = acc
        part[at, HEAD_WIDTH:2 * HEAD_WIDTH] = jnp.broadcast_to(top, (rows, HEAD_WIDTH))
        part[at, 2 * HEAD_WIDTH:] = jnp.broadcast_to(total, (rows, HEAD_WIDTH))

    attend(
        rq[...].astype(f32), q_rows, rk, rv, rtk[...].astype(f32), rtv[...].astype(f32),
        side * keys, resident_length[0], side == 1, emit_part,
    )

    def own(ref):
        picked = []
        for n in range(steps):
            block = ref[n].astype(f32)
            here = lax.broadcasted_iota(jnp.int32, block.shape, 0) == owner
            picked.append(jnp.sum(jnp.where(here, block, 0.0), axis=0, keepdims=True))
        return jnp.concatenate(picked, axis=0)

    def emit_out(kv, top, total, acc):
        own_out[kv * rows:(kv + 1) * rows, :] = acc / total

    attend(own(nq), q_rows, nk, nv, own(ntk), own(ntv), 0, lengths[owner], side >= 0, emit_out)


def finish_kernel(dp, steps, a, b, everyone, resident, new, o_rows):
    w = HEAD_WIDTH
    heads = resident.shape[1] // w
    top = jnp.maximum(a[:, w:2 * w], b[:, w:2 * w])
    ga = jnp.exp(a[:, w:2 * w] - top)
    gb = jnp.exp(b[:, w:2 * w] - top)
    o_rows[...] = (a[:, 0:w] * ga + b[:, 0:w] * gb) / (a[:, 2 * w:] * ga + b[:, 2 * w:] * gb)
    for h in range(heads):
        resident[:, h * w:(h + 1) * w] = o_rows[h * steps:(h + 1) * steps, :].astype(resident.dtype)
    side, me = lax.axis_index("side"), lax.axis_index("dp")
    count = everyone.shape[0]
    order = []
    for r in range(count):
        far = lax.bitwise_xor(me, r % dp) if dp & (dp - 1) == 0 else lax.rem(me - r % dp + dp, dp)
        order.append(far * 2 + lax.bitwise_xor(side, r // dp))
    at_row = lax.broadcasted_iota(jnp.int32, (count, w), 0)
    for n in range(steps):
        for h in range(heads):
            k = h * steps + n
            block = jnp.zeros((count, w), jnp.float32)
            for r in range(count):
                block = jnp.where(at_row == r, everyone[order[r], k:k + 1, :], block)
            new[n, :, h * w:(h + 1) * w] = block.astype(new.dtype)


def units_at(start):
    return pl.ds(pl.multiple_of(start, UNIT), UNIT)


def last_unit(length):
    return (length + UNIT - 1) // UNIT * UNIT - UNIT


def mask_unit(ref, first, length):
    row = lax.broadcasted_iota(jnp.int32, (UNIT, ref.shape[1]), 0)
    block = ref[units_at(first), :]
    ref[units_at(first), :] = jnp.where(first + row < length, block, jnp.zeros_like(block))


def plan_kernel(dp, half, ring_units, lengths, goal, pk, pv, table):
    side, me = lax.axis_index("side"), lax.axis_index("dp")
    f32 = jnp.float32
    full = 2 * half
    count = lengths.shape[0]
    wide = table.shape[1]
    id_row = lax.broadcasted_iota(jnp.int32, (count, count), 1).astype(f32)
    id_col = lax.broadcasted_iota(jnp.int32, (count, count), 0).astype(f32)
    eye = id_row == id_col

    def col(row):
        return jnp.sum(jnp.where(eye, jnp.broadcast_to(row, (count, count)), 0.0), axis=1, keepdims=True)

    def spread(scalars):
        row = jnp.zeros((1, count), jnp.int32)
        lane = lax.broadcasted_iota(jnp.int32, (1, count), 1)
        for r in range(count):
            row = jnp.where(lane == r, scalars[r], row)
        return row.astype(f32)

    ids = id_row[0:1]
    late = jnp.where(ids >= dp, 1.0, 0.0)
    src0 = ids - dp * late
    goal0 = spread(goal)
    side_f, me_f = side.astype(f32), me.astype(f32)
    units = jnp.floor((spread(lengths) + (UNIT - 1)) * (1.0 / UNIT))
    units_col, late_col, goal0_col, src0_col = col(units), col(late), col(goal0), col(src0)
    slot = jnp.sum(jnp.where((goal0_col == goal0) & (id_col < id_row), 1.0, 0.0), axis=0, keepdims=True)
    slot_col = col(slot)
    time = lax.broadcasted_iota(jnp.int32, (1, wide), 1).astype(f32)
    here_col = jnp.where(late_col == side_f, 0.0, 1.0)
    steps = jnp.zeros((1, 1), f32)
    sends, passes, ends = [], [], []
    for flip in (False, True):
        turned = (lambda x: dp - 1 - x) if flip else (lambda x: x)
        s, g, m, s_col, g_col = turned(src0), turned(goal0), turned(me_f), turned(src0_col), turned(goal0_col)
        crosses, bases, times = [], [], []
        for d in range(dp - 1):
            cross = (s <= d) & (g > d)
            cross_col = (s_col <= d) & (g_col > d)
            ready = jnp.zeros((1, count), f32)
            if d > 0:
                ready = jnp.where(s == d, 0.0, times[-1] + LAG * PER)
            ready_col = col(ready)
            ahead = (ready_col < ready) | (
                (ready_col == ready) & ((g_col > g) | ((g_col == g) & (id_col < id_row)))
            )
            base = jnp.sum(jnp.where(ahead & cross_col, units_col, 0.0), axis=0, keepdims=True)
            slack = jnp.where((ahead | eye) & cross_col, ready_col - col(base), 0.0)
            start = base + jnp.max(slack, axis=0, keepdims=True)
            end = jnp.max(jnp.where(cross, start + units, 0.0), axis=1, keepdims=True)
            steps = jnp.maximum(steps, jnp.floor((end + (PER - 1)) * (1.0 / PER)))
            crosses.append(cross)
            bases.append(base)
            times.append(start)

        def at(link):
            base, start, used = (jnp.zeros((1, count), f32) for _ in range(3))
            for d in range(dp - 1):
                base = jnp.where(link == d, bases[d], base)
                start = jnp.where(link == d, times[d], start)
                used = jnp.where(link == d, jnp.where(crosses[d], units, 0.0), used)
            return col(base), col(start), col(used)

        def ring_row(p):
            return (p - ring_units * jnp.floor((p + 0.5) * (1.0 / ring_units))) * UNIT

        def pick(hit, value):
            return jnp.sum(jnp.where(hit, value + 1.0, 0.0), axis=0, keepdims=True) - 1.0

        base, start, used = at(m)
        c = time - start
        hit = (c >= 0) & (c < used)
        own = here_col * full + c * UNIT
        sends.append(jnp.maximum(pick(hit, jnp.where(s_col == m, own, 2 * full + ring_row(base + c))), 0.0))
        _, start, used = at(m - 1)
        c = time - start
        hit = (c >= 0) & (c < used)
        passes.append(pick(hit & (g_col != m), 2 * full + ring_row(base + c)))
        row = c * UNIT - half * side_f
        ends.append(pick(hit & (g_col == m) & (row >= 0) & (row < half), slot_col * half + row))
    right = side_f == 0.0
    for r, row in enumerate((
        jnp.where(right, sends[0], sends[1]), jnp.where(right, passes[0], passes[1]),
        jnp.where(right, ends[0], ends[1]), jnp.where(right, ends[1], ends[0]),
    )):
        table[r:r + 1, :] = row.astype(jnp.int32)
    stay = jnp.where((src0 == me_f) & (goal0 == me_f), slot + 1.0, 0.0)
    home = [
        jnp.sum(jnp.where(late == which, stay, 0.0), axis=1, keepdims=True) - 1.0 for which in (side_f, 1.0 - side_f)
    ]
    last = jnp.where(time == 0, steps, jnp.where(time == 1, home[0], home[1]))
    table[4:5, :] = last.astype(jnp.int32)
    table[5:8, :] = jnp.zeros((3, wide), jnp.int32)


def first_kernel(dp, table, lengths, pk, pv, xk, xv, send):
    side, me = lax.axis_index("side"), lax.axis_index("dp")
    full = pk.shape[0]
    for j, pair in enumerate(((pk, pv), (xk, xv))):
        length = lengths[lax.bitwise_xor(side, j) * dp + me]
        last = last_unit(length)
        for i in range(PER):
            row = table[0, i] - j * full

            @pl.when((row >= 0) & (row < full))
            def _():
                for n in range(2):
                    send[n, i * UNIT:(i + 1) * UNIT, :] = pair[n][units_at(row), :]

            @pl.when(row == last)
            def _():
                for n in range(2):
                    mask_unit(send.at[n, i * UNIT:(i + 1) * UNIT], 0, length - last)


def pool_kernel(
    dp, table, lengths, pk, pv, xk, xv, pool, send, out_k, out_v, blank, stage, fill_sem, load_sem, pool_sem, home_sem
):
    side, me = lax.axis_index("side"), lax.axis_index("dp")
    full = xk.shape[0]
    half = full // 2
    loads = [
        pltpu.make_async_copy(a, stage.at[j, n], load_sem.at[j, n])
        for j, pair in enumerate(((pk, pv), (xk, xv))) for n, a in enumerate(pair)
    ]
    for copy in loads:
        copy.start()
    blank[...] = jnp.zeros_like(blank)
    fills = [
        pltpu.make_async_copy(blank, out.at[pl.ds(slot * half, half)], fill_sem.at[i, slot])
        for i, out in enumerate((out_k, out_v)) for slot in range(CAP)
    ]
    for fill in fills:
        fill.start()
    stores, homes = [], []
    for j in range(2):
        length = lengths[lax.bitwise_xor(side, j) * dp + me]
        last = last_unit(length)
        for n in range(2):
            loads[2 * j + n].wait()
            mask_unit(stage.at[j, n], last, length)
        store = pltpu.make_async_copy(stage.at[j], pool.at[:, pl.ds(j * full, full)], pool_sem.at[j])
        store.start()
        stores.append(store)
        slot = table[4, 1 + j]
        count = jnp.where(slot >= 0, jnp.clip((last + UNIT - side * half) // UNIT, 0, half // UNIT), 0)

        def home(u, wait, j=j, slot=slot):
            for n, out in enumerate((out_k, out_v)):
                copy = pltpu.make_async_copy(
                    stage.at[j, n, units_at(side * half + u * UNIT)], out.at[units_at(slot * half + u * UNIT)],
                    home_sem.at[j, n, u],
                )
                copy.wait() if wait else copy.start()

        homes.append((count, home))
    for fill in fills:
        fill.wait()
    for count, home in homes:
        pl.loop(0, count)(functools.partial(home, wait=False))
    for i in range(PER):
        code = table[0, PER + i]
        j = jnp.clip(code // full, 0, 1)
        row = jnp.clip(code - j * full, 0, full - UNIT)
        for n in range(2):
            send[n, i * UNIT:(i + 1) * UNIT, :] = stage[j, n, units_at(row), :]
    for count, home in homes:
        pl.loop(0, count)(functools.partial(home, wait=True))
    for store in stores:
        store.wait()


def end_copies(table, t, row, take, out_k, out_v, sem):
    copies = []
    for i in range(PER):
        code = table[row, t * PER + i]
        to = units_at(jnp.maximum(code, 0))
        copies.append((code >= 0, [
            pltpu.make_async_copy(take.at[n, pl.ds(i * UNIT, UNIT)], out.at[to], sem.at[i, n])
            for n, out in enumerate((out_k, out_v))
        ]))
    return copies


def when_all(copies, act):
    @pl.when(functools.reduce(jnp.logical_or, [on for on, _ in copies]))
    def _():
        for on, group in copies:
            @pl.when(on)
            def _():
                for copy in group:
                    act(copy)


def step_kernel(
    table, now, got, mirrored, pool_in, ok, ov, send, pool, out_k, out_v, pass_sem, got_sem, mirror_sem, send_sem
):
    t = now[0]
    passes = []
    for i in range(PER):
        code = table[1, t * PER + i]
        to = pool.at[:, units_at(jnp.maximum(code, 0))]
        passes.append((code >= 0, [pltpu.make_async_copy(got.at[:, pl.ds(i * UNIT, UNIT)], to, pass_sem.at[i])]))
    when_all(passes, lambda copy: copy.start())
    ends = [end_copies(table, t, 2, got, out_k, out_v, got_sem)]
    if mirrored is not None:
        ends.append(end_copies(table, t - 1, 3, mirrored, out_k, out_v, mirror_sem))
    for copies in ends:
        when_all(copies, lambda copy: copy.start())
    when_all(passes, lambda copy: copy.wait())
    if send is not None:
        lay = [
            pltpu.make_async_copy(
                pool.at[:, units_at(table[0, (t + LAG) * PER + i])], send.at[:, pl.ds(i * UNIT, UNIT)], send_sem.at[i]
            )
            for i in range(PER)
        ]
        for copy in lay:
            copy.start()
        for copy in lay:
            copy.wait()
    for copies in ends:
        when_all(copies, lambda copy: copy.wait())


def last_kernel(table, now, mirrored, ok, ov, out_k, out_v, sem):
    ends = end_copies(table, now[0] - 1, 3, mirrored, out_k, out_v, sem)
    when_all(ends, lambda copy: copy.start())
    when_all(ends, lambda copy: copy.wait())


def gather_stages(own, dp):
    block = jnp.stack([own, lax.ppermute(own, "side", [(0, 1), (1, 0)])])
    yield block
    if dp & (dp - 1):
        rest = [lax.ppermute(block, "dp", [(i, (i + x) % dp) for i in range(dp)]) for x in range(1, dp)]
        block = jnp.concatenate([block] + (yield rest))
    else:
        for stage in range(dp.bit_length() - 1):
            reach = 1 << stage
            hops = [(z, z - reach) for z in range(dp) if z & reach] + [
                (dp + z, dp + z + reach) for z in range(dp) if not z & reach
            ]
            came = yield lax.ppermute(block, ("side", "dp"), hops)
            shared = yield lax.ppermute(came, "side", [(0, 1), (1, 0)])
            shared = shared.reshape(-1, 2, *own.shape)[:, ::-1].reshape(block.shape)
            block = jnp.concatenate([block, came + shared])
    yield block


def body(
    prompt_keys,
    prompt_values,
    prompt_lengths,
    assignment,
    new_queries,
    incoming_token_keys,
    incoming_token_values,
    stored_keys,
    stored_values,
    resident_lengths,
    resident_queries,
    stored_token_keys,
    stored_token_values,
):
    step_count = resident_queries.shape[0]
    dp = lax.axis_size("dp")
    request_count = prompt_lengths.shape[0]
    full, width = prompt_keys.shape[1:]
    query_width = new_queries.shape[2]
    half = full // 2
    bf16, f32, i32 = jnp.bfloat16, jnp.float32, jnp.int32
    swap = [(0, 1), (1, 0)]
    shape = jax.ShapeDtypeStruct
    dma = pltpu.SemaphoreType.DMA
    roomy = pltpu.CompilerParams(vmem_limit_bytes=44 << 20)

    pk, pv = prompt_keys[0], prompt_values[0]
    xk, xv = lax.ppermute(pk, "side", swap), lax.ppermute(pv, "side", swap)

    most = full // UNIT
    ring_units = 2 * most + (LAG + 1) * PER
    steps_max = -(-request_count * most // PER) + LAG * dp + PEEL + ENDS[-1] + LAG
    wide = -(-steps_max * PER // 128) * 128
    slots = shape((CAP * half, width), bf16)
    table = pl.pallas_call(
        functools.partial(plan_kernel, dp, half, ring_units),
        out_shape=shape((8, wide), i32),
        in_specs=[SM, SM, VM, VM],
        out_specs=VM,
        compiler_params=pltpu.CompilerParams(vmem_limit_bytes=58 << 20),
    )(prompt_lengths, jnp.reshape(assignment, (request_count,)), pk, pv)
    last = table[4, 0]

    message = shape((2, MESSAGE, width), bf16)
    pool_shape = shape((2, max(2 * full + ring_units * UNIT, POOL_ROWS), width), bf16)
    first = pl.pallas_call(
        functools.partial(first_kernel, dp),
        out_shape=message,
        in_specs=[SM, SM] + [VM] * 4,
        out_specs=VM,
        compiler_params=roomy,
    )(table, prompt_lengths, pk, pv, xk, xv)

    held = lax.optimization_barrier((new_queries, first))[0]
    rows = step_count * query_width // HEAD_WIDTH
    part, own_out = pl.pallas_call(
        functools.partial(attention_kernel, dp),
        out_shape=(shape((rows, 3 * HEAD_WIDTH), f32), shape((rows, HEAD_WIDTH), f32)),
        in_specs=[SM, SM] + [VM] * 10,
        out_specs=[VM, VM],
        scratch_shapes=[pltpu.VMEM((step_count * query_width // width, HEAD_WIDTH), f32)],
        compiler_params=roomy,
    )(
        resident_lengths, prompt_lengths,
        resident_queries[:, 0], stored_keys[0], stored_values[0], stored_token_keys[:, 0], stored_token_values[:, 0],
        held, pk, pv, incoming_token_keys, incoming_token_values,
    )

    tied = lax.optimization_barrier((table, first))
    pool, second, out_k, out_v = pl.pallas_call(
        functools.partial(pool_kernel, dp),
        out_shape=(pool_shape, message, slots, slots),
        in_specs=[SM, SM] + [VM] * 4,
        out_specs=[HBM, VM, HBM, HBM],
        scratch_shapes=[
            pltpu.VMEM((half, width), bf16), pltpu.VMEM((2, 2, full, width), bf16),
            dma((2, CAP)), dma((2, 2)), dma((2,)), dma((2, 2, half // UNIT)),
        ],
        compiler_params=roomy,
    )(tied[0], prompt_lengths, pk, pv, xk, xv)

    hops = [(i, i + 1) for i in range(dp - 1)] + [(dp + i + 1, dp + i) for i in range(dp - 1)]

    def cross(send):
        return lax.ppermute(send, ("side", "dp"), hops)

    def mirror(got):
        return lax.ppermute(got, "side", swap)

    def place(t, got, mirrored, pool, out_k, out_v, lay):
        news = [message] if lay else []
        first_kept = len(news)
        mirrors = [] if mirrored is None else [mirrored]

        def kernel(table, now, got, *refs):
            refs = list(refs)
            mirrored = refs.pop(0) if mirrors else None
            send = refs.pop(3) if lay else None
            step_kernel(table, now, got, mirrored, *refs[:3], send, *refs[3:])

        kept = 3 + len(mirrors)
        outs = pl.pallas_call(
            kernel,
            out_shape=(*news, pool_shape, slots, slots),
            in_specs=[SM, SM, VM] + [VM] * len(mirrors) + [HBM] * 3,
            out_specs=[VM] * len(news) + [HBM] * 3,
            scratch_shapes=[dma((PER,)), dma((PER, 2)), dma((PER, 2)), dma((PER,))],
            input_output_aliases={kept + i: first_kept + i for i in range(3)},
            compiler_params=roomy,
        )(table, jnp.full((1,), t, i32), got, *mirrors, pool, out_k, out_v)
        return outs if lay else (None, *outs)

    def finish(t, mirrored, out_k, out_v):
        return pl.pallas_call(
            last_kernel,
            out_shape=(slots, slots),
            in_specs=[SM, SM, VM, HBM, HBM],
            out_specs=[HBM, HBM],
            scratch_shapes=[dma((PER, 2))],
            input_output_aliases={3: 0, 4: 1},
            compiler_params=roomy,
        )(table, jnp.full((1,), t, i32), mirrored, out_k, out_v)

    def advance(count, state, beside=None):
        t, got, a, mirrored, pool, out_k, out_v = state
        for i in range(count):
            coming = cross(a)
            if beside is not None:
                got = beside(i, got, a)
            a, pool, out_k, out_v = place(t + i, got, mirrored, pool, out_k, out_v, True)
            got, mirrored = coming, mirror(got)
        return t + count, got, a, mirrored, pool, out_k, out_v

    part_other = lax.ppermute(part, "side", swap)
    stages = gather_stages(own_out, dp)
    second, part_other, here = lax.optimization_barrier((second, part_other, next(stages)))
    small = next(stages)
    exchanges = 1 if dp & (dp - 1) else 2 * (dp.bit_length() - 1)

    def beside(i, got, a):
        nonlocal small
        for taken in range(i - 1, exchanges if i == PEEL - 2 else min(i, exchanges)):
            if taken >= 0:
                small = stages.send(lax.optimization_barrier((small, a))[0])
        return lax.optimization_barrier((got, small))[0] if i else got

    state = advance(PEEL - 1, (0, cross(first), second, None, pool, out_k, out_v), beside)
    everyone = small
    resident_out, new_out = pl.pallas_call(
        functools.partial(finish_kernel, dp, step_count),
        out_shape=(shape((step_count, query_width), bf16), shape((step_count, request_count, query_width), bf16)),
        in_specs=[VM] * 3,
        out_specs=[VM, VM],
        scratch_shapes=[pltpu.VMEM((rows, HEAD_WIDTH), f32)],
    )(part, part_other, everyone)
    resident_out, new_out, a = lax.optimization_barrier((resident_out, new_out, state[2]))
    t, got, _, mirrored, pool, out_k, out_v = state
    left = jnp.maximum(last - PEEL, 0)
    crowd = max(min(2 * (d + 1), CAP * (dp - 1 - d)) for d in range(dp - 1))
    if -(-crowd * most // PER) + LAG * (dp - 2) > PEEL + ENDS[-1]:
        left, (t, got, a, mirrored, pool, out_k, out_v) = lax.while_loop(
            lambda state: state[0] > ENDS[-1],
            lambda state: (state[0] - TURN, advance(TURN, state[1])),
            (left, (jnp.asarray(t, i32), got, a, mirrored, pool, out_k, out_v)),
        )

    def end(count, state):
        _, pool, out_k, out_v = state
        now = [got, a, mirrored]
        for i in range(count + 1):
            arrived, message, passed = now
            coming = cross(message) if i < count else None
            message, pool, out_k, out_v = place(t + i, arrived, passed, pool, out_k, out_v, i + 1 < count)
            now = [coming, message, mirror(arrived)]
        out_k, out_v = finish(t + count + 1, now[2], out_k, out_v)
        return jnp.full((), -1, i32), pool, out_k, out_v

    state = (left, pool, out_k, out_v)
    for lower, count in zip((-1, *ENDS), ENDS):
        state = lax.while_loop(
            lambda state, lower=lower, count=count: (state[0] > lower) & (state[0] <= count),
            functools.partial(end, count), state,
        )
    _, _, out_k, out_v = state
    out_k, out_v = (out.reshape(CAP, half, width) for out in (out_k, out_v))
    return (resident_out[:, None, :], new_out, out_k, out_v)


def solution(mesh):
    placed = (
        P(("side", "dp"), None, "tp"),
        P(("side", "dp"), None, "tp"),
        P(),
        P(),
        P(None, None, "tp"),
        P(None, None, "tp"),
        P(None, None, "tp"),
        P("dp", "side", "tp"),
        P("dp", "side", "tp"),
        P("dp"),
        P(None, "dp", "tp"),
        P(None, "dp", "tp"),
        P(None, "dp", "tp"),
    )
    return jax.shard_map(
        body,
        mesh=mesh,
        in_specs=placed,
        out_specs=(
            P(None, "dp", "tp"),
            P(None, None, "tp"),
            P("dp", "side", "tp"),
            P("dp", "side", "tp"),
        ),
        check_vma=False,
    )
```

```python
import functools

import jax
import jax.numpy as jnp
from jax import lax
from jax.experimental import pallas as pl
from jax.experimental.pallas import tpu as pltpu
from jax.sharding import PartitionSpec as P

HEAD_WIDTH = 128
CAP = 4
UNIT = 128
PER = 6
MESSAGE = UNIT * PER
PEEL = 6
ENDS = (0, 1, 2, 3, 4, 5, 7, 9)
TURN = 3
POOL_ROWS = 22528
LAG = 2
LOW = -1e30

HBM = pl.BlockSpec(memory_space=pltpu.HBM)
VM = pl.BlockSpec(memory_space=pltpu.VMEM)
SM = pl.BlockSpec(memory_space=pltpu.SMEM)


def attend(q, q_rows, k_ref, v_ref, tk, tv, first, length, tokens_on, emit):
    steps = q.shape[0]
    keys, width = k_ref.shape
    heads_kv = width // HEAD_WIDTH
    members = q.shape[1] // width
    rows = members * steps
    scale = HEAD_WIDTH ** -0.5
    for kv in range(heads_kv):
        lanes = slice(kv * HEAD_WIDTH, (kv + 1) * HEAD_WIDTH)
        for g in range(members):
            at = (kv * members + g) * HEAD_WIDTH
            q_rows[g * steps:(g + 1) * steps, :] = q[:, at:at + HEAD_WIDTH]
        q32 = q_rows[...]
        scores = lax.dot_general(
            q32.astype(jnp.bfloat16), k_ref[:, lanes], (((1,), (1,)), ((), ())), preferred_element_type=jnp.float32
        ) * scale
        usable = first + lax.broadcasted_iota(jnp.int32, (rows, keys), 1) < length
        scores = jnp.where(usable, scores, LOW)
        row_step = lax.rem(lax.broadcasted_iota(jnp.int32, (rows, 1), 0), steps)
        top = jnp.max(scores, axis=1, keepdims=True)
        extra = []
        for n in range(steps):
            s = jnp.sum(q32 * tk[n:n + 1, lanes], axis=1, keepdims=True) * scale
            on = (row_step >= n) & tokens_on
            s = jnp.where(on, s, LOW)
            extra.append((on, s))
            top = jnp.maximum(top, s)
        weight = jnp.where(usable, jnp.exp(scores - top), 0.0)
        total = jnp.sum(weight, axis=1, keepdims=True)
        acc = lax.dot_general(
            weight.astype(jnp.bfloat16), v_ref[:, lanes], (((1,), (0,)), ((), ())), preferred_element_type=jnp.float32
        )
        for n, (on, s) in enumerate(extra):
            w = jnp.where(on, jnp.exp(s - top), 0.0)
            total = total + w
            acc = acc + w.astype(jnp.bfloat16).astype(jnp.float32) * tv[n:n + 1, lanes]
        emit(kv, top, total, acc)


def attention_kernel(
    dp, resident_length, lengths, rq, rk, rv, rtk, rtv, nq, nk, nv, ntk, ntv, part, own_out, q_rows
):
    side = lax.axis_index("side")
    owner = side * dp + lax.axis_index("dp")
    steps = rq.shape[0]
    keys, width = rk.shape
    rows = steps * rq.shape[1] // width
    f32 = jnp.float32

    def emit_part(kv, top, total, acc):
        at = slice(kv * rows, (kv + 1) * rows)
        part[at, 0:HEAD_WIDTH] = acc
        part[at, HEAD_WIDTH:2 * HEAD_WIDTH] = jnp.broadcast_to(top, (rows, HEAD_WIDTH))
        part[at, 2 * HEAD_WIDTH:] = jnp.broadcast_to(total, (rows, HEAD_WIDTH))

    attend(
        rq[...].astype(f32), q_rows, rk, rv, rtk[...].astype(f32), rtv[...].astype(f32),
        side * keys, resident_length[0], side == 1, emit_part,
    )

    def own(ref):
        picked = []
        for n in range(steps):
            block = ref[n].astype(f32)
            here = lax.broadcasted_iota(jnp.int32, block.shape, 0) == owner
            picked.append(jnp.sum(jnp.where(here, block, 0.0), axis=0, keepdims=True))
        return jnp.concatenate(picked, axis=0)

    def emit_out(kv, top, total, acc):
        own_out[kv * rows:(kv + 1) * rows, :] = acc / total

    attend(own(nq), q_rows, nk, nv, own(ntk), own(ntv), 0, lengths[owner], side >= 0, emit_out)


def finish_kernel(dp, steps, a, b, own, pair, *refs):
    *others, resident, new, o_rows = refs
    w = HEAD_WIDTH
    heads = resident.shape[1] // w
    top = jnp.maximum(a[:, w:2 * w], b[:, w:2 * w])
    ga = jnp.exp(a[:, w:2 * w] - top)
    gb = jnp.exp(b[:, w:2 * w] - top)
    o_rows[...] = (a[:, 0:w] * ga + b[:, 0:w] * gb) / (a[:, 2 * w:] * ga + b[:, 2 * w:] * gb)
    for h in range(heads):
        resident[:, h * w:(h + 1) * w] = o_rows[h * steps:(h + 1) * steps, :].astype(resident.dtype)
    side, me = lax.axis_index("side"), lax.axis_index("dp")
    count = 2 * dp
    blocks = [own, pair] + [other.at[y] for other in others for y in range(2)]
    places = [
        lax.bitwise_xor(side, y) * dp + lax.rem(me - x + dp, dp) for x in range(dp) for y in range(2)
    ]
    at_row = lax.broadcasted_iota(jnp.int32, (count, w), 0)
    for n in range(steps):
        for h in range(heads):
            k = h * steps + n
            block = jnp.zeros((count, w), jnp.float32)
            for place, source in zip(places, blocks):
                block = jnp.where(at_row == place, source[k:k + 1, :], block)
            new[n, :, h * w:(h + 1) * w] = block.astype(new.dtype)


def units_at(start):
    return pl.ds(pl.multiple_of(start, UNIT), UNIT)


def last_unit(length):
    return (length + UNIT - 1) // UNIT * UNIT - UNIT


def mask_unit(ref, first, length):
    row = lax.broadcasted_iota(jnp.int32, (UNIT, ref.shape[1]), 0)
    block = ref[units_at(first), :]
    ref[units_at(first), :] = jnp.where(first + row < length, block, jnp.zeros_like(block))


def plan_kernel(dp, half, ring_units, lengths, goal, pk, pv, table):
    side, me = lax.axis_index("side"), lax.axis_index("dp")
    f32 = jnp.float32
    full = 2 * half
    count = lengths.shape[0]
    wide = table.shape[1]
    id_row = lax.broadcasted_iota(jnp.int32, (count, count), 1).astype(f32)
    id_col = lax.broadcasted_iota(jnp.int32, (count, count), 0).astype(f32)
    eye = id_row == id_col

    def col(row):
        return jnp.sum(jnp.where(eye, jnp.broadcast_to(row, (count, count)), 0.0), axis=1, keepdims=True)

    def spread(scalars):
        row = jnp.zeros((1, count), jnp.int32)
        lane = lax.broadcasted_iota(jnp.int32, (1, count), 1)
        for r in range(count):
            row = jnp.where(lane == r, scalars[r], row)
        return row.astype(f32)

    ids = id_row[0:1]
    late = jnp.where(ids >= dp, 1.0, 0.0)
    src0 = ids - dp * late
    goal0 = spread(goal)
    side_f, me_f = side.astype(f32), me.astype(f32)
    units = jnp.floor((spread(lengths) + (UNIT - 1)) * (1.0 / UNIT))
    units_col, late_col, goal0_col, src0_col = col(units), col(late), col(goal0), col(src0)
    slot = jnp.sum(jnp.where((goal0_col == goal0) & (id_col < id_row), 1.0, 0.0), axis=0, keepdims=True)
    slot_col = col(slot)
    time = lax.broadcasted_iota(jnp.int32, (1, wide), 1).astype(f32)
    here_col = jnp.where(late_col == side_f, 0.0, 1.0)
    steps = jnp.zeros((1, 1), f32)
    sends, passes, ends = [], [], []
    for flip in (False, True):
        turned = (lambda x: dp - 1 - x) if flip else (lambda x: x)
        s, g, m, s_col, g_col = turned(src0), turned(goal0), turned(me_f), turned(src0_col), turned(goal0_col)
        crosses, bases, times = [], [], []
        for d in range(dp - 1):
            cross = (s <= d) & (g > d)
            cross_col = (s_col <= d) & (g_col > d)
            ready = jnp.zeros((1, count), f32)
            if d > 0:
                ready = jnp.where(s == d, 0.0, times[-1] + LAG * PER)
            ready_col = col(ready)
            ahead = (ready_col < ready) | (
                (ready_col == ready) & ((g_col > g) | ((g_col == g) & (id_col < id_row)))
            )
            base = jnp.sum(jnp.where(ahead & cross_col, units_col, 0.0), axis=0, keepdims=True)
            slack = jnp.where((ahead | eye) & cross_col, ready_col - col(base), 0.0)
            start = base + jnp.max(slack, axis=0, keepdims=True)
            end = jnp.max(jnp.where(cross, start + units, 0.0), axis=1, keepdims=True)
            steps = jnp.maximum(steps, jnp.floor((end + (PER - 1)) * (1.0 / PER)))
            crosses.append(cross)
            bases.append(base)
            times.append(start)

        def at(link):
            base, start, used = (jnp.zeros((1, count), f32) for _ in range(3))
            for d in range(dp - 1):
                base = jnp.where(link == d, bases[d], base)
                start = jnp.where(link == d, times[d], start)
                used = jnp.where(link == d, jnp.where(crosses[d], units, 0.0), used)
            return col(base), col(start), col(used)

        def ring_row(p):
            return (p - ring_units * jnp.floor((p + 0.5) * (1.0 / ring_units))) * UNIT

        def pick(hit, value):
            return jnp.sum(jnp.where(hit, value + 1.0, 0.0), axis=0, keepdims=True) - 1.0

        base, start, used = at(m)
        c = time - start
        hit = (c >= 0) & (c < used)
        own = here_col * full + c * UNIT
        sends.append(jnp.maximum(pick(hit, jnp.where(s_col == m, own, 2 * full + ring_row(base + c))), 0.0))
        _, start, used = at(m - 1)
        c = time - start
        hit = (c >= 0) & (c < used)
        passes.append(pick(hit & (g_col != m), 2 * full + ring_row(base + c)))
        row = c * UNIT - half * side_f
        ends.append(pick(hit & (g_col == m) & (row >= 0) & (row < half), slot_col * half + row))
    right = side_f == 0.0
    for r, row in enumerate((
        jnp.where(right, sends[0], sends[1]), jnp.where(right, passes[0], passes[1]),
        jnp.where(right, ends[0], ends[1]), jnp.where(right, ends[1], ends[0]),
    )):
        table[r:r + 1, :] = row.astype(jnp.int32)
    stay = jnp.where((src0 == me_f) & (goal0 == me_f), slot + 1.0, 0.0)
    home = [
        jnp.sum(jnp.where(late == which, stay, 0.0), axis=1, keepdims=True) - 1.0 for which in (side_f, 1.0 - side_f)
    ]
    last = jnp.where(time == 0, steps, jnp.where(time == 1, home[0], home[1]))
    table[4:5, :] = last.astype(jnp.int32)
    table[5:8, :] = jnp.zeros((3, wide), jnp.int32)


def first_kernel(dp, table, lengths, pk, pv, xk, xv, send):
    side, me = lax.axis_index("side"), lax.axis_index("dp")
    full = pk.shape[0]
    for j, pair in enumerate(((pk, pv), (xk, xv))):
        length = lengths[lax.bitwise_xor(side, j) * dp + me]
        last = last_unit(length)
        for i in range(PER):
            row = table[0, i] - j * full

            @pl.when((row >= 0) & (row < full))
            def _():
                for n in range(2):
                    send[n, i * UNIT:(i + 1) * UNIT, :] = pair[n][units_at(row), :]

            @pl.when(row == last)
            def _():
                for n in range(2):
                    mask_unit(send.at[n, i * UNIT:(i + 1) * UNIT], 0, length - last)


def pool_kernel(
    dp, table, lengths, pk, pv, xk, xv, pool, send, out_k, out_v, blank, stage, fill_sem, load_sem, pool_sem, home_sem
):
    side, me = lax.axis_index("side"), lax.axis_index("dp")
    full = xk.shape[0]
    half = full // 2
    loads = [
        pltpu.make_async_copy(a, stage.at[j, n], load_sem.at[j, n])
        for j, pair in enumerate(((pk, pv), (xk, xv))) for n, a in enumerate(pair)
    ]
    for copy in loads:
        copy.start()
    blank[...] = jnp.zeros_like(blank)
    fills = [
        pltpu.make_async_copy(blank, out.at[pl.ds(slot * half, half)], fill_sem.at[i, slot])
        for i, out in enumerate((out_k, out_v)) for slot in range(CAP)
    ]
    for fill in fills:
        fill.start()
    stores, homes = [], []
    for j in range(2):
        length = lengths[lax.bitwise_xor(side, j) * dp + me]
        last = last_unit(length)
        for n in range(2):
            loads[2 * j + n].wait()
            mask_unit(stage.at[j, n], last, length)
        store = pltpu.make_async_copy(stage.at[j], pool.at[:, pl.ds(j * full, full)], pool_sem.at[j])
        store.start()
        stores.append(store)
        slot = table[4, 1 + j]
        count = jnp.where(slot >= 0, jnp.clip((last + UNIT - side * half) // UNIT, 0, half // UNIT), 0)

        def home(u, wait, j=j, slot=slot):
            for n, out in enumerate((out_k, out_v)):
                copy = pltpu.make_async_copy(
                    stage.at[j, n, units_at(side * half + u * UNIT)], out.at[units_at(slot * half + u * UNIT)],
                    home_sem.at[j, n, u],
                )
                copy.wait() if wait else copy.start()

        homes.append((count, home))
    for fill in fills:
        fill.wait()
    for count, home in homes:
        pl.loop(0, count)(functools.partial(home, wait=False))
    for i in range(PER):
        code = table[0, PER + i]
        j = jnp.clip(code // full, 0, 1)
        row = jnp.clip(code - j * full, 0, full - UNIT)
        for n in range(2):
            send[n, i * UNIT:(i + 1) * UNIT, :] = stage[j, n, units_at(row), :]
    for count, home in homes:
        pl.loop(0, count)(functools.partial(home, wait=True))
    for store in stores:
        store.wait()


def end_copies(table, t, row, take, out_k, out_v, sem):
    copies = []
    for i in range(PER):
        code = table[row, t * PER + i]
        to = units_at(jnp.maximum(code, 0))
        copies.append((code >= 0, [
            pltpu.make_async_copy(take.at[n, pl.ds(i * UNIT, UNIT)], out.at[to], sem.at[i, n])
            for n, out in enumerate((out_k, out_v))
        ]))
    return copies


def when_all(copies, act):
    @pl.when(functools.reduce(jnp.logical_or, [on for on, _ in copies]))
    def _():
        for on, group in copies:
            @pl.when(on)
            def _():
                for copy in group:
                    act(copy)


def step_kernel(
    table, now, got, mirrored, pool_in, ok, ov, send, pool, out_k, out_v, pass_sem, got_sem, mirror_sem, send_sem
):
    t = now[0]
    passes = []
    for i in range(PER):
        code = table[1, t * PER + i]
        to = pool.at[:, units_at(jnp.maximum(code, 0))]
        passes.append((code >= 0, [pltpu.make_async_copy(got.at[:, pl.ds(i * UNIT, UNIT)], to, pass_sem.at[i])]))
    when_all(passes, lambda copy: copy.start())
    ends = [end_copies(table, t, 2, got, out_k, out_v, got_sem)]
    if mirrored is not None:
        ends.append(end_copies(table, t - 1, 3, mirrored, out_k, out_v, mirror_sem))
    for copies in ends:
        when_all(copies, lambda copy: copy.start())
    when_all(passes, lambda copy: copy.wait())
    if send is not None:
        lay = [
            pltpu.make_async_copy(
                pool.at[:, units_at(table[0, (t + LAG) * PER + i])], send.at[:, pl.ds(i * UNIT, UNIT)], send_sem.at[i]
            )
            for i in range(PER)
        ]
        for copy in lay:
            copy.start()
        for copy in lay:
            copy.wait()
    for copies in ends:
        when_all(copies, lambda copy: copy.wait())


def last_kernel(table, now, mirrored, ok, ov, out_k, out_v, sem):
    ends = end_copies(table, now[0] - 1, 3, mirrored, out_k, out_v, sem)
    when_all(ends, lambda copy: copy.start())
    when_all(ends, lambda copy: copy.wait())


def body(
    prompt_keys,
    prompt_values,
    prompt_lengths,
    assignment,
    new_queries,
    incoming_token_keys,
    incoming_token_values,
    stored_keys,
    stored_values,
    resident_lengths,
    resident_queries,
    stored_token_keys,
    stored_token_values,
):
    step_count = resident_queries.shape[0]
    dp = lax.axis_size("dp")
    request_count = prompt_lengths.shape[0]
    full, width = prompt_keys.shape[1:]
    query_width = new_queries.shape[2]
    half = full // 2
    bf16, f32, i32 = jnp.bfloat16, jnp.float32, jnp.int32
    swap = [(0, 1), (1, 0)]
    shape = jax.ShapeDtypeStruct
    dma = pltpu.SemaphoreType.DMA
    roomy = pltpu.CompilerParams(vmem_limit_bytes=44 << 20)

    pk, pv = prompt_keys[0], prompt_values[0]
    xk, xv = lax.ppermute(pk, "side", swap), lax.ppermute(pv, "side", swap)

    most = full // UNIT
    ring_units = 2 * most + (LAG + 1) * PER
    steps_max = -(-request_count * most // PER) + LAG * dp + PEEL + ENDS[-1] + LAG
    wide = -(-steps_max * PER // 128) * 128
    slots = shape((CAP * half, width), bf16)
    table = pl.pallas_call(
        functools.partial(plan_kernel, dp, half, ring_units),
        out_shape=shape((8, wide), i32),
        in_specs=[SM, SM, VM, VM],
        out_specs=VM,
        compiler_params=pltpu.CompilerParams(vmem_limit_bytes=58 << 20),
    )(prompt_lengths, jnp.reshape(assignment, (request_count,)), pk, pv)
    last = table[4, 0]

    message = shape((2, MESSAGE, width), bf16)
    pool_shape = shape((2, max(2 * full + ring_units * UNIT, POOL_ROWS), width), bf16)
    first = pl.pallas_call(
        functools.partial(first_kernel, dp),
        out_shape=message,
        in_specs=[SM, SM] + [VM] * 4,
        out_specs=VM,
        compiler_params=roomy,
    )(table, prompt_lengths, pk, pv, xk, xv)

    held = lax.optimization_barrier((new_queries, first))[0]
    rows = step_count * query_width // HEAD_WIDTH
    part, own_out = pl.pallas_call(
        functools.partial(attention_kernel, dp),
        out_shape=(shape((rows, 3 * HEAD_WIDTH), f32), shape((rows, HEAD_WIDTH), f32)),
        in_specs=[SM, SM] + [VM] * 10,
        out_specs=[VM, VM],
        scratch_shapes=[pltpu.VMEM((step_count * query_width // width, HEAD_WIDTH), f32)],
        compiler_params=roomy,
    )(
        resident_lengths, prompt_lengths,
        resident_queries[:, 0], stored_keys[0], stored_values[0], stored_token_keys[:, 0], stored_token_values[:, 0],
        held, pk, pv, incoming_token_keys, incoming_token_values,
    )

    tied = lax.optimization_barrier((table, first))
    pool, second, out_k, out_v = pl.pallas_call(
        functools.partial(pool_kernel, dp),
        out_shape=(pool_shape, message, slots, slots),
        in_specs=[SM, SM] + [VM] * 4,
        out_specs=[HBM, VM, HBM, HBM],
        scratch_shapes=[
            pltpu.VMEM((half, width), bf16), pltpu.VMEM((2, 2, full, width), bf16),
            dma((2, CAP)), dma((2, 2)), dma((2,)), dma((2, 2, half // UNIT)),
        ],
        compiler_params=roomy,
    )(tied[0], prompt_lengths, pk, pv, xk, xv)

    hops = [(i, i + 1) for i in range(dp - 1)] + [(dp + i + 1, dp + i) for i in range(dp - 1)]

    def cross(send):
        return lax.ppermute(send, ("side", "dp"), hops)

    def mirror(got):
        return lax.ppermute(got, "side", swap)

    def place(t, got, mirrored, pool, out_k, out_v, lay):
        news = [message] if lay else []
        first_kept = len(news)
        mirrors = [] if mirrored is None else [mirrored]

        def kernel(table, now, got, *refs):
            refs = list(refs)
            mirrored = refs.pop(0) if mirrors else None
            send = refs.pop(3) if lay else None
            step_kernel(table, now, got, mirrored, *refs[:3], send, *refs[3:])

        kept = 3 + len(mirrors)
        outs = pl.pallas_call(
            kernel,
            out_shape=(*news, pool_shape, slots, slots),
            in_specs=[SM, SM, VM] + [VM] * len(mirrors) + [HBM] * 3,
            out_specs=[VM] * len(news) + [HBM] * 3,
            scratch_shapes=[dma((PER,)), dma((PER, 2)), dma((PER, 2)), dma((PER,))],
            input_output_aliases={kept + i: first_kept + i for i in range(3)},
            compiler_params=roomy,
        )(table, jnp.full((1,), t, i32), got, *mirrors, pool, out_k, out_v)
        return outs if lay else (None, *outs)

    def finish(t, mirrored, out_k, out_v):
        return pl.pallas_call(
            last_kernel,
            out_shape=(slots, slots),
            in_specs=[SM, SM, VM, HBM, HBM],
            out_specs=[HBM, HBM],
            scratch_shapes=[dma((PER, 2))],
            input_output_aliases={3: 0, 4: 1},
            compiler_params=roomy,
        )(table, jnp.full((1,), t, i32), mirrored, out_k, out_v)

    def advance(count, state):
        t, got, a, mirrored, pool, out_k, out_v = state
        for i in range(count):
            coming = cross(a)
            a, pool, out_k, out_v = place(t + i, got, mirrored, pool, out_k, out_v, True)
            got, mirrored = coming, mirror(got)
        return t + count, got, a, mirrored, pool, out_k, out_v

    part_other = lax.ppermute(part, "side", swap)
    pair = lax.ppermute(own_out, "side", swap)
    second, part_other, pair = lax.optimization_barrier((second, part_other, pair))

    state = advance(PEEL - 1, (0, cross(first), second, None, pool, out_k, out_v))

    both, _ = lax.optimization_barrier((jnp.stack([own_out, pair]), state[2]))
    others = [lax.ppermute(both, "dp", [(z, (z + x) % dp) for z in range(dp)]) for x in range(1, dp)]
    resident_out, new_out = pl.pallas_call(
        functools.partial(finish_kernel, dp, step_count),
        out_shape=(shape((step_count, query_width), bf16), shape((step_count, request_count, query_width), bf16)),
        in_specs=[VM] * (3 + dp),
        out_specs=[VM, VM],
        scratch_shapes=[pltpu.VMEM((rows, HEAD_WIDTH), f32)],
    )(part, part_other, own_out, pair, *others)
    resident_out, new_out, a = lax.optimization_barrier((resident_out, new_out, state[2]))
    t, got, _, mirrored, pool, out_k, out_v = state
    left = jnp.maximum(last - PEEL, 0)
    crowd = max(min(2 * (d + 1), CAP * (dp - 1 - d)) for d in range(dp - 1))
    if -(-crowd * most // PER) + LAG * (dp - 2) > PEEL + ENDS[-1]:
        left, (t, got, a, mirrored, pool, out_k, out_v) = lax.while_loop(
            lambda state: state[0] > ENDS[-1],
            lambda state: (state[0] - TURN, advance(TURN, state[1])),
            (left, (jnp.asarray(t, i32), got, a, mirrored, pool, out_k, out_v)),
        )

    def end(count, state):
        _, pool, out_k, out_v = state
        now = [got, a, mirrored]
        for i in range(count + 1):
            arrived, message, passed = now
            coming = cross(message) if i < count else None
            message, pool, out_k, out_v = place(t + i, arrived, passed, pool, out_k, out_v, i + 1 < count)
            now = [coming, message, mirror(arrived)]
        out_k, out_v = finish(t + count + 1, now[2], out_k, out_v)
        return jnp.full((), -1, i32), pool, out_k, out_v

    state = (left, pool, out_k, out_v)
    for lower, count in zip((-1, *ENDS), ENDS):
        state = lax.while_loop(
            lambda state, lower=lower, count=count: (state[0] > lower) & (state[0] <= count),
            functools.partial(end, count), state,
        )
    _, _, out_k, out_v = state
    out_k, out_v = (out.reshape(CAP, half, width) for out in (out_k, out_v))
    return (resident_out[:, None, :], new_out, out_k, out_v)


def solution(mesh):
    placed = (
        P(("side", "dp"), None, "tp"),
        P(("side", "dp"), None, "tp"),
        P(),
        P(),
        P(None, None, "tp"),
        P(None, None, "tp"),
        P(None, None, "tp"),
        P("dp", "side", "tp"),
        P("dp", "side", "tp"),
        P("dp"),
        P(None, "dp", "tp"),
        P(None, "dp", "tp"),
        P(None, "dp", "tp"),
    )
    return jax.shard_map(
        body,
        mesh=mesh,
        in_specs=placed,
        out_specs=(
            P(None, "dp", "tp"),
            P(None, None, "tp"),
            P("dp", "side", "tp"),
            P("dp", "side", "tp"),
        ),
        check_vma=False,
    )
```

```python
import functools

import jax
import jax.numpy as jnp
from jax import lax
from jax.experimental import pallas as pl
from jax.experimental.pallas import tpu as pltpu
from jax.sharding import PartitionSpec as P

HEAD_WIDTH = 128
CAP = 4
UNIT = 128
PER = 6
MESSAGE = UNIT * PER
PEEL = 6
ENDS = (0, 1, 2, 3, 4, 5, 7, 9)
TURN = 3
POOL_ROWS = 22528
LAG = 2
LOW = -1e30

HBM = pl.BlockSpec(memory_space=pltpu.HBM)
VM = pl.BlockSpec(memory_space=pltpu.VMEM)
SM = pl.BlockSpec(memory_space=pltpu.SMEM)


def attend(q, q_rows, k_ref, v_ref, tk, tv, first, length, tokens_on, emit):
    steps = q.shape[0]
    keys, width = k_ref.shape
    heads_kv = width // HEAD_WIDTH
    members = q.shape[1] // width
    rows = members * steps
    scale = HEAD_WIDTH ** -0.5
    for kv in range(heads_kv):
        lanes = slice(kv * HEAD_WIDTH, (kv + 1) * HEAD_WIDTH)
        for g in range(members):
            at = (kv * members + g) * HEAD_WIDTH
            q_rows[g * steps:(g + 1) * steps, :] = q[:, at:at + HEAD_WIDTH]
        q32 = q_rows[...]
        scores = lax.dot_general(
            q32.astype(jnp.bfloat16), k_ref[:, lanes], (((1,), (1,)), ((), ())), preferred_element_type=jnp.float32
        ) * scale
        usable = first + lax.broadcasted_iota(jnp.int32, (rows, keys), 1) < length
        scores = jnp.where(usable, scores, LOW)
        row_step = lax.rem(lax.broadcasted_iota(jnp.int32, (rows, 1), 0), steps)
        top = jnp.max(scores, axis=1, keepdims=True)
        extra = []
        for n in range(steps):
            s = jnp.sum(q32 * tk[n:n + 1, lanes], axis=1, keepdims=True) * scale
            on = (row_step >= n) & tokens_on
            s = jnp.where(on, s, LOW)
            extra.append((on, s))
            top = jnp.maximum(top, s)
        weight = jnp.where(usable, jnp.exp(scores - top), 0.0)
        total = jnp.sum(weight, axis=1, keepdims=True)
        acc = lax.dot_general(
            weight.astype(jnp.bfloat16), v_ref[:, lanes], (((1,), (0,)), ((), ())), preferred_element_type=jnp.float32
        )
        for n, (on, s) in enumerate(extra):
            w = jnp.where(on, jnp.exp(s - top), 0.0)
            total = total + w
            acc = acc + w.astype(jnp.bfloat16).astype(jnp.float32) * tv[n:n + 1, lanes]
        emit(kv, top, total, acc)


def attention_kernel(
    dp, resident_length, lengths, rq, rk, rv, rtk, rtv, nq, nk, nv, ntk, ntv, part, own_out, q_rows
):
    side = lax.axis_index("side")
    owner = side * dp + lax.axis_index("dp")
    steps = rq.shape[0]
    keys, width = rk.shape
    rows = steps * rq.shape[1] // width
    f32 = jnp.float32

    def emit_part(kv, top, total, acc):
        at = slice(kv * rows, (kv + 1) * rows)
        part[at, 0:HEAD_WIDTH] = acc
        part[at, HEAD_WIDTH:2 * HEAD_WIDTH] = jnp.broadcast_to(top, (rows, HEAD_WIDTH))
        part[at, 2 * HEAD_WIDTH:] = jnp.broadcast_to(total, (rows, HEAD_WIDTH))

    attend(
        rq[...].astype(f32), q_rows, rk, rv, rtk[...].astype(f32), rtv[...].astype(f32),
        side * keys, resident_length[0], side == 1, emit_part,
    )

    def own(ref):
        picked = []
        for n in range(steps):
            block = ref[n].astype(f32)
            here = lax.broadcasted_iota(jnp.int32, block.shape, 0) == owner
            picked.append(jnp.sum(jnp.where(here, block, 0.0), axis=0, keepdims=True))
        return jnp.concatenate(picked, axis=0)

    def emit_out(kv, top, total, acc):
        own_out[kv * rows:(kv + 1) * rows, :] = acc / total

    attend(own(nq), q_rows, nk, nv, own(ntk), own(ntv), 0, lengths[owner], side >= 0, emit_out)


def finish_kernel(dp, steps, a, b, own, pair, *refs):
    *others, resident, new, o_rows = refs
    w = HEAD_WIDTH
    heads = resident.shape[1] // w
    top = jnp.maximum(a[:, w:2 * w], b[:, w:2 * w])
    ga = jnp.exp(a[:, w:2 * w] - top)
    gb = jnp.exp(b[:, w:2 * w] - top)
    o_rows[...] = (a[:, 0:w] * ga + b[:, 0:w] * gb) / (a[:, 2 * w:] * ga + b[:, 2 * w:] * gb)
    for h in range(heads):
        resident[:, h * w:(h + 1) * w] = o_rows[h * steps:(h + 1) * steps, :].astype(resident.dtype)
    side, me = lax.axis_index("side"), lax.axis_index("dp")
    count = 2 * dp
    blocks = [own, pair] + [other.at[y] for other in others for y in range(2)]
    places = [
        lax.bitwise_xor(side, y) * dp + lax.rem(me - x + dp, dp) for x in range(dp) for y in range(2)
    ]
    at_row = lax.broadcasted_iota(jnp.int32, (count, w), 0)
    for n in range(steps):
        for h in range(heads):
            k = h * steps + n
            block = jnp.zeros((count, w), jnp.float32)
            for place, source in zip(places, blocks):
                block = jnp.where(at_row == place, source[k:k + 1, :], block)
            new[n, :, h * w:(h + 1) * w] = block.astype(new.dtype)


def units_at(start):
    return pl.ds(pl.multiple_of(start, UNIT), UNIT)


def last_unit(length):
    return (length + UNIT - 1) // UNIT * UNIT - UNIT


def mask_unit(ref, first, length):
    row = lax.broadcasted_iota(jnp.int32, (UNIT, ref.shape[1]), 0)
    block = ref[units_at(first), :]
    ref[units_at(first), :] = jnp.where(first + row < length, block, jnp.zeros_like(block))


def plan_kernel(dp, half, ring_units, lengths, goal, pk, pv, table):
    side, me = lax.axis_index("side"), lax.axis_index("dp")
    f32 = jnp.float32
    full = 2 * half
    count = lengths.shape[0]
    wide = table.shape[1]
    id_row = lax.broadcasted_iota(jnp.int32, (count, count), 1).astype(f32)
    id_col = lax.broadcasted_iota(jnp.int32, (count, count), 0).astype(f32)
    eye = id_row == id_col

    def col(row):
        return jnp.sum(jnp.where(eye, jnp.broadcast_to(row, (count, count)), 0.0), axis=1, keepdims=True)

    def spread(scalars):
        row = jnp.zeros((1, count), jnp.int32)
        lane = lax.broadcasted_iota(jnp.int32, (1, count), 1)
        for r in range(count):
            row = jnp.where(lane == r, scalars[r], row)
        return row.astype(f32)

    ids = id_row[0:1]
    late = jnp.where(ids >= dp, 1.0, 0.0)
    src0 = ids - dp * late
    goal0 = spread(goal)
    side_f, me_f = side.astype(f32), me.astype(f32)
    units = jnp.floor((spread(lengths) + (UNIT - 1)) * (1.0 / UNIT))
    units_col, late_col, goal0_col, src0_col = col(units), col(late), col(goal0), col(src0)
    slot = jnp.sum(jnp.where((goal0_col == goal0) & (id_col < id_row), 1.0, 0.0), axis=0, keepdims=True)
    slot_col = col(slot)
    time = lax.broadcasted_iota(jnp.int32, (1, wide), 1).astype(f32)
    here_col = jnp.where(late_col == side_f, 0.0, 1.0)
    steps = jnp.zeros((1, 1), f32)
    sends, passes, ends = [], [], []
    for flip in (False, True):
        turned = (lambda x: dp - 1 - x) if flip else (lambda x: x)
        s, g, m, s_col, g_col = turned(src0), turned(goal0), turned(me_f), turned(src0_col), turned(goal0_col)
        crosses, bases, times = [], [], []
        for d in range(dp - 1):
            cross = (s <= d) & (g > d)
            cross_col = (s_col <= d) & (g_col > d)
            ready = jnp.zeros((1, count), f32)
            if d > 0:
                ready = jnp.where(s == d, 0.0, times[-1] + LAG * PER)
            ready_col = col(ready)
            ahead = (ready_col < ready) | (
                (ready_col == ready) & ((g_col > g) | ((g_col == g) & (id_col < id_row)))
            )
            base = jnp.sum(jnp.where(ahead & cross_col, units_col, 0.0), axis=0, keepdims=True)
            slack = jnp.where((ahead | eye) & cross_col, ready_col - col(base), 0.0)
            start = base + jnp.max(slack, axis=0, keepdims=True)
            end = jnp.max(jnp.where(cross, start + units, 0.0), axis=1, keepdims=True)
            steps = jnp.maximum(steps, jnp.floor((end + (PER - 1)) * (1.0 / PER)))
            crosses.append(cross)
            bases.append(base)
            times.append(start)

        def at(link):
            base, start, used = (jnp.zeros((1, count), f32) for _ in range(3))
            for d in range(dp - 1):
                base = jnp.where(link == d, bases[d], base)
                start = jnp.where(link == d, times[d], start)
                used = jnp.where(link == d, jnp.where(crosses[d], units, 0.0), used)
            return col(base), col(start), col(used)

        def ring_row(p):
            return (p - ring_units * jnp.floor((p + 0.5) * (1.0 / ring_units))) * UNIT

        def pick(hit, value):
            return jnp.sum(jnp.where(hit, value + 1.0, 0.0), axis=0, keepdims=True) - 1.0

        base, start, used = at(m)
        c = time - start
        hit = (c >= 0) & (c < used)
        own = here_col * full + c * UNIT
        sends.append(jnp.maximum(pick(hit, jnp.where(s_col == m, own, 2 * full + ring_row(base + c))), 0.0))
        _, start, used = at(m - 1)
        c = time - start
        hit = (c >= 0) & (c < used)
        passes.append(pick(hit & (g_col != m), 2 * full + ring_row(base + c)))
        row = c * UNIT - half * side_f
        ends.append(pick(hit & (g_col == m) & (row >= 0) & (row < half), slot_col * half + row))
    right = side_f == 0.0
    for r, row in enumerate((
        jnp.where(right, sends[0], sends[1]), jnp.where(right, passes[0], passes[1]),
        jnp.where(right, ends[0], ends[1]), jnp.where(right, ends[1], ends[0]),
    )):
        table[r:r + 1, :] = row.astype(jnp.int32)
    stay = jnp.where((src0 == me_f) & (goal0 == me_f), slot + 1.0, 0.0)
    home = [
        jnp.sum(jnp.where(late == which, stay, 0.0), axis=1, keepdims=True) - 1.0 for which in (side_f, 1.0 - side_f)
    ]
    last = jnp.where(time == 0, steps, jnp.where(time == 1, home[0], home[1]))
    table[4:5, :] = last.astype(jnp.int32)
    table[5:8, :] = jnp.zeros((3, wide), jnp.int32)


def first_kernel(dp, table, lengths, pk, pv, xk, xv, send):
    side, me = lax.axis_index("side"), lax.axis_index("dp")
    full = pk.shape[0]
    for j, pair in enumerate(((pk, pv), (xk, xv))):
        length = lengths[lax.bitwise_xor(side, j) * dp + me]
        last = last_unit(length)
        for i in range(PER):
            row = table[0, i] - j * full

            @pl.when((row >= 0) & (row < full))
            def _():
                for n in range(2):
                    send[n, i * UNIT:(i + 1) * UNIT, :] = pair[n][units_at(row), :]

            @pl.when(row == last)
            def _():
                for n in range(2):
                    mask_unit(send.at[n, i * UNIT:(i + 1) * UNIT], 0, length - last)


def pool_kernel(
    dp, table, lengths, pk, pv, xk, xv, pool, send, out_k, out_v, blank, stage, fill_sem, load_sem, pool_sem, home_sem
):
    side, me = lax.axis_index("side"), lax.axis_index("dp")
    full = xk.shape[0]
    half = full // 2
    loads = [
        pltpu.make_async_copy(a, stage.at[j, n], load_sem.at[j, n])
        for j, pair in enumerate(((pk, pv), (xk, xv))) for n, a in enumerate(pair)
    ]
    for copy in loads:
        copy.start()
    blank[...] = jnp.zeros_like(blank)
    fills = [
        pltpu.make_async_copy(blank, out.at[pl.ds(slot * half, half)], fill_sem.at[i, slot])
        for i, out in enumerate((out_k, out_v)) for slot in range(CAP)
    ]
    for fill in fills:
        fill.start()
    stores, homes = [], []
    for j in range(2):
        length = lengths[lax.bitwise_xor(side, j) * dp + me]
        last = last_unit(length)
        for n in range(2):
            loads[2 * j + n].wait()
            mask_unit(stage.at[j, n], last, length)
        store = pltpu.make_async_copy(stage.at[j], pool.at[:, pl.ds(j * full, full)], pool_sem.at[j])
        store.start()
        stores.append(store)
        slot = table[4, 1 + j]
        count = jnp.where(slot >= 0, jnp.clip((last + UNIT - side * half) // UNIT, 0, half // UNIT), 0)

        def home(u, wait, j=j, slot=slot):
            for n, out in enumerate((out_k, out_v)):
                copy = pltpu.make_async_copy(
                    stage.at[j, n, units_at(side * half + u * UNIT)], out.at[units_at(slot * half + u * UNIT)],
                    home_sem.at[j, n, u],
                )
                copy.wait() if wait else copy.start()

        homes.append((count, home))
    for fill in fills:
        fill.wait()
    for count, home in homes:
        pl.loop(0, count)(functools.partial(home, wait=False))
    for i in range(PER):
        code = table[0, PER + i]
        j = jnp.clip(code // full, 0, 1)
        row = jnp.clip(code - j * full, 0, full - UNIT)
        for n in range(2):
            send[n, i * UNIT:(i + 1) * UNIT, :] = stage[j, n, units_at(row), :]
    for count, home in homes:
        pl.loop(0, count)(functools.partial(home, wait=True))
    for store in stores:
        store.wait()


def end_copies(table, t, row, take, out_k, out_v, sem):
    copies = []
    for i in range(PER):
        code = table[row, t * PER + i]
        to = units_at(jnp.maximum(code, 0))
        copies.append((code >= 0, [
            pltpu.make_async_copy(take.at[n, pl.ds(i * UNIT, UNIT)], out.at[to], sem.at[i, n])
            for n, out in enumerate((out_k, out_v))
        ]))
    return copies


def when_all(copies, act):
    @pl.when(functools.reduce(jnp.logical_or, [on for on, _ in copies]))
    def _():
        for on, group in copies:
            @pl.when(on)
            def _():
                for copy in group:
                    act(copy)


def step_kernel(
    table, now, got, mirrored, pool_in, ok, ov, send, pool, out_k, out_v, pass_sem, got_sem, mirror_sem, send_sem
):
    t = now[0]
    passes = []
    for i in range(PER):
        code = table[1, t * PER + i]
        to = pool.at[:, units_at(jnp.maximum(code, 0))]
        passes.append((code >= 0, [pltpu.make_async_copy(got.at[:, pl.ds(i * UNIT, UNIT)], to, pass_sem.at[i])]))
    when_all(passes, lambda copy: copy.start())
    ends = [end_copies(table, t, 2, got, out_k, out_v, got_sem)]
    if mirrored is not None:
        ends.append(end_copies(table, t - 1, 3, mirrored, out_k, out_v, mirror_sem))
    for copies in ends:
        when_all(copies, lambda copy: copy.start())
    when_all(passes, lambda copy: copy.wait())
    if send is not None:
        lay = [
            pltpu.make_async_copy(
                pool.at[:, units_at(table[0, (t + LAG) * PER + i])], send.at[:, pl.ds(i * UNIT, UNIT)], send_sem.at[i]
            )
            for i in range(PER)
        ]
        for copy in lay:
            copy.start()
        for copy in lay:
            copy.wait()
    for copies in ends:
        when_all(copies, lambda copy: copy.wait())


def last_kernel(table, now, mirrored, ok, ov, out_k, out_v, sem):
    ends = end_copies(table, now[0] - 1, 3, mirrored, out_k, out_v, sem)
    when_all(ends, lambda copy: copy.start())
    when_all(ends, lambda copy: copy.wait())


def body(
    prompt_keys,
    prompt_values,
    prompt_lengths,
    assignment,
    new_queries,
    incoming_token_keys,
    incoming_token_values,
    stored_keys,
    stored_values,
    resident_lengths,
    resident_queries,
    stored_token_keys,
    stored_token_values,
):
    step_count = resident_queries.shape[0]
    dp = lax.axis_size("dp")
    request_count = prompt_lengths.shape[0]
    full, width = prompt_keys.shape[1:]
    query_width = new_queries.shape[2]
    half = full // 2
    bf16, f32, i32 = jnp.bfloat16, jnp.float32, jnp.int32
    swap = [(0, 1), (1, 0)]
    shape = jax.ShapeDtypeStruct
    dma = pltpu.SemaphoreType.DMA
    roomy = pltpu.CompilerParams(vmem_limit_bytes=44 << 20)

    pk, pv = prompt_keys[0], prompt_values[0]
    xk, xv = lax.ppermute(pk, "side", swap), lax.ppermute(pv, "side", swap)

    most = full // UNIT
    ring_units = 2 * most + (LAG + 1) * PER
    steps_max = -(-request_count * most // PER) + LAG * dp + PEEL + ENDS[-1] + LAG
    wide = -(-steps_max * PER // 128) * 128
    slots = shape((CAP * half, width), bf16)
    table = pl.pallas_call(
        functools.partial(plan_kernel, dp, half, ring_units),
        out_shape=shape((8, wide), i32),
        in_specs=[SM, SM, VM, VM],
        out_specs=VM,
        compiler_params=pltpu.CompilerParams(vmem_limit_bytes=58 << 20),
    )(prompt_lengths, jnp.reshape(assignment, (request_count,)), pk, pv)
    last = table[4, 0]

    message = shape((2, MESSAGE, width), bf16)
    pool_shape = shape((2, max(2 * full + ring_units * UNIT, POOL_ROWS), width), bf16)
    first = pl.pallas_call(
        functools.partial(first_kernel, dp),
        out_shape=message,
        in_specs=[SM, SM] + [VM] * 4,
        out_specs=VM,
        compiler_params=roomy,
    )(table, prompt_lengths, pk, pv, xk, xv)

    tied = lax.optimization_barrier((table, first))
    pool, second, out_k, out_v = pl.pallas_call(
        functools.partial(pool_kernel, dp),
        out_shape=(pool_shape, message, slots, slots),
        in_specs=[SM, SM] + [VM] * 4,
        out_specs=[HBM, VM, HBM, HBM],
        scratch_shapes=[
            pltpu.VMEM((half, width), bf16), pltpu.VMEM((2, 2, full, width), bf16),
            dma((2, CAP)), dma((2, 2)), dma((2,)), dma((2, 2, half // UNIT)),
        ],
        compiler_params=roomy,
    )(tied[0], prompt_lengths, pk, pv, xk, xv)

    held = lax.optimization_barrier((new_queries, second))[0]
    rows = step_count * query_width // HEAD_WIDTH
    part, own_out = pl.pallas_call(
        functools.partial(attention_kernel, dp),
        out_shape=(shape((rows, 3 * HEAD_WIDTH), f32), shape((rows, HEAD_WIDTH), f32)),
        in_specs=[SM, SM] + [VM] * 10,
        out_specs=[VM, VM],
        scratch_shapes=[pltpu.VMEM((step_count * query_width // width, HEAD_WIDTH), f32)],
        compiler_params=roomy,
    )(
        resident_lengths, prompt_lengths,
        resident_queries[:, 0], stored_keys[0], stored_values[0], stored_token_keys[:, 0], stored_token_values[:, 0],
        held, pk, pv, incoming_token_keys, incoming_token_values,
    )

    hops = [(i, i + 1) for i in range(dp - 1)] + [(dp + i + 1, dp + i) for i in range(dp - 1)]

    def cross(send):
        return lax.ppermute(send, ("side", "dp"), hops)

    def mirror(got):
        return lax.ppermute(got, "side", swap)

    def place(t, got, mirrored, pool, out_k, out_v, lay):
        news = [message] if lay else []
        first_kept = len(news)
        mirrors = [] if mirrored is None else [mirrored]

        def kernel(table, now, got, *refs):
            refs = list(refs)
            mirrored = refs.pop(0) if mirrors else None
            send = refs.pop(3) if lay else None
            step_kernel(table, now, got, mirrored, *refs[:3], send, *refs[3:])

        kept = 3 + len(mirrors)
        outs = pl.pallas_call(
            kernel,
            out_shape=(*news, pool_shape, slots, slots),
            in_specs=[SM, SM, VM] + [VM] * len(mirrors) + [HBM] * 3,
            out_specs=[VM] * len(news) + [HBM] * 3,
            scratch_shapes=[dma((PER,)), dma((PER, 2)), dma((PER, 2)), dma((PER,))],
            input_output_aliases={kept + i: first_kept + i for i in range(3)},
            compiler_params=roomy,
        )(table, jnp.full((1,), t, i32), got, *mirrors, pool, out_k, out_v)
        return outs if lay else (None, *outs)

    def finish(t, mirrored, out_k, out_v):
        return pl.pallas_call(
            last_kernel,
            out_shape=(slots, slots),
            in_specs=[SM, SM, VM, HBM, HBM],
            out_specs=[HBM, HBM],
            scratch_shapes=[dma((PER, 2))],
            input_output_aliases={3: 0, 4: 1},
            compiler_params=roomy,
        )(table, jnp.full((1,), t, i32), mirrored, out_k, out_v)

    def advance(count, state):
        t, got, a, mirrored, pool, out_k, out_v = state
        for i in range(count):
            coming = cross(a)
            a, pool, out_k, out_v = place(t + i, got, mirrored, pool, out_k, out_v, True)
            got, mirrored = coming, mirror(got)
        return t + count, got, a, mirrored, pool, out_k, out_v

    part_other = lax.ppermute(part, "side", swap)
    pair = lax.ppermute(own_out, "side", swap)
    got, part_other, pair = lax.optimization_barrier((cross(first), part_other, pair))
    state = advance(PEEL - 2, (0, got, second, None, pool, out_k, out_v))
    both, _ = lax.optimization_barrier((jnp.stack([own_out, pair]), state[2]))
    others = [lax.ppermute(both, "dp", [(z, (z + x) % dp) for z in range(dp)]) for x in range(1, dp)]
    state = advance(1, state)
    others, _ = lax.optimization_barrier((others, state[2]))
    resident_out, new_out = pl.pallas_call(
        functools.partial(finish_kernel, dp, step_count),
        out_shape=(shape((step_count, query_width), bf16), shape((step_count, request_count, query_width), bf16)),
        in_specs=[VM] * (3 + dp),
        out_specs=[VM, VM],
        scratch_shapes=[pltpu.VMEM((rows, HEAD_WIDTH), f32)],
        compiler_params=pltpu.CompilerParams(vmem_limit_bytes=8 << 20),
    )(part, part_other, own_out, pair, *others)
    resident_out, new_out, a = lax.optimization_barrier((resident_out, new_out, state[2]))
    t, got, _, mirrored, pool, out_k, out_v = state
    left = jnp.maximum(last - PEEL, 0)
    crowd = max(min(2 * (d + 1), CAP * (dp - 1 - d)) for d in range(dp - 1))
    if -(-crowd * most // PER) + LAG * (dp - 2) > PEEL + ENDS[-1]:
        left, (t, got, a, mirrored, pool, out_k, out_v) = lax.while_loop(
            lambda state: state[0] > ENDS[-1],
            lambda state: (state[0] - TURN, advance(TURN, state[1])),
            (left, (jnp.asarray(t, i32), got, a, mirrored, pool, out_k, out_v)),
        )

    def end(count, state):
        _, pool, out_k, out_v = state
        now = [got, a, mirrored]
        for i in range(count + 1):
            arrived, message, passed = now
            coming = cross(message) if i < count else None
            message, pool, out_k, out_v = place(t + i, arrived, passed, pool, out_k, out_v, i + 1 < count)
            now = [coming, message, mirror(arrived)]
        out_k, out_v = finish(t + count + 1, now[2], out_k, out_v)
        return jnp.full((), -1, i32), pool, out_k, out_v

    state = (left, pool, out_k, out_v)
    for lower, count in zip((-1, *ENDS), ENDS):
        state = lax.while_loop(
            lambda state, lower=lower, count=count: (state[0] > lower) & (state[0] <= count),
            functools.partial(end, count), state,
        )
    _, _, out_k, out_v = state
    out_k, out_v = (out.reshape(CAP, half, width) for out in (out_k, out_v))
    return (resident_out[:, None, :], new_out, out_k, out_v)


def solution(mesh):
    placed = (
        P(("side", "dp"), None, "tp"),
        P(("side", "dp"), None, "tp"),
        P(),
        P(),
        P(None, None, "tp"),
        P(None, None, "tp"),
        P(None, None, "tp"),
        P("dp", "side", "tp"),
        P("dp", "side", "tp"),
        P("dp"),
        P(None, "dp", "tp"),
        P(None, "dp", "tp"),
        P(None, "dp", "tp"),
    )
    return jax.shard_map(
        body,
        mesh=mesh,
        in_specs=placed,
        out_specs=(
            P(None, "dp", "tp"),
            P(None, None, "tp"),
            P("dp", "side", "tp"),
            P("dp", "side", "tp"),
        ),
        check_vma=False,
    )
```

```python
import functools

import jax
import jax.numpy as jnp
from jax import lax
from jax.experimental import pallas as pl
from jax.experimental.pallas import tpu as pltpu
from jax.sharding import PartitionSpec as P

HEAD_WIDTH = 128
CAP = 4
UNIT = 128
PER = 6
MESSAGE = UNIT * PER
PEEL = 6
ENDS = (0, 1, 2, 3, 4, 5, 7, 9)
TURN = 3
POOL_ROWS = 22528
LAG = 2
LOW = -1e30

HBM = pl.BlockSpec(memory_space=pltpu.HBM)
VM = pl.BlockSpec(memory_space=pltpu.VMEM)
SM = pl.BlockSpec(memory_space=pltpu.SMEM)


def attend(q, q_rows, k_ref, v_ref, tk, tv, first, length, tokens_on, emit):
    steps = q.shape[0]
    keys, width = k_ref.shape
    heads_kv = width // HEAD_WIDTH
    members = q.shape[1] // width
    rows = members * steps
    scale = HEAD_WIDTH ** -0.5
    for kv in range(heads_kv):
        lanes = slice(kv * HEAD_WIDTH, (kv + 1) * HEAD_WIDTH)
        for g in range(members):
            at = (kv * members + g) * HEAD_WIDTH
            q_rows[g * steps:(g + 1) * steps, :] = q[:, at:at + HEAD_WIDTH]
        q32 = q_rows[...]
        scores = lax.dot_general(
            q32.astype(jnp.bfloat16), k_ref[:, lanes], (((1,), (1,)), ((), ())), preferred_element_type=jnp.float32
        ) * scale
        usable = first + lax.broadcasted_iota(jnp.int32, (rows, keys), 1) < length
        scores = jnp.where(usable, scores, LOW)
        row_step = lax.rem(lax.broadcasted_iota(jnp.int32, (rows, 1), 0), steps)
        top = jnp.max(scores, axis=1, keepdims=True)
        extra = []
        for n in range(steps):
            s = jnp.sum(q32 * tk[n:n + 1, lanes], axis=1, keepdims=True) * scale
            on = (row_step >= n) & tokens_on
            s = jnp.where(on, s, LOW)
            extra.append((on, s))
            top = jnp.maximum(top, s)
        weight = jnp.where(usable, jnp.exp(scores - top), 0.0)
        total = jnp.sum(weight, axis=1, keepdims=True)
        acc = lax.dot_general(
            weight.astype(jnp.bfloat16), v_ref[:, lanes], (((1,), (0,)), ((), ())), preferred_element_type=jnp.float32
        )
        for n, (on, s) in enumerate(extra):
            w = jnp.where(on, jnp.exp(s - top), 0.0)
            total = total + w
            acc = acc + w.astype(jnp.bfloat16).astype(jnp.float32) * tv[n:n + 1, lanes]
        emit(kv, top, total, acc)


def attention_kernel(
    dp, resident_length, lengths, rq, rk, rv, rtk, rtv, nq, nk, nv, ntk, ntv, part, own_out, q_rows
):
    side = lax.axis_index("side")
    owner = side * dp + lax.axis_index("dp")
    steps = rq.shape[0]
    keys, width = rk.shape
    rows = steps * rq.shape[1] // width
    f32 = jnp.float32

    def emit_part(kv, top, total, acc):
        at = slice(kv * rows, (kv + 1) * rows)
        part[at, 0:HEAD_WIDTH] = acc
        part[at, HEAD_WIDTH:2 * HEAD_WIDTH] = jnp.broadcast_to(top, (rows, HEAD_WIDTH))
        part[at, 2 * HEAD_WIDTH:] = jnp.broadcast_to(total, (rows, HEAD_WIDTH))

    attend(
        rq[...].astype(f32), q_rows, rk, rv, rtk[...].astype(f32), rtv[...].astype(f32),
        side * keys, resident_length[0], side == 1, emit_part,
    )

    def own(ref):
        picked = []
        for n in range(steps):
            block = ref[n].astype(f32)
            here = lax.broadcasted_iota(jnp.int32, block.shape, 0) == owner
            picked.append(jnp.sum(jnp.where(here, block, 0.0), axis=0, keepdims=True))
        return jnp.concatenate(picked, axis=0)

    def emit_out(kv, top, total, acc):
        own_out[kv * rows:(kv + 1) * rows, :] = acc / total

    attend(own(nq), q_rows, nk, nv, own(ntk), own(ntv), 0, lengths[owner], side >= 0, emit_out)


def finish_kernel(dp, steps, a, b, own, pair, *refs):
    *others, resident, new, o_rows = refs
    w = HEAD_WIDTH
    heads = resident.shape[1] // w
    top = jnp.maximum(a[:, w:2 * w], b[:, w:2 * w])
    ga = jnp.exp(a[:, w:2 * w] - top)
    gb = jnp.exp(b[:, w:2 * w] - top)
    o_rows[...] = (a[:, 0:w] * ga + b[:, 0:w] * gb) / (a[:, 2 * w:] * ga + b[:, 2 * w:] * gb)
    for h in range(heads):
        resident[:, h * w:(h + 1) * w] = o_rows[h * steps:(h + 1) * steps, :].astype(resident.dtype)
    side, me = lax.axis_index("side"), lax.axis_index("dp")
    count = 2 * dp
    blocks = [own, pair] + [other.at[y] for other in others for y in range(2)]
    places = [
        lax.bitwise_xor(side, y) * dp + lax.rem(me - x + dp, dp) for x in range(dp) for y in range(2)
    ]
    at_row = lax.broadcasted_iota(jnp.int32, (count, w), 0)
    for n in range(steps):
        for h in range(heads):
            k = h * steps + n
            block = jnp.zeros((count, w), jnp.float32)
            for place, source in zip(places, blocks):
                block = jnp.where(at_row == place, source[k:k + 1, :], block)
            new[n, :, h * w:(h + 1) * w] = block.astype(new.dtype)


def units_at(start):
    return pl.ds(pl.multiple_of(start, UNIT), UNIT)


def last_unit(length):
    return (length + UNIT - 1) // UNIT * UNIT - UNIT


def mask_unit(ref, first, length):
    row = lax.broadcasted_iota(jnp.int32, (UNIT, ref.shape[1]), 0)
    block = ref[units_at(first), :]
    ref[units_at(first), :] = jnp.where(first + row < length, block, jnp.zeros_like(block))


def plan_kernel(dp, half, ring_units, lengths, goal, pk, pv, table):
    side, me = lax.axis_index("side"), lax.axis_index("dp")
    f32 = jnp.float32
    full = 2 * half
    count = lengths.shape[0]
    wide = table.shape[1]
    id_row = lax.broadcasted_iota(jnp.int32, (count, count), 1).astype(f32)
    id_col = lax.broadcasted_iota(jnp.int32, (count, count), 0).astype(f32)
    eye = id_row == id_col

    def col(row):
        return jnp.sum(jnp.where(eye, jnp.broadcast_to(row, (count, count)), 0.0), axis=1, keepdims=True)

    def spread(scalars):
        row = jnp.zeros((1, count), jnp.int32)
        lane = lax.broadcasted_iota(jnp.int32, (1, count), 1)
        for r in range(count):
            row = jnp.where(lane == r, scalars[r], row)
        return row.astype(f32)

    ids = id_row[0:1]
    late = jnp.where(ids >= dp, 1.0, 0.0)
    src0 = ids - dp * late
    goal0 = spread(goal)
    side_f, me_f = side.astype(f32), me.astype(f32)
    units = jnp.floor((spread(lengths) + (UNIT - 1)) * (1.0 / UNIT))
    units_col, late_col, goal0_col, src0_col = col(units), col(late), col(goal0), col(src0)
    slot = jnp.sum(jnp.where((goal0_col == goal0) & (id_col < id_row), 1.0, 0.0), axis=0, keepdims=True)
    slot_col = col(slot)
    time = lax.broadcasted_iota(jnp.int32, (1, wide), 1).astype(f32)
    here_col = jnp.where(late_col == side_f, 0.0, 1.0)
    steps = jnp.zeros((1, 1), f32)
    sends, passes, ends = [], [], []
    for flip in (False, True):
        turned = (lambda x: dp - 1 - x) if flip else (lambda x: x)
        s, g, m, s_col, g_col = turned(src0), turned(goal0), turned(me_f), turned(src0_col), turned(goal0_col)
        crosses, bases, times = [], [], []
        for d in range(dp - 1):
            cross = (s <= d) & (g > d)
            cross_col = (s_col <= d) & (g_col > d)
            ready = jnp.zeros((1, count), f32)
            if d > 0:
                ready = jnp.where(s == d, 0.0, times[-1] + LAG * PER)
            ready_col = col(ready)
            ahead = (ready_col < ready) | (
                (ready_col == ready) & ((g_col > g) | ((g_col == g) & (id_col < id_row)))
            )
            base = jnp.sum(jnp.where(ahead & cross_col, units_col, 0.0), axis=0, keepdims=True)
            slack = jnp.where((ahead | eye) & cross_col, ready_col - col(base), 0.0)
            start = base + jnp.max(slack, axis=0, keepdims=True)
            end = jnp.max(jnp.where(cross, start + units, 0.0), axis=1, keepdims=True)
            steps = jnp.maximum(steps, jnp.floor((end + (PER - 1)) * (1.0 / PER)))
            crosses.append(cross)
            bases.append(base)
            times.append(start)

        def at(link):
            base, start, used = (jnp.zeros((1, count), f32) for _ in range(3))
            for d in range(dp - 1):
                base = jnp.where(link == d, bases[d], base)
                start = jnp.where(link == d, times[d], start)
                used = jnp.where(link == d, jnp.where(crosses[d], units, 0.0), used)
            return col(base), col(start), col(used)

        def ring_row(p):
            return (p - ring_units * jnp.floor((p + 0.5) * (1.0 / ring_units))) * UNIT

        def pick(hit, value):
            return jnp.sum(jnp.where(hit, value + 1.0, 0.0), axis=0, keepdims=True) - 1.0

        base, start, used = at(m)
        c = time - start
        hit = (c >= 0) & (c < used)
        own = here_col * full + c * UNIT
        sends.append(jnp.maximum(pick(hit, jnp.where(s_col == m, own, 2 * full + ring_row(base + c))), 0.0))
        _, start, used = at(m - 1)
        c = time - start
        hit = (c >= 0) & (c < used)
        passes.append(pick(hit & (g_col != m), 2 * full + ring_row(base + c)))
        row = c * UNIT - half * side_f
        ends.append(pick(hit & (g_col == m) & (row >= 0) & (row < half), slot_col * half + row))
    right = side_f == 0.0
    for r, row in enumerate((
        jnp.where(right, sends[0], sends[1]), jnp.where(right, passes[0], passes[1]),
        jnp.where(right, ends[0], ends[1]), jnp.where(right, ends[1], ends[0]),
    )):
        table[r:r + 1, :] = row.astype(jnp.int32)
    stay = jnp.where((src0 == me_f) & (goal0 == me_f), slot + 1.0, 0.0)
    home = [
        jnp.sum(jnp.where(late == which, stay, 0.0), axis=1, keepdims=True) - 1.0 for which in (side_f, 1.0 - side_f)
    ]
    last = jnp.where(time == 0, steps, jnp.where(time == 1, home[0], home[1]))
    table[4:5, :] = last.astype(jnp.int32)
    table[5:8, :] = jnp.zeros((3, wide), jnp.int32)


def first_kernel(dp, table, lengths, pk, pv, xk, xv, send):
    side, me = lax.axis_index("side"), lax.axis_index("dp")
    full = pk.shape[0]
    for j, pair in enumerate(((pk, pv), (xk, xv))):
        length = lengths[lax.bitwise_xor(side, j) * dp + me]
        last = last_unit(length)
        for i in range(PER):
            row = table[0, i] - j * full

            @pl.when((row >= 0) & (row < full))
            def _():
                for n in range(2):
                    send[n, i * UNIT:(i + 1) * UNIT, :] = pair[n][units_at(row), :]

            @pl.when(row == last)
            def _():
                for n in range(2):
                    mask_unit(send.at[n, i * UNIT:(i + 1) * UNIT], 0, length - last)


def pool_kernel(
    dp, table, lengths, pk, pv, xk, xv, pool, send, out_k, out_v, blank, stage, fill_sem, load_sem, pool_sem, home_sem
):
    side, me = lax.axis_index("side"), lax.axis_index("dp")
    full = xk.shape[0]
    half = full // 2
    loads = [
        pltpu.make_async_copy(a, stage.at[j, n], load_sem.at[j, n])
        for j, pair in enumerate(((pk, pv), (xk, xv))) for n, a in enumerate(pair)
    ]
    for copy in loads:
        copy.start()
    blank[...] = jnp.zeros_like(blank)
    fills = [
        pltpu.make_async_copy(blank, out.at[pl.ds(slot * half, half)], fill_sem.at[i, slot])
        for i, out in enumerate((out_k, out_v)) for slot in range(CAP)
    ]
    for fill in fills:
        fill.start()
    stores, homes = [], []
    for j in range(2):
        length = lengths[lax.bitwise_xor(side, j) * dp + me]
        last = last_unit(length)
        for n in range(2):
            loads[2 * j + n].wait()
            mask_unit(stage.at[j, n], last, length)
        store = pltpu.make_async_copy(stage.at[j], pool.at[:, pl.ds(j * full, full)], pool_sem.at[j])
        store.start()
        stores.append(store)
        slot = table[4, 1 + j]
        count = jnp.where(slot >= 0, jnp.clip((last + UNIT - side * half) // UNIT, 0, half // UNIT), 0)

        def home(u, wait, j=j, slot=slot):
            for n, out in enumerate((out_k, out_v)):
                copy = pltpu.make_async_copy(
                    stage.at[j, n, units_at(side * half + u * UNIT)], out.at[units_at(slot * half + u * UNIT)],
                    home_sem.at[j, n, u],
                )
                copy.wait() if wait else copy.start()

        homes.append((count, home))
    for fill in fills:
        fill.wait()
    for count, home in homes:
        pl.loop(0, count)(functools.partial(home, wait=False))
    for i in range(PER):
        code = table[0, PER + i]
        j = jnp.clip(code // full, 0, 1)
        row = jnp.clip(code - j * full, 0, full - UNIT)
        for n in range(2):
            send[n, i * UNIT:(i + 1) * UNIT, :] = stage[j, n, units_at(row), :]
    for count, home in homes:
        pl.loop(0, count)(functools.partial(home, wait=True))
    for store in stores:
        store.wait()


def end_copies(table, t, row, take, out_k, out_v, sem):
    copies = []
    for i in range(PER):
        code = table[row, t * PER + i]
        to = units_at(jnp.maximum(code, 0))
        copies.append((code >= 0, [
            pltpu.make_async_copy(take.at[n, pl.ds(i * UNIT, UNIT)], out.at[to], sem.at[i, n])
            for n, out in enumerate((out_k, out_v))
        ]))
    return copies


def when_all(copies, act):
    @pl.when(functools.reduce(jnp.logical_or, [on for on, _ in copies]))
    def _():
        for on, group in copies:
            @pl.when(on)
            def _():
                for copy in group:
                    act(copy)


def step_kernel(
    table, now, got, mirrored, pool_in, ok, ov, send, pool, out_k, out_v, pass_sem, got_sem, mirror_sem, send_sem
):
    t = now[0]
    passes = []
    for i in range(PER):
        code = table[1, t * PER + i]
        to = pool.at[:, units_at(jnp.maximum(code, 0))]
        passes.append((code >= 0, [pltpu.make_async_copy(got.at[:, pl.ds(i * UNIT, UNIT)], to, pass_sem.at[i])]))
    when_all(passes, lambda copy: copy.start())
    ends = [end_copies(table, t, 2, got, out_k, out_v, got_sem)]
    if mirrored is not None:
        ends.append(end_copies(table, t - 1, 3, mirrored, out_k, out_v, mirror_sem))
    for copies in ends:
        when_all(copies, lambda copy: copy.start())
    when_all(passes, lambda copy: copy.wait())
    if send is not None:
        lay = [
            pltpu.make_async_copy(
                pool.at[:, units_at(table[0, (t + LAG) * PER + i])], send.at[:, pl.ds(i * UNIT, UNIT)], send_sem.at[i]
            )
            for i in range(PER)
        ]
        for copy in lay:
            copy.start()
        for copy in lay:
            copy.wait()
    for copies in ends:
        when_all(copies, lambda copy: copy.wait())


def last_kernel(table, now, mirrored, ok, ov, out_k, out_v, sem):
    ends = end_copies(table, now[0] - 1, 3, mirrored, out_k, out_v, sem)
    when_all(ends, lambda copy: copy.start())
    when_all(ends, lambda copy: copy.wait())


def body(
    prompt_keys,
    prompt_values,
    prompt_lengths,
    assignment,
    new_queries,
    incoming_token_keys,
    incoming_token_values,
    stored_keys,
    stored_values,
    resident_lengths,
    resident_queries,
    stored_token_keys,
    stored_token_values,
):
    step_count = resident_queries.shape[0]
    dp = lax.axis_size("dp")
    request_count = prompt_lengths.shape[0]
    full, width = prompt_keys.shape[1:]
    query_width = new_queries.shape[2]
    half = full // 2
    bf16, f32, i32 = jnp.bfloat16, jnp.float32, jnp.int32
    swap = [(0, 1), (1, 0)]
    shape = jax.ShapeDtypeStruct
    dma = pltpu.SemaphoreType.DMA
    roomy = pltpu.CompilerParams(vmem_limit_bytes=44 << 20)

    pk, pv = prompt_keys[0], prompt_values[0]
    xk, xv = lax.ppermute(pk, "side", swap), lax.ppermute(pv, "side", swap)

    most = full // UNIT
    ring_units = 2 * most + (LAG + 1) * PER
    steps_max = -(-request_count * most // PER) + LAG * dp + PEEL + ENDS[-1] + LAG
    wide = -(-steps_max * PER // 128) * 128
    slots = shape((CAP * half, width), bf16)
    table = pl.pallas_call(
        functools.partial(plan_kernel, dp, half, ring_units),
        out_shape=shape((8, wide), i32),
        in_specs=[SM, SM, VM, VM],
        out_specs=VM,
        compiler_params=pltpu.CompilerParams(vmem_limit_bytes=58 << 20),
    )(prompt_lengths, jnp.reshape(assignment, (request_count,)), pk, pv)
    last = table[4, 0]

    message = shape((2, MESSAGE, width), bf16)
    pool_shape = shape((2, max(2 * full + ring_units * UNIT, POOL_ROWS), width), bf16)
    first = pl.pallas_call(
        functools.partial(first_kernel, dp),
        out_shape=message,
        in_specs=[SM, SM] + [VM] * 4,
        out_specs=VM,
        compiler_params=roomy,
    )(table, prompt_lengths, pk, pv, xk, xv)

    tied = lax.optimization_barrier((table, first))
    pool, second, out_k, out_v = pl.pallas_call(
        functools.partial(pool_kernel, dp),
        out_shape=(pool_shape, message, slots, slots),
        in_specs=[SM, SM] + [VM] * 4,
        out_specs=[HBM, VM, HBM, HBM],
        scratch_shapes=[
            pltpu.VMEM((half, width), bf16), pltpu.VMEM((2, 2, full, width), bf16),
            dma((2, CAP)), dma((2, 2)), dma((2,)), dma((2, 2, half // UNIT)),
        ],
        compiler_params=roomy,
    )(tied[0], prompt_lengths, pk, pv, xk, xv)

    held = lax.optimization_barrier((new_queries, second))[0]
    rows = step_count * query_width // HEAD_WIDTH
    part, own_out = pl.pallas_call(
        functools.partial(attention_kernel, dp),
        out_shape=(shape((rows, 3 * HEAD_WIDTH), f32), shape((rows, HEAD_WIDTH), f32)),
        in_specs=[SM, SM] + [VM] * 10,
        out_specs=[VM, VM],
        scratch_shapes=[pltpu.VMEM((step_count * query_width // width, HEAD_WIDTH), f32)],
        compiler_params=roomy,
    )(
        resident_lengths, prompt_lengths,
        resident_queries[:, 0], stored_keys[0], stored_values[0], stored_token_keys[:, 0], stored_token_values[:, 0],
        held, pk, pv, incoming_token_keys, incoming_token_values,
    )

    hops = [(i, i + 1) for i in range(dp - 1)] + [(dp + i + 1, dp + i) for i in range(dp - 1)]

    def cross(send):
        return lax.ppermute(send, ("side", "dp"), hops)

    def mirror(got):
        return lax.ppermute(got, "side", swap)

    def place(t, got, mirrored, pool, out_k, out_v, lay):
        news = [message] if lay else []
        first_kept = len(news)
        mirrors = [] if mirrored is None else [mirrored]

        def kernel(table, now, got, *refs):
            refs = list(refs)
            mirrored = refs.pop(0) if mirrors else None
            send = refs.pop(3) if lay else None
            step_kernel(table, now, got, mirrored, *refs[:3], send, *refs[3:])

        kept = 3 + len(mirrors)
        outs = pl.pallas_call(
            kernel,
            out_shape=(*news, pool_shape, slots, slots),
            in_specs=[SM, SM, VM] + [VM] * len(mirrors) + [HBM] * 3,
            out_specs=[VM] * len(news) + [HBM] * 3,
            scratch_shapes=[dma((PER,)), dma((PER, 2)), dma((PER, 2)), dma((PER,))],
            input_output_aliases={kept + i: first_kept + i for i in range(3)},
            compiler_params=roomy,
        )(table, jnp.full((1,), t, i32), got, *mirrors, pool, out_k, out_v)
        return outs if lay else (None, *outs)

    def finish(t, mirrored, out_k, out_v):
        return pl.pallas_call(
            last_kernel,
            out_shape=(slots, slots),
            in_specs=[SM, SM, VM, HBM, HBM],
            out_specs=[HBM, HBM],
            scratch_shapes=[dma((PER, 2))],
            input_output_aliases={3: 0, 4: 1},
            compiler_params=roomy,
        )(table, jnp.full((1,), t, i32), mirrored, out_k, out_v)

    def advance(count, state):
        t, got, a, mirrored, pool, out_k, out_v = state
        for i in range(count):
            coming = cross(a)
            a, pool, out_k, out_v = place(t + i, got, mirrored, pool, out_k, out_v, True)
            got, mirrored = coming, mirror(got)
        return t + count, got, a, mirrored, pool, out_k, out_v

    part_other = lax.ppermute(part, "side", swap)
    pair = lax.ppermute(own_out, "side", swap)
    got, part_other, pair = lax.optimization_barrier((cross(first), part_other, pair))
    state = advance(PEEL - 2, (0, got, second, None, pool, out_k, out_v))
    both, _ = lax.optimization_barrier((jnp.stack([own_out, pair]), state[2]))
    others = [lax.ppermute(both, "dp", [(z, (z + x) % dp) for z in range(dp)]) for x in range(1, dp)]
    state = advance(1, state)
    others, _ = lax.optimization_barrier((others, state[2]))

    def lay_out():
        return pl.pallas_call(
            functools.partial(finish_kernel, dp, step_count),
            out_shape=(shape((step_count, query_width), bf16), shape((step_count, request_count, query_width), bf16)),
            in_specs=[VM] * (3 + dp),
            out_specs=[VM, VM],
            scratch_shapes=[pltpu.VMEM((rows, HEAD_WIDTH), f32)],
            compiler_params=pltpu.CompilerParams(vmem_limit_bytes=8 << 20),
        )(part, part_other, own_out, pair, *others)

    a = state[2]
    t, got, _, mirrored, pool, out_k, out_v = state
    left = jnp.maximum(last - PEEL, 0)
    crowd = max(min(2 * (d + 1), CAP * (dp - 1 - d)) for d in range(dp - 1))
    if -(-crowd * most // PER) + LAG * (dp - 2) > PEEL + ENDS[-1]:
        left, (t, got, a, mirrored, pool, out_k, out_v) = lax.while_loop(
            lambda state: state[0] > ENDS[-1],
            lambda state: (state[0] - TURN, advance(TURN, state[1])),
            (left, (jnp.asarray(t, i32), got, a, mirrored, pool, out_k, out_v)),
        )

    def end(count, state):
        _, pool, out_k, out_v, _, _ = state
        now = [got, a, mirrored]
        resident_out, new_out = lay_out()
        for i in range(count + 1):
            arrived, message, passed = now
            coming = cross(message) if i < count else None
            message, pool, out_k, out_v = place(t + i, arrived, passed, pool, out_k, out_v, i + 1 < count)
            now = [coming, message, mirror(arrived)]
        out_k, out_v = finish(t + count + 1, now[2], out_k, out_v)
        return jnp.full((), -1, i32), pool, out_k, out_v, resident_out, new_out

    state = (
        left, pool, out_k, out_v,
        jnp.zeros((step_count, query_width), bf16), jnp.zeros((step_count, request_count, query_width), bf16),
    )
    for lower, count in zip((-1, *ENDS), ENDS):
        state = lax.while_loop(
            lambda state, lower=lower, count=count: (state[0] > lower) & (state[0] <= count),
            functools.partial(end, count), state,
        )
    _, _, out_k, out_v, resident_out, new_out = state
    out_k, out_v = (out.reshape(CAP, half, width) for out in (out_k, out_v))
    return (resident_out[:, None, :], new_out, out_k, out_v)


def solution(mesh):
    placed = (
        P(("side", "dp"), None, "tp"),
        P(("side", "dp"), None, "tp"),
        P(),
        P(),
        P(None, None, "tp"),
        P(None, None, "tp"),
        P(None, None, "tp"),
        P("dp", "side", "tp"),
        P("dp", "side", "tp"),
        P("dp"),
        P(None, "dp", "tp"),
        P(None, "dp", "tp"),
        P(None, "dp", "tp"),
    )
    return jax.shard_map(
        body,
        mesh=mesh,
        in_specs=placed,
        out_specs=(
            P(None, "dp", "tp"),
            P(None, None, "tp"),
            P("dp", "side", "tp"),
            P("dp", "side", "tp"),
        ),
        check_vma=False,
    )
```

```python
import functools

import jax
import jax.numpy as jnp
from jax import lax
from jax.experimental import pallas as pl
from jax.experimental.pallas import tpu as pltpu
from jax.sharding import PartitionSpec as P

HEAD_WIDTH = 128
CAP = 4
UNIT = 128
PER = 6
MESSAGE = UNIT * PER
PEEL = 6
ENDS = (0, 1, 2, 3, 4, 5, 7, 9)
TURN = 3
POOL_ROWS = 22528
LAG = 2
LOW = -1e30

HBM = pl.BlockSpec(memory_space=pltpu.HBM)
VM = pl.BlockSpec(memory_space=pltpu.VMEM)
SM = pl.BlockSpec(memory_space=pltpu.SMEM)


def attend(q, q_rows, k_ref, v_ref, tk, tv, first, length, tokens_on, emit):
    steps = q.shape[0]
    keys, width = k_ref.shape
    heads_kv = width // HEAD_WIDTH
    members = q.shape[1] // width
    rows = members * steps
    scale = HEAD_WIDTH ** -0.5
    for kv in range(heads_kv):
        lanes = slice(kv * HEAD_WIDTH, (kv + 1) * HEAD_WIDTH)
        for g in range(members):
            at = (kv * members + g) * HEAD_WIDTH
            q_rows[g * steps:(g + 1) * steps, :] = q[:, at:at + HEAD_WIDTH]
        q32 = q_rows[...]
        scores = lax.dot_general(
            q32.astype(jnp.bfloat16), k_ref[:, lanes], (((1,), (1,)), ((), ())), preferred_element_type=jnp.float32
        ) * scale
        usable = first + lax.broadcasted_iota(jnp.int32, (rows, keys), 1) < length
        scores = jnp.where(usable, scores, LOW)
        row_step = lax.rem(lax.broadcasted_iota(jnp.int32, (rows, 1), 0), steps)
        top = jnp.max(scores, axis=1, keepdims=True)
        extra = []
        for n in range(steps):
            s = jnp.sum(q32 * tk[n:n + 1, lanes], axis=1, keepdims=True) * scale
            on = (row_step >= n) & tokens_on
            s = jnp.where(on, s, LOW)
            extra.append((on, s))
            top = jnp.maximum(top, s)
        weight = jnp.where(usable, jnp.exp(scores - top), 0.0)
        total = jnp.sum(weight, axis=1, keepdims=True)
        acc = lax.dot_general(
            weight.astype(jnp.bfloat16), v_ref[:, lanes], (((1,), (0,)), ((), ())), preferred_element_type=jnp.float32
        )
        for n, (on, s) in enumerate(extra):
            w = jnp.where(on, jnp.exp(s - top), 0.0)
            total = total + w
            acc = acc + w.astype(jnp.bfloat16).astype(jnp.float32) * tv[n:n + 1, lanes]
        emit(kv, top, total, acc)


def attention_kernel(
    dp, resident_length, lengths, rq, rk, rv, rtk, rtv, nq, nk, nv, ntk, ntv, part, own_out, resident, new, q_rows
):
    side = lax.axis_index("side")
    owner = side * dp + lax.axis_index("dp")
    steps = rq.shape[0]
    keys, width = rk.shape
    rows = steps * rq.shape[1] // width
    f32 = jnp.float32

    def emit_part(kv, top, total, acc):
        at = slice(kv * rows, (kv + 1) * rows)
        part[at, 0:HEAD_WIDTH] = acc
        part[at, HEAD_WIDTH:2 * HEAD_WIDTH] = jnp.broadcast_to(top, (rows, HEAD_WIDTH))
        part[at, 2 * HEAD_WIDTH:] = jnp.broadcast_to(total, (rows, HEAD_WIDTH))

    attend(
        rq[...].astype(f32), q_rows, rk, rv, rtk[...].astype(f32), rtv[...].astype(f32),
        side * keys, resident_length[0], side == 1, emit_part,
    )

    def own(ref):
        picked = []
        for n in range(steps):
            block = ref[n].astype(f32)
            here = lax.broadcasted_iota(jnp.int32, block.shape, 0) == owner
            picked.append(jnp.sum(jnp.where(here, block, 0.0), axis=0, keepdims=True))
        return jnp.concatenate(picked, axis=0)

    def emit_out(kv, top, total, acc):
        own_out[kv * rows:(kv + 1) * rows, :] = acc / total

    attend(own(nq), q_rows, nk, nv, own(ntk), own(ntv), 0, lengths[owner], side >= 0, emit_out)


def finish_kernel(dp, steps, a, b, own, pair, *refs):
    *others, resident, new, o_rows = refs
    w = HEAD_WIDTH
    heads = resident.shape[1] // w
    top = jnp.maximum(a[:, w:2 * w], b[:, w:2 * w])
    ga = jnp.exp(a[:, w:2 * w] - top)
    gb = jnp.exp(b[:, w:2 * w] - top)
    o_rows[...] = (a[:, 0:w] * ga + b[:, 0:w] * gb) / (a[:, 2 * w:] * ga + b[:, 2 * w:] * gb)
    for h in range(heads):
        resident[:, h * w:(h + 1) * w] = o_rows[h * steps:(h + 1) * steps, :].astype(resident.dtype)
    side, me = lax.axis_index("side"), lax.axis_index("dp")
    count = 2 * dp
    blocks = [own, pair] + [other.at[y] for other in others for y in range(2)]
    places = [
        lax.bitwise_xor(side, y) * dp + lax.rem(me - x + dp, dp) for x in range(dp) for y in range(2)
    ]
    at_row = lax.broadcasted_iota(jnp.int32, (count, w), 0)
    for n in range(steps):
        for h in range(heads):
            k = h * steps + n
            block = jnp.zeros((count, w), jnp.float32)
            for place, source in zip(places, blocks):
                block = jnp.where(at_row == place, source[k:k + 1, :], block)
            new[n, :, h * w:(h + 1) * w] = block.astype(new.dtype)


def units_at(start):
    return pl.ds(pl.multiple_of(start, UNIT), UNIT)


def last_unit(length):
    return (length + UNIT - 1) // UNIT * UNIT - UNIT


def mask_unit(ref, first, length):
    row = lax.broadcasted_iota(jnp.int32, (UNIT, ref.shape[1]), 0)
    block = ref[units_at(first), :]
    ref[units_at(first), :] = jnp.where(first + row < length, block, jnp.zeros_like(block))


def plan_kernel(dp, half, ring_units, lengths, goal, pk, pv, table):
    side, me = lax.axis_index("side"), lax.axis_index("dp")
    f32 = jnp.float32
    full = 2 * half
    count = lengths.shape[0]
    wide = table.shape[1]
    id_row = lax.broadcasted_iota(jnp.int32, (count, count), 1).astype(f32)
    id_col = lax.broadcasted_iota(jnp.int32, (count, count), 0).astype(f32)
    eye = id_row == id_col

    def col(row):
        return jnp.sum(jnp.where(eye, jnp.broadcast_to(row, (count, count)), 0.0), axis=1, keepdims=True)

    def spread(scalars):
        row = jnp.zeros((1, count), jnp.int32)
        lane = lax.broadcasted_iota(jnp.int32, (1, count), 1)
        for r in range(count):
            row = jnp.where(lane == r, scalars[r], row)
        return row.astype(f32)

    ids = id_row[0:1]
    late = jnp.where(ids >= dp, 1.0, 0.0)
    src0 = ids - dp * late
    goal0 = spread(goal)
    side_f, me_f = side.astype(f32), me.astype(f32)
    units = jnp.floor((spread(lengths) + (UNIT - 1)) * (1.0 / UNIT))
    units_col, late_col, goal0_col, src0_col = col(units), col(late), col(goal0), col(src0)
    slot = jnp.sum(jnp.where((goal0_col == goal0) & (id_col < id_row), 1.0, 0.0), axis=0, keepdims=True)
    slot_col = col(slot)
    time = lax.broadcasted_iota(jnp.int32, (1, wide), 1).astype(f32)
    here_col = jnp.where(late_col == side_f, 0.0, 1.0)
    steps = jnp.zeros((1, 1), f32)
    sends, passes, ends = [], [], []
    for flip in (False, True):
        turned = (lambda x: dp - 1 - x) if flip else (lambda x: x)
        s, g, m, s_col, g_col = turned(src0), turned(goal0), turned(me_f), turned(src0_col), turned(goal0_col)
        crosses, bases, times = [], [], []
        for d in range(dp - 1):
            cross = (s <= d) & (g > d)
            cross_col = (s_col <= d) & (g_col > d)
            ready = jnp.zeros((1, count), f32)
            if d > 0:
                ready = jnp.where(s == d, 0.0, times[-1] + LAG * PER)
            ready_col = col(ready)
            ahead = (ready_col < ready) | (
                (ready_col == ready) & ((g_col > g) | ((g_col == g) & (id_col < id_row)))
            )
            base = jnp.sum(jnp.where(ahead & cross_col, units_col, 0.0), axis=0, keepdims=True)
            slack = jnp.where((ahead | eye) & cross_col, ready_col - col(base), 0.0)
            start = base + jnp.max(slack, axis=0, keepdims=True)
            end = jnp.max(jnp.where(cross, start + units, 0.0), axis=1, keepdims=True)
            steps = jnp.maximum(steps, jnp.floor((end + (PER - 1)) * (1.0 / PER)))
            crosses.append(cross)
            bases.append(base)
            times.append(start)

        def at(link):
            base, start, used = (jnp.zeros((1, count), f32) for _ in range(3))
            for d in range(dp - 1):
                base = jnp.where(link == d, bases[d], base)
                start = jnp.where(link == d, times[d], start)
                used = jnp.where(link == d, jnp.where(crosses[d], units, 0.0), used)
            return col(base), col(start), col(used)

        def ring_row(p):
            return (p - ring_units * jnp.floor((p + 0.5) * (1.0 / ring_units))) * UNIT

        def pick(hit, value):
            return jnp.sum(jnp.where(hit, value + 1.0, 0.0), axis=0, keepdims=True) - 1.0

        base, start, used = at(m)
        c = time - start
        hit = (c >= 0) & (c < used)
        own = here_col * full + c * UNIT
        sends.append(jnp.maximum(pick(hit, jnp.where(s_col == m, own, 2 * full + ring_row(base + c))), 0.0))
        _, start, used = at(m - 1)
        c = time - start
        hit = (c >= 0) & (c < used)
        passes.append(pick(hit & (g_col != m), 2 * full + ring_row(base + c)))
        row = c * UNIT - half * side_f
        ends.append(pick(hit & (g_col == m) & (row >= 0) & (row < half), slot_col * half + row))
    right = side_f == 0.0
    for r, row in enumerate((
        jnp.where(right, sends[0], sends[1]), jnp.where(right, passes[0], passes[1]),
        jnp.where(right, ends[0], ends[1]), jnp.where(right, ends[1], ends[0]),
    )):
        table[r:r + 1, :] = row.astype(jnp.int32)
    stay = jnp.where((src0 == me_f) & (goal0 == me_f), slot + 1.0, 0.0)
    home = [
        jnp.sum(jnp.where(late == which, stay, 0.0), axis=1, keepdims=True) - 1.0 for which in (side_f, 1.0 - side_f)
    ]
    last = jnp.where(time == 0, steps, jnp.where(time == 1, home[0], home[1]))
    table[4:5, :] = last.astype(jnp.int32)
    table[5:8, :] = jnp.zeros((3, wide), jnp.int32)


def first_kernel(dp, table, lengths, pk, pv, xk, xv, send):
    side, me = lax.axis_index("side"), lax.axis_index("dp")
    full = pk.shape[0]
    for j, pair in enumerate(((pk, pv), (xk, xv))):
        length = lengths[lax.bitwise_xor(side, j) * dp + me]
        last = last_unit(length)
        for i in range(PER):
            row = table[0, i] - j * full

            @pl.when((row >= 0) & (row < full))
            def _():
                for n in range(2):
                    send[n, i * UNIT:(i + 1) * UNIT, :] = pair[n][units_at(row), :]

            @pl.when(row == last)
            def _():
                for n in range(2):
                    mask_unit(send.at[n, i * UNIT:(i + 1) * UNIT], 0, length - last)


def pool_kernel(
    dp, table, lengths, pk, pv, xk, xv, pool, send, out_k, out_v, blank, stage, fill_sem, load_sem, pool_sem, home_sem
):
    side, me = lax.axis_index("side"), lax.axis_index("dp")
    full = xk.shape[0]
    half = full // 2
    loads = [
        pltpu.make_async_copy(a, stage.at[j, n], load_sem.at[j, n])
        for j, pair in enumerate(((pk, pv), (xk, xv))) for n, a in enumerate(pair)
    ]
    for copy in loads:
        copy.start()
    blank[...] = jnp.zeros_like(blank)
    fills = [
        pltpu.make_async_copy(blank, out.at[pl.ds(slot * half, half)], fill_sem.at[i, slot])
        for i, out in enumerate((out_k, out_v)) for slot in range(CAP)
    ]
    for fill in fills:
        fill.start()
    stores, homes = [], []
    for j in range(2):
        length = lengths[lax.bitwise_xor(side, j) * dp + me]
        last = last_unit(length)
        for n in range(2):
            loads[2 * j + n].wait()
            mask_unit(stage.at[j, n], last, length)
        store = pltpu.make_async_copy(stage.at[j], pool.at[:, pl.ds(j * full, full)], pool_sem.at[j])
        store.start()
        stores.append(store)
        slot = table[4, 1 + j]
        count = jnp.where(slot >= 0, jnp.clip((last + UNIT - side * half) // UNIT, 0, half // UNIT), 0)

        def home(u, wait, j=j, slot=slot):
            for n, out in enumerate((out_k, out_v)):
                copy = pltpu.make_async_copy(
                    stage.at[j, n, units_at(side * half + u * UNIT)], out.at[units_at(slot * half + u * UNIT)],
                    home_sem.at[j, n, u],
                )
                copy.wait() if wait else copy.start()

        homes.append((count, home))
    for fill in fills:
        fill.wait()
    for count, home in homes:
        pl.loop(0, count)(functools.partial(home, wait=False))
    for i in range(PER):
        code = table[0, PER + i]
        j = jnp.clip(code // full, 0, 1)
        row = jnp.clip(code - j * full, 0, full - UNIT)
        for n in range(2):
            send[n, i * UNIT:(i + 1) * UNIT, :] = stage[j, n, units_at(row), :]
    for count, home in homes:
        pl.loop(0, count)(functools.partial(home, wait=True))
    for store in stores:
        store.wait()


def end_copies(table, t, row, take, out_k, out_v, sem):
    copies = []
    for i in range(PER):
        code = table[row, t * PER + i]
        to = units_at(jnp.maximum(code, 0))
        copies.append((code >= 0, [
            pltpu.make_async_copy(take.at[n, pl.ds(i * UNIT, UNIT)], out.at[to], sem.at[i, n])
            for n, out in enumerate((out_k, out_v))
        ]))
    return copies


def when_all(copies, act):
    @pl.when(functools.reduce(jnp.logical_or, [on for on, _ in copies]))
    def _():
        for on, group in copies:
            @pl.when(on)
            def _():
                for copy in group:
                    act(copy)


def step_kernel(
    table, now, got, mirrored, pool_in, ok, ov, send, pool, out_k, out_v, pass_sem, got_sem, mirror_sem, send_sem
):
    t = now[0]
    passes = []
    for i in range(PER):
        code = table[1, t * PER + i]
        to = pool.at[:, units_at(jnp.maximum(code, 0))]
        passes.append((code >= 0, [pltpu.make_async_copy(got.at[:, pl.ds(i * UNIT, UNIT)], to, pass_sem.at[i])]))
    when_all(passes, lambda copy: copy.start())
    ends = [end_copies(table, t, 2, got, out_k, out_v, got_sem)]
    if mirrored is not None:
        ends.append(end_copies(table, t - 1, 3, mirrored, out_k, out_v, mirror_sem))
    for copies in ends:
        when_all(copies, lambda copy: copy.start())
    when_all(passes, lambda copy: copy.wait())
    if send is not None:
        lay = [
            pltpu.make_async_copy(
                pool.at[:, units_at(table[0, (t + LAG) * PER + i])], send.at[:, pl.ds(i * UNIT, UNIT)], send_sem.at[i]
            )
            for i in range(PER)
        ]
        for copy in lay:
            copy.start()
        for copy in lay:
            copy.wait()
    for copies in ends:
        when_all(copies, lambda copy: copy.wait())


def last_kernel(table, now, mirrored, ok, ov, out_k, out_v, sem):
    ends = end_copies(table, now[0] - 1, 3, mirrored, out_k, out_v, sem)
    when_all(ends, lambda copy: copy.start())
    when_all(ends, lambda copy: copy.wait())


def body(
    prompt_keys,
    prompt_values,
    prompt_lengths,
    assignment,
    new_queries,
    incoming_token_keys,
    incoming_token_values,
    stored_keys,
    stored_values,
    resident_lengths,
    resident_queries,
    stored_token_keys,
    stored_token_values,
):
    step_count = resident_queries.shape[0]
    dp = lax.axis_size("dp")
    request_count = prompt_lengths.shape[0]
    full, width = prompt_keys.shape[1:]
    query_width = new_queries.shape[2]
    half = full // 2
    bf16, f32, i32 = jnp.bfloat16, jnp.float32, jnp.int32
    swap = [(0, 1), (1, 0)]
    shape = jax.ShapeDtypeStruct
    dma = pltpu.SemaphoreType.DMA
    roomy = pltpu.CompilerParams(vmem_limit_bytes=44 << 20)

    pk, pv = prompt_keys[0], prompt_values[0]
    xk, xv = lax.ppermute(pk, "side", swap), lax.ppermute(pv, "side", swap)

    most = full // UNIT
    ring_units = 2 * most + (LAG + 1) * PER
    steps_max = -(-request_count * most // PER) + LAG * dp + PEEL + ENDS[-1] + LAG
    wide = -(-steps_max * PER // 128) * 128
    slots = shape((CAP * half, width), bf16)
    table = pl.pallas_call(
        functools.partial(plan_kernel, dp, half, ring_units),
        out_shape=shape((8, wide), i32),
        in_specs=[SM, SM, VM, VM],
        out_specs=VM,
        compiler_params=pltpu.CompilerParams(vmem_limit_bytes=58 << 20),
    )(prompt_lengths, jnp.reshape(assignment, (request_count,)), pk, pv)
    last = table[4, 0]

    message = shape((2, MESSAGE, width), bf16)
    pool_shape = shape((2, max(2 * full + ring_units * UNIT, POOL_ROWS), width), bf16)
    first = pl.pallas_call(
        functools.partial(first_kernel, dp),
        out_shape=message,
        in_specs=[SM, SM] + [VM] * 4,
        out_specs=VM,
        compiler_params=roomy,
    )(table, prompt_lengths, pk, pv, xk, xv)

    tied = lax.optimization_barrier((table, first))
    pool, second, out_k, out_v = pl.pallas_call(
        functools.partial(pool_kernel, dp),
        out_shape=(pool_shape, message, slots, slots),
        in_specs=[SM, SM] + [VM] * 4,
        out_specs=[HBM, VM, HBM, HBM],
        scratch_shapes=[
            pltpu.VMEM((half, width), bf16), pltpu.VMEM((2, 2, full, width), bf16),
            dma((2, CAP)), dma((2, 2)), dma((2,)), dma((2, 2, half // UNIT)),
        ],
        compiler_params=roomy,
    )(tied[0], prompt_lengths, pk, pv, xk, xv)

    held = lax.optimization_barrier((new_queries, second))[0]
    rows = step_count * query_width // HEAD_WIDTH
    resident_shape = shape((step_count, query_width), bf16)
    new_shape = shape((step_count, request_count, query_width), bf16)
    part, own_out, resident_out, new_out = pl.pallas_call(
        functools.partial(attention_kernel, dp),
        out_shape=(shape((rows, 3 * HEAD_WIDTH), f32), shape((rows, HEAD_WIDTH), f32), resident_shape, new_shape),
        in_specs=[SM, SM] + [VM] * 10,
        out_specs=[VM, VM, HBM, HBM],
        scratch_shapes=[pltpu.VMEM((step_count * query_width // width, HEAD_WIDTH), f32)],
        compiler_params=roomy,
    )(
        resident_lengths, prompt_lengths,
        resident_queries[:, 0], stored_keys[0], stored_values[0], stored_token_keys[:, 0], stored_token_values[:, 0],
        held, pk, pv, incoming_token_keys, incoming_token_values,
    )

    hops = [(i, i + 1) for i in range(dp - 1)] + [(dp + i + 1, dp + i) for i in range(dp - 1)]

    def cross(send):
        return lax.ppermute(send, ("side", "dp"), hops)

    def mirror(got):
        return lax.ppermute(got, "side", swap)

    def place(t, got, mirrored, pool, out_k, out_v, lay):
        news = [message] if lay else []
        first_kept = len(news)
        mirrors = [] if mirrored is None else [mirrored]

        def kernel(table, now, got, *refs):
            refs = list(refs)
            mirrored = refs.pop(0) if mirrors else None
            send = refs.pop(3) if lay else None
            step_kernel(table, now, got, mirrored, *refs[:3], send, *refs[3:])

        kept = 3 + len(mirrors)
        outs = pl.pallas_call(
            kernel,
            out_shape=(*news, pool_shape, slots, slots),
            in_specs=[SM, SM, VM] + [VM] * len(mirrors) + [HBM] * 3,
            out_specs=[VM] * len(news) + [HBM] * 3,
            scratch_shapes=[dma((PER,)), dma((PER, 2)), dma((PER, 2)), dma((PER,))],
            input_output_aliases={kept + i: first_kept + i for i in range(3)},
            compiler_params=roomy,
        )(table, jnp.full((1,), t, i32), got, *mirrors, pool, out_k, out_v)
        return outs if lay else (None, *outs)

    def finish(t, mirrored, out_k, out_v):
        return pl.pallas_call(
            last_kernel,
            out_shape=(slots, slots),
            in_specs=[SM, SM, VM, HBM, HBM],
            out_specs=[HBM, HBM],
            scratch_shapes=[dma((PER, 2))],
            input_output_aliases={3: 0, 4: 1},
            compiler_params=roomy,
        )(table, jnp.full((1,), t, i32), mirrored, out_k, out_v)

    def advance(count, state):
        t, got, a, mirrored, pool, out_k, out_v = state
        for i in range(count):
            coming = cross(a)
            a, pool, out_k, out_v = place(t + i, got, mirrored, pool, out_k, out_v, True)
            got, mirrored = coming, mirror(got)
        return t + count, got, a, mirrored, pool, out_k, out_v

    part_other = lax.ppermute(part, "side", swap)
    pair = lax.ppermute(own_out, "side", swap)
    got, part_other, pair = lax.optimization_barrier((cross(first), part_other, pair))
    state = advance(PEEL - 2, (0, got, second, None, pool, out_k, out_v))
    both, _ = lax.optimization_barrier((jnp.stack([own_out, pair]), state[2]))
    others = [lax.ppermute(both, "dp", [(z, (z + x) % dp) for z in range(dp)]) for x in range(1, dp)]
    state = advance(1, state)
    others, _ = lax.optimization_barrier((others, state[2]))

    def lay_out():
        return pl.pallas_call(
            functools.partial(finish_kernel, dp, step_count),
            out_shape=(resident_shape, new_shape),
            in_specs=[VM] * (3 + dp),
            out_specs=[VM, VM],
            scratch_shapes=[pltpu.VMEM((rows, HEAD_WIDTH), f32)],
            compiler_params=pltpu.CompilerParams(vmem_limit_bytes=8 << 20),
        )(part, part_other, own_out, pair, *others)

    a = state[2]
    t, got, _, mirrored, pool, out_k, out_v = state
    left = jnp.maximum(last - PEEL, 0)
    crowd = max(min(2 * (d + 1), CAP * (dp - 1 - d)) for d in range(dp - 1))
    if -(-crowd * most // PER) + LAG * (dp - 2) > PEEL + ENDS[-1]:
        left, (t, got, a, mirrored, pool, out_k, out_v) = lax.while_loop(
            lambda state: state[0] > ENDS[-1],
            lambda state: (state[0] - TURN, advance(TURN, state[1])),
            (left, (jnp.asarray(t, i32), got, a, mirrored, pool, out_k, out_v)),
        )

    def end(count, state):
        _, pool, out_k, out_v, _, _ = state
        now = [got, a, mirrored]
        resident_out, new_out = lay_out()
        for i in range(count + 1):
            arrived, message, passed = now
            coming = cross(message) if i < count else None
            message, pool, out_k, out_v = place(t + i, arrived, passed, pool, out_k, out_v, i + 1 < count)
            now = [coming, message, mirror(arrived)]
        out_k, out_v = finish(t + count + 1, now[2], out_k, out_v)
        return jnp.full((), -1, i32), pool, out_k, out_v, resident_out, new_out

    state = (left, pool, out_k, out_v, resident_out, new_out)
    for lower, count in zip((-1, *ENDS), ENDS):
        state = lax.while_loop(
            lambda state, lower=lower, count=count: (state[0] > lower) & (state[0] <= count),
            functools.partial(end, count), state,
        )
    _, _, out_k, out_v, resident_out, new_out = state
    out_k, out_v = (out.reshape(CAP, half, width) for out in (out_k, out_v))
    return (resident_out[:, None, :], new_out, out_k, out_v)


def solution(mesh):
    placed = (
        P(("side", "dp"), None, "tp"),
        P(("side", "dp"), None, "tp"),
        P(),
        P(),
        P(None, None, "tp"),
        P(None, None, "tp"),
        P(None, None, "tp"),
        P("dp", "side", "tp"),
        P("dp", "side", "tp"),
        P("dp"),
        P(None, "dp", "tp"),
        P(None, "dp", "tp"),
        P(None, "dp", "tp"),
    )
    return jax.shard_map(
        body,
        mesh=mesh,
        in_specs=placed,
        out_specs=(
            P(None, "dp", "tp"),
            P(None, None, "tp"),
            P("dp", "side", "tp"),
            P("dp", "side", "tp"),
        ),
        check_vma=False,
    )
```

```python
import functools

import jax
import jax.numpy as jnp
from jax import lax
from jax.experimental import pallas as pl
from jax.experimental.pallas import tpu as pltpu
from jax.sharding import PartitionSpec as P

HEAD_WIDTH = 128
CAP = 4
UNIT = 128
PER = 6
MESSAGE = UNIT * PER
PEEL = 6
ENDS = (0, 1, 2, 3, 4, 5, 7, 9)
TURN = 3
POOL_ROWS = 22528
LAG = 2
LOW = -1e30

HBM = pl.BlockSpec(memory_space=pltpu.HBM)
VM = pl.BlockSpec(memory_space=pltpu.VMEM)
SM = pl.BlockSpec(memory_space=pltpu.SMEM)


def attend(q, q_rows, k_ref, v_ref, tk, tv, first, length, tokens_on, emit):
    steps = q.shape[0]
    keys, width = k_ref.shape
    heads_kv = width // HEAD_WIDTH
    members = q.shape[1] // width
    rows = members * steps
    scale = HEAD_WIDTH ** -0.5
    for kv in range(heads_kv):
        lanes = slice(kv * HEAD_WIDTH, (kv + 1) * HEAD_WIDTH)
        for g in range(members):
            at = (kv * members + g) * HEAD_WIDTH
            q_rows[g * steps:(g + 1) * steps, :] = q[:, at:at + HEAD_WIDTH]
        q32 = q_rows[...]
        scores = lax.dot_general(
            q32.astype(jnp.bfloat16), k_ref[:, lanes], (((1,), (1,)), ((), ())), preferred_element_type=jnp.float32
        ) * scale
        usable = first + lax.broadcasted_iota(jnp.int32, (rows, keys), 1) < length
        scores = jnp.where(usable, scores, LOW)
        row_step = lax.rem(lax.broadcasted_iota(jnp.int32, (rows, 1), 0), steps)
        top = jnp.max(scores, axis=1, keepdims=True)
        extra = []
        for n in range(steps):
            s = jnp.sum(q32 * tk[n:n + 1, lanes], axis=1, keepdims=True) * scale
            on = (row_step >= n) & tokens_on
            s = jnp.where(on, s, LOW)
            extra.append((on, s))
            top = jnp.maximum(top, s)
        weight = jnp.where(usable, jnp.exp(scores - top), 0.0)
        total = jnp.sum(weight, axis=1, keepdims=True)
        acc = lax.dot_general(
            weight.astype(jnp.bfloat16), v_ref[:, lanes], (((1,), (0,)), ((), ())), preferred_element_type=jnp.float32
        )
        for n, (on, s) in enumerate(extra):
            w = jnp.where(on, jnp.exp(s - top), 0.0)
            total = total + w
            acc = acc + w.astype(jnp.bfloat16).astype(jnp.float32) * tv[n:n + 1, lanes]
        emit(kv, top, total, acc)


def attention_kernel(
    dp, resident_length, lengths, rq, rk, rv, rtk, rtv, nq, nk, nv, ntk, ntv, part, own_out, resident, new, q_rows
):
    side = lax.axis_index("side")
    owner = side * dp + lax.axis_index("dp")
    steps = rq.shape[0]
    keys, width = rk.shape
    rows = steps * rq.shape[1] // width
    f32 = jnp.float32

    def emit_part(kv, top, total, acc):
        at = slice(kv * rows, (kv + 1) * rows)
        part[at, 0:HEAD_WIDTH] = acc
        part[at, HEAD_WIDTH:2 * HEAD_WIDTH] = jnp.broadcast_to(top, (rows, HEAD_WIDTH))
        part[at, 2 * HEAD_WIDTH:] = jnp.broadcast_to(total, (rows, HEAD_WIDTH))

    attend(
        rq[...].astype(f32), q_rows, rk, rv, rtk[...].astype(f32), rtv[...].astype(f32),
        side * keys, resident_length[0], side == 1, emit_part,
    )

    def own(ref):
        picked = []
        for n in range(steps):
            block = ref[n].astype(f32)
            here = lax.broadcasted_iota(jnp.int32, block.shape, 0) == owner
            picked.append(jnp.sum(jnp.where(here, block, 0.0), axis=0, keepdims=True))
        return jnp.concatenate(picked, axis=0)

    def emit_out(kv, top, total, acc):
        own_out[kv * rows:(kv + 1) * rows, :] = acc / total

    attend(own(nq), q_rows, nk, nv, own(ntk), own(ntv), 0, lengths[owner], side >= 0, emit_out)


def finish_kernel(dp, steps, a, b, own, pair, *refs):
    *others, resident, new, o_rows = refs
    w = HEAD_WIDTH
    heads = resident.shape[1] // w
    top = jnp.maximum(a[:, w:2 * w], b[:, w:2 * w])
    ga = jnp.exp(a[:, w:2 * w] - top)
    gb = jnp.exp(b[:, w:2 * w] - top)
    o_rows[...] = (a[:, 0:w] * ga + b[:, 0:w] * gb) / (a[:, 2 * w:] * ga + b[:, 2 * w:] * gb)
    for h in range(heads):
        resident[:, h * w:(h + 1) * w] = o_rows[h * steps:(h + 1) * steps, :].astype(resident.dtype)
    side, me = lax.axis_index("side"), lax.axis_index("dp")
    count = 2 * dp
    blocks = [own, pair] + [other.at[y] for other in others for y in range(2)]
    places = [
        lax.bitwise_xor(side, y) * dp + lax.rem(me - x + dp, dp) for x in range(dp) for y in range(2)
    ]
    at_row = lax.broadcasted_iota(jnp.int32, (count, w), 0)
    for n in range(steps):
        for h in range(heads):
            k = h * steps + n
            block = jnp.zeros((count, w), jnp.float32)
            for place, source in zip(places, blocks):
                block = jnp.where(at_row == place, source[k:k + 1, :], block)
            new[n, :, h * w:(h + 1) * w] = block.astype(new.dtype)


def units_at(start):
    return pl.ds(pl.multiple_of(start, UNIT), UNIT)


def last_unit(length):
    return (length + UNIT - 1) // UNIT * UNIT - UNIT


def mask_unit(ref, first, length):
    row = lax.broadcasted_iota(jnp.int32, (UNIT, ref.shape[1]), 0)
    block = ref[units_at(first), :]
    ref[units_at(first), :] = jnp.where(first + row < length, block, jnp.zeros_like(block))


def plan_kernel(dp, half, ring_units, lengths, goal, pk, pv, table):
    side, me = lax.axis_index("side"), lax.axis_index("dp")
    f32 = jnp.float32
    full = 2 * half
    count = lengths.shape[0]
    wide = table.shape[1]
    id_row = lax.broadcasted_iota(jnp.int32, (count, count), 1).astype(f32)
    id_col = lax.broadcasted_iota(jnp.int32, (count, count), 0).astype(f32)
    eye = id_row == id_col

    def col(row):
        return jnp.sum(jnp.where(eye, jnp.broadcast_to(row, (count, count)), 0.0), axis=1, keepdims=True)

    def spread(scalars):
        row = jnp.zeros((1, count), jnp.int32)
        lane = lax.broadcasted_iota(jnp.int32, (1, count), 1)
        for r in range(count):
            row = jnp.where(lane == r, scalars[r], row)
        return row.astype(f32)

    ids = id_row[0:1]
    late = jnp.where(ids >= dp, 1.0, 0.0)
    src0 = ids - dp * late
    goal0 = spread(goal)
    side_f, me_f = side.astype(f32), me.astype(f32)
    units = jnp.floor((spread(lengths) + (UNIT - 1)) * (1.0 / UNIT))
    units_col, late_col, goal0_col, src0_col = col(units), col(late), col(goal0), col(src0)
    slot = jnp.sum(jnp.where((goal0_col == goal0) & (id_col < id_row), 1.0, 0.0), axis=0, keepdims=True)
    slot_col = col(slot)
    time = lax.broadcasted_iota(jnp.int32, (1, wide), 1).astype(f32)
    here_col = jnp.where(late_col == side_f, 0.0, 1.0)
    steps = jnp.zeros((1, 1), f32)
    sends, passes, ends = [], [], []
    for flip in (False, True):
        turned = (lambda x: dp - 1 - x) if flip else (lambda x: x)
        s, g, m, s_col, g_col = turned(src0), turned(goal0), turned(me_f), turned(src0_col), turned(goal0_col)
        crosses, bases, times = [], [], []
        for d in range(dp - 1):
            cross = (s <= d) & (g > d)
            cross_col = (s_col <= d) & (g_col > d)
            ready = jnp.zeros((1, count), f32)
            if d > 0:
                ready = jnp.where(s == d, 0.0, times[-1] + LAG * PER)
            ready_col = col(ready)
            ahead = (ready_col < ready) | (
                (ready_col == ready) & ((g_col > g) | ((g_col == g) & (id_col < id_row)))
            )
            base = jnp.sum(jnp.where(ahead & cross_col, units_col, 0.0), axis=0, keepdims=True)
            slack = jnp.where((ahead | eye) & cross_col, ready_col - col(base), 0.0)
            start = base + jnp.max(slack, axis=0, keepdims=True)
            end = jnp.max(jnp.where(cross, start + units, 0.0), axis=1, keepdims=True)
            steps = jnp.maximum(steps, jnp.floor((end + (PER - 1)) * (1.0 / PER)))
            crosses.append(cross)
            bases.append(base)
            times.append(start)

        def at(link):
            base, start, used = (jnp.zeros((1, count), f32) for _ in range(3))
            for d in range(dp - 1):
                base = jnp.where(link == d, bases[d], base)
                start = jnp.where(link == d, times[d], start)
                used = jnp.where(link == d, jnp.where(crosses[d], units, 0.0), used)
            return col(base), col(start), col(used)

        def ring_row(p):
            return (p - ring_units * jnp.floor((p + 0.5) * (1.0 / ring_units))) * UNIT

        def pick(hit, value):
            return jnp.sum(jnp.where(hit, value + 1.0, 0.0), axis=0, keepdims=True) - 1.0

        base, start, used = at(m)
        c = time - start
        hit = (c >= 0) & (c < used)
        own = here_col * full + c * UNIT
        sends.append(jnp.maximum(pick(hit, jnp.where(s_col == m, own, 2 * full + ring_row(base + c))), 0.0))
        _, start, used = at(m - 1)
        c = time - start
        hit = (c >= 0) & (c < used)
        passes.append(pick(hit & (g_col != m), 2 * full + ring_row(base + c)))
        row = c * UNIT - half * side_f
        ends.append(pick(hit & (g_col == m) & (row >= 0) & (row < half), slot_col * half + row))
    right = side_f == 0.0
    for r, row in enumerate((
        jnp.where(right, sends[0], sends[1]), jnp.where(right, passes[0], passes[1]),
        jnp.where(right, ends[0], ends[1]), jnp.where(right, ends[1], ends[0]),
    )):
        table[r:r + 1, :] = row.astype(jnp.int32)
    stay = jnp.where((src0 == me_f) & (goal0 == me_f), slot + 1.0, 0.0)
    home = [
        jnp.sum(jnp.where(late == which, stay, 0.0), axis=1, keepdims=True) - 1.0 for which in (side_f, 1.0 - side_f)
    ]
    last = jnp.where(time == 0, steps, jnp.where(time == 1, home[0], home[1]))
    table[4:5, :] = last.astype(jnp.int32)
    table[5:8, :] = jnp.zeros((3, wide), jnp.int32)


def first_kernel(dp, table, lengths, pk, pv, xk, xv, send):
    side, me = lax.axis_index("side"), lax.axis_index("dp")
    full = pk.shape[0]
    for j, pair in enumerate(((pk, pv), (xk, xv))):
        length = lengths[lax.bitwise_xor(side, j) * dp + me]
        last = last_unit(length)
        for i in range(PER):
            row = table[0, i] - j * full

            @pl.when((row >= 0) & (row < full))
            def _():
                for n in range(2):
                    send[n, i * UNIT:(i + 1) * UNIT, :] = pair[n][units_at(row), :]

            @pl.when(row == last)
            def _():
                for n in range(2):
                    mask_unit(send.at[n, i * UNIT:(i + 1) * UNIT], 0, length - last)


def pool_kernel(
    dp, table, lengths, pk, pv, xk, xv, pool, send, out_k, out_v, blank, stage, fill_sem, load_sem, pool_sem, home_sem
):
    side, me = lax.axis_index("side"), lax.axis_index("dp")
    full = xk.shape[0]
    half = full // 2
    loads = [
        pltpu.make_async_copy(a, stage.at[j, n], load_sem.at[j, n])
        for j, pair in enumerate(((pk, pv), (xk, xv))) for n, a in enumerate(pair)
    ]
    for copy in loads:
        copy.start()
    blank[...] = jnp.zeros_like(blank)
    fills = [
        pltpu.make_async_copy(blank, out.at[pl.ds(slot * half, half)], fill_sem.at[i, slot])
        for i, out in enumerate((out_k, out_v)) for slot in range(CAP)
    ]
    for fill in fills:
        fill.start()
    stores, homes = [], []
    for j in range(2):
        length = lengths[lax.bitwise_xor(side, j) * dp + me]
        last = last_unit(length)
        for n in range(2):
            loads[2 * j + n].wait()
            mask_unit(stage.at[j, n], last, length)
        store = pltpu.make_async_copy(stage.at[j], pool.at[:, pl.ds(j * full, full)], pool_sem.at[j])
        store.start()
        stores.append(store)
        slot = table[4, 1 + j]
        count = jnp.where(slot >= 0, jnp.clip((last + UNIT - side * half) // UNIT, 0, half // UNIT), 0)

        def home(u, wait, j=j, slot=slot):
            for n, out in enumerate((out_k, out_v)):
                copy = pltpu.make_async_copy(
                    stage.at[j, n, units_at(side * half + u * UNIT)], out.at[units_at(slot * half + u * UNIT)],
                    home_sem.at[j, n, u],
                )
                copy.wait() if wait else copy.start()

        homes.append((count, home))
    for fill in fills:
        fill.wait()
    for count, home in homes:
        pl.loop(0, count)(functools.partial(home, wait=False))
    for i in range(PER):
        code = table[0, PER + i]
        j = jnp.clip(code // full, 0, 1)
        row = jnp.clip(code - j * full, 0, full - UNIT)
        for n in range(2):
            send[n, i * UNIT:(i + 1) * UNIT, :] = stage[j, n, units_at(row), :]
    for count, home in homes:
        pl.loop(0, count)(functools.partial(home, wait=True))
    for store in stores:
        store.wait()


def end_copies(table, t, row, take, out_k, out_v, sem):
    copies = []
    for i in range(PER):
        code = table[row, t * PER + i]
        to = units_at(jnp.maximum(code, 0))
        copies.append((code >= 0, [
            pltpu.make_async_copy(take.at[n, pl.ds(i * UNIT, UNIT)], out.at[to], sem.at[i, n])
            for n, out in enumerate((out_k, out_v))
        ]))
    return copies


def when_all(copies, act):
    @pl.when(functools.reduce(jnp.logical_or, [on for on, _ in copies]))
    def _():
        for on, group in copies:
            @pl.when(on)
            def _():
                for copy in group:
                    act(copy)


def step_kernel(
    table, now, got, mirrored, pool_in, ok, ov, send, pool, out_k, out_v, pass_sem, got_sem, mirror_sem, send_sem
):
    t = now[0]
    passes = []
    for i in range(PER):
        code = table[1, t * PER + i]
        to = pool.at[:, units_at(jnp.maximum(code, 0))]
        passes.append((code >= 0, [pltpu.make_async_copy(got.at[:, pl.ds(i * UNIT, UNIT)], to, pass_sem.at[i])]))
    when_all(passes, lambda copy: copy.start())
    when_all(passes, lambda copy: copy.wait())
    lay = []
    if send is not None:
        lay = [
            pltpu.make_async_copy(
                pool.at[:, units_at(table[0, (t + LAG) * PER + i])], send.at[:, pl.ds(i * UNIT, UNIT)], send_sem.at[i]
            )
            for i in range(PER)
        ]
    for copy in lay:
        copy.start()
    ends = [end_copies(table, t, 2, got, out_k, out_v, got_sem)]
    if mirrored is not None:
        ends.append(end_copies(table, t - 1, 3, mirrored, out_k, out_v, mirror_sem))
    for copies in ends:
        when_all(copies, lambda copy: copy.start())
    for copy in lay:
        copy.wait()
    for copies in ends:
        when_all(copies, lambda copy: copy.wait())


def last_kernel(table, now, mirrored, ok, ov, out_k, out_v, sem):
    ends = end_copies(table, now[0] - 1, 3, mirrored, out_k, out_v, sem)
    when_all(ends, lambda copy: copy.start())
    when_all(ends, lambda copy: copy.wait())


def body(
    prompt_keys,
    prompt_values,
    prompt_lengths,
    assignment,
    new_queries,
    incoming_token_keys,
    incoming_token_values,
    stored_keys,
    stored_values,
    resident_lengths,
    resident_queries,
    stored_token_keys,
    stored_token_values,
):
    step_count = resident_queries.shape[0]
    dp = lax.axis_size("dp")
    request_count = prompt_lengths.shape[0]
    full, width = prompt_keys.shape[1:]
    query_width = new_queries.shape[2]
    half = full // 2
    bf16, f32, i32 = jnp.bfloat16, jnp.float32, jnp.int32
    swap = [(0, 1), (1, 0)]
    shape = jax.ShapeDtypeStruct
    dma = pltpu.SemaphoreType.DMA
    roomy = pltpu.CompilerParams(vmem_limit_bytes=44 << 20)

    pk, pv = prompt_keys[0], prompt_values[0]
    xk, xv = lax.ppermute(pk, "side", swap), lax.ppermute(pv, "side", swap)

    most = full // UNIT
    ring_units = 2 * most + (LAG + 1) * PER
    steps_max = -(-request_count * most // PER) + LAG * dp + PEEL + ENDS[-1] + LAG
    wide = -(-steps_max * PER // 128) * 128
    slots = shape((CAP * half, width), bf16)
    table = pl.pallas_call(
        functools.partial(plan_kernel, dp, half, ring_units),
        out_shape=shape((8, wide), i32),
        in_specs=[SM, SM, VM, VM],
        out_specs=VM,
        compiler_params=pltpu.CompilerParams(vmem_limit_bytes=58 << 20),
    )(prompt_lengths, jnp.reshape(assignment, (request_count,)), pk, pv)
    last = table[4, 0]

    message = shape((2, MESSAGE, width), bf16)
    pool_shape = shape((2, max(2 * full + ring_units * UNIT, POOL_ROWS), width), bf16)
    first = pl.pallas_call(
        functools.partial(first_kernel, dp),
        out_shape=message,
        in_specs=[SM, SM] + [VM] * 4,
        out_specs=VM,
        compiler_params=roomy,
    )(table, prompt_lengths, pk, pv, xk, xv)

    tied = lax.optimization_barrier((table, first))
    pool, second, out_k, out_v = pl.pallas_call(
        functools.partial(pool_kernel, dp),
        out_shape=(pool_shape, message, slots, slots),
        in_specs=[SM, SM] + [VM] * 4,
        out_specs=[HBM, VM, HBM, HBM],
        scratch_shapes=[
            pltpu.VMEM((half, width), bf16), pltpu.VMEM((2, 2, full, width), bf16),
            dma((2, CAP)), dma((2, 2)), dma((2,)), dma((2, 2, half // UNIT)),
        ],
        compiler_params=roomy,
    )(tied[0], prompt_lengths, pk, pv, xk, xv)

    held = lax.optimization_barrier((new_queries, second))[0]
    rows = step_count * query_width // HEAD_WIDTH
    resident_shape = shape((step_count, query_width), bf16)
    new_shape = shape((step_count, request_count, query_width), bf16)
    part, own_out, resident_out, new_out = pl.pallas_call(
        functools.partial(attention_kernel, dp),
        out_shape=(shape((rows, 3 * HEAD_WIDTH), f32), shape((rows, HEAD_WIDTH), f32), resident_shape, new_shape),
        in_specs=[SM, SM] + [VM] * 10,
        out_specs=[VM, VM, HBM, HBM],
        scratch_shapes=[pltpu.VMEM((step_count * query_width // width, HEAD_WIDTH), f32)],
        compiler_params=roomy,
    )(
        resident_lengths, prompt_lengths,
        resident_queries[:, 0], stored_keys[0], stored_values[0], stored_token_keys[:, 0], stored_token_values[:, 0],
        held, pk, pv, incoming_token_keys, incoming_token_values,
    )

    hops = [(i, i + 1) for i in range(dp - 1)] + [(dp + i + 1, dp + i) for i in range(dp - 1)]

    def cross(send):
        return lax.ppermute(send, ("side", "dp"), hops)

    def mirror(got):
        return lax.ppermute(got, "side", swap)

    def place(t, got, mirrored, pool, out_k, out_v, lay):
        news = [message] if lay else []
        first_kept = len(news)
        mirrors = [] if mirrored is None else [mirrored]

        def kernel(table, now, got, *refs):
            refs = list(refs)
            mirrored = refs.pop(0) if mirrors else None
            send = refs.pop(3) if lay else None
            step_kernel(table, now, got, mirrored, *refs[:3], send, *refs[3:])

        kept = 3 + len(mirrors)
        outs = pl.pallas_call(
            kernel,
            out_shape=(*news, pool_shape, slots, slots),
            in_specs=[SM, SM, VM] + [VM] * len(mirrors) + [HBM] * 3,
            out_specs=[VM] * len(news) + [HBM] * 3,
            scratch_shapes=[dma((PER,)), dma((PER, 2)), dma((PER, 2)), dma((PER,))],
            input_output_aliases={kept + i: first_kept + i for i in range(3)},
            compiler_params=roomy,
        )(table, jnp.full((1,), t, i32), got, *mirrors, pool, out_k, out_v)
        return outs if lay else (None, *outs)

    def finish(t, mirrored, out_k, out_v):
        return pl.pallas_call(
            last_kernel,
            out_shape=(slots, slots),
            in_specs=[SM, SM, VM, HBM, HBM],
            out_specs=[HBM, HBM],
            scratch_shapes=[dma((PER, 2))],
            input_output_aliases={3: 0, 4: 1},
            compiler_params=roomy,
        )(table, jnp.full((1,), t, i32), mirrored, out_k, out_v)

    def advance(count, state):
        t, got, a, mirrored, pool, out_k, out_v = state
        for i in range(count):
            coming = cross(a)
            a, pool, out_k, out_v = place(t + i, got, mirrored, pool, out_k, out_v, True)
            got, mirrored = coming, mirror(got)
        return t + count, got, a, mirrored, pool, out_k, out_v

    part_other = lax.ppermute(part, "side", swap)
    pair = lax.ppermute(own_out, "side", swap)
    got, part_other, pair = lax.optimization_barrier((cross(first), part_other, pair))
    state = advance(PEEL - 2, (0, got, second, None, pool, out_k, out_v))
    both, _ = lax.optimization_barrier((jnp.stack([own_out, pair]), state[2]))
    others = [lax.ppermute(both, "dp", [(z, (z + x) % dp) for z in range(dp)]) for x in range(1, dp)]
    state = advance(1, state)
    others, _ = lax.optimization_barrier((others, state[2]))

    def lay_out():
        return pl.pallas_call(
            functools.partial(finish_kernel, dp, step_count),
            out_shape=(resident_shape, new_shape),
            in_specs=[VM] * (3 + dp),
            out_specs=[VM, VM],
            scratch_shapes=[pltpu.VMEM((rows, HEAD_WIDTH), f32)],
            compiler_params=pltpu.CompilerParams(vmem_limit_bytes=8 << 20),
        )(part, part_other, own_out, pair, *others)

    a = state[2]
    t, got, _, mirrored, pool, out_k, out_v = state
    left = jnp.maximum(last - PEEL, 0)
    crowd = max(min(2 * (d + 1), CAP * (dp - 1 - d)) for d in range(dp - 1))
    if -(-crowd * most // PER) + LAG * (dp - 2) > PEEL + ENDS[-1]:
        left, (t, got, a, mirrored, pool, out_k, out_v) = lax.while_loop(
            lambda state: state[0] > ENDS[-1],
            lambda state: (state[0] - TURN, advance(TURN, state[1])),
            (left, (jnp.asarray(t, i32), got, a, mirrored, pool, out_k, out_v)),
        )

    def end(count, state):
        _, pool, out_k, out_v, _, _ = state
        now = [got, a, mirrored]
        resident_out, new_out = lay_out()
        for i in range(count + 1):
            arrived, message, passed = now
            coming = cross(message) if i < count else None
            message, pool, out_k, out_v = place(t + i, arrived, passed, pool, out_k, out_v, i + 1 < count)
            now = [coming, message, mirror(arrived)]
        out_k, out_v = finish(t + count + 1, now[2], out_k, out_v)
        return jnp.full((), -1, i32), pool, out_k, out_v, resident_out, new_out

    state = (left, pool, out_k, out_v, resident_out, new_out)
    for lower, count in zip((-1, *ENDS), ENDS):
        state = lax.while_loop(
            lambda state, lower=lower, count=count: (state[0] > lower) & (state[0] <= count),
            functools.partial(end, count), state,
        )
    _, _, out_k, out_v, resident_out, new_out = state
    out_k, out_v = (out.reshape(CAP, half, width) for out in (out_k, out_v))
    return (resident_out[:, None, :], new_out, out_k, out_v)


def solution(mesh):
    placed = (
        P(("side", "dp"), None, "tp"),
        P(("side", "dp"), None, "tp"),
        P(),
        P(),
        P(None, None, "tp"),
        P(None, None, "tp"),
        P(None, None, "tp"),
        P("dp", "side", "tp"),
        P("dp", "side", "tp"),
        P("dp"),
        P(None, "dp", "tp"),
        P(None, "dp", "tp"),
        P(None, "dp", "tp"),
    )
    return jax.shard_map(
        body,
        mesh=mesh,
        in_specs=placed,
        out_specs=(
            P(None, "dp", "tp"),
            P(None, None, "tp"),
            P("dp", "side", "tp"),
            P("dp", "side", "tp"),
        ),
        check_vma=False,
    )
```

```python
import functools

import jax
import jax.numpy as jnp
from jax import lax
from jax.experimental import pallas as pl
from jax.experimental.pallas import tpu as pltpu
from jax.sharding import PartitionSpec as P

HEAD_WIDTH = 128
CAP = 4
UNIT = 128
PER = 6
MESSAGE = UNIT * PER
PEEL = 6
ENDS = (0, 1, 2, 3, 4, 5, 7, 9)
TURN = 3
POOL_ROWS = 22528
LAG = 2
LOW = -1e30

HBM = pl.BlockSpec(memory_space=pltpu.HBM)
VM = pl.BlockSpec(memory_space=pltpu.VMEM)
SM = pl.BlockSpec(memory_space=pltpu.SMEM)


def attend(q, q_rows, k_ref, v_ref, tk, tv, first, length, tokens_on, emit):
    steps = q.shape[0]
    keys, width = k_ref.shape
    heads_kv = width // HEAD_WIDTH
    members = q.shape[1] // width
    rows = members * steps
    scale = HEAD_WIDTH ** -0.5
    for kv in range(heads_kv):
        lanes = slice(kv * HEAD_WIDTH, (kv + 1) * HEAD_WIDTH)
        for g in range(members):
            at = (kv * members + g) * HEAD_WIDTH
            q_rows[g * steps:(g + 1) * steps, :] = q[:, at:at + HEAD_WIDTH]
        q32 = q_rows[...]
        scores = lax.dot_general(
            q32.astype(jnp.bfloat16), k_ref[:, lanes], (((1,), (1,)), ((), ())), preferred_element_type=jnp.float32
        ) * scale
        usable = first + lax.broadcasted_iota(jnp.int32, (rows, keys), 1) < length
        scores = jnp.where(usable, scores, LOW)
        row_step = lax.rem(lax.broadcasted_iota(jnp.int32, (rows, 1), 0), steps)
        top = jnp.max(scores, axis=1, keepdims=True)
        extra = []
        for n in range(steps):
            s = jnp.sum(q32 * tk[n:n + 1, lanes], axis=1, keepdims=True) * scale
            on = (row_step >= n) & tokens_on
            s = jnp.where(on, s, LOW)
            extra.append((on, s))
            top = jnp.maximum(top, s)
        weight = jnp.where(usable, jnp.exp(scores - top), 0.0)
        total = jnp.sum(weight, axis=1, keepdims=True)
        acc = lax.dot_general(
            weight.astype(jnp.bfloat16), v_ref[:, lanes], (((1,), (0,)), ((), ())), preferred_element_type=jnp.float32
        )
        for n, (on, s) in enumerate(extra):
            w = jnp.where(on, jnp.exp(s - top), 0.0)
            total = total + w
            acc = acc + w.astype(jnp.bfloat16).astype(jnp.float32) * tv[n:n + 1, lanes]
        emit(kv, top, total, acc)


def attention_kernel(
    dp, resident_length, lengths, rq, rk, rv, rtk, rtv, nq, nk, nv, ntk, ntv, part, own_out, resident, new, q_rows
):
    side = lax.axis_index("side")
    owner = side * dp + lax.axis_index("dp")
    steps = rq.shape[0]
    keys, width = rk.shape
    rows = steps * rq.shape[1] // width
    f32 = jnp.float32

    def emit_part(kv, top, total, acc):
        at = slice(kv * rows, (kv + 1) * rows)
        part[at, 0:HEAD_WIDTH] = acc
        part[at, HEAD_WIDTH:2 * HEAD_WIDTH] = jnp.broadcast_to(top, (rows, HEAD_WIDTH))
        part[at, 2 * HEAD_WIDTH:] = jnp.broadcast_to(total, (rows, HEAD_WIDTH))

    attend(
        rq[...].astype(f32), q_rows, rk, rv, rtk[...].astype(f32), rtv[...].astype(f32),
        side * keys, resident_length[0], side == 1, emit_part,
    )

    def own(ref):
        picked = []
        for n in range(steps):
            block = ref[n].astype(f32)
            here = lax.broadcasted_iota(jnp.int32, block.shape, 0) == owner
            picked.append(jnp.sum(jnp.where(here, block, 0.0), axis=0, keepdims=True))
        return jnp.concatenate(picked, axis=0)

    def emit_out(kv, top, total, acc):
        own_out[kv * rows:(kv + 1) * rows, :] = acc / total

    attend(own(nq), q_rows, nk, nv, own(ntk), own(ntv), 0, lengths[owner], side >= 0, emit_out)


def finish_kernel(dp, steps, a, b, own, pair, *refs):
    *others, resident, new, o_rows = refs
    w = HEAD_WIDTH
    heads = resident.shape[1] // w
    top = jnp.maximum(a[:, w:2 * w], b[:, w:2 * w])
    ga = jnp.exp(a[:, w:2 * w] - top)
    gb = jnp.exp(b[:, w:2 * w] - top)
    o_rows[...] = (a[:, 0:w] * ga + b[:, 0:w] * gb) / (a[:, 2 * w:] * ga + b[:, 2 * w:] * gb)
    for h in range(heads):
        resident[:, h * w:(h + 1) * w] = o_rows[h * steps:(h + 1) * steps, :].astype(resident.dtype)
    side, me = lax.axis_index("side"), lax.axis_index("dp")
    count = 2 * dp
    blocks = [own, pair] + [other.at[y] for other in others for y in range(2)]
    places = [
        lax.bitwise_xor(side, y) * dp + lax.rem(me - x + dp, dp) for x in range(dp) for y in range(2)
    ]
    at_row = lax.broadcasted_iota(jnp.int32, (count, w), 0)
    for n in range(steps):
        for h in range(heads):
            k = h * steps + n
            block = jnp.zeros((count, w), jnp.float32)
            for place, source in zip(places, blocks):
                block = jnp.where(at_row == place, source[k:k + 1, :], block)
            new[n, :, h * w:(h + 1) * w] = block.astype(new.dtype)


def units_at(start):
    return pl.ds(pl.multiple_of(start, UNIT), UNIT)


def last_unit(length):
    return (length + UNIT - 1) // UNIT * UNIT - UNIT


def mask_unit(ref, first, length):
    row = lax.broadcasted_iota(jnp.int32, (UNIT, ref.shape[1]), 0)
    block = ref[units_at(first), :]
    ref[units_at(first), :] = jnp.where(first + row < length, block, jnp.zeros_like(block))


def plan_kernel(dp, half, ring_units, lengths, goal, pk, pv, table):
    side, me = lax.axis_index("side"), lax.axis_index("dp")
    f32 = jnp.float32
    full = 2 * half
    count = lengths.shape[0]
    wide = table.shape[1]
    id_row = lax.broadcasted_iota(jnp.int32, (count, count), 1).astype(f32)
    id_col = lax.broadcasted_iota(jnp.int32, (count, count), 0).astype(f32)
    eye = id_row == id_col

    def col(row):
        return jnp.sum(jnp.where(eye, jnp.broadcast_to(row, (count, count)), 0.0), axis=1, keepdims=True)

    def spread(scalars):
        row = jnp.zeros((1, count), jnp.int32)
        lane = lax.broadcasted_iota(jnp.int32, (1, count), 1)
        for r in range(count):
            row = jnp.where(lane == r, scalars[r], row)
        return row.astype(f32)

    ids = id_row[0:1]
    late = jnp.where(ids >= dp, 1.0, 0.0)
    src0 = ids - dp * late
    goal0 = spread(goal)
    side_f, me_f = side.astype(f32), me.astype(f32)
    units = jnp.floor((spread(lengths) + (UNIT - 1)) * (1.0 / UNIT))
    units_col, late_col, goal0_col, src0_col = col(units), col(late), col(goal0), col(src0)
    slot = jnp.sum(jnp.where((goal0_col == goal0) & (id_col < id_row), 1.0, 0.0), axis=0, keepdims=True)
    slot_col = col(slot)
    time = lax.broadcasted_iota(jnp.int32, (1, wide), 1).astype(f32)
    here_col = jnp.where(late_col == side_f, 0.0, 1.0)
    steps = jnp.zeros((1, 1), f32)
    sends, passes, ends = [], [], []
    for flip in (False, True):
        turned = (lambda x: dp - 1 - x) if flip else (lambda x: x)
        s, g, m, s_col, g_col = turned(src0), turned(goal0), turned(me_f), turned(src0_col), turned(goal0_col)
        crosses, bases, times = [], [], []
        for d in range(dp - 1):
            cross = (s <= d) & (g > d)
            cross_col = (s_col <= d) & (g_col > d)
            ready = jnp.zeros((1, count), f32)
            if d > 0:
                ready = jnp.where(s == d, 0.0, times[-1] + LAG * PER)
            ready_col = col(ready)
            ahead = (ready_col < ready) | (
                (ready_col == ready) & ((g_col > g) | ((g_col == g) & (id_col < id_row)))
            )
            base = jnp.sum(jnp.where(ahead & cross_col, units_col, 0.0), axis=0, keepdims=True)
            slack = jnp.where((ahead | eye) & cross_col, ready_col - col(base), 0.0)
            start = base + jnp.max(slack, axis=0, keepdims=True)
            end = jnp.max(jnp.where(cross, start + units, 0.0), axis=1, keepdims=True)
            steps = jnp.maximum(steps, jnp.floor((end + (PER - 1)) * (1.0 / PER)))
            crosses.append(cross)
            bases.append(base)
            times.append(start)

        def at(link):
            base, start, used = (jnp.zeros((1, count), f32) for _ in range(3))
            for d in range(dp - 1):
                base = jnp.where(link == d, bases[d], base)
                start = jnp.where(link == d, times[d], start)
                used = jnp.where(link == d, jnp.where(crosses[d], units, 0.0), used)
            return col(base), col(start), col(used)

        def ring_row(p):
            return (p - ring_units * jnp.floor((p + 0.5) * (1.0 / ring_units))) * UNIT

        def pick(hit, value):
            return jnp.sum(jnp.where(hit, value + 1.0, 0.0), axis=0, keepdims=True) - 1.0

        base, start, used = at(m)
        c = time - start
        hit = (c >= 0) & (c < used)
        own = here_col * full + c * UNIT
        sends.append(jnp.maximum(pick(hit, jnp.where(s_col == m, own, 2 * full + ring_row(base + c))), 0.0))
        _, start, used = at(m - 1)
        c = time - start
        hit = (c >= 0) & (c < used)
        passes.append(pick(hit & (g_col != m), 2 * full + ring_row(base + c)))
        row = c * UNIT - half * side_f
        ends.append(pick(hit & (g_col == m) & (row >= 0) & (row < half), slot_col * half + row))
    right = side_f == 0.0
    for r, row in enumerate((
        jnp.where(right, sends[0], sends[1]), jnp.where(right, passes[0], passes[1]),
        jnp.where(right, ends[0], ends[1]), jnp.where(right, ends[1], ends[0]),
    )):
        table[r:r + 1, :] = row.astype(jnp.int32)
    stay = jnp.where((src0 == me_f) & (goal0 == me_f), slot + 1.0, 0.0)
    home = [
        jnp.sum(jnp.where(late == which, stay, 0.0), axis=1, keepdims=True) - 1.0 for which in (side_f, 1.0 - side_f)
    ]
    last = jnp.where(time == 0, steps, jnp.where(time == 1, home[0], home[1]))
    table[4:5, :] = last.astype(jnp.int32)
    table[5:8, :] = jnp.zeros((3, wide), jnp.int32)


def first_kernel(dp, table, lengths, pk, pv, xk, xv, send):
    side, me = lax.axis_index("side"), lax.axis_index("dp")
    full = pk.shape[0]
    for j, pair in enumerate(((pk, pv), (xk, xv))):
        length = lengths[lax.bitwise_xor(side, j) * dp + me]
        last = last_unit(length)
        for i in range(PER):
            row = table[0, i] - j * full

            @pl.when((row >= 0) & (row < full))
            def _():
                for n in range(2):
                    send[n, i * UNIT:(i + 1) * UNIT, :] = pair[n][units_at(row), :]

            @pl.when(row == last)
            def _():
                for n in range(2):
                    mask_unit(send.at[n, i * UNIT:(i + 1) * UNIT], 0, length - last)


def pool_kernel(
    dp, table, lengths, pk, pv, xk, xv, pool, send, out_k, out_v, blank, stage, fill_sem, load_sem, pool_sem, home_sem
):
    side, me = lax.axis_index("side"), lax.axis_index("dp")
    full = xk.shape[0]
    half = full // 2
    loads = [
        pltpu.make_async_copy(a, stage.at[j, n], load_sem.at[j, n])
        for j, pair in enumerate(((pk, pv), (xk, xv))) for n, a in enumerate(pair)
    ]
    for copy in loads:
        copy.start()
    blank[...] = jnp.zeros_like(blank)
    fills = [
        pltpu.make_async_copy(blank, out.at[pl.ds(slot * half, half)], fill_sem.at[i, slot])
        for i, out in enumerate((out_k, out_v)) for slot in range(CAP)
    ]
    for fill in fills:
        fill.start()
    stores, homes = [], []
    for j in range(2):
        length = lengths[lax.bitwise_xor(side, j) * dp + me]
        last = last_unit(length)
        for n in range(2):
            loads[2 * j + n].wait()
            mask_unit(stage.at[j, n], last, length)
        store = pltpu.make_async_copy(stage.at[j], pool.at[:, pl.ds(j * full, full)], pool_sem.at[j])
        store.start()
        stores.append(store)
        slot = table[4, 1 + j]
        count = jnp.where(slot >= 0, jnp.clip((last + UNIT - side * half) // UNIT, 0, half // UNIT), 0)

        def home(u, wait, j=j, slot=slot):
            for n, out in enumerate((out_k, out_v)):
                copy = pltpu.make_async_copy(
                    stage.at[j, n, units_at(side * half + u * UNIT)], out.at[units_at(slot * half + u * UNIT)],
                    home_sem.at[j, n, u],
                )
                copy.wait() if wait else copy.start()

        homes.append((count, home))
    for fill in fills:
        fill.wait()
    for count, home in homes:
        pl.loop(0, count)(functools.partial(home, wait=False))
    for i in range(PER):
        code = table[0, PER + i]
        j = jnp.clip(code // full, 0, 1)
        row = jnp.clip(code - j * full, 0, full - UNIT)
        for n in range(2):
            send[n, i * UNIT:(i + 1) * UNIT, :] = stage[j, n, units_at(row), :]
    for count, home in homes:
        pl.loop(0, count)(functools.partial(home, wait=True))
    for store in stores:
        store.wait()


def end_copies(table, t, row, take, out_k, out_v, sem):
    copies = []
    for i in range(PER):
        code = table[row, t * PER + i]
        to = units_at(jnp.maximum(code, 0))
        copies.append((code >= 0, [
            pltpu.make_async_copy(take.at[n, pl.ds(i * UNIT, UNIT)], out.at[to], sem.at[i, n])
            for n, out in enumerate((out_k, out_v))
        ]))
    return copies


def when_all(copies, act):
    @pl.when(functools.reduce(jnp.logical_or, [on for on, _ in copies]))
    def _():
        for on, group in copies:
            @pl.when(on)
            def _():
                for copy in group:
                    act(copy)


def step_kernel(
    table, now, got, mirrored, pool_in, ok, ov, send, pool, out_k, out_v, pass_sem, got_sem, mirror_sem, send_sem
):
    t = now[0]
    passes = []
    for i in range(PER):
        code = table[1, t * PER + i]
        to = pool.at[:, units_at(jnp.maximum(code, 0))]
        passes.append((code >= 0, [pltpu.make_async_copy(got.at[:, pl.ds(i * UNIT, UNIT)], to, pass_sem.at[i])]))
    when_all(passes, lambda copy: copy.start())
    when_all(passes, lambda copy: copy.wait())
    lay = []
    if send is not None:
        lay = [
            pltpu.make_async_copy(
                pool.at[:, units_at(table[0, (t + LAG) * PER + i])], send.at[:, pl.ds(i * UNIT, UNIT)], send_sem.at[i]
            )
            for i in range(PER)
        ]
    for copy in lay:
        copy.start()
    ends = [end_copies(table, t, 2, got, out_k, out_v, got_sem)]
    if mirrored is not None:
        ends.append(end_copies(table, t - 1, 3, mirrored, out_k, out_v, mirror_sem))
    for copies in ends:
        when_all(copies, lambda copy: copy.start())
    for copy in lay:
        copy.wait()
    for copies in ends:
        when_all(copies, lambda copy: copy.wait())


def last_kernel(table, now, mirrored, ok, ov, out_k, out_v, sem):
    ends = end_copies(table, now[0] - 1, 3, mirrored, out_k, out_v, sem)
    when_all(ends, lambda copy: copy.start())
    when_all(ends, lambda copy: copy.wait())


def body(
    prompt_keys,
    prompt_values,
    prompt_lengths,
    assignment,
    new_queries,
    incoming_token_keys,
    incoming_token_values,
    stored_keys,
    stored_values,
    resident_lengths,
    resident_queries,
    stored_token_keys,
    stored_token_values,
):
    step_count = resident_queries.shape[0]
    dp = lax.axis_size("dp")
    request_count = prompt_lengths.shape[0]
    full, width = prompt_keys.shape[1:]
    query_width = new_queries.shape[2]
    half = full // 2
    bf16, f32, i32 = jnp.bfloat16, jnp.float32, jnp.int32
    swap = [(0, 1), (1, 0)]
    shape = jax.ShapeDtypeStruct
    dma = pltpu.SemaphoreType.DMA
    roomy = pltpu.CompilerParams(vmem_limit_bytes=44 << 20)

    pk, pv = prompt_keys[0], prompt_values[0]
    xk, xv = lax.ppermute(pk, "side", swap), lax.ppermute(pv, "side", swap)

    most = full // UNIT
    ring_units = 2 * most + (LAG + 1) * PER
    steps_max = -(-request_count * most // PER) + LAG * dp + PEEL + ENDS[-1] + LAG
    wide = -(-steps_max * PER // 128) * 128
    slots = shape((CAP * half, width), bf16)
    table = pl.pallas_call(
        functools.partial(plan_kernel, dp, half, ring_units),
        out_shape=shape((8, wide), i32),
        in_specs=[SM, SM, VM, VM],
        out_specs=VM,
        compiler_params=pltpu.CompilerParams(vmem_limit_bytes=58 << 20),
    )(prompt_lengths, jnp.reshape(assignment, (request_count,)), pk, pv)
    last = table[4, 0]

    message = shape((2, MESSAGE, width), bf16)
    pool_shape = shape((2, max(2 * full + ring_units * UNIT, POOL_ROWS), width), bf16)
    first = pl.pallas_call(
        functools.partial(first_kernel, dp),
        out_shape=message,
        in_specs=[SM, SM] + [VM] * 4,
        out_specs=VM,
        compiler_params=roomy,
    )(table, prompt_lengths, pk, pv, xk, xv)

    tied = lax.optimization_barrier((table, first))
    pool, second, out_k, out_v = pl.pallas_call(
        functools.partial(pool_kernel, dp),
        out_shape=(pool_shape, message, slots, slots),
        in_specs=[SM, SM] + [VM] * 4,
        out_specs=[HBM, VM, HBM, HBM],
        scratch_shapes=[
            pltpu.VMEM((half, width), bf16), pltpu.VMEM((2, 2, full, width), bf16),
            dma((2, CAP)), dma((2, 2)), dma((2,)), dma((2, 2, half // UNIT)),
        ],
        compiler_params=roomy,
    )(tied[0], prompt_lengths, pk, pv, xk, xv)

    held = lax.optimization_barrier((new_queries, second))[0]
    rows = step_count * query_width // HEAD_WIDTH
    resident_shape = shape((step_count, query_width), bf16)
    new_shape = shape((step_count, request_count, query_width), bf16)
    part, own_out, resident_out, new_out = pl.pallas_call(
        functools.partial(attention_kernel, dp),
        out_shape=(shape((rows, 3 * HEAD_WIDTH), f32), shape((rows, HEAD_WIDTH), f32), resident_shape, new_shape),
        in_specs=[SM, SM] + [VM] * 10,
        out_specs=[VM, VM, HBM, HBM],
        scratch_shapes=[pltpu.VMEM((step_count * query_width // width, HEAD_WIDTH), f32)],
        compiler_params=roomy,
    )(
        resident_lengths, prompt_lengths,
        resident_queries[:, 0], stored_keys[0], stored_values[0], stored_token_keys[:, 0], stored_token_values[:, 0],
        held, pk, pv, incoming_token_keys, incoming_token_values,
    )

    hops = [(i, i + 1) for i in range(dp - 1)] + [(dp + i + 1, dp + i) for i in range(dp - 1)]

    def cross(send):
        return lax.ppermute(send, ("side", "dp"), hops)

    def mirror(got):
        return lax.ppermute(got, "side", swap)

    def place(t, got, mirrored, pool, out_k, out_v, lay):
        news = [message] if lay else []
        first_kept = len(news)
        mirrors = [] if mirrored is None else [mirrored]

        def kernel(table, now, got, *refs):
            refs = list(refs)
            mirrored = refs.pop(0) if mirrors else None
            send = refs.pop(3) if lay else None
            step_kernel(table, now, got, mirrored, *refs[:3], send, *refs[3:])

        kept = 3 + len(mirrors)
        outs = pl.pallas_call(
            kernel,
            out_shape=(*news, pool_shape, slots, slots),
            in_specs=[SM, SM, VM] + [VM] * len(mirrors) + [HBM] * 3,
            out_specs=[VM] * len(news) + [HBM] * 3,
            scratch_shapes=[dma((PER,)), dma((PER, 2)), dma((PER, 2)), dma((PER,))],
            input_output_aliases={kept + i: first_kept + i for i in range(3)},
            compiler_params=roomy,
        )(table, jnp.full((1,), t, i32), got, *mirrors, pool, out_k, out_v)
        return outs if lay else (None, *outs)

    def finish(t, mirrored, out_k, out_v):
        return pl.pallas_call(
            last_kernel,
            out_shape=(slots, slots),
            in_specs=[SM, SM, VM, HBM, HBM],
            out_specs=[HBM, HBM],
            scratch_shapes=[dma((PER, 2))],
            input_output_aliases={3: 0, 4: 1},
            compiler_params=roomy,
        )(table, jnp.full((1,), t, i32), mirrored, out_k, out_v)

    def advance(count, state):
        t, got, a, mirrored, pool, out_k, out_v = state
        for i in range(count):
            coming = cross(a)
            a, pool, out_k, out_v = place(t + i, got, mirrored, pool, out_k, out_v, True)
            got, mirrored = coming, mirror(got)
        return t + count, got, a, mirrored, pool, out_k, out_v

    part_other = lax.ppermute(part, "side", swap)
    pair = lax.ppermute(own_out, "side", swap)
    got, part_other, pair = lax.optimization_barrier((cross(first), part_other, pair))
    state = advance(PEEL - 2, (0, got, second, None, pool, out_k, out_v))
    both, _ = lax.optimization_barrier((jnp.stack([own_out, pair]), state[2]))
    others = [lax.ppermute(both, "dp", [(z, (z + x) % dp) for z in range(dp)]) for x in range(1, dp)]
    state = advance(1, state)
    others, _ = lax.optimization_barrier((others, state[2]))

    def lay_out():
        return pl.pallas_call(
            functools.partial(finish_kernel, dp, step_count),
            out_shape=(resident_shape, new_shape),
            in_specs=[VM] * (3 + dp),
            out_specs=[VM, VM],
            scratch_shapes=[pltpu.VMEM((rows, HEAD_WIDTH), f32)],
            compiler_params=pltpu.CompilerParams(vmem_limit_bytes=8 << 20),
        )(part, part_other, own_out, pair, *others)

    a = state[2]
    t, got, _, mirrored, pool, out_k, out_v = state
    left = jnp.maximum(last - PEEL, 0)
    crowd = max(min(2 * (d + 1), CAP * (dp - 1 - d)) for d in range(dp - 1))
    if -(-crowd * most // PER) + LAG * (dp - 2) > PEEL + ENDS[-1]:
        left, (t, got, a, mirrored, pool, out_k, out_v) = lax.while_loop(
            lambda state: state[0] > ENDS[-1],
            lambda state: (state[0] - TURN, advance(TURN, state[1])),
            (left, (jnp.asarray(t, i32), got, a, mirrored, pool, out_k, out_v)),
        )

    def end(count, state):
        _, pool, out_k, out_v, _, _ = state
        now = [got, a, mirrored]
        resident_out, new_out = lay_out()
        for i in range(count + 1):
            arrived, message, passed = now
            coming = cross(message) if i < count else None
            message, pool, out_k, out_v = place(t + i, arrived, passed, pool, out_k, out_v, i + 1 < count)
            if i < count:
                coming, out_k, resident_out = lax.optimization_barrier((coming, out_k, resident_out))
            now = [coming, message, mirror(arrived)]
        out_k, out_v = finish(t + count + 1, now[2], out_k, out_v)
        return jnp.full((), -1, i32), pool, out_k, out_v, resident_out, new_out

    state = (left, pool, out_k, out_v, resident_out, new_out)
    for lower, count in zip((-1, *ENDS), ENDS):
        state = lax.while_loop(
            lambda state, lower=lower, count=count: (state[0] > lower) & (state[0] <= count),
            functools.partial(end, count), state,
        )
    _, _, out_k, out_v, resident_out, new_out = state
    out_k, out_v = (out.reshape(CAP, half, width) for out in (out_k, out_v))
    return (resident_out[:, None, :], new_out, out_k, out_v)


def solution(mesh):
    placed = (
        P(("side", "dp"), None, "tp"),
        P(("side", "dp"), None, "tp"),
        P(),
        P(),
        P(None, None, "tp"),
        P(None, None, "tp"),
        P(None, None, "tp"),
        P("dp", "side", "tp"),
        P("dp", "side", "tp"),
        P("dp"),
        P(None, "dp", "tp"),
        P(None, "dp", "tp"),
        P(None, "dp", "tp"),
    )
    return jax.shard_map(
        body,
        mesh=mesh,
        in_specs=placed,
        out_specs=(
            P(None, "dp", "tp"),
            P(None, None, "tp"),
            P("dp", "side", "tp"),
            P("dp", "side", "tp"),
        ),
        check_vma=False,
    )
```

```python
import functools

import jax
import jax.numpy as jnp
from jax import lax
from jax.experimental import pallas as pl
from jax.experimental.pallas import tpu as pltpu
from jax.sharding import PartitionSpec as P

HEAD_WIDTH = 128
CAP = 4
UNIT = 128
PER = 6
MESSAGE = UNIT * PER
PEEL = 6
ENDS = (0, 1, 2, 3, 4, 5, 7, 9)
TURN = 3
POOL_ROWS = 22528
LAG = 2
LOW = -1e30

HBM = pl.BlockSpec(memory_space=pltpu.HBM)
VM = pl.BlockSpec(memory_space=pltpu.VMEM)
SM = pl.BlockSpec(memory_space=pltpu.SMEM)


def attend(q, q_rows, k_ref, v_ref, tk, tv, first, length, tokens_on, emit):
    steps = q.shape[0]
    keys, width = k_ref.shape
    heads_kv = width // HEAD_WIDTH
    members = q.shape[1] // width
    rows = members * steps
    scale = HEAD_WIDTH ** -0.5
    for kv in range(heads_kv):
        lanes = slice(kv * HEAD_WIDTH, (kv + 1) * HEAD_WIDTH)
        for g in range(members):
            at = (kv * members + g) * HEAD_WIDTH
            q_rows[g * steps:(g + 1) * steps, :] = q[:, at:at + HEAD_WIDTH]
        q32 = q_rows[...]
        scores = lax.dot_general(
            q32.astype(jnp.bfloat16), k_ref[:, lanes], (((1,), (1,)), ((), ())), preferred_element_type=jnp.float32
        ) * scale
        usable = first + lax.broadcasted_iota(jnp.int32, (rows, keys), 1) < length
        scores = jnp.where(usable, scores, LOW)
        row_step = lax.rem(lax.broadcasted_iota(jnp.int32, (rows, 1), 0), steps)
        top = jnp.max(scores, axis=1, keepdims=True)
        extra = []
        for n in range(steps):
            s = jnp.sum(q32 * tk[n:n + 1, lanes], axis=1, keepdims=True) * scale
            on = (row_step >= n) & tokens_on
            s = jnp.where(on, s, LOW)
            extra.append((on, s))
            top = jnp.maximum(top, s)
        weight = jnp.where(usable, jnp.exp(scores - top), 0.0)
        total = jnp.sum(weight, axis=1, keepdims=True)
        acc = lax.dot_general(
            weight.astype(jnp.bfloat16), v_ref[:, lanes], (((1,), (0,)), ((), ())), preferred_element_type=jnp.float32
        )
        for n, (on, s) in enumerate(extra):
            w = jnp.where(on, jnp.exp(s - top), 0.0)
            total = total + w
            acc = acc + w.astype(jnp.bfloat16).astype(jnp.float32) * tv[n:n + 1, lanes]
        emit(kv, top, total, acc)


def attention_kernel(
    dp, resident_length, lengths, rq, rk, rv, rtk, rtv, nq, nk, nv, ntk, ntv, part, own_out, resident, new, q_rows
):
    side = lax.axis_index("side")
    owner = side * dp + lax.axis_index("dp")
    steps = rq.shape[0]
    keys, width = rk.shape
    rows = steps * rq.shape[1] // width
    f32 = jnp.float32

    def emit_part(kv, top, total, acc):
        at = slice(kv * rows, (kv + 1) * rows)
        part[at, 0:HEAD_WIDTH] = acc
        part[at, HEAD_WIDTH:2 * HEAD_WIDTH] = jnp.broadcast_to(top, (rows, HEAD_WIDTH))
        part[at, 2 * HEAD_WIDTH:] = jnp.broadcast_to(total, (rows, HEAD_WIDTH))

    attend(
        rq[...].astype(f32), q_rows, rk, rv, rtk[...].astype(f32), rtv[...].astype(f32),
        side * keys, resident_length[0], side == 1, emit_part,
    )

    def own(ref):
        picked = []
        for n in range(steps):
            block = ref[n].astype(f32)
            here = lax.broadcasted_iota(jnp.int32, block.shape, 0) == owner
            picked.append(jnp.sum(jnp.where(here, block, 0.0), axis=0, keepdims=True))
        return jnp.concatenate(picked, axis=0)

    def emit_out(kv, top, total, acc):
        own_out[kv * rows:(kv + 1) * rows, :] = acc / total

    attend(own(nq), q_rows, nk, nv, own(ntk), own(ntv), 0, lengths[owner], side >= 0, emit_out)


def finish_kernel(dp, steps, a, b, own, pair, *refs):
    *others, resident, new, o_rows = refs
    w = HEAD_WIDTH
    heads = resident.shape[1] // w
    top = jnp.maximum(a[:, w:2 * w], b[:, w:2 * w])
    ga = jnp.exp(a[:, w:2 * w] - top)
    gb = jnp.exp(b[:, w:2 * w] - top)
    o_rows[...] = (a[:, 0:w] * ga + b[:, 0:w] * gb) / (a[:, 2 * w:] * ga + b[:, 2 * w:] * gb)
    for h in range(heads):
        resident[:, h * w:(h + 1) * w] = o_rows[h * steps:(h + 1) * steps, :].astype(resident.dtype)
    side, me = lax.axis_index("side"), lax.axis_index("dp")
    count = 2 * dp
    blocks = [own, pair] + [other.at[y] for other in others for y in range(2)]
    places = [
        lax.bitwise_xor(side, y) * dp + lax.rem(me - x + dp, dp) for x in range(dp) for y in range(2)
    ]
    at_row = lax.broadcasted_iota(jnp.int32, (count, w), 0)
    for n in range(steps):
        for h in range(heads):
            k = h * steps + n
            block = jnp.zeros((count, w), jnp.float32)
            for place, source in zip(places, blocks):
                block = jnp.where(at_row == place, source[k:k + 1, :], block)
            new[n, :, h * w:(h + 1) * w] = block.astype(new.dtype)


def units_at(start):
    return pl.ds(pl.multiple_of(start, UNIT), UNIT)


def last_unit(length):
    return (length + UNIT - 1) // UNIT * UNIT - UNIT


def mask_unit(ref, first, length):
    row = lax.broadcasted_iota(jnp.int32, (UNIT, ref.shape[1]), 0)
    block = ref[units_at(first), :]
    ref[units_at(first), :] = jnp.where(first + row < length, block, jnp.zeros_like(block))


def plan_kernel(dp, half, ring_units, lengths, goal, pk, pv, table):
    side, me = lax.axis_index("side"), lax.axis_index("dp")
    f32 = jnp.float32
    full = 2 * half
    count = lengths.shape[0]
    wide = table.shape[1]
    id_row = lax.broadcasted_iota(jnp.int32, (count, count), 1).astype(f32)
    id_col = lax.broadcasted_iota(jnp.int32, (count, count), 0).astype(f32)
    eye = id_row == id_col

    def col(row):
        return jnp.sum(jnp.where(eye, jnp.broadcast_to(row, (count, count)), 0.0), axis=1, keepdims=True)

    def spread(scalars):
        row = jnp.zeros((1, count), jnp.int32)
        lane = lax.broadcasted_iota(jnp.int32, (1, count), 1)
        for r in range(count):
            row = jnp.where(lane == r, scalars[r], row)
        return row.astype(f32)

    ids = id_row[0:1]
    late = jnp.where(ids >= dp, 1.0, 0.0)
    src0 = ids - dp * late
    goal0 = spread(goal)
    side_f, me_f = side.astype(f32), me.astype(f32)
    units = jnp.floor((spread(lengths) + (UNIT - 1)) * (1.0 / UNIT))
    units_col, late_col, goal0_col, src0_col = col(units), col(late), col(goal0), col(src0)
    slot = jnp.sum(jnp.where((goal0_col == goal0) & (id_col < id_row), 1.0, 0.0), axis=0, keepdims=True)
    slot_col = col(slot)
    time = lax.broadcasted_iota(jnp.int32, (1, wide), 1).astype(f32)
    here_col = jnp.where(late_col == side_f, 0.0, 1.0)
    steps = jnp.zeros((1, 1), f32)
    sends, passes, ends = [], [], []
    for flip in (False, True):
        turned = (lambda x: dp - 1 - x) if flip else (lambda x: x)
        s, g, m, s_col, g_col = turned(src0), turned(goal0), turned(me_f), turned(src0_col), turned(goal0_col)
        crosses, bases, times = [], [], []
        for d in range(dp - 1):
            cross = (s <= d) & (g > d)
            cross_col = (s_col <= d) & (g_col > d)
            ready = jnp.zeros((1, count), f32)
            if d > 0:
                ready = jnp.where(s == d, 0.0, times[-1] + LAG * PER)
            ready_col = col(ready)
            ahead = (ready_col < ready) | (
                (ready_col == ready) & ((g_col > g) | ((g_col == g) & (id_col < id_row)))
            )
            base = jnp.sum(jnp.where(ahead & cross_col, units_col, 0.0), axis=0, keepdims=True)
            slack = jnp.where((ahead | eye) & cross_col, ready_col - col(base), 0.0)
            start = base + jnp.max(slack, axis=0, keepdims=True)
            end = jnp.max(jnp.where(cross, start + units, 0.0), axis=1, keepdims=True)
            steps = jnp.maximum(steps, jnp.floor((end + (PER - 1)) * (1.0 / PER)))
            crosses.append(cross)
            bases.append(base)
            times.append(start)

        def at(link):
            base, start, used = (jnp.zeros((1, count), f32) for _ in range(3))
            for d in range(dp - 1):
                base = jnp.where(link == d, bases[d], base)
                start = jnp.where(link == d, times[d], start)
                used = jnp.where(link == d, jnp.where(crosses[d], units, 0.0), used)
            return col(base), col(start), col(used)

        def ring_row(p):
            return (p - ring_units * jnp.floor((p + 0.5) * (1.0 / ring_units))) * UNIT

        def pick(hit, value):
            return jnp.sum(jnp.where(hit, value + 1.0, 0.0), axis=0, keepdims=True) - 1.0

        base, start, used = at(m)
        c = time - start
        hit = (c >= 0) & (c < used)
        own = here_col * full + c * UNIT
        sends.append(jnp.maximum(pick(hit, jnp.where(s_col == m, own, 2 * full + ring_row(base + c))), 0.0))
        _, start, used = at(m - 1)
        c = time - start
        hit = (c >= 0) & (c < used)
        passes.append(pick(hit & (g_col != m), 2 * full + ring_row(base + c)))
        row = c * UNIT - half * side_f
        ends.append(pick(hit & (g_col == m) & (row >= 0) & (row < half), slot_col * half + row))
    right = side_f == 0.0
    for r, row in enumerate((
        jnp.where(right, sends[0], sends[1]), jnp.where(right, passes[0], passes[1]),
        jnp.where(right, ends[0], ends[1]), jnp.where(right, ends[1], ends[0]),
    )):
        table[r:r + 1, :] = row.astype(jnp.int32)
    stay = jnp.where((src0 == me_f) & (goal0 == me_f), slot + 1.0, 0.0)
    home = [
        jnp.sum(jnp.where(late == which, stay, 0.0), axis=1, keepdims=True) - 1.0 for which in (side_f, 1.0 - side_f)
    ]
    last = jnp.where(time == 0, steps, jnp.where(time == 1, home[0], home[1]))
    table[4:5, :] = last.astype(jnp.int32)
    table[5:8, :] = jnp.zeros((3, wide), jnp.int32)


def first_kernel(dp, table, lengths, pk, pv, xk, xv, send):
    side, me = lax.axis_index("side"), lax.axis_index("dp")
    full = pk.shape[0]
    for j, pair in enumerate(((pk, pv), (xk, xv))):
        length = lengths[lax.bitwise_xor(side, j) * dp + me]
        last = last_unit(length)
        for i in range(PER):
            row = table[0, i] - j * full

            @pl.when((row >= 0) & (row < full))
            def _():
                for n in range(2):
                    send[n, i * UNIT:(i + 1) * UNIT, :] = pair[n][units_at(row), :]

            @pl.when(row == last)
            def _():
                for n in range(2):
                    mask_unit(send.at[n, i * UNIT:(i + 1) * UNIT], 0, length - last)


def pool_kernel(
    dp, table, lengths, pk, pv, xk, xv, pool, send, out_k, out_v, blank, stage, fill_sem, load_sem, pool_sem, home_sem
):
    side, me = lax.axis_index("side"), lax.axis_index("dp")
    full = xk.shape[0]
    half = full // 2
    loads = [
        pltpu.make_async_copy(a, stage.at[j, n], load_sem.at[j, n])
        for j, pair in enumerate(((pk, pv), (xk, xv))) for n, a in enumerate(pair)
    ]
    for copy in loads:
        copy.start()
    blank[...] = jnp.zeros_like(blank)
    fills = [
        pltpu.make_async_copy(blank, out.at[pl.ds(slot * half, half)], fill_sem.at[i, slot])
        for i, out in enumerate((out_k, out_v)) for slot in range(CAP)
    ]
    for fill in fills:
        fill.start()
    stores, homes = [], []
    for j in range(2):
        length = lengths[lax.bitwise_xor(side, j) * dp + me]
        last = last_unit(length)
        for n in range(2):
            loads[2 * j + n].wait()
            mask_unit(stage.at[j, n], last, length)
        store = pltpu.make_async_copy(stage.at[j], pool.at[:, pl.ds(j * full, full)], pool_sem.at[j])
        store.start()
        stores.append(store)
        slot = table[4, 1 + j]
        count = jnp.where(slot >= 0, jnp.clip((last + UNIT - side * half) // UNIT, 0, half // UNIT), 0)

        def home(u, wait, j=j, slot=slot):
            for n, out in enumerate((out_k, out_v)):
                copy = pltpu.make_async_copy(
                    stage.at[j, n, units_at(side * half + u * UNIT)], out.at[units_at(slot * half + u * UNIT)],
                    home_sem.at[j, n, u],
                )
                copy.wait() if wait else copy.start()

        homes.append((count, home))
    for fill in fills:
        fill.wait()
    for count, home in homes:
        pl.loop(0, count)(functools.partial(home, wait=False))
    for i in range(PER):
        code = table[0, PER + i]
        j = jnp.clip(code // full, 0, 1)
        row = jnp.clip(code - j * full, 0, full - UNIT)
        for n in range(2):
            send[n, i * UNIT:(i + 1) * UNIT, :] = stage[j, n, units_at(row), :]
    for count, home in homes:
        pl.loop(0, count)(functools.partial(home, wait=True))
    for store in stores:
        store.wait()


def end_copies(table, t, row, take, out_k, out_v, sem):
    copies = []
    for i in range(PER):
        code = table[row, t * PER + i]
        to = units_at(jnp.maximum(code, 0))
        copies.append((code >= 0, [
            pltpu.make_async_copy(take.at[n, pl.ds(i * UNIT, UNIT)], out.at[to], sem.at[i, n])
            for n, out in enumerate((out_k, out_v))
        ]))
    return copies


def when_all(copies, act):
    @pl.when(functools.reduce(jnp.logical_or, [on for on, _ in copies]))
    def _():
        for on, group in copies:
            @pl.when(on)
            def _():
                for copy in group:
                    act(copy)


def step_kernel(
    table, now, got, mirrored, pool_in, ok, ov, send, pool, out_k, out_v, pass_sem, got_sem, mirror_sem, send_sem
):
    t = now[0]
    passes = []
    for i in range(PER):
        code = table[1, t * PER + i]
        to = pool.at[:, units_at(jnp.maximum(code, 0))]
        passes.append((code >= 0, [pltpu.make_async_copy(got.at[:, pl.ds(i * UNIT, UNIT)], to, pass_sem.at[i])]))
    when_all(passes, lambda copy: copy.start())
    when_all(passes, lambda copy: copy.wait())
    lay = []
    if send is not None:
        rows = [table[0, (t + LAG) * PER + i] for i in range(PER)]
        whole = functools.reduce(jnp.logical_and, [rows[i] == rows[0] + i * UNIT for i in range(1, PER)])
        lay = [
            (whole, [pltpu.make_async_copy(
                pool.at[:, pl.ds(pl.multiple_of(rows[0], UNIT), MESSAGE)], send, send_sem.at[0]
            )]),
            (jnp.logical_not(whole), [
                pltpu.make_async_copy(pool.at[:, units_at(row)], send.at[:, pl.ds(i * UNIT, UNIT)], send_sem.at[i])
                for i, row in enumerate(rows)
            ]),
        ]
        when_all(lay, lambda copy: copy.start())
    ends = [end_copies(table, t, 2, got, out_k, out_v, got_sem)]
    if mirrored is not None:
        ends.append(end_copies(table, t - 1, 3, mirrored, out_k, out_v, mirror_sem))
    for copies in ends:
        when_all(copies, lambda copy: copy.start())
    if lay:
        when_all(lay, lambda copy: copy.wait())
    for copies in ends:
        when_all(copies, lambda copy: copy.wait())


def last_kernel(table, now, mirrored, ok, ov, out_k, out_v, sem):
    ends = end_copies(table, now[0] - 1, 3, mirrored, out_k, out_v, sem)
    when_all(ends, lambda copy: copy.start())
    when_all(ends, lambda copy: copy.wait())


def body(
    prompt_keys,
    prompt_values,
    prompt_lengths,
    assignment,
    new_queries,
    incoming_token_keys,
    incoming_token_values,
    stored_keys,
    stored_values,
    resident_lengths,
    resident_queries,
    stored_token_keys,
    stored_token_values,
):
    step_count = resident_queries.shape[0]
    dp = lax.axis_size("dp")
    request_count = prompt_lengths.shape[0]
    full, width = prompt_keys.shape[1:]
    query_width = new_queries.shape[2]
    half = full // 2
    bf16, f32, i32 = jnp.bfloat16, jnp.float32, jnp.int32
    swap = [(0, 1), (1, 0)]
    shape = jax.ShapeDtypeStruct
    dma = pltpu.SemaphoreType.DMA
    roomy = pltpu.CompilerParams(vmem_limit_bytes=44 << 20)

    pk, pv = prompt_keys[0], prompt_values[0]
    xk, xv = lax.ppermute(pk, "side", swap), lax.ppermute(pv, "side", swap)

    most = full // UNIT
    ring_units = 2 * most + (LAG + 1) * PER
    steps_max = -(-request_count * most // PER) + LAG * dp + PEEL + ENDS[-1] + LAG
    wide = -(-steps_max * PER // 128) * 128
    slots = shape((CAP * half, width), bf16)
    table = pl.pallas_call(
        functools.partial(plan_kernel, dp, half, ring_units),
        out_shape=shape((8, wide), i32),
        in_specs=[SM, SM, VM, VM],
        out_specs=VM,
        compiler_params=pltpu.CompilerParams(vmem_limit_bytes=58 << 20),
    )(prompt_lengths, jnp.reshape(assignment, (request_count,)), pk, pv)
    last = table[4, 0]

    message = shape((2, MESSAGE, width), bf16)
    pool_shape = shape((2, max(2 * full + ring_units * UNIT, POOL_ROWS), width), bf16)
    first = pl.pallas_call(
        functools.partial(first_kernel, dp),
        out_shape=message,
        in_specs=[SM, SM] + [VM] * 4,
        out_specs=VM,
        compiler_params=roomy,
    )(table, prompt_lengths, pk, pv, xk, xv)

    tied = lax.optimization_barrier((table, first))
    pool, second, out_k, out_v = pl.pallas_call(
        functools.partial(pool_kernel, dp),
        out_shape=(pool_shape, message, slots, slots),
        in_specs=[SM, SM] + [VM] * 4,
        out_specs=[HBM, VM, HBM, HBM],
        scratch_shapes=[
            pltpu.VMEM((half, width), bf16), pltpu.VMEM((2, 2, full, width), bf16),
            dma((2, CAP)), dma((2, 2)), dma((2,)), dma((2, 2, half // UNIT)),
        ],
        compiler_params=roomy,
    )(tied[0], prompt_lengths, pk, pv, xk, xv)

    held = lax.optimization_barrier((new_queries, second))[0]
    rows = step_count * query_width // HEAD_WIDTH
    resident_shape = shape((step_count, query_width), bf16)
    new_shape = shape((step_count, request_count, query_width), bf16)
    part, own_out, resident_out, new_out = pl.pallas_call(
        functools.partial(attention_kernel, dp),
        out_shape=(shape((rows, 3 * HEAD_WIDTH), f32), shape((rows, HEAD_WIDTH), f32), resident_shape, new_shape),
        in_specs=[SM, SM] + [VM] * 10,
        out_specs=[VM, VM, HBM, HBM],
        scratch_shapes=[pltpu.VMEM((step_count * query_width // width, HEAD_WIDTH), f32)],
        compiler_params=roomy,
    )(
        resident_lengths, prompt_lengths,
        resident_queries[:, 0], stored_keys[0], stored_values[0], stored_token_keys[:, 0], stored_token_values[:, 0],
        held, pk, pv, incoming_token_keys, incoming_token_values,
    )

    hops = [(i, i + 1) for i in range(dp - 1)] + [(dp + i + 1, dp + i) for i in range(dp - 1)]

    def cross(send):
        return lax.ppermute(send, ("side", "dp"), hops)

    def mirror(got):
        return lax.ppermute(got, "side", swap)

    def place(t, got, mirrored, pool, out_k, out_v, lay):
        news = [message] if lay else []
        first_kept = len(news)
        mirrors = [] if mirrored is None else [mirrored]

        def kernel(table, now, got, *refs):
            refs = list(refs)
            mirrored = refs.pop(0) if mirrors else None
            send = refs.pop(3) if lay else None
            step_kernel(table, now, got, mirrored, *refs[:3], send, *refs[3:])

        kept = 3 + len(mirrors)
        outs = pl.pallas_call(
            kernel,
            out_shape=(*news, pool_shape, slots, slots),
            in_specs=[SM, SM, VM] + [VM] * len(mirrors) + [HBM] * 3,
            out_specs=[VM] * len(news) + [HBM] * 3,
            scratch_shapes=[dma((PER,)), dma((PER, 2)), dma((PER, 2)), dma((PER,))],
            input_output_aliases={kept + i: first_kept + i for i in range(3)},
            compiler_params=roomy,
        )(table, jnp.full((1,), t, i32), got, *mirrors, pool, out_k, out_v)
        return outs if lay else (None, *outs)

    def finish(t, mirrored, out_k, out_v):
        return pl.pallas_call(
            last_kernel,
            out_shape=(slots, slots),
            in_specs=[SM, SM, VM, HBM, HBM],
            out_specs=[HBM, HBM],
            scratch_shapes=[dma((PER, 2))],
            input_output_aliases={3: 0, 4: 1},
            compiler_params=roomy,
        )(table, jnp.full((1,), t, i32), mirrored, out_k, out_v)

    def advance(count, state):
        t, got, a, mirrored, pool, out_k, out_v = state
        for i in range(count):
            coming = cross(a)
            a, pool, out_k, out_v = place(t + i, got, mirrored, pool, out_k, out_v, True)
            got, mirrored = coming, mirror(got)
        return t + count, got, a, mirrored, pool, out_k, out_v

    part_other = lax.ppermute(part, "side", swap)
    pair = lax.ppermute(own_out, "side", swap)
    got, part_other, pair = lax.optimization_barrier((cross(first), part_other, pair))
    state = advance(PEEL - 2, (0, got, second, None, pool, out_k, out_v))
    both, _ = lax.optimization_barrier((jnp.stack([own_out, pair]), state[2]))
    others = [lax.ppermute(both, "dp", [(z, (z + x) % dp) for z in range(dp)]) for x in range(1, dp)]
    state = advance(1, state)
    others, _ = lax.optimization_barrier((others, state[2]))

    def lay_out():
        return pl.pallas_call(
            functools.partial(finish_kernel, dp, step_count),
            out_shape=(resident_shape, new_shape),
            in_specs=[VM] * (3 + dp),
            out_specs=[VM, VM],
            scratch_shapes=[pltpu.VMEM((rows, HEAD_WIDTH), f32)],
            compiler_params=pltpu.CompilerParams(vmem_limit_bytes=8 << 20),
        )(part, part_other, own_out, pair, *others)

    a = state[2]
    t, got, _, mirrored, pool, out_k, out_v = state
    left = jnp.maximum(last - PEEL, 0)
    crowd = max(min(2 * (d + 1), CAP * (dp - 1 - d)) for d in range(dp - 1))
    if -(-crowd * most // PER) + LAG * (dp - 2) > PEEL + ENDS[-1]:
        left, (t, got, a, mirrored, pool, out_k, out_v) = lax.while_loop(
            lambda state: state[0] > ENDS[-1],
            lambda state: (state[0] - TURN, advance(TURN, state[1])),
            (left, (jnp.asarray(t, i32), got, a, mirrored, pool, out_k, out_v)),
        )

    def end(count, state):
        _, pool, out_k, out_v, _, _ = state
        now = [got, a, mirrored]
        resident_out, new_out = lay_out()
        for i in range(count + 1):
            arrived, message, passed = now
            coming = cross(message) if i < count else None
            message, pool, out_k, out_v = place(t + i, arrived, passed, pool, out_k, out_v, i + 1 < count)
            if i < count:
                coming, out_k, resident_out = lax.optimization_barrier((coming, out_k, resident_out))
            now = [coming, message, mirror(arrived)]
        out_k, out_v = finish(t + count + 1, now[2], out_k, out_v)
        return jnp.full((), -1, i32), pool, out_k, out_v, resident_out, new_out

    state = (left, pool, out_k, out_v, resident_out, new_out)
    for lower, count in zip((-1, *ENDS), ENDS):
        state = lax.while_loop(
            lambda state, lower=lower, count=count: (state[0] > lower) & (state[0] <= count),
            functools.partial(end, count), state,
        )
    _, _, out_k, out_v, resident_out, new_out = state
    out_k, out_v = (out.reshape(CAP, half, width) for out in (out_k, out_v))
    return (resident_out[:, None, :], new_out, out_k, out_v)


def solution(mesh):
    placed = (
        P(("side", "dp"), None, "tp"),
        P(("side", "dp"), None, "tp"),
        P(),
        P(),
        P(None, None, "tp"),
        P(None, None, "tp"),
        P(None, None, "tp"),
        P("dp", "side", "tp"),
        P("dp", "side", "tp"),
        P("dp"),
        P(None, "dp", "tp"),
        P(None, "dp", "tp"),
        P(None, "dp", "tp"),
    )
    return jax.shard_map(
        body,
        mesh=mesh,
        in_specs=placed,
        out_specs=(
            P(None, "dp", "tp"),
            P(None, None, "tp"),
            P("dp", "side", "tp"),
            P("dp", "side", "tp"),
        ),
        check_vma=False,
    )
```
